32 devices in a mesh: group: 2 (over x), seq: 8 (over z, y), fsdp: 2 (over core).
Axes of the slice: x: 2, y: 2, z: 4, core: 2. Of those that a mesh axis runs over, the one named last changes fastest.
Arguments:
- q_img: bfloat16 [2048, 2048], P(('group', 'seq'), 'fsdp'), parts along dimension 0, may hold values from -6 to 6
- k_img: bfloat16 [2048, 2048], P(('group', 'seq'), 'fsdp'), parts along dimension 0, may hold values from -6 to 6
- v_img: bfloat16 [2048, 2048], P(('group', 'seq'), 'fsdp'), parts along dimension 0, may hold values from -6 to 6
- k_txt: bfloat16 [1024, 2048], P('group', 'fsdp'), parts along dimension 0, may hold values from -6 to 6
- v_txt: bfloat16 [1024, 2048], P('group', 'fsdp'), parts along dimension 0, may hold values from -6 to 6
- out_weight: bfloat16 [3072, 2048], P('seq', 'fsdp'), may hold values from -0.125 to 0.125
- d_out: bfloat16 [2048, 3072], P(('group', 'seq')), parts along dimension 0, may hold values from -12 to 12
Outputs:
- q_grad: bfloat16 [2048, 2048], P(('group', 'seq'), 'fsdp'), parts along dimension 0
- k_grad: bfloat16 [2048, 2048], P(('group', 'seq'), 'fsdp'), parts along dimension 0
- v_grad: bfloat16 [2048, 2048], P(('group', 'seq'), 'fsdp'), parts along dimension 0
- d_weight: float32 [6144, 2048], P(('group', 'seq'), 'fsdp'), parts along dimension 0
The draws below stay inside these ranges and needn't reach their ends.
There are 2 independent parts, one for each index of `group`. The reference program is written for one: setup_inputs(seed, part) draws one part's arguments, and reference() takes and returns one part's arrays. A program takes and returns all parts, laid end to end along the dimension named above; an argument that names none is the same for every part. Nothing has to cross between parts.
All inputs are finite; a program needn't handle non-finite values.
Results may differ from the reference program's by a relative error of at most 0.015.
Values may be sent and summed in bfloat16 or wider, within the bound.
No kernel may reach another device: no remote copies, remote signals or barrier semaphores. Data moves between devices by JAX's collectives and lax.ppermute only.
A program may use at most 128 MiB of HBM per device.

```python
import jax
import jax.numpy as jnp
from jax import lax

D = 3072
HEADS = 16
HD = 128
TXT = 512
TOK = 128
IMG = 1024
N_SEQ = 8


def draw_q_img(key, part):
    key = jax.random.fold_in(key, 3)
    return jnp.clip(1.5 * jax.random.normal(key, (IMG, HEADS * HD), jnp.float32), -6.0, 6.0).astype(jnp.bfloat16)


def draw_k_img(key, part):
    key = jax.random.fold_in(key, 5)
    return jnp.clip(1.5 * jax.random.normal(key, (IMG, HEADS * HD), jnp.float32), -6.0, 6.0).astype(jnp.bfloat16)


def with_spikes(entries, rng, source, target, shards_of, factor):
    owner, partner = [(jnp.arange(entries.shape[dim]) // (entries.shape[dim] // shards_of)).reshape([-1 if axis == dim else 1 for axis in range(entries.ndim)]) for dim in (source, target)]
    chosen = jax.random.permutation(rng, shards_of)[partner]
    strong = (owner == chosen) | (owner == (partner + shards_of // 2) % shards_of)
    return jnp.where(strong, factor * entries, entries)


def levels(key, dims, pieces, low, largest):
    def one(position, parts):
        steps = jax.random.uniform(jax.random.fold_in(jax.random.fold_in(key, 6), position), (parts,), jnp.float32, low / len(pieces), largest / len(pieces))
        return jnp.repeat(jnp.exp(steps), dims[position] // parts).reshape((-1,) + (1,) * (len(dims) - position - 1))

    factor_of = one(*pieces[0])
    for cut in pieces[1:]:
        factor_of = factor_of * one(*cut)
    return factor_of


def centred(own_key, shape, deviation, limit, cuts=(), kind=jnp.bfloat16):
    gain = levels(own_key, shape, cuts, -0.22, 0.18) if cuts else 1.0
    drawn = jax.random.normal(own_key, shape, jnp.float32) * deviation * gain
    return jnp.minimum(jnp.maximum(drawn, -limit), limit).astype(kind)


def gaussian_with(own_key, shape, spread, bound, cuts, heavy, held_as=jnp.bfloat16):
    values = spread * jax.random.normal(own_key, shape, jnp.float32)
    if cuts:
        values = values * levels(own_key, shape, cuts, -0.22, 0.18)
    return jnp.clip(with_spikes(values, jax.random.fold_in(own_key, 3), *heavy), -bound, bound).astype(held_as)


def setup_inputs(seed: int = 0, part: int = 0) -> dict:
    arg_keys = jax.random.split(jax.random.key(seed), 8)
    own_keys = jax.random.split(jax.random.fold_in(arg_keys[7], part), 8)
    return {
        "q_img": draw_q_img(jax.random.fold_in(jax.random.fold_in(arg_keys[7], part), 71), part),
        "k_img": draw_k_img(jax.random.fold_in(jax.random.fold_in(arg_keys[7], part), 71), part),
        "v_img": centred(own_keys[2], (IMG, HEADS * HD), 1.0, 6.0, ((0, 8), (1, 2))),
        "k_txt": centred(own_keys[3], (TXT, HEADS * HD), 1.5, 6.0, ((1, 2),)),
        "v_txt": centred(own_keys[4], (TXT, HEADS * HD), 1.0, 6.0, ((1, 2),)),
        "out_weight": centred(arg_keys[5], (D, HEADS * HD), (HEADS * HD) ** -0.5, 0.125, ((0, 8), (1, 2))),
        "d_out": gaussian_with(own_keys[6], (IMG, D), 2.0, 12.0, ((0, 8),), (0, 1, 8, 2.0)),
    }


def attend(queries, cotangents, key_rows, value_rows, block_rows):
    score_scale = HD ** -0.5
    query_count = queries.shape[0]
    block_count = query_count // block_rows
    query_blocks = queries.reshape(block_count, block_rows, HD)
    grad_blocks = cotangents.reshape(block_count, block_rows, HD)

    def one_block(accumulated, pair_item):
        query_block, grad_block = pair_item
        scores = jnp.dot(query_block, key_rows.T, preferred_element_type=jnp.float32) * score_scale
        row_max = jnp.max(scores, axis=1, keepdims=True)
        probs = jnp.exp(scores - row_max)
        probs = probs / jnp.sum(probs, axis=1, keepdims=True)
        probs_low = probs.astype(jnp.bfloat16)
        out_rows = jnp.dot(probs_low, value_rows, preferred_element_type=jnp.float32).astype(jnp.bfloat16)
        prob_grad = jnp.dot(grad_block, value_rows.T, preferred_element_type=jnp.float32)
        row_dot = jnp.sum(grad_block.astype(jnp.float32) * out_rows.astype(jnp.float32), axis=1, keepdims=True)
        score_grad = (probs * (prob_grad - row_dot)).astype(jnp.bfloat16)
        query_grad = (jnp.dot(score_grad, key_rows, preferred_element_type=jnp.float32) * score_scale).astype(jnp.bfloat16)
        key_grad = accumulated[0] + jnp.dot(score_grad.T, query_block, preferred_element_type=jnp.float32) * score_scale
        value_grad = accumulated[1] + jnp.dot(probs_low.T, grad_block, preferred_element_type=jnp.float32)
        return (key_grad, value_grad), (query_grad, out_rows)

    empty = jnp.zeros((key_rows.shape[0], HD), jnp.float32)
    (key_grad, value_grad), (query_grad, out_rows) = lax.scan(one_block, (empty, empty), (query_blocks, grad_blocks))
    return query_grad.reshape(query_count, HD), out_rows.reshape(query_count, HD), key_grad, value_grad


def reference(q_img, k_img, v_img, k_txt, v_txt, out_weight, d_out):
    attn_grad = jnp.dot(d_out, out_weight, preferred_element_type=jnp.float32).astype(jnp.bfloat16)
    key_all = jnp.concatenate([k_img, k_txt], axis=0)
    value_all = jnp.concatenate([v_img, v_txt], axis=0)

    def one_head(head_index):
        col_start = head_index * HD

        def column_cut(array_in):
            return lax.dynamic_slice_in_dim(array_in, col_start, HD, 1)

        query_grad, out_rows, key_grad, value_grad = attend(column_cut(q_img), column_cut(attn_grad), column_cut(key_all), column_cut(value_all), min(512, IMG))
        return query_grad, out_rows, key_grad[:IMG].astype(jnp.bfloat16), value_grad[:IMG].astype(jnp.bfloat16)

    query_grad, attn_out, key_grad, value_grad = lax.map(one_head, jnp.arange(HEADS, dtype=jnp.int32))

    def join_heads(stacked):
        return stacked.transpose(1, 0, 2).reshape(stacked.shape[1], HEADS * HD)

    attn_out = join_heads(attn_out)

    def add_part(running, block_index):
        row_block = lax.dynamic_slice_in_dim(d_out, block_index * TOK, TOK, 0)
        out_block = lax.dynamic_slice_in_dim(attn_out, block_index * TOK, TOK, 0)
        part_low = jnp.dot(row_block.T, out_block, preferred_element_type=jnp.float32).astype(jnp.bfloat16)
        part_low = lax.optimization_barrier(part_low)
        return running + part_low.astype(jnp.float32), None

    d_weight, _ = lax.scan(add_part, jnp.zeros((D, HEADS * HD), jnp.float32), jnp.arange(N_SEQ, dtype=jnp.int32))
    return join_heads(query_grad), join_heads(key_grad), join_heads(value_grad), d_weight
```

```python
import functools
import math

import jax
import jax.numpy as jnp
from jax import lax
from jax.experimental import pallas as pl
from jax.experimental.pallas import tpu as pltpu
from jax.sharding import PartitionSpec as P

HD = 128
F32 = jnp.float32
BF16 = jnp.bfloat16
LIMIT = 48 * 1024 * 1024
NT = (((1,), (1,)), ((), ()))


def attend(queries, cotangents, key_rows, value_rows, block_rows):
    score_scale = HD ** (-0.5)
    query_count = queries.shape[0]
    block_count = query_count // block_rows
    query_blocks = queries.reshape(block_count, block_rows, HD)
    grad_blocks = cotangents.reshape(block_count, block_rows, HD)

    def one_block(accumulated, pair_item):
        query_block, grad_block = pair_item
        scores = jnp.dot(query_block, key_rows.T, preferred_element_type=jnp.float32) * score_scale
        row_max = jnp.max(scores, axis=1, keepdims=True)
        probs = jnp.exp(scores - row_max)
        probs = probs / jnp.sum(probs, axis=1, keepdims=True)
        probs_low = probs.astype(jnp.bfloat16)
        out_rows = jnp.dot(probs_low, value_rows, preferred_element_type=jnp.float32).astype(
            jnp.bfloat16
        )
        prob_grad = jnp.dot(grad_block, value_rows.T, preferred_element_type=jnp.float32)
        row_dot = jnp.sum(
            grad_block.astype(jnp.float32) * out_rows.astype(jnp.float32), axis=1, keepdims=True
        )
        score_grad = (probs * (prob_grad - row_dot)).astype(jnp.bfloat16)
        query_grad = (
            jnp.dot(score_grad, key_rows, preferred_element_type=jnp.float32) * score_scale
        ).astype(jnp.bfloat16)
        key_grad = (
            accumulated[0]
            + jnp.dot(score_grad.T, query_block, preferred_element_type=jnp.float32) * score_scale
        )
        value_grad = accumulated[1] + jnp.dot(
            probs_low.T, grad_block, preferred_element_type=jnp.float32
        )
        return ((key_grad, value_grad), (query_grad, out_rows))

    empty = jnp.zeros((key_rows.shape[0], HD), jnp.float32)
    (key_grad, value_grad), (query_grad, out_rows) = lax.scan(
        one_block, (empty, empty), (query_blocks, grad_blocks)
    )
    return (
        query_grad.reshape(query_count, HD),
        out_rows.reshape(query_count, HD),
        key_grad,
        value_grad,
    )


def local_general(q_img, k_img, v_img, k_txt, v_txt, out_weight, d_out):
    rows_here = q_img.shape[0]
    heads_here = q_img.shape[1] // HD
    seq_count = lax.axis_size("seq")
    share_count = seq_count // heads_here
    part_rows = rows_here // share_count
    seq_index = lax.axis_index("seq")
    head_index = seq_index // share_count
    column_cut = d_out
    attn_grad = jnp.dot(
        column_cut,
        lax.all_gather(out_weight, "seq", axis=0, tiled=True),
        preferred_element_type=jnp.float32,
    ).astype(jnp.bfloat16)

    def to_heads(array_in):
        shaped = array_in.reshape(share_count, part_rows, heads_here, HD).transpose(2, 0, 1, 3)
        return shaped.reshape(seq_count, part_rows, HD)

    def whole_heads(array_in):
        shaped = array_in.reshape(rows_here, heads_here, HD).transpose(1, 0, 2)
        shaped = jnp.broadcast_to(shaped[:, None], (heads_here, share_count, rows_here, HD))
        return shaped.reshape(seq_count, rows_here, HD)

    def from_heads(array_in):
        shaped = array_in.reshape(heads_here, share_count, part_rows, HD).transpose(1, 2, 0, 3)
        return shaped.reshape(rows_here, heads_here * HD)

    text_keys = lax.dynamic_slice_in_dim(k_txt, head_index * HD, HD, 1)
    text_values = lax.dynamic_slice_in_dim(v_txt, head_index * HD, HD, 1)
    query_side = jnp.concatenate([to_heads(q_img), to_heads(attn_grad)], axis=2)
    key_side = jnp.concatenate([whole_heads(k_img), whole_heads(v_img)], axis=2)
    packed = jnp.concatenate([query_side, key_side], axis=1)
    received = lax.all_to_all(packed, "seq", split_axis=0, concat_axis=0, tiled=True)
    queries = received[:, :part_rows, :HD].reshape(seq_count * part_rows, HD)
    cotangents = received[:, :part_rows, HD:].reshape(seq_count * part_rows, HD)
    image_keys = received[:, part_rows:, :HD].reshape(seq_count * rows_here, HD)
    image_values = received[:, part_rows:, HD:].reshape(seq_count * rows_here, HD)
    key_rows = jnp.concatenate([image_keys, text_keys], axis=0)
    value_rows = jnp.concatenate([image_values, text_values], axis=0)
    query_grad, out_rows, key_grad, value_grad = attend(
        queries, cotangents, key_rows, value_rows, min(512, queries.shape[0])
    )
    image_count = image_keys.shape[0]
    query_part = (
        jnp.concatenate([query_grad, out_rows], axis=1)
        .astype(jnp.float32)
        .reshape(seq_count, part_rows, 2 * HD)
    )
    key_part = jnp.concatenate([key_grad[:image_count], value_grad[:image_count]], axis=1).reshape(
        seq_count, rows_here, 2 * HD
    )
    returned = lax.all_to_all(
        jnp.concatenate([query_part, key_part], axis=1).astype(jnp.bfloat16),
        "seq",
        split_axis=0,
        concat_axis=0,
        tiled=True,
    ).astype(jnp.float32)
    q_grad = from_heads(returned[:, :part_rows, :HD]).astype(jnp.bfloat16)
    out_tok = from_heads(returned[:, :part_rows, HD:]).astype(jnp.bfloat16)
    summed = jnp.sum(
        returned[:, part_rows:, :].reshape(heads_here, share_count, rows_here, 2 * HD), axis=1
    )
    summed = summed.transpose(1, 0, 2)
    k_grad = summed[:, :, :HD].reshape(rows_here, heads_here * HD).astype(jnp.bfloat16)
    v_grad = summed[:, :, HD:].reshape(rows_here, heads_here * HD).astype(jnp.bfloat16)
    column_cut = d_out
    d_weight = lax.psum_scatter(
        jnp.dot(column_cut.T, out_tok, preferred_element_type=jnp.float32).astype(jnp.bfloat16),
        "seq",
        scatter_dimension=0,
        tiled=True,
    ).astype(jnp.float32)
    return (q_grad, k_grad, v_grad, d_weight)


def call(kernel, outs, args, specs=None, scratch=(), scalars=0, out_specs=None, flops=0, moved=0):
    vmem = pl.BlockSpec(memory_space=pltpu.VMEM)
    if specs is None:
        specs = [vmem] * (len(args) - scalars)
    if out_specs is None:
        out_specs = [vmem] * len(outs)
    return pl.pallas_call(
        kernel,
        out_shape=outs,
        grid_spec=pltpu.PrefetchScalarGridSpec(
            num_scalar_prefetch=scalars,
            grid=(1,),
            in_specs=specs,
            out_specs=out_specs,
            scratch_shapes=list(scratch),
        ),
        compiler_params=pltpu.CompilerParams(vmem_limit_bytes=LIMIT),
        cost_estimate=pl.CostEstimate(flops=flops, bytes_accessed=moved, transcendentals=0),
    )(*args)


def pack_kernel(q_ref, k_ref, v_ref, w_ref, tok_ref, wt_ref):
    heads = tok_ref.shape[0]
    rows = q_ref.shape[0]
    for h in range(heads):
        cols = slice(h * HD, (h + 1) * HD)
        tok_ref[h, 0:rows, :] = q_ref[:, cols]
        tok_ref[h, rows : 2 * rows, :] = k_ref[:, cols]
        tok_ref[h, 2 * rows : 3 * rows, :] = v_ref[:, cols]
        wt_ref[h, :, :] = w_ref[:, cols]


def forward_kernel(me_ref, tok_ref, kt_ref, vt_ref, probs_ref, out_ref, keys, vals_t, *, chunk):
    n, three, _ = tok_ref.shape
    rows = three // 3
    image = n * rows
    text = kt_ref.shape[0]
    keys[0:image, :] = tok_ref[:, rows : 2 * rows, :].reshape(image, HD)
    keys[image : image + text, :] = kt_ref[...]
    vals_t[:, 0:image] = tok_ref[:, 2 * rows : 3 * rows, :].reshape(image, HD).T
    vals_t[:, image : image + text] = vt_ref[...].T
    factor = HD ** (-0.5) * math.log2(math.e)
    per = chunk // rows
    for c in range(image // chunk):
        queries = tok_ref[c * per : (c + 1) * per, 0:rows, :].reshape(chunk, HD)
        scores = lax.dot_general(keys[...], queries, NT, preferred_element_type=F32)
        top = jnp.max(scores, axis=0, keepdims=True)
        weights = jnp.exp2((scores - top) * factor)
        total = jnp.sum(weights, axis=0, keepdims=True)
        low = (weights * (1.0 / total)).astype(BF16)
        probs_ref[:, c * chunk : (c + 1) * chunk] = low
        out_ref[:, c * chunk : (c + 1) * chunk] = jnp.dot(
            vals_t[...], low, preferred_element_type=F32
        ).astype(BF16)


def project_kernel(place_ref, *refs, pieces):
    blocks = refs[: len(pieces)]
    w_ref, out_ref, grad_ref, dw_ref, cot, sems = refs[len(pieces) :]
    n, depth, _ = w_ref.shape
    copies = []
    for i, rows in enumerate(pieces):
        at = pl.multiple_of(place_ref[i], 16)
        copies.append(pltpu.make_async_copy(blocks[i], cot.at[pl.ds(at, rows), :], sems.at[i]))
    for copy in copies:
        copy.start()
    for copy in copies:
        copy.wait()
    weight = w_ref[...].reshape(n * depth, HD)
    step = 256

    @pl.loop(0, cot.shape[0] // step)
    def _(i):
        at = pl.ds(pl.multiple_of(i * step, step), step)
        grad_ref[at, :] = jnp.dot(cot[at, :], weight, preferred_element_type=F32).astype(BF16)

    @pl.loop(0, n)
    def _(i):
        cols = pl.ds(pl.multiple_of(i * depth, depth), depth)
        dw_ref[i] = jnp.dot(out_ref[...], cot[:, cols], preferred_element_type=F32).astype(BF16)


def backward_kernel(
    me_ref, tok_ref, kt_ref, vt_ref, probs_ref, out_ref, grad_ref, send_ref, keys_t, vals, dk, dv, *, chunk
):
    n, three, _ = tok_ref.shape
    rows = three // 3
    image = n * rows
    text = kt_ref.shape[0]
    scale = HD ** (-0.5)
    vals[0:image, :] = tok_ref[:, 2 * rows : 3 * rows, :].reshape(image, HD)
    vals[image : image + text, :] = vt_ref[...]
    keys_t[:, 0:image] = tok_ref[:, rows : 2 * rows, :].reshape(image, HD).T
    keys_t[:, image : image + text] = kt_ref[...].T
    per = chunk // rows
    for c in range(image // chunk):
        span = slice(c * chunk, (c + 1) * chunk)
        grads = grad_ref[span, :]
        queries = tok_ref[c * per : (c + 1) * per, 0:rows, :].reshape(chunk, HD)
        row_dot = jnp.sum(
            grads.astype(F32).T * out_ref[:, span].astype(F32), axis=0, keepdims=True
        )
        prob_grad = lax.dot_general(vals[...], grads, NT, preferred_element_type=F32)
        low = probs_ref[:, span]
        score_grad = (low.astype(F32) * (prob_grad - row_dot)).astype(BF16)
        dq_t = jnp.dot(keys_t[...], score_grad, preferred_element_type=F32) * scale
        send_ref[c * per : (c + 1) * per, 0:rows, :] = dq_t.T.astype(BF16).reshape(per, rows, HD)
        dk_part = jnp.dot(score_grad[0:image, :], queries, preferred_element_type=F32)
        dv_part = jnp.dot(low[0:image, :], grads, preferred_element_type=F32)
        if c == 0:
            dk[...] = dk_part
            dv[...] = dv_part
        else:
            dk[...] += dk_part
            dv[...] += dv_part
    send_ref[:, rows : 2 * rows, :] = (dk[...] * scale).astype(BF16).reshape(n, rows, HD)
    send_ref[:, 2 * rows : 3 * rows, :] = dv[...].astype(BF16).reshape(n, rows, HD)


def unpack_kernel(tok_ref, dw_ref, q_ref, k_ref, v_ref, w_ref):
    heads, three, _ = tok_ref.shape
    rows = three // 3
    for h in range(heads):
        cols = slice(h * HD, (h + 1) * HD)
        q_ref[:, cols] = tok_ref[h, 0:rows, :]
        k_ref[:, cols] = tok_ref[h, rows : 2 * rows, :]
        v_ref[:, cols] = tok_ref[h, 2 * rows : 3 * rows, :]
        w_ref[:, cols] = dw_ref[h].astype(F32).T


def ring_order(n):
    return list(range(0, n, 2)) + list(range(n - 1, 0, -2))


def gather_cotangents(d_out, n):
    rows = d_out.shape[0]
    ring = ring_order(n)
    onward, swap = [], []
    for pos, s in enumerate(ring):
        onward.append((2 * s, 2 * ring[(pos + 1) % n]))
        onward.append((2 * s + 1, 2 * ring[(pos - 1) % n] + 1))
    for s in range(n):
        swap += [(2 * s, 2 * s + 1), (2 * s + 1, 2 * s)]
    axes = ("seq", "fsdp")
    core = lax.axis_index("fsdp")
    position = [0] * n
    for pos, s in enumerate(ring):
        position[s] = pos
    here = jnp.asarray(position, jnp.int32)[lax.axis_index("seq")]
    ring_now = jnp.asarray(ring, jnp.int32)
    sign = 2 * core - 1
    pieces, places = [d_out], [lax.axis_index("seq") * rows]
    held = d_out
    for hop in range(1, n // 2 + 1):
        if hop == n // 2:
            half = rows // 2
            held = jnp.where(core == 0, held[:half], held[half:])
        held = lax.ppermute(held, axes, onward)
        other = lax.ppermute(held, axes, swap)
        mine = ring_now[(here + sign * hop) % n] * rows
        theirs = ring_now[(here - sign * hop) % n] * rows
        if hop == n // 2:
            mine = mine + core * half
            theirs = theirs + (1 - core) * half
        pieces += [held, other]
        places += [mine, theirs]
    return pieces, jnp.stack(places).astype(jnp.int32)


def local(q_img, k_img, v_img, k_txt, v_txt, out_weight, d_out):
    n = lax.axis_size("seq")
    rows, width = q_img.shape
    args = (q_img, k_img, v_img, k_txt, v_txt, out_weight, d_out)
    if width // HD != n or lax.axis_size("fsdp") != 2 or n % 2 or rows % 32:
        return local_general(*args)
    depth = out_weight.shape[0]
    image = n * rows
    text = k_txt.shape[0]
    total = image + text
    chunk = 2 * rows
    shape = jax.ShapeDtypeStruct
    vmem = pl.BlockSpec(memory_space=pltpu.VMEM)

    pieces, places = gather_cotangents(d_out, n)
    tok_out, w_out = call(
        pack_kernel,
        [shape((n, 3 * rows, HD), BF16), shape((n, depth, HD), BF16)],
        [q_img, k_img, v_img, out_weight],
        moved=4 * (3 * rows + depth) * width,
    )
    tok_in = lax.all_to_all(tok_out, "seq", split_axis=0, concat_axis=0, tiled=True)
    w_in = lax.all_to_all(w_out, "seq", split_axis=0, concat_axis=0, tiled=True)

    me = lax.axis_index("seq").astype(jnp.int32)[None]
    text_spec = pl.BlockSpec((text, HD), lambda i, me_ref: (0, me_ref[0]))
    probs, out_t = call(
        functools.partial(forward_kernel, chunk=chunk),
        [shape((total, image), BF16), shape((HD, image), BF16)],
        [me, tok_in, k_txt, v_txt],
        specs=[vmem, text_spec, text_spec],
        scratch=[pltpu.VMEM((total, HD), BF16), pltpu.VMEM((HD, total), BF16)],
        scalars=1,
        flops=4 * total * image * HD,
        moved=4 * total * image,
    )
    grads, dw_out = call(
        functools.partial(project_kernel, pieces=[p.shape[0] for p in pieces]),
        [shape((image, HD), BF16), shape((n, HD, depth), BF16)],
        [places, *pieces, w_in, out_t],
        specs=[pl.BlockSpec(memory_space=pl.ANY)] * len(pieces) + [vmem, vmem],
        scratch=[pltpu.VMEM((image, n * depth), BF16), pltpu.SemaphoreType.DMA((len(pieces),))],
        scalars=1,
        flops=4 * image * n * depth * HD,
        moved=2 * image * n * depth,
    )
    dw_in = lax.all_to_all(dw_out, "seq", split_axis=0, concat_axis=0, tiled=True)
    (grad_out,) = call(
        functools.partial(backward_kernel, chunk=chunk),
        [shape((n, 3 * rows, HD), BF16)],
        [me, tok_in, k_txt, v_txt, probs, out_t, grads],
        specs=[vmem, text_spec, text_spec, vmem, vmem, vmem],
        scratch=[
            pltpu.VMEM((HD, total), BF16),
            pltpu.VMEM((total, HD), BF16),
            pltpu.VMEM((image, HD), F32),
            pltpu.VMEM((image, HD), F32),
        ],
        scalars=1,
        flops=8 * total * image * HD,
        moved=4 * total * image,
    )
    grad_in = lax.all_to_all(grad_out, "seq", split_axis=0, concat_axis=0, tiled=True)
    return call(
        unpack_kernel,
        [shape((rows, width), BF16)] * 3 + [shape((depth, width), F32)],
        [grad_in, dw_in],
        moved=4 * 3 * rows * width + 6 * depth * width,
    )


def solution(mesh):
    in_specs = (
        P(("group", "seq"), "fsdp"),
        P(("group", "seq"), "fsdp"),
        P(("group", "seq"), "fsdp"),
        P("group", "fsdp"),
        P("group", "fsdp"),
        P("seq", "fsdp"),
        P(("group", "seq"), None),
    )
    out_specs = (
        P(("group", "seq"), "fsdp"),
        P(("group", "seq"), "fsdp"),
        P(("group", "seq"), "fsdp"),
        P(("group", "seq"), "fsdp"),
    )
    return jax.shard_map(local, mesh=mesh, in_specs=in_specs, out_specs=out_specs, check_vma=False)
```

```python
import functools
import math

import jax
import jax.numpy as jnp
from jax import lax
from jax.experimental import pallas as pl
from jax.experimental.pallas import tpu as pltpu
from jax.sharding import PartitionSpec as P

HD = 128
F32 = jnp.float32
BF16 = jnp.bfloat16
LIMIT = 60 * 1024 * 1024
NT = (((1,), (1,)), ((), ()))


def attend(queries, cotangents, key_rows, value_rows, block_rows):
    score_scale = HD ** (-0.5)
    query_count = queries.shape[0]
    block_count = query_count // block_rows
    query_blocks = queries.reshape(block_count, block_rows, HD)
    grad_blocks = cotangents.reshape(block_count, block_rows, HD)

    def one_block(accumulated, pair_item):
        query_block, grad_block = pair_item
        scores = jnp.dot(query_block, key_rows.T, preferred_element_type=jnp.float32) * score_scale
        row_max = jnp.max(scores, axis=1, keepdims=True)
        probs = jnp.exp(scores - row_max)
        probs = probs / jnp.sum(probs, axis=1, keepdims=True)
        probs_low = probs.astype(jnp.bfloat16)
        out_rows = jnp.dot(probs_low, value_rows, preferred_element_type=jnp.float32).astype(
            jnp.bfloat16
        )
        prob_grad = jnp.dot(grad_block, value_rows.T, preferred_element_type=jnp.float32)
        row_dot = jnp.sum(
            grad_block.astype(jnp.float32) * out_rows.astype(jnp.float32), axis=1, keepdims=True
        )
        score_grad = (probs * (prob_grad - row_dot)).astype(jnp.bfloat16)
        query_grad = (
            jnp.dot(score_grad, key_rows, preferred_element_type=jnp.float32) * score_scale
        ).astype(jnp.bfloat16)
        key_grad = (
            accumulated[0]
            + jnp.dot(score_grad.T, query_block, preferred_element_type=jnp.float32) * score_scale
        )
        value_grad = accumulated[1] + jnp.dot(
            probs_low.T, grad_block, preferred_element_type=jnp.float32
        )
        return ((key_grad, value_grad), (query_grad, out_rows))

    empty = jnp.zeros((key_rows.shape[0], HD), jnp.float32)
    (key_grad, value_grad), (query_grad, out_rows) = lax.scan(
        one_block, (empty, empty), (query_blocks, grad_blocks)
    )
    return (
        query_grad.reshape(query_count, HD),
        out_rows.reshape(query_count, HD),
        key_grad,
        value_grad,
    )


def local_general(q_img, k_img, v_img, k_txt, v_txt, out_weight, d_out):
    rows_here = q_img.shape[0]
    heads_here = q_img.shape[1] // HD
    seq_count = lax.axis_size("seq")
    share_count = seq_count // heads_here
    part_rows = rows_here // share_count
    seq_index = lax.axis_index("seq")
    head_index = seq_index // share_count
    column_cut = d_out
    attn_grad = jnp.dot(
        column_cut,
        lax.all_gather(out_weight, "seq", axis=0, tiled=True),
        preferred_element_type=jnp.float32,
    ).astype(jnp.bfloat16)

    def to_heads(array_in):
        shaped = array_in.reshape(share_count, part_rows, heads_here, HD).transpose(2, 0, 1, 3)
        return shaped.reshape(seq_count, part_rows, HD)

    def whole_heads(array_in):
        shaped = array_in.reshape(rows_here, heads_here, HD).transpose(1, 0, 2)
        shaped = jnp.broadcast_to(shaped[:, None], (heads_here, share_count, rows_here, HD))
        return shaped.reshape(seq_count, rows_here, HD)

    def from_heads(array_in):
        shaped = array_in.reshape(heads_here, share_count, part_rows, HD).transpose(1, 2, 0, 3)
        return shaped.reshape(rows_here, heads_here * HD)

    text_keys = lax.dynamic_slice_in_dim(k_txt, head_index * HD, HD, 1)
    text_values = lax.dynamic_slice_in_dim(v_txt, head_index * HD, HD, 1)
    query_side = jnp.concatenate([to_heads(q_img), to_heads(attn_grad)], axis=2)
    key_side = jnp.concatenate([whole_heads(k_img), whole_heads(v_img)], axis=2)
    packed = jnp.concatenate([query_side, key_side], axis=1)
    received = lax.all_to_all(packed, "seq", split_axis=0, concat_axis=0, tiled=True)
    queries = received[:, :part_rows, :HD].reshape(seq_count * part_rows, HD)
    cotangents = received[:, :part_rows, HD:].reshape(seq_count * part_rows, HD)
    image_keys = received[:, part_rows:, :HD].reshape(seq_count * rows_here, HD)
    image_values = received[:, part_rows:, HD:].reshape(seq_count * rows_here, HD)
    key_rows = jnp.concatenate([image_keys, text_keys], axis=0)
    value_rows = jnp.concatenate([image_values, text_values], axis=0)
    query_grad, out_rows, key_grad, value_grad = attend(
        queries, cotangents, key_rows, value_rows, min(512, queries.shape[0])
    )
    image_count = image_keys.shape[0]
    query_part = (
        jnp.concatenate([query_grad, out_rows], axis=1)
        .astype(jnp.float32)
        .reshape(seq_count, part_rows, 2 * HD)
    )
    key_part = jnp.concatenate([key_grad[:image_count], value_grad[:image_count]], axis=1).reshape(
        seq_count, rows_here, 2 * HD
    )
    returned = lax.all_to_all(
        jnp.concatenate([query_part, key_part], axis=1).astype(jnp.bfloat16),
        "seq",
        split_axis=0,
        concat_axis=0,
        tiled=True,
    ).astype(jnp.float32)
    q_grad = from_heads(returned[:, :part_rows, :HD]).astype(jnp.bfloat16)
    out_tok = from_heads(returned[:, :part_rows, HD:]).astype(jnp.bfloat16)
    summed = jnp.sum(
        returned[:, part_rows:, :].reshape(heads_here, share_count, rows_here, 2 * HD), axis=1
    )
    summed = summed.transpose(1, 0, 2)
    k_grad = summed[:, :, :HD].reshape(rows_here, heads_here * HD).astype(jnp.bfloat16)
    v_grad = summed[:, :, HD:].reshape(rows_here, heads_here * HD).astype(jnp.bfloat16)
    column_cut = d_out
    d_weight = lax.psum_scatter(
        jnp.dot(column_cut.T, out_tok, preferred_element_type=jnp.float32).astype(jnp.bfloat16),
        "seq",
        scatter_dimension=0,
        tiled=True,
    ).astype(jnp.float32)
    return (q_grad, k_grad, v_grad, d_weight)


def call(kernel, outs, args, specs=None, scratch=(), scalars=0, out_specs=None, flops=0, moved=0):
    vmem = pl.BlockSpec(memory_space=pltpu.VMEM)
    if specs is None:
        specs = [vmem] * (len(args) - scalars)
    if out_specs is None:
        out_specs = [vmem] * len(outs)
    return pl.pallas_call(
        kernel,
        out_shape=outs,
        grid_spec=pltpu.PrefetchScalarGridSpec(
            num_scalar_prefetch=scalars,
            grid=(1,),
            in_specs=specs,
            out_specs=out_specs,
            scratch_shapes=list(scratch),
        ),
        compiler_params=pltpu.CompilerParams(vmem_limit_bytes=LIMIT),
        cost_estimate=pl.CostEstimate(flops=flops, bytes_accessed=moved, transcendentals=0),
    )(*args)


def pack_kernel(q_ref, k_ref, v_ref, w_ref, tok_ref, wt_ref):
    heads = tok_ref.shape[0]
    rows = q_ref.shape[0]
    for h in range(heads):
        cols = slice(h * HD, (h + 1) * HD)
        tok_ref[h, 0:rows, :] = q_ref[:, cols]
        tok_ref[h, rows : 2 * rows, :] = k_ref[:, cols]
        tok_ref[h, 2 * rows : 3 * rows, :] = v_ref[:, cols]
        wt_ref[h, :, :] = w_ref[:, cols]


def forward_kernel(me_ref, tok_ref, kt_ref, vt_ref, probs_ref, out_ref, keys, vals_t, *, chunk):
    n, three, _ = tok_ref.shape
    rows = three // 3
    image = n * rows
    text = kt_ref.shape[0]
    keys[0:image, :] = tok_ref[:, rows : 2 * rows, :].reshape(image, HD)
    keys[image : image + text, :] = kt_ref[...]
    vals_t[:, 0:image] = tok_ref[:, 2 * rows : 3 * rows, :].reshape(image, HD).T
    vals_t[:, image : image + text] = vt_ref[...].T
    factor = HD ** (-0.5) * math.log2(math.e)
    per = chunk // rows
    for c in range(image // chunk):
        queries = tok_ref[c * per : (c + 1) * per, 0:rows, :].reshape(chunk, HD)
        scores = lax.dot_general(keys[...], queries, NT, preferred_element_type=F32)
        top = jnp.max(scores, axis=0, keepdims=True)
        weights = jnp.exp2((scores - top) * factor)
        total = jnp.sum(weights, axis=0, keepdims=True)
        low = (weights * (1.0 / total)).astype(BF16)
        probs_ref[:, c * chunk : (c + 1) * chunk] = low
        out_ref[:, c * chunk : (c + 1) * chunk] = jnp.dot(
            vals_t[...], low, preferred_element_type=F32
        ).astype(BF16)


def ring_order(n):
    return list(range(0, n, 2)) + list(range(n - 1, 0, -2))


def ring_index(position, n):
    position = lax.rem(position + n, n)
    return jnp.where(position < n // 2, 2 * position, 2 * (n - position) - 1)


def piece_places(n, rows):
    me = lax.axis_index("seq")
    core = lax.axis_index("fsdp")
    here = jnp.where(lax.rem(me, 2) == 0, me // 2, n - 1 - me // 2)
    sign = 2 * core - 1
    places = [me * rows]
    for hop in range(1, n // 2 + 1):
        mine = ring_index(here + sign * hop, n) * rows
        theirs = ring_index(here - sign * hop, n) * rows
        if hop == n // 2:
            mine = mine + core * (rows // 2)
            theirs = theirs + (1 - core) * (rows // 2)
        places += [mine, theirs]
    return places


def load_pieces(blocks, cot, sems, n):
    places = piece_places(n, blocks[0].shape[0])
    copies = []
    for i, block in enumerate(blocks):
        rows = block.shape[0]
        at = pl.ds(pl.multiple_of(places[i], 16), rows)
        copies.append(pltpu.make_async_copy(block, cot.at[at, :], sems.at[i]))
    for copy in copies:
        copy.start()
    for copy in copies:
        copy.wait()


def attn_grad_kernel(*refs):
    *blocks, w_ref, grad_ref, cot, sems = refs
    n, depth, _ = w_ref.shape
    load_pieces(blocks, cot, sems, n)
    weight = w_ref[...].reshape(n * depth, HD)
    step = 256

    @pl.loop(0, cot.shape[0] // step)
    def _(i):
        at = pl.ds(pl.multiple_of(i * step, step), step)
        grad_ref[at, :] = jnp.dot(cot[at, :], weight, preferred_element_type=F32).astype(BF16)


def weight_grad_kernel(*refs):
    *blocks, out_ref, dw_ref, cot, sems = refs
    n, _, depth = dw_ref.shape
    load_pieces(blocks, cot, sems, n)

    @pl.loop(0, n)
    def _(i):
        cols = pl.ds(pl.multiple_of(i * depth, depth), depth)
        dw_ref[i] = jnp.dot(out_ref[...], cot[:, cols], preferred_element_type=F32).astype(BF16)


def backward_kernel(
    me_ref, tok_ref, kt_ref, vt_ref, probs_ref, out_ref, grad_ref, send_ref, keys_t, vals, dk, dv, *, chunk
):
    n, three, _ = tok_ref.shape
    rows = three // 3
    image = n * rows
    text = kt_ref.shape[0]
    scale = HD ** (-0.5)
    vals[0:image, :] = tok_ref[:, 2 * rows : 3 * rows, :].reshape(image, HD)
    vals[image : image + text, :] = vt_ref[...]
    keys_t[:, 0:image] = tok_ref[:, rows : 2 * rows, :].reshape(image, HD).T
    keys_t[:, image : image + text] = kt_ref[...].T
    per = chunk // rows
    for c in range(image // chunk):
        span = slice(c * chunk, (c + 1) * chunk)
        grads = grad_ref[span, :]
        queries = tok_ref[c * per : (c + 1) * per, 0:rows, :].reshape(chunk, HD)
        row_dot = jnp.sum(
            grads.astype(F32).T * out_ref[:, span].astype(F32), axis=0, keepdims=True
        )
        prob_grad = lax.dot_general(vals[...], grads, NT, preferred_element_type=F32)
        low = probs_ref[:, span]
        score_grad = (low.astype(F32) * (prob_grad - row_dot)).astype(BF16)
        dq_t = jnp.dot(keys_t[...], score_grad, preferred_element_type=F32) * scale
        send_ref[c * per : (c + 1) * per, 0:rows, :] = dq_t.T.astype(BF16).reshape(per, rows, HD)
        dk_part = jnp.dot(score_grad[0:image, :], queries, preferred_element_type=F32)
        dv_part = jnp.dot(low[0:image, :], grads, preferred_element_type=F32)
        if c == 0:
            dk[...] = dk_part
            dv[...] = dv_part
        else:
            dk[...] += dk_part
            dv[...] += dv_part
    send_ref[:, rows : 2 * rows, :] = (dk[...] * scale).astype(BF16).reshape(n, rows, HD)
    send_ref[:, 2 * rows : 3 * rows, :] = dv[...].astype(BF16).reshape(n, rows, HD)


def unpack_kernel(tok_ref, dw_ref, q_ref, k_ref, v_ref, w_ref):
    heads, three, _ = tok_ref.shape
    rows = three // 3
    for h in range(heads):
        cols = slice(h * HD, (h + 1) * HD)
        q_ref[:, cols] = tok_ref[h, 0:rows, :]
        k_ref[:, cols] = tok_ref[h, rows : 2 * rows, :]
        v_ref[:, cols] = tok_ref[h, 2 * rows : 3 * rows, :]
        w_ref[:, cols] = dw_ref[h].astype(F32).T


def gather_cotangents(d_out, n):
    rows = d_out.shape[0]
    ring = ring_order(n)
    onward, swap = [], []
    for pos, s in enumerate(ring):
        onward.append((2 * s, 2 * ring[(pos + 1) % n]))
        onward.append((2 * s + 1, 2 * ring[(pos - 1) % n] + 1))
        swap += [(2 * s, 2 * s + 1), (2 * s + 1, 2 * s)]
    axes = ("seq", "fsdp")
    pieces = [d_out]
    held = d_out
    for hop in range(1, n // 2 + 1):
        if hop == n // 2:
            half = rows // 2
            held = lax.dynamic_slice_in_dim(held, lax.axis_index("fsdp") * half, half, 0)
        held = lax.ppermute(held, axes, onward)
        pieces += [held, lax.ppermute(held, axes, swap)]
    return pieces


def local(q_img, k_img, v_img, k_txt, v_txt, out_weight, d_out):
    n = lax.axis_size("seq")
    rows, width = q_img.shape
    args = (q_img, k_img, v_img, k_txt, v_txt, out_weight, d_out)
    if width // HD != n or lax.axis_size("fsdp") != 2 or n % 2 or rows % 32:
        return local_general(*args)
    depth = out_weight.shape[0]
    image = n * rows
    text = k_txt.shape[0]
    total = image + text
    chunk = 2 * rows
    shape = jax.ShapeDtypeStruct
    vmem = pl.BlockSpec(memory_space=pltpu.VMEM)

    pieces = gather_cotangents(d_out, n)
    tok_out, w_out = call(
        pack_kernel,
        [shape((n, 3 * rows, HD), BF16), shape((n, depth, HD), BF16)],
        [q_img, k_img, v_img, out_weight],
        moved=4 * (3 * rows + depth) * width,
    )
    tok_in = lax.all_to_all(tok_out, "seq", split_axis=0, concat_axis=0, tiled=True)
    w_in = lax.all_to_all(w_out, "seq", split_axis=0, concat_axis=0, tiled=True)

    me = lax.axis_index("seq").astype(jnp.int32)[None]
    text_spec = pl.BlockSpec((text, HD), lambda i, me_ref: (0, me_ref[0]))
    probs, out_t = call(
        functools.partial(forward_kernel, chunk=chunk),
        [shape((total, image), BF16), shape((HD, image), BF16)],
        [me, tok_in, k_txt, v_txt],
        specs=[vmem, text_spec, text_spec],
        scratch=[pltpu.VMEM((total, HD), BF16), pltpu.VMEM((HD, total), BF16)],
        scalars=1,
        flops=4 * total * image * HD,
        moved=4 * total * image,
    )
    anywhere = [pl.BlockSpec(memory_space=pl.ANY)] * len(pieces)
    landing = [pltpu.VMEM((image, n * depth), BF16), pltpu.SemaphoreType.DMA((len(pieces),))]
    (dw_out,) = call(
        weight_grad_kernel,
        [shape((n, HD, depth), BF16)],
        [*pieces, out_t],
        specs=anywhere + [vmem],
        scratch=landing,
        flops=2 * image * n * depth * HD,
        moved=2 * image * n * depth,
    )
    (grads,) = call(
        attn_grad_kernel,
        [shape((image, HD), BF16)],
        [*pieces, w_in],
        specs=anywhere + [vmem],
        scratch=landing,
        flops=2 * image * n * depth * HD,
        moved=2 * image * n * depth,
    )
    dw_in = lax.all_to_all(dw_out, "seq", split_axis=0, concat_axis=0, tiled=True)
    (grad_out,) = call(
        functools.partial(backward_kernel, chunk=chunk),
        [shape((n, 3 * rows, HD), BF16)],
        [me, tok_in, k_txt, v_txt, probs, out_t, grads],
        specs=[vmem, text_spec, text_spec, vmem, vmem, vmem],
        scratch=[
            pltpu.VMEM((HD, total), BF16),
            pltpu.VMEM((total, HD), BF16),
            pltpu.VMEM((image, HD), F32),
            pltpu.VMEM((image, HD), F32),
        ],
        scalars=1,
        flops=8 * total * image * HD,
        moved=4 * total * image,
    )
    grad_out, dw_in = lax.optimization_barrier((grad_out, dw_in))
    grad_in = lax.all_to_all(grad_out, "seq", split_axis=0, concat_axis=0, tiled=True)
    return tuple(call(
        unpack_kernel,
        [shape((rows, width), BF16)] * 3 + [shape((depth, width), F32)],
        [grad_in, dw_in],
        moved=4 * 3 * rows * width + 6 * depth * width,
    ))


def solution(mesh):
    in_specs = (
        P(("group", "seq"), "fsdp"),
        P(("group", "seq"), "fsdp"),
        P(("group", "seq"), "fsdp"),
        P("group", "fsdp"),
        P("group", "fsdp"),
        P("seq", "fsdp"),
        P(("group", "seq"), None),
    )
    out_specs = (
        P(("group", "seq"), "fsdp"),
        P(("group", "seq"), "fsdp"),
        P(("group", "seq"), "fsdp"),
        P(("group", "seq"), "fsdp"),
    )
    return jax.shard_map(local, mesh=mesh, in_specs=in_specs, out_specs=out_specs, check_vma=False)
```

```python
import functools
import math

import jax
import jax.numpy as jnp
from jax import lax
from jax.experimental import pallas as pl
from jax.experimental.pallas import tpu as pltpu
from jax.sharding import PartitionSpec as P

HD = 128
F32 = jnp.float32
BF16 = jnp.bfloat16
LIMIT = 60 * 1024 * 1024
NT = (((1,), (1,)), ((), ()))


def attend(queries, cotangents, key_rows, value_rows, block_rows):
    score_scale = HD ** (-0.5)
    query_count = queries.shape[0]
    block_count = query_count // block_rows
    query_blocks = queries.reshape(block_count, block_rows, HD)
    grad_blocks = cotangents.reshape(block_count, block_rows, HD)

    def one_block(accumulated, pair_item):
        query_block, grad_block = pair_item
        scores = jnp.dot(query_block, key_rows.T, preferred_element_type=jnp.float32) * score_scale
        row_max = jnp.max(scores, axis=1, keepdims=True)
        probs = jnp.exp(scores - row_max)
        probs = probs / jnp.sum(probs, axis=1, keepdims=True)
        probs_low = probs.astype(jnp.bfloat16)
        out_rows = jnp.dot(probs_low, value_rows, preferred_element_type=jnp.float32).astype(
            jnp.bfloat16
        )
        prob_grad = jnp.dot(grad_block, value_rows.T, preferred_element_type=jnp.float32)
        row_dot = jnp.sum(
            grad_block.astype(jnp.float32) * out_rows.astype(jnp.float32), axis=1, keepdims=True
        )
        score_grad = (probs * (prob_grad - row_dot)).astype(jnp.bfloat16)
        query_grad = (
            jnp.dot(score_grad, key_rows, preferred_element_type=jnp.float32) * score_scale
        ).astype(jnp.bfloat16)
        key_grad = (
            accumulated[0]
            + jnp.dot(score_grad.T, query_block, preferred_element_type=jnp.float32) * score_scale
        )
        value_grad = accumulated[1] + jnp.dot(
            probs_low.T, grad_block, preferred_element_type=jnp.float32
        )
        return ((key_grad, value_grad), (query_grad, out_rows))

    empty = jnp.zeros((key_rows.shape[0], HD), jnp.float32)
    (key_grad, value_grad), (query_grad, out_rows) = lax.scan(
        one_block, (empty, empty), (query_blocks, grad_blocks)
    )
    return (
        query_grad.reshape(query_count, HD),
        out_rows.reshape(query_count, HD),
        key_grad,
        value_grad,
    )


def local_general(q_img, k_img, v_img, k_txt, v_txt, out_weight, d_out):
    rows_here = q_img.shape[0]
    heads_here = q_img.shape[1] // HD
    seq_count = lax.axis_size("seq")
    share_count = seq_count // heads_here
    part_rows = rows_here // share_count
    seq_index = lax.axis_index("seq")
    head_index = seq_index // share_count
    column_cut = d_out
    attn_grad = jnp.dot(
        column_cut,
        lax.all_gather(out_weight, "seq", axis=0, tiled=True),
        preferred_element_type=jnp.float32,
    ).astype(jnp.bfloat16)

    def to_heads(array_in):
        shaped = array_in.reshape(share_count, part_rows, heads_here, HD).transpose(2, 0, 1, 3)
        return shaped.reshape(seq_count, part_rows, HD)

    def whole_heads(array_in):
        shaped = array_in.reshape(rows_here, heads_here, HD).transpose(1, 0, 2)
        shaped = jnp.broadcast_to(shaped[:, None], (heads_here, share_count, rows_here, HD))
        return shaped.reshape(seq_count, rows_here, HD)

    def from_heads(array_in):
        shaped = array_in.reshape(heads_here, share_count, part_rows, HD).transpose(1, 2, 0, 3)
        return shaped.reshape(rows_here, heads_here * HD)

    text_keys = lax.dynamic_slice_in_dim(k_txt, head_index * HD, HD, 1)
    text_values = lax.dynamic_slice_in_dim(v_txt, head_index * HD, HD, 1)
    query_side = jnp.concatenate([to_heads(q_img), to_heads(attn_grad)], axis=2)
    key_side = jnp.concatenate([whole_heads(k_img), whole_heads(v_img)], axis=2)
    packed = jnp.concatenate([query_side, key_side], axis=1)
    received = lax.all_to_all(packed, "seq", split_axis=0, concat_axis=0, tiled=True)
    queries = received[:, :part_rows, :HD].reshape(seq_count * part_rows, HD)
    cotangents = received[:, :part_rows, HD:].reshape(seq_count * part_rows, HD)
    image_keys = received[:, part_rows:, :HD].reshape(seq_count * rows_here, HD)
    image_values = received[:, part_rows:, HD:].reshape(seq_count * rows_here, HD)
    key_rows = jnp.concatenate([image_keys, text_keys], axis=0)
    value_rows = jnp.concatenate([image_values, text_values], axis=0)
    query_grad, out_rows, key_grad, value_grad = attend(
        queries, cotangents, key_rows, value_rows, min(512, queries.shape[0])
    )
    image_count = image_keys.shape[0]
    query_part = (
        jnp.concatenate([query_grad, out_rows], axis=1)
        .astype(jnp.float32)
        .reshape(seq_count, part_rows, 2 * HD)
    )
    key_part = jnp.concatenate([key_grad[:image_count], value_grad[:image_count]], axis=1).reshape(
        seq_count, rows_here, 2 * HD
    )
    returned = lax.all_to_all(
        jnp.concatenate([query_part, key_part], axis=1).astype(jnp.bfloat16),
        "seq",
        split_axis=0,
        concat_axis=0,
        tiled=True,
    ).astype(jnp.float32)
    q_grad = from_heads(returned[:, :part_rows, :HD]).astype(jnp.bfloat16)
    out_tok = from_heads(returned[:, :part_rows, HD:]).astype(jnp.bfloat16)
    summed = jnp.sum(
        returned[:, part_rows:, :].reshape(heads_here, share_count, rows_here, 2 * HD), axis=1
    )
    summed = summed.transpose(1, 0, 2)
    k_grad = summed[:, :, :HD].reshape(rows_here, heads_here * HD).astype(jnp.bfloat16)
    v_grad = summed[:, :, HD:].reshape(rows_here, heads_here * HD).astype(jnp.bfloat16)
    column_cut = d_out
    d_weight = lax.psum_scatter(
        jnp.dot(column_cut.T, out_tok, preferred_element_type=jnp.float32).astype(jnp.bfloat16),
        "seq",
        scatter_dimension=0,
        tiled=True,
    ).astype(jnp.float32)
    return (q_grad, k_grad, v_grad, d_weight)


def call(kernel, outs, args, specs=None, scratch=(), scalars=0, out_specs=None, flops=0, moved=0):
    vmem = pl.BlockSpec(memory_space=pltpu.VMEM)
    if specs is None:
        specs = [vmem] * (len(args) - scalars)
    if out_specs is None:
        out_specs = [vmem] * len(outs)
    return pl.pallas_call(
        kernel,
        out_shape=outs,
        grid_spec=pltpu.PrefetchScalarGridSpec(
            num_scalar_prefetch=scalars,
            grid=(1,),
            in_specs=specs,
            out_specs=out_specs,
            scratch_shapes=list(scratch),
        ),
        compiler_params=pltpu.CompilerParams(vmem_limit_bytes=LIMIT),
        cost_estimate=pl.CostEstimate(flops=flops, bytes_accessed=moved, transcendentals=0),
    )(*args)


def halves():
    each = lax.axis_size("seq") // 2
    me = lax.axis_index("seq")
    return me // each, lax.rem(me, each)


def pack_kernel(q_ref, k_ref, v_ref, w_ref, tok_ref, *wt_refs):
    heads = tok_ref.shape[0]
    rows = q_ref.shape[0]
    for h in range(heads):
        cols = slice(h * HD, (h + 1) * HD)
        tok_ref[h, 0:rows, :] = q_ref[:, cols]
        tok_ref[h, rows : 2 * rows, :] = k_ref[:, cols]
        tok_ref[h, 2 * rows : 3 * rows, :] = v_ref[:, cols]
    half, place = halves()
    each = heads // 2
    for d, wt_ref in enumerate(wt_refs):
        to = jnp.bitwise_xor(place, d)
        for i, side in enumerate((half, 1 - half)):
            at = pl.multiple_of((side * each + to) * HD, HD)
            wt_ref[:, i * HD : (i + 1) * HD] = w_ref[:, pl.ds(at, HD)]


def forward_kernel(me_ref, tok_ref, kt_ref, vt_ref, probs_ref, out_ref, keys, vals_t, *, chunk):
    n, three, _ = tok_ref.shape
    rows = three // 3
    image = n * rows
    text = kt_ref.shape[0]
    keys[0:image, :] = tok_ref[:, rows : 2 * rows, :].reshape(image, HD)
    keys[image : image + text, :] = kt_ref[...]
    vals_t[:, 0:image] = tok_ref[:, 2 * rows : 3 * rows, :].reshape(image, HD).T
    vals_t[:, image : image + text] = vt_ref[...].T
    factor = HD ** (-0.5) * math.log2(math.e)
    per = chunk // rows
    for c in range(image // chunk):
        queries = tok_ref[c * per : (c + 1) * per, 0:rows, :].reshape(chunk, HD)
        scores = lax.dot_general(keys[...], queries, NT, preferred_element_type=F32)
        top = jnp.max(scores, axis=0, keepdims=True)
        weights = jnp.exp2((scores - top) * factor)
        total = jnp.sum(weights, axis=0, keepdims=True)
        low = (weights * (1.0 / total)).astype(BF16)
        probs_ref[:, c * chunk : (c + 1) * chunk] = low
        out_ref[:, c * chunk : (c + 1) * chunk] = jnp.dot(
            vals_t[...], low, preferred_element_type=F32
        ).astype(BF16)


def load_cotangents(pieces, cot, sems):
    half, place = halves()
    core = lax.axis_index("fsdp")
    each = len(pieces) // 2
    rows = pieces[0].shape[0]
    copies = []
    for i, piece in enumerate(pieces):
        source = jnp.bitwise_xor(place, i % each)
        shift = (core if i < each else 1 - core) * (rows // 2)
        for j, side in enumerate((half, 1 - half)):
            at = pl.multiple_of((side * each + source) * rows + shift, 16)
            copies.append(
                pltpu.make_async_copy(
                    piece.at[pl.ds(j * (rows // 2), rows // 2), :],
                    cot.at[pl.ds(at, rows // 2), :],
                    sems.at[2 * i + j],
                )
            )
    return copies


def partial_kernel(*refs, count):
    pieces, weights = refs[:count], refs[count : count + count // 2]
    mine_ref, theirs_ref, cot, weight, sems, wsems = refs[count + count // 2 :]
    _, place = halves()
    depth = weights[0].shape[0]
    copies = load_cotangents(pieces, cot, sems)
    for d, block in enumerate(weights):
        at = pl.multiple_of(jnp.bitwise_xor(place, d) * depth, 16)
        copies.append(pltpu.make_async_copy(block, weight.at[pl.ds(at, depth), :], wsems.at[d]))
    for copy in copies:
        copy.start()
    for copy in copies:
        copy.wait()
    step = 256

    @pl.loop(0, cot.shape[0] // step)
    def _(i):
        at = pl.ds(pl.multiple_of(i * step, step), step)
        part = jnp.dot(cot[at, :], weight[...], preferred_element_type=F32)
        mine_ref[at, :] = part[:, :HD]
        theirs_ref[at, :] = part[:, HD:].astype(BF16)


def weight_grad_kernel(*refs, count):
    pieces = refs[:count]
    mine_ref, theirs_ref = refs[count : count + 2]
    dw_refs = refs[count + 2 : count + 2 + count // 2]
    cot, outs, sems = refs[count + 2 + count // 2 :]
    copies = load_cotangents(pieces, cot, sems)
    for copy in copies:
        copy.start()
    outs[0:HD, :] = mine_ref[...]
    outs[HD : 2 * HD, :] = theirs_ref[...]
    for copy in copies:
        copy.wait()
    _, place = halves()
    for d, dw_ref in enumerate(dw_refs):
        depth = dw_ref.shape[1]
        at = pl.multiple_of(jnp.bitwise_xor(place, d) * depth, HD)
        dw_ref[...] = jnp.dot(outs[...], cot[:, pl.ds(at, depth)], preferred_element_type=F32).astype(BF16)


def backward_kernel(
    me_ref, tok_ref, kt_ref, vt_ref, probs_ref, out_ref, mine_ref, theirs_ref, send_ref, keys_t, vals, dk, dv, *, chunk
):
    n, three, _ = tok_ref.shape
    rows = three // 3
    image = n * rows
    text = kt_ref.shape[0]
    scale = HD ** (-0.5)
    vals[0:image, :] = tok_ref[:, 2 * rows : 3 * rows, :].reshape(image, HD)
    vals[image : image + text, :] = vt_ref[...]
    keys_t[:, 0:image] = tok_ref[:, rows : 2 * rows, :].reshape(image, HD).T
    keys_t[:, image : image + text] = kt_ref[...].T
    per = chunk // rows
    for c in range(image // chunk):
        span = slice(c * chunk, (c + 1) * chunk)
        grads = (mine_ref[span, :] + theirs_ref[span, :].astype(F32)).astype(BF16)
        queries = tok_ref[c * per : (c + 1) * per, 0:rows, :].reshape(chunk, HD)
        row_dot = jnp.sum(
            grads.astype(F32).T * out_ref[:, span].astype(F32), axis=0, keepdims=True
        )
        prob_grad = lax.dot_general(vals[...], grads, NT, preferred_element_type=F32)
        low = probs_ref[:, span]
        score_grad = (low.astype(F32) * (prob_grad - row_dot)).astype(BF16)
        dq_t = jnp.dot(keys_t[...], score_grad, preferred_element_type=F32) * scale
        send_ref[c * per : (c + 1) * per, 0:rows, :] = dq_t.T.astype(BF16).reshape(per, rows, HD)
        dk_part = jnp.dot(score_grad[0:image, :], queries, preferred_element_type=F32)
        dv_part = jnp.dot(low[0:image, :], grads, preferred_element_type=F32)
        if c == 0:
            dk[...] = dk_part
            dv[...] = dv_part
        else:
            dk[...] += dk_part
            dv[...] += dv_part
    send_ref[:, rows : 2 * rows, :] = (dk[...] * scale).astype(BF16).reshape(n, rows, HD)
    send_ref[:, 2 * rows : 3 * rows, :] = dv[...].astype(BF16).reshape(n, rows, HD)


def unpack_kernel(tok_ref, *refs):
    *dw_refs, q_ref, k_ref, v_ref, w_ref = refs
    heads, three, _ = tok_ref.shape
    rows = three // 3
    for h in range(heads):
        cols = slice(h * HD, (h + 1) * HD)
        q_ref[:, cols] = tok_ref[h, 0:rows, :]
        k_ref[:, cols] = tok_ref[h, rows : 2 * rows, :]
        v_ref[:, cols] = tok_ref[h, 2 * rows : 3 * rows, :]
    half, place = halves()
    each = heads // 2
    for d, dw_ref in enumerate(dw_refs):
        source = jnp.bitwise_xor(place, d)
        for i, side in enumerate((half, 1 - half)):
            at = pl.multiple_of((side * each + source) * HD, HD)
            w_ref[:, pl.ds(at, HD)] = dw_ref[i * HD : (i + 1) * HD, :].astype(F32).T


def exchange(array, distance=0, cores=False):
    size = 2 * lax.axis_size("seq")
    pairs = [(i, i ^ (2 * distance + int(cores))) for i in range(size)]
    return lax.ppermute(array, ("seq", "fsdp"), pairs)


def gather_cotangents(d_out, n):
    rows, width = d_out.shape
    part, columns = rows // 2, width // 2
    half, _ = halves()
    first = lax.axis_index("fsdp") * part
    away = lax.dynamic_slice(d_out, (first, (1 - half) * columns), (part, columns))
    kept = lax.dynamic_slice(d_out, (first, half * columns), (part, columns))
    both = jnp.concatenate([kept, exchange(away, n // 2)], axis=0)
    pieces = [both] + [exchange(both, d) for d in range(1, n // 2)]
    return pieces + [exchange(piece, cores=True) for piece in pieces]


def local(q_img, k_img, v_img, k_txt, v_txt, out_weight, d_out):
    n = lax.axis_size("seq")
    rows, width = q_img.shape
    args = (q_img, k_img, v_img, k_txt, v_txt, out_weight, d_out)
    if width // HD != n or lax.axis_size("fsdp") != 2 or n < 4 or n & (n - 1) or rows % 32:
        return local_general(*args)
    depth = out_weight.shape[0]
    image = n * rows
    text = k_txt.shape[0]
    total = image + text
    chunk = 2 * rows
    shape = jax.ShapeDtypeStruct
    vmem = pl.BlockSpec(memory_space=pltpu.VMEM)

    pieces = gather_cotangents(d_out, n)
    each = n // 2
    tok_out, *w_out = call(
        pack_kernel,
        [shape((n, 3 * rows, HD), BF16)] + [shape((depth, 2 * HD), BF16)] * each,
        [q_img, k_img, v_img, out_weight],
        moved=4 * (3 * rows + depth) * width,
    )
    tok_in = lax.all_to_all(tok_out, "seq", split_axis=0, concat_axis=0, tiled=True)
    w_in = [w_out[0]] + [exchange(w_out[d], d) for d in range(1, each)]

    me = lax.axis_index("seq").astype(jnp.int32)[None]
    text_spec = pl.BlockSpec((text, HD), lambda i, me_ref: (0, me_ref[0]))
    probs, out_t = call(
        functools.partial(forward_kernel, chunk=chunk),
        [shape((total, image), BF16), shape((HD, image), BF16)],
        [me, tok_in, k_txt, v_txt],
        specs=[vmem, text_spec, text_spec],
        scratch=[pltpu.VMEM((total, HD), BF16), pltpu.VMEM((HD, total), BF16)],
        scalars=1,
        flops=4 * total * image * HD,
        moved=4 * total * image,
    )
    count = len(pieces)
    anywhere = [pl.BlockSpec(memory_space=pl.ANY)]
    half_width = d_out.shape[1] // 2
    mine, theirs = call(
        functools.partial(partial_kernel, count=count),
        [shape((image, HD), F32), shape((image, HD), BF16)],
        [*pieces, *w_in],
        specs=anywhere * (count + each),
        scratch=[
            pltpu.VMEM((image, half_width), BF16),
            pltpu.VMEM((half_width, 2 * HD), BF16),
            pltpu.SemaphoreType.DMA((2 * count,)),
            pltpu.SemaphoreType.DMA((each,)),
        ],
        flops=4 * image * half_width * HD,
        moved=2 * image * half_width,
    )
    theirs = exchange(theirs, each)
    out_other = exchange(out_t, each)
    (grad_out,) = call(
        functools.partial(backward_kernel, chunk=chunk),
        [shape((n, 3 * rows, HD), BF16)],
        [me, tok_in, k_txt, v_txt, probs, out_t, mine, theirs],
        specs=[vmem, text_spec, text_spec] + [vmem] * 4,
        scratch=[
            pltpu.VMEM((HD, total), BF16),
            pltpu.VMEM((total, HD), BF16),
            pltpu.VMEM((image, HD), F32),
            pltpu.VMEM((image, HD), F32),
        ],
        scalars=1,
        flops=8 * total * image * HD,
        moved=4 * total * image,
    )
    grad_in = lax.all_to_all(grad_out, "seq", split_axis=0, concat_axis=0, tiled=True)
    out_other, _ = lax.optimization_barrier((out_other, grad_out))
    dw_out = call(
        functools.partial(weight_grad_kernel, count=count),
        [shape((2 * HD, depth), BF16)] * each,
        [*pieces, out_t, out_other],
        specs=anywhere * count + [vmem, vmem],
        scratch=[
            pltpu.VMEM((image, half_width), BF16),
            pltpu.VMEM((2 * HD, image), BF16),
            pltpu.SemaphoreType.DMA((2 * count,)),
        ],
        flops=4 * image * half_width * HD,
        moved=2 * image * half_width,
    )
    dw_in = [dw_out[0]] + [exchange(dw_out[d], d) for d in range(1, each)]
    return tuple(
        call(
            unpack_kernel,
            [shape((rows, width), BF16)] * 3 + [shape((depth, width), F32)],
            [grad_in, *dw_in],
            moved=4 * 3 * rows * width + 6 * depth * width,
        )
    )


def solution(mesh):
    in_specs = (
        P(("group", "seq"), "fsdp"),
        P(("group", "seq"), "fsdp"),
        P(("group", "seq"), "fsdp"),
        P("group", "fsdp"),
        P("group", "fsdp"),
        P("seq", "fsdp"),
        P(("group", "seq"), None),
    )
    out_specs = (
        P(("group", "seq"), "fsdp"),
        P(("group", "seq"), "fsdp"),
        P(("group", "seq"), "fsdp"),
        P(("group", "seq"), "fsdp"),
    )
    return jax.shard_map(local, mesh=mesh, in_specs=in_specs, out_specs=out_specs, check_vma=False)
```

```python
import functools
import math

import jax
import jax.numpy as jnp
from jax import lax
from jax.experimental import pallas as pl
from jax.experimental.pallas import tpu as pltpu
from jax.sharding import PartitionSpec as P

HD = 128
F32 = jnp.float32
BF16 = jnp.bfloat16
LIMIT = 28 * 1024 * 1024
NT = (((1,), (1,)), ((), ()))


def attend(queries, cotangents, key_rows, value_rows, block_rows):
    score_scale = HD ** (-0.5)
    query_count = queries.shape[0]
    block_count = query_count // block_rows
    query_blocks = queries.reshape(block_count, block_rows, HD)
    grad_blocks = cotangents.reshape(block_count, block_rows, HD)

    def one_block(accumulated, pair_item):
        query_block, grad_block = pair_item
        scores = jnp.dot(query_block, key_rows.T, preferred_element_type=jnp.float32) * score_scale
        row_max = jnp.max(scores, axis=1, keepdims=True)
        probs = jnp.exp(scores - row_max)
        probs = probs / jnp.sum(probs, axis=1, keepdims=True)
        probs_low = probs.astype(jnp.bfloat16)
        out_rows = jnp.dot(probs_low, value_rows, preferred_element_type=jnp.float32).astype(
            jnp.bfloat16
        )
        prob_grad = jnp.dot(grad_block, value_rows.T, preferred_element_type=jnp.float32)
        row_dot = jnp.sum(
            grad_block.astype(jnp.float32) * out_rows.astype(jnp.float32), axis=1, keepdims=True
        )
        score_grad = (probs * (prob_grad - row_dot)).astype(jnp.bfloat16)
        query_grad = (
            jnp.dot(score_grad, key_rows, preferred_element_type=jnp.float32) * score_scale
        ).astype(jnp.bfloat16)
        key_grad = (
            accumulated[0]
            + jnp.dot(score_grad.T, query_block, preferred_element_type=jnp.float32) * score_scale
        )
        value_grad = accumulated[1] + jnp.dot(
            probs_low.T, grad_block, preferred_element_type=jnp.float32
        )
        return ((key_grad, value_grad), (query_grad, out_rows))

    empty = jnp.zeros((key_rows.shape[0], HD), jnp.float32)
    (key_grad, value_grad), (query_grad, out_rows) = lax.scan(
        one_block, (empty, empty), (query_blocks, grad_blocks)
    )
    return (
        query_grad.reshape(query_count, HD),
        out_rows.reshape(query_count, HD),
        key_grad,
        value_grad,
    )


def local_general(q_img, k_img, v_img, k_txt, v_txt, out_weight, d_out):
    rows_here = q_img.shape[0]
    heads_here = q_img.shape[1] // HD
    seq_count = lax.axis_size("seq")
    share_count = seq_count // heads_here
    part_rows = rows_here // share_count
    seq_index = lax.axis_index("seq")
    head_index = seq_index // share_count
    column_cut = d_out
    attn_grad = jnp.dot(
        column_cut,
        lax.all_gather(out_weight, "seq", axis=0, tiled=True),
        preferred_element_type=jnp.float32,
    ).astype(jnp.bfloat16)

    def to_heads(array_in):
        shaped = array_in.reshape(share_count, part_rows, heads_here, HD).transpose(2, 0, 1, 3)
        return shaped.reshape(seq_count, part_rows, HD)

    def whole_heads(array_in):
        shaped = array_in.reshape(rows_here, heads_here, HD).transpose(1, 0, 2)
        shaped = jnp.broadcast_to(shaped[:, None], (heads_here, share_count, rows_here, HD))
        return shaped.reshape(seq_count, rows_here, HD)

    def from_heads(array_in):
        shaped = array_in.reshape(heads_here, share_count, part_rows, HD).transpose(1, 2, 0, 3)
        return shaped.reshape(rows_here, heads_here * HD)

    text_keys = lax.dynamic_slice_in_dim(k_txt, head_index * HD, HD, 1)
    text_values = lax.dynamic_slice_in_dim(v_txt, head_index * HD, HD, 1)
    query_side = jnp.concatenate([to_heads(q_img), to_heads(attn_grad)], axis=2)
    key_side = jnp.concatenate([whole_heads(k_img), whole_heads(v_img)], axis=2)
    packed = jnp.concatenate([query_side, key_side], axis=1)
    received = lax.all_to_all(packed, "seq", split_axis=0, concat_axis=0, tiled=True)
    queries = received[:, :part_rows, :HD].reshape(seq_count * part_rows, HD)
    cotangents = received[:, :part_rows, HD:].reshape(seq_count * part_rows, HD)
    image_keys = received[:, part_rows:, :HD].reshape(seq_count * rows_here, HD)
    image_values = received[:, part_rows:, HD:].reshape(seq_count * rows_here, HD)
    key_rows = jnp.concatenate([image_keys, text_keys], axis=0)
    value_rows = jnp.concatenate([image_values, text_values], axis=0)
    query_grad, out_rows, key_grad, value_grad = attend(
        queries, cotangents, key_rows, value_rows, min(512, queries.shape[0])
    )
    image_count = image_keys.shape[0]
    query_part = (
        jnp.concatenate([query_grad, out_rows], axis=1)
        .astype(jnp.float32)
        .reshape(seq_count, part_rows, 2 * HD)
    )
    key_part = jnp.concatenate([key_grad[:image_count], value_grad[:image_count]], axis=1).reshape(
        seq_count, rows_here, 2 * HD
    )
    returned = lax.all_to_all(
        jnp.concatenate([query_part, key_part], axis=1).astype(jnp.bfloat16),
        "seq",
        split_axis=0,
        concat_axis=0,
        tiled=True,
    ).astype(jnp.float32)
    q_grad = from_heads(returned[:, :part_rows, :HD]).astype(jnp.bfloat16)
    out_tok = from_heads(returned[:, :part_rows, HD:]).astype(jnp.bfloat16)
    summed = jnp.sum(
        returned[:, part_rows:, :].reshape(heads_here, share_count, rows_here, 2 * HD), axis=1
    )
    summed = summed.transpose(1, 0, 2)
    k_grad = summed[:, :, :HD].reshape(rows_here, heads_here * HD).astype(jnp.bfloat16)
    v_grad = summed[:, :, HD:].reshape(rows_here, heads_here * HD).astype(jnp.bfloat16)
    column_cut = d_out
    d_weight = lax.psum_scatter(
        jnp.dot(column_cut.T, out_tok, preferred_element_type=jnp.float32).astype(jnp.bfloat16),
        "seq",
        scatter_dimension=0,
        tiled=True,
    ).astype(jnp.float32)
    return (q_grad, k_grad, v_grad, d_weight)


def call(kernel, outs, args, specs=None, scratch=(), scalars=0, out_specs=None, flops=0, moved=0, limit=LIMIT):
    vmem = pl.BlockSpec(memory_space=pltpu.VMEM)
    if specs is None:
        specs = [vmem] * (len(args) - scalars)
    if out_specs is None:
        out_specs = [vmem] * len(outs)
    return pl.pallas_call(
        kernel,
        out_shape=outs,
        grid_spec=pltpu.PrefetchScalarGridSpec(
            num_scalar_prefetch=scalars,
            grid=(1,),
            in_specs=specs,
            out_specs=out_specs,
            scratch_shapes=list(scratch),
        ),
        compiler_params=pltpu.CompilerParams(vmem_limit_bytes=limit),
        cost_estimate=pl.CostEstimate(flops=flops, bytes_accessed=moved, transcendentals=0),
    )(*args)


def halves():
    each = lax.axis_size("seq") // 2
    me = lax.axis_index("seq")
    return me // each, lax.rem(me, each)


def pack_kernel(q_ref, k_ref, v_ref, w_ref, tok_ref, *wt_refs):
    heads = tok_ref.shape[0]
    rows = q_ref.shape[0]
    for h in range(heads):
        cols = slice(h * HD, (h + 1) * HD)
        tok_ref[h, 0:rows, :] = q_ref[:, cols]
        tok_ref[h, rows : 2 * rows, :] = k_ref[:, cols]
        tok_ref[h, 2 * rows : 3 * rows, :] = v_ref[:, cols]
    half, place = halves()
    each = heads // 2
    for d, wt_ref in enumerate(wt_refs):
        to = jnp.bitwise_xor(place, d)
        for i, side in enumerate((half, 1 - half)):
            at = pl.multiple_of((side * each + to) * HD, HD)
            wt_ref[:, i * HD : (i + 1) * HD] = w_ref[:, pl.ds(at, HD)]


def forward_kernel(me_ref, tok_ref, kt_ref, vt_ref, probs_ref, out_ref, keys, vals_t, *, chunk):
    n, three, _ = tok_ref.shape
    rows = three // 3
    image = n * rows
    text = kt_ref.shape[0]
    keys[0:image, :] = tok_ref[:, rows : 2 * rows, :].reshape(image, HD)
    keys[image : image + text, :] = kt_ref[...]
    vals_t[:, 0:image] = tok_ref[:, 2 * rows : 3 * rows, :].reshape(image, HD).T
    vals_t[:, image : image + text] = vt_ref[...].T
    factor = HD ** (-0.5) * math.log2(math.e)
    per = chunk // rows
    for c in range(image // chunk):
        queries = tok_ref[c * per : (c + 1) * per, 0:rows, :].reshape(chunk, HD)
        scores = lax.dot_general(keys[...], queries, NT, preferred_element_type=F32)
        top = jnp.max(scores, axis=0, keepdims=True)
        weights = jnp.exp2((scores - top) * factor)
        total = jnp.sum(weights, axis=0, keepdims=True)
        low = (weights * (1.0 / total)).astype(BF16)
        probs_ref[:, c * chunk : (c + 1) * chunk] = low
        out_ref[:, c * chunk : (c + 1) * chunk] = jnp.dot(
            vals_t[...], low, preferred_element_type=F32
        ).astype(BF16)


def load_cotangents(pieces, cot, sems):
    half, place = halves()
    core = lax.axis_index("fsdp")
    each = len(pieces) // 2
    rows = pieces[0].shape[0]
    copies = []
    for i, piece in enumerate(pieces):
        source = jnp.bitwise_xor(place, i % each)
        shift = (core if i < each else 1 - core) * (rows // 2)
        for j, side in enumerate((half, 1 - half)):
            at = pl.multiple_of((side * each + source) * rows + shift, 16)
            copies.append(
                pltpu.make_async_copy(
                    piece.at[pl.ds(j * (rows // 2), rows // 2), :],
                    cot.at[pl.ds(at, rows // 2), :],
                    sems.at[2 * i + j],
                )
            )
    return copies


def partial_kernel(*refs, count):
    pieces, weights = refs[:count], refs[count : count + count // 2]
    mine_ref, theirs_ref, cot, weight, sems, wsems = refs[count + count // 2 :]
    _, place = halves()
    depth = weights[0].shape[0]
    copies = load_cotangents(pieces, cot, sems)
    for d, block in enumerate(weights):
        at = pl.multiple_of(jnp.bitwise_xor(place, d) * depth, 16)
        copies.append(pltpu.make_async_copy(block, weight.at[pl.ds(at, depth), :], wsems.at[d]))
    for copy in copies:
        copy.start()
    for copy in copies:
        copy.wait()
    step = 256

    @pl.loop(0, cot.shape[0] // step)
    def _(i):
        at = pl.ds(pl.multiple_of(i * step, step), step)
        part = jnp.dot(cot[at, :], weight[...], preferred_element_type=F32)
        mine_ref[at, :] = part[:, :HD]
        theirs_ref[at, :] = part[:, HD:].astype(BF16)


def weight_grad_kernel(*refs, count):
    pieces = refs[:count]
    mine_ref, theirs_ref = refs[count : count + 2]
    dw_refs = refs[count + 2 : count + 2 + count // 2]
    cot, outs, sems = refs[count + 2 + count // 2 :]
    copies = load_cotangents(pieces, cot, sems)
    for copy in copies:
        copy.start()
    outs[0:HD, :] = mine_ref[...]
    outs[HD : 2 * HD, :] = theirs_ref[...]
    for copy in copies:
        copy.wait()
    _, place = halves()
    for d, dw_ref in enumerate(dw_refs):
        depth = dw_ref.shape[1]
        at = pl.multiple_of(jnp.bitwise_xor(place, d) * depth, HD)
        dw_ref[...] = jnp.dot(outs[...], cot[:, pl.ds(at, depth)], preferred_element_type=F32).astype(BF16)


def backward_kernel(
    me_ref, tok_ref, kt_ref, vt_ref, probs_ref, out_ref, mine_ref, theirs_ref, send_ref, keys_t, vals, dk, dv, *, chunk
):
    n, three, _ = tok_ref.shape
    rows = three // 3
    image = n * rows
    text = kt_ref.shape[0]
    scale = HD ** (-0.5)
    vals[0:image, :] = tok_ref[:, 2 * rows : 3 * rows, :].reshape(image, HD)
    vals[image : image + text, :] = vt_ref[...]
    keys_t[:, 0:image] = tok_ref[:, rows : 2 * rows, :].reshape(image, HD).T
    keys_t[:, image : image + text] = kt_ref[...].T
    per = chunk // rows
    for c in range(image // chunk):
        span = slice(c * chunk, (c + 1) * chunk)
        grads = (mine_ref[span, :] + theirs_ref[span, :].astype(F32)).astype(BF16)
        queries = tok_ref[c * per : (c + 1) * per, 0:rows, :].reshape(chunk, HD)
        row_dot = jnp.sum(
            grads.astype(F32).T * out_ref[:, span].astype(F32), axis=0, keepdims=True
        )
        prob_grad = lax.dot_general(vals[...], grads, NT, preferred_element_type=F32)
        low = probs_ref[:, span]
        score_grad = (low.astype(F32) * (prob_grad - row_dot)).astype(BF16)
        dq_t = jnp.dot(keys_t[...], score_grad, preferred_element_type=F32) * scale
        send_ref[c * per : (c + 1) * per, 0:rows, :] = dq_t.T.astype(BF16).reshape(per, rows, HD)
        dk_part = jnp.dot(score_grad[0:image, :], queries, preferred_element_type=F32)
        dv_part = jnp.dot(low[0:image, :], grads, preferred_element_type=F32)
        if c == 0:
            dk[...] = dk_part
            dv[...] = dv_part
        else:
            dk[...] += dk_part
            dv[...] += dv_part
    send_ref[:, rows : 2 * rows, :] = (dk[...] * scale).astype(BF16).reshape(n, rows, HD)
    send_ref[:, 2 * rows : 3 * rows, :] = dv[...].astype(BF16).reshape(n, rows, HD)


def unpack_kernel(tok_ref, *refs):
    *dw_refs, q_ref, k_ref, v_ref, w_ref = refs
    heads, three, _ = tok_ref.shape
    rows = three // 3
    for h in range(heads):
        cols = slice(h * HD, (h + 1) * HD)
        q_ref[:, cols] = tok_ref[h, 0:rows, :]
        k_ref[:, cols] = tok_ref[h, rows : 2 * rows, :]
        v_ref[:, cols] = tok_ref[h, 2 * rows : 3 * rows, :]
    half, place = halves()
    each = heads // 2
    for d, dw_ref in enumerate(dw_refs):
        source = jnp.bitwise_xor(place, d)
        for i, side in enumerate((half, 1 - half)):
            at = pl.multiple_of((side * each + source) * HD, HD)
            w_ref[:, pl.ds(at, HD)] = dw_ref[i * HD : (i + 1) * HD, :].astype(F32).T


def exchange(array, distance=0, cores=False):
    size = 2 * lax.axis_size("seq")
    pairs = [(i, i ^ (2 * distance + int(cores))) for i in range(size)]
    return lax.ppermute(array, ("seq", "fsdp"), pairs)


def gather_cotangents(d_out, n):
    rows, width = d_out.shape
    part, columns = rows // 2, width // 2
    half, _ = halves()
    first = lax.axis_index("fsdp") * part
    away = lax.dynamic_slice(d_out, (first, (1 - half) * columns), (part, columns))
    kept = lax.dynamic_slice(d_out, (first, half * columns), (part, columns))
    both = jnp.concatenate([kept, exchange(away, n // 2)], axis=0)
    pieces = [both] + [exchange(both, d) for d in range(1, n // 2)]
    return pieces + [exchange(piece, cores=True) for piece in pieces]


def local(q_img, k_img, v_img, k_txt, v_txt, out_weight, d_out):
    n = lax.axis_size("seq")
    rows, width = q_img.shape
    args = (q_img, k_img, v_img, k_txt, v_txt, out_weight, d_out)
    if width // HD != n or lax.axis_size("fsdp") != 2 or n < 4 or n & (n - 1) or rows % 32:
        return local_general(*args)
    depth = out_weight.shape[0]
    image = n * rows
    text = k_txt.shape[0]
    total = image + text
    chunk = 2 * rows
    shape = jax.ShapeDtypeStruct
    vmem = pl.BlockSpec(memory_space=pltpu.VMEM)

    pieces = gather_cotangents(d_out, n)
    each = n // 2
    tok_out, *w_out = call(
        pack_kernel,
        [shape((n, 3 * rows, HD), BF16)] + [shape((depth, 2 * HD), BF16)] * each,
        [q_img, k_img, v_img, out_weight],
        moved=4 * (3 * rows + depth) * width,
        limit=60 * 1024 * 1024,
    )
    tok_in = lax.all_to_all(tok_out, "seq", split_axis=0, concat_axis=0, tiled=True)
    w_in = [w_out[0]] + [exchange(w_out[d], d) for d in range(1, each)]

    me = lax.axis_index("seq").astype(jnp.int32)[None]
    text_spec = pl.BlockSpec((text, HD), lambda i, me_ref: (0, me_ref[0]))
    probs, out_t = call(
        functools.partial(forward_kernel, chunk=chunk),
        [shape((total, image), BF16), shape((HD, image), BF16)],
        [me, tok_in, k_txt, v_txt],
        specs=[vmem, text_spec, text_spec],
        scratch=[pltpu.VMEM((total, HD), BF16), pltpu.VMEM((HD, total), BF16)],
        scalars=1,
        flops=4 * total * image * HD,
        moved=4 * total * image,
    )
    count = len(pieces)
    anywhere = [pl.BlockSpec(memory_space=pl.ANY)]
    half_width = d_out.shape[1] // 2
    out_other = exchange(out_t, each)
    w_own, _ = lax.optimization_barrier((w_in[0], out_t))
    mine, theirs = call(
        functools.partial(partial_kernel, count=count),
        [shape((image, HD), F32), shape((image, HD), BF16)],
        [*pieces, w_own, *w_in[1:]],
        specs=anywhere * (count + each),
        scratch=[
            pltpu.VMEM((image, half_width), BF16),
            pltpu.VMEM((half_width, 2 * HD), BF16),
            pltpu.SemaphoreType.DMA((2 * count,)),
            pltpu.SemaphoreType.DMA((each,)),
        ],
        flops=4 * image * half_width * HD,
        moved=2 * image * half_width,
    )
    theirs = exchange(theirs, each)
    out_other, mine = lax.optimization_barrier((out_other, mine))
    dw_out = call(
        functools.partial(weight_grad_kernel, count=count),
        [shape((2 * HD, depth), BF16)] * each,
        [*pieces, out_t, out_other],
        specs=anywhere * count + [vmem, vmem],
        scratch=[
            pltpu.VMEM((image, half_width), BF16),
            pltpu.VMEM((2 * HD, image), BF16),
            pltpu.SemaphoreType.DMA((2 * count,)),
        ],
        flops=4 * image * half_width * HD,
        moved=2 * image * half_width,
    )
    mine, *dw_out = lax.optimization_barrier((mine, *dw_out))
    (grad_out,) = call(
        functools.partial(backward_kernel, chunk=chunk),
        [shape((n, 3 * rows, HD), BF16)],
        [me, tok_in, k_txt, v_txt, probs, out_t, mine, theirs],
        specs=[vmem, text_spec, text_spec] + [vmem] * 4,
        scratch=[
            pltpu.VMEM((HD, total), BF16),
            pltpu.VMEM((total, HD), BF16),
            pltpu.VMEM((image, HD), F32),
            pltpu.VMEM((image, HD), F32),
        ],
        scalars=1,
        flops=8 * total * image * HD,
        moved=4 * total * image,
    )
    dw_in = [dw_out[0]] + [exchange(dw_out[d], d) for d in range(1, each)]
    grad_in = lax.all_to_all(grad_out, "seq", split_axis=0, concat_axis=0, tiled=True)
    return tuple(
        call(
            unpack_kernel,
            [shape((rows, width), BF16)] * 3 + [shape((depth, width), F32)],
            [grad_in, *dw_in],
            moved=4 * 3 * rows * width + 6 * depth * width,
        )
    )


def solution(mesh):
    in_specs = (
        P(("group", "seq"), "fsdp"),
        P(("group", "seq"), "fsdp"),
        P(("group", "seq"), "fsdp"),
        P("group", "fsdp"),
        P("group", "fsdp"),
        P("seq", "fsdp"),
        P(("group", "seq"), None),
    )
    out_specs = (
        P(("group", "seq"), "fsdp"),
        P(("group", "seq"), "fsdp"),
        P(("group", "seq"), "fsdp"),
        P(("group", "seq"), "fsdp"),
    )
    return jax.shard_map(local, mesh=mesh, in_specs=in_specs, out_specs=out_specs, check_vma=False)
```

```python
import functools
import math

import jax
import jax.numpy as jnp
from jax import lax
from jax.experimental import pallas as pl
from jax.experimental.pallas import tpu as pltpu
from jax.sharding import PartitionSpec as P

HD = 128
F32 = jnp.float32
BF16 = jnp.bfloat16
LIMIT = 28 * 1024 * 1024
NT = (((1,), (1,)), ((), ()))


def attend(queries, cotangents, key_rows, value_rows, block_rows):
    score_scale = HD ** (-0.5)
    query_count = queries.shape[0]
    block_count = query_count // block_rows
    query_blocks = queries.reshape(block_count, block_rows, HD)
    grad_blocks = cotangents.reshape(block_count, block_rows, HD)

    def one_block(accumulated, pair_item):
        query_block, grad_block = pair_item
        scores = jnp.dot(query_block, key_rows.T, preferred_element_type=jnp.float32) * score_scale
        row_max = jnp.max(scores, axis=1, keepdims=True)
        probs = jnp.exp(scores - row_max)
        probs = probs / jnp.sum(probs, axis=1, keepdims=True)
        probs_low = probs.astype(jnp.bfloat16)
        out_rows = jnp.dot(probs_low, value_rows, preferred_element_type=jnp.float32).astype(
            jnp.bfloat16
        )
        prob_grad = jnp.dot(grad_block, value_rows.T, preferred_element_type=jnp.float32)
        row_dot = jnp.sum(
            grad_block.astype(jnp.float32) * out_rows.astype(jnp.float32), axis=1, keepdims=True
        )
        score_grad = (probs * (prob_grad - row_dot)).astype(jnp.bfloat16)
        query_grad = (
            jnp.dot(score_grad, key_rows, preferred_element_type=jnp.float32) * score_scale
        ).astype(jnp.bfloat16)
        key_grad = (
            accumulated[0]
            + jnp.dot(score_grad.T, query_block, preferred_element_type=jnp.float32) * score_scale
        )
        value_grad = accumulated[1] + jnp.dot(
            probs_low.T, grad_block, preferred_element_type=jnp.float32
        )
        return ((key_grad, value_grad), (query_grad, out_rows))

    empty = jnp.zeros((key_rows.shape[0], HD), jnp.float32)
    (key_grad, value_grad), (query_grad, out_rows) = lax.scan(
        one_block, (empty, empty), (query_blocks, grad_blocks)
    )
    return (
        query_grad.reshape(query_count, HD),
        out_rows.reshape(query_count, HD),
        key_grad,
        value_grad,
    )


def local_general(q_img, k_img, v_img, k_txt, v_txt, out_weight, d_out):
    rows_here = q_img.shape[0]
    heads_here = q_img.shape[1] // HD
    seq_count = lax.axis_size("seq")
    share_count = seq_count // heads_here
    part_rows = rows_here // share_count
    seq_index = lax.axis_index("seq")
    head_index = seq_index // share_count
    column_cut = d_out
    attn_grad = jnp.dot(
        column_cut,
        lax.all_gather(out_weight, "seq", axis=0, tiled=True),
        preferred_element_type=jnp.float32,
    ).astype(jnp.bfloat16)

    def to_heads(array_in):
        shaped = array_in.reshape(share_count, part_rows, heads_here, HD).transpose(2, 0, 1, 3)
        return shaped.reshape(seq_count, part_rows, HD)

    def whole_heads(array_in):
        shaped = array_in.reshape(rows_here, heads_here, HD).transpose(1, 0, 2)
        shaped = jnp.broadcast_to(shaped[:, None], (heads_here, share_count, rows_here, HD))
        return shaped.reshape(seq_count, rows_here, HD)

    def from_heads(array_in):
        shaped = array_in.reshape(heads_here, share_count, part_rows, HD).transpose(1, 2, 0, 3)
        return shaped.reshape(rows_here, heads_here * HD)

    text_keys = lax.dynamic_slice_in_dim(k_txt, head_index * HD, HD, 1)
    text_values = lax.dynamic_slice_in_dim(v_txt, head_index * HD, HD, 1)
    query_side = jnp.concatenate([to_heads(q_img), to_heads(attn_grad)], axis=2)
    key_side = jnp.concatenate([whole_heads(k_img), whole_heads(v_img)], axis=2)
    packed = jnp.concatenate([query_side, key_side], axis=1)
    received = lax.all_to_all(packed, "seq", split_axis=0, concat_axis=0, tiled=True)
    queries = received[:, :part_rows, :HD].reshape(seq_count * part_rows, HD)
    cotangents = received[:, :part_rows, HD:].reshape(seq_count * part_rows, HD)
    image_keys = received[:, part_rows:, :HD].reshape(seq_count * rows_here, HD)
    image_values = received[:, part_rows:, HD:].reshape(seq_count * rows_here, HD)
    key_rows = jnp.concatenate([image_keys, text_keys], axis=0)
    value_rows = jnp.concatenate([image_values, text_values], axis=0)
    query_grad, out_rows, key_grad, value_grad = attend(
        queries, cotangents, key_rows, value_rows, min(512, queries.shape[0])
    )
    image_count = image_keys.shape[0]
    query_part = (
        jnp.concatenate([query_grad, out_rows], axis=1)
        .astype(jnp.float32)
        .reshape(seq_count, part_rows, 2 * HD)
    )
    key_part = jnp.concatenate([key_grad[:image_count], value_grad[:image_count]], axis=1).reshape(
        seq_count, rows_here, 2 * HD
    )
    returned = lax.all_to_all(
        jnp.concatenate([query_part, key_part], axis=1).astype(jnp.bfloat16),
        "seq",
        split_axis=0,
        concat_axis=0,
        tiled=True,
    ).astype(jnp.float32)
    q_grad = from_heads(returned[:, :part_rows, :HD]).astype(jnp.bfloat16)
    out_tok = from_heads(returned[:, :part_rows, HD:]).astype(jnp.bfloat16)
    summed = jnp.sum(
        returned[:, part_rows:, :].reshape(heads_here, share_count, rows_here, 2 * HD), axis=1
    )
    summed = summed.transpose(1, 0, 2)
    k_grad = summed[:, :, :HD].reshape(rows_here, heads_here * HD).astype(jnp.bfloat16)
    v_grad = summed[:, :, HD:].reshape(rows_here, heads_here * HD).astype(jnp.bfloat16)
    column_cut = d_out
    d_weight = lax.psum_scatter(
        jnp.dot(column_cut.T, out_tok, preferred_element_type=jnp.float32).astype(jnp.bfloat16),
        "seq",
        scatter_dimension=0,
        tiled=True,
    ).astype(jnp.float32)
    return (q_grad, k_grad, v_grad, d_weight)


def call(kernel, outs, args, specs=None, scratch=(), scalars=0, out_specs=None, flops=0, moved=0, limit=LIMIT):
    vmem = pl.BlockSpec(memory_space=pltpu.VMEM)
    if specs is None:
        specs = [vmem] * (len(args) - scalars)
    if out_specs is None:
        out_specs = [vmem] * len(outs)
    return pl.pallas_call(
        kernel,
        out_shape=outs,
        grid_spec=pltpu.PrefetchScalarGridSpec(
            num_scalar_prefetch=scalars,
            grid=(1,),
            in_specs=specs,
            out_specs=out_specs,
            scratch_shapes=list(scratch),
        ),
        compiler_params=pltpu.CompilerParams(vmem_limit_bytes=limit),
        cost_estimate=pl.CostEstimate(flops=flops, bytes_accessed=moved, transcendentals=0),
    )(*args)


def halves():
    each = lax.axis_size("seq") // 2
    me = lax.axis_index("seq")
    return me // each, lax.rem(me, each)


def pack_kernel(q_ref, k_ref, v_ref, tok_ref, sems):
    heads = tok_ref.shape[0]
    rows = q_ref.shape[0]
    copies = []
    for h in range(heads):
        for i, ref in enumerate((q_ref, k_ref, v_ref)):
            copies.append(
                pltpu.make_async_copy(
                    ref.at[:, h * HD : (h + 1) * HD],
                    tok_ref.at[h, i * rows : (i + 1) * rows, :],
                    sems.at[i, h],
                )
            )
    for copy in copies:
        copy.start()
    for copy in copies:
        copy.wait()


def pack_weight_kernel(w_ref, kt_ref, vt_ref, *refs):
    *wt_refs, kh_ref, vh_ref, sems, text_sems = refs
    half, place = halves()
    each = len(wt_refs)
    copies = []
    here = pl.ds(pl.multiple_of(lax.axis_index("seq") * HD, HD), HD)
    for i, (whole, head) in enumerate(((kt_ref, kh_ref), (vt_ref, vh_ref))):
        copies.append(pltpu.make_async_copy(whole.at[:, here], head, text_sems.at[i]))
    for d, wt_ref in enumerate(wt_refs):
        to = jnp.bitwise_xor(place, d)
        for i, side in enumerate((half, 1 - half)):
            at = pl.multiple_of((side * each + to) * HD, HD)
            copies.append(
                pltpu.make_async_copy(
                    w_ref.at[:, pl.ds(at, HD)], wt_ref.at[:, i * HD : (i + 1) * HD], sems.at[d, i]
                )
            )
    for copy in copies:
        copy.start()
    for copy in copies:
        copy.wait()


def forward_kernel(tok_ref, kt_ref, vt_ref, probs_ref, out_ref, keys, vals_t, *, chunk):
    n, three, _ = tok_ref.shape
    rows = three // 3
    image = n * rows
    text = kt_ref.shape[0]
    keys[0:image, :] = tok_ref[:, rows : 2 * rows, :].reshape(image, HD)
    keys[image : image + text, :] = kt_ref[...]
    vals_t[:, 0:image] = tok_ref[:, 2 * rows : 3 * rows, :].reshape(image, HD).T
    vals_t[:, image : image + text] = vt_ref[...].T
    factor = HD ** (-0.5) * math.log2(math.e)
    per = chunk // rows
    for c in range(image // chunk):
        queries = tok_ref[c * per : (c + 1) * per, 0:rows, :].reshape(chunk, HD)
        scores = lax.dot_general(keys[...], queries, NT, preferred_element_type=F32)
        top = jnp.max(scores, axis=0, keepdims=True)
        weights = jnp.exp2((scores - top) * factor)
        total = jnp.sum(weights, axis=0, keepdims=True)
        low = (weights * (1.0 / total)).astype(BF16)
        probs_ref[:, c * chunk : (c + 1) * chunk] = low
        out_ref[:, c * chunk : (c + 1) * chunk] = jnp.dot(
            vals_t[...], low, preferred_element_type=F32
        ).astype(BF16)


def load_cotangents(pieces, cot, sems):
    half, place = halves()
    core = lax.axis_index("fsdp")
    each = len(pieces) // 2
    rows = pieces[0].shape[0]
    copies = []
    for i, piece in enumerate(pieces):
        source = jnp.bitwise_xor(place, i % each)
        shift = (core if i < each else 1 - core) * (rows // 2)
        for j, side in enumerate((half, 1 - half)):
            at = pl.multiple_of((side * each + source) * rows + shift, 16)
            copies.append(
                pltpu.make_async_copy(
                    piece.at[pl.ds(j * (rows // 2), rows // 2), :],
                    cot.at[pl.ds(at, rows // 2), :],
                    sems.at[2 * i + j],
                )
            )
    return copies


def partial_kernel(*refs, count):
    pieces, weights = refs[:count], refs[count : count + count // 2]
    mine_ref, theirs_ref, cot, weight, sems, wsems = refs[count + count // 2 :]
    _, place = halves()
    depth = weights[0].shape[0]
    copies = load_cotangents(pieces, cot, sems)
    for d, block in enumerate(weights):
        at = pl.multiple_of(jnp.bitwise_xor(place, d) * depth, 16)
        copies.append(pltpu.make_async_copy(block, weight.at[pl.ds(at, depth), :], wsems.at[d]))
    for copy in copies:
        copy.start()
    for copy in copies:
        copy.wait()
    step = 256

    @pl.loop(0, cot.shape[0] // step)
    def _(i):
        at = pl.ds(pl.multiple_of(i * step, step), step)
        part = jnp.dot(cot[at, :], weight[...], preferred_element_type=F32)
        mine_ref[at, :] = part[:, :HD]
        theirs_ref[at, :] = part[:, HD:].astype(BF16)


def weight_grad_kernel(cot_ref, mine_ref, theirs_ref, *refs):
    *dw_refs, outs = refs
    outs[0:HD, :] = mine_ref[...]
    outs[HD : 2 * HD, :] = theirs_ref[...]
    _, place = halves()
    for d, dw_ref in enumerate(dw_refs):
        depth = dw_ref.shape[1]
        at = pl.multiple_of(jnp.bitwise_xor(place, d) * depth, HD)
        dw_ref[...] = jnp.dot(outs[...], cot_ref[:, pl.ds(at, depth)], preferred_element_type=F32).astype(BF16)


def backward_kernel(
    tok_ref, kt_ref, vt_ref, probs_ref, out_ref, mine_ref, theirs_ref, send_ref, keys_t, vals, dk, dv, *, chunk
):
    n, three, _ = tok_ref.shape
    rows = three // 3
    image = n * rows
    text = kt_ref.shape[0]
    scale = HD ** (-0.5)
    vals[0:image, :] = tok_ref[:, 2 * rows : 3 * rows, :].reshape(image, HD)
    vals[image : image + text, :] = vt_ref[...]
    keys_t[:, 0:image] = tok_ref[:, rows : 2 * rows, :].reshape(image, HD).T
    keys_t[:, image : image + text] = kt_ref[...].T
    per = chunk // rows
    for c in range(image // chunk):
        span = slice(c * chunk, (c + 1) * chunk)
        grads = (mine_ref[span, :] + theirs_ref[span, :].astype(F32)).astype(BF16)
        queries = tok_ref[c * per : (c + 1) * per, 0:rows, :].reshape(chunk, HD)
        row_dot = jnp.sum(
            grads.astype(F32).T * out_ref[:, span].astype(F32), axis=0, keepdims=True
        )
        prob_grad = lax.dot_general(vals[...], grads, NT, preferred_element_type=F32)
        low = probs_ref[:, span]
        score_grad = (low.astype(F32) * (prob_grad - row_dot)).astype(BF16)
        dq_t = jnp.dot(keys_t[...], score_grad, preferred_element_type=F32) * scale
        send_ref[c * per : (c + 1) * per, 0:rows, :] = dq_t.T.astype(BF16).reshape(per, rows, HD)
        dk_part = jnp.dot(score_grad[0:image, :], queries, preferred_element_type=F32)
        dv_part = jnp.dot(low[0:image, :], grads, preferred_element_type=F32)
        if c == 0:
            dk[...] = dk_part
            dv[...] = dv_part
        else:
            dk[...] += dk_part
            dv[...] += dv_part
    send_ref[:, rows : 2 * rows, :] = (dk[...] * scale).astype(BF16).reshape(n, rows, HD)
    send_ref[:, 2 * rows : 3 * rows, :] = dv[...].astype(BF16).reshape(n, rows, HD)


def unpack_kernel(tok_ref, *refs):
    *dw_refs, q_ref, k_ref, v_ref, w_ref = refs
    heads, three, _ = tok_ref.shape
    rows = three // 3
    for h in range(heads):
        cols = slice(h * HD, (h + 1) * HD)
        q_ref[:, cols] = tok_ref[h, 0:rows, :]
        k_ref[:, cols] = tok_ref[h, rows : 2 * rows, :]
        v_ref[:, cols] = tok_ref[h, 2 * rows : 3 * rows, :]
    half, place = halves()
    each = heads // 2
    for d, dw_ref in enumerate(dw_refs):
        source = jnp.bitwise_xor(place, d)
        for i, side in enumerate((half, 1 - half)):
            at = pl.multiple_of((side * each + source) * HD, HD)
            w_ref[:, pl.ds(at, HD)] = dw_ref[i * HD : (i + 1) * HD, :].astype(F32).T


def exchange(array, distance=0, cores=False):
    size = 2 * lax.axis_size("seq")
    pairs = [(i, i ^ (2 * distance + int(cores))) for i in range(size)]
    return lax.ppermute(array, ("seq", "fsdp"), pairs)


def cross_cotangents(d_out, n):
    rows, width = d_out.shape
    part, columns = rows // 2, width // 2
    half, _ = halves()
    first = lax.axis_index("fsdp") * part
    away = lax.dynamic_slice(d_out, (first, (1 - half) * columns), (part, columns))
    kept = lax.dynamic_slice(d_out, (first, half * columns), (part, columns))
    return kept, exchange(away, n // 2)


def gather_cotangents(kept, received, n):
    both = jnp.concatenate([kept, received], axis=0)
    pieces = [both] + [exchange(both, d) for d in range(1, n // 2)]
    return pieces + [exchange(piece, cores=True) for piece in pieces]


def local(q_img, k_img, v_img, k_txt, v_txt, out_weight, d_out):
    n = lax.axis_size("seq")
    rows, width = q_img.shape
    args = (q_img, k_img, v_img, k_txt, v_txt, out_weight, d_out)
    if width // HD != n or lax.axis_size("fsdp") != 2 or n < 4 or n & (n - 1) or rows % 32:
        return local_general(*args)
    depth = out_weight.shape[0]
    image = n * rows
    text = k_txt.shape[0]
    total = image + text
    chunk = 2 * rows
    shape = jax.ShapeDtypeStruct
    vmem = pl.BlockSpec(memory_space=pltpu.VMEM)

    kept, received = cross_cotangents(d_out, n)
    each = n // 2
    hbm = pl.BlockSpec(memory_space=pltpu.HBM)
    *w_out, k_head, v_head = call(
        pack_weight_kernel,
        [shape((depth, 2 * HD), BF16)] * each + [shape((text, HD), BF16)] * 2,
        [out_weight, k_txt, v_txt],
        specs=[hbm] * 3,
        out_specs=[hbm] * (each + 2),
        scratch=[pltpu.SemaphoreType.DMA((each, 2)), pltpu.SemaphoreType.DMA((2,))],
        moved=4 * depth * width,
        limit=60 * 1024 * 1024,
    )
    w_in = [w_out[0]] + [exchange(w_out[d], d) for d in range(1, each)]
    (tok_out,) = call(
        pack_kernel,
        [shape((n, 3 * rows, HD), BF16)],
        [q_img, k_img, v_img],
        specs=[hbm] * 3,
        out_specs=[hbm],
        scratch=[pltpu.SemaphoreType.DMA((3, n))],
        moved=4 * 3 * rows * width,
        limit=60 * 1024 * 1024,
    )
    tok_out, received = lax.optimization_barrier((tok_out, received))
    received, w_in = lax.optimization_barrier((received, w_in))
    pieces = gather_cotangents(kept, received, n)
    tok_in = lax.all_to_all(tok_out, "seq", split_axis=0, concat_axis=0, tiled=True)

    probs, out_t = call(
        functools.partial(forward_kernel, chunk=chunk),
        [shape((total, image), BF16), shape((HD, image), BF16)],
        [tok_in, k_head, v_head],
        scratch=[pltpu.VMEM((total, HD), BF16), pltpu.VMEM((HD, total), BF16)],
        flops=4 * total * image * HD,
        moved=4 * total * image,
    )
    count = len(pieces)
    half_width = d_out.shape[1] // 2
    out_other = exchange(out_t, each)
    mine, theirs, cot = call(
        functools.partial(partial_kernel, count=count),
        [shape((image, HD), F32), shape((image, HD), BF16), shape((image, half_width), BF16)],
        [*pieces, *w_in],
        specs=[hbm] * (count + each),
        scratch=[
            pltpu.VMEM((half_width, 2 * HD), BF16),
            pltpu.SemaphoreType.DMA((2 * count,)),
            pltpu.SemaphoreType.DMA((each,)),
        ],
        flops=4 * image * half_width * HD,
        moved=2 * image * half_width,
    )
    theirs = exchange(theirs, each)
    (grad_out,) = call(
        functools.partial(backward_kernel, chunk=chunk),
        [shape((n, 3 * rows, HD), BF16)],
        [tok_in, k_head, v_head, probs, out_t, mine, theirs],

        scratch=[
            pltpu.VMEM((HD, total), BF16),
            pltpu.VMEM((total, HD), BF16),
            pltpu.VMEM((image, HD), F32),
            pltpu.VMEM((image, HD), F32),
        ],
        flops=8 * total * image * HD,
        moved=4 * total * image,
    )
    grad_out, out_other = lax.optimization_barrier((grad_out, out_other))
    grad_in = lax.all_to_all(grad_out, "seq", split_axis=0, concat_axis=0, tiled=True)
    dw_out = call(
        weight_grad_kernel,
        [shape((2 * HD, depth), BF16)] * each,
        [cot, out_t, out_other],
        scratch=[pltpu.VMEM((2 * HD, image), BF16)],
        flops=4 * image * half_width * HD,
        moved=2 * image * half_width,
    )
    dw_in = [dw_out[0]] + [exchange(dw_out[d], d) for d in range(1, each)]
    return tuple(
        call(
            unpack_kernel,
            [shape((rows, width), BF16)] * 3 + [shape((depth, width), F32)],
            [grad_in, *dw_in],
            moved=4 * 3 * rows * width + 6 * depth * width,
        )
    )


def solution(mesh):
    in_specs = (
        P(("group", "seq"), "fsdp"),
        P(("group", "seq"), "fsdp"),
        P(("group", "seq"), "fsdp"),
        P("group", "fsdp"),
        P("group", "fsdp"),
        P("seq", "fsdp"),
        P(("group", "seq"), None),
    )
    out_specs = (
        P(("group", "seq"), "fsdp"),
        P(("group", "seq"), "fsdp"),
        P(("group", "seq"), "fsdp"),
        P(("group", "seq"), "fsdp"),
    )
    return jax.shard_map(local, mesh=mesh, in_specs=in_specs, out_specs=out_specs, check_vma=False)
```

```python
import functools
import math

import jax
import jax.numpy as jnp
from jax import lax
from jax.experimental import pallas as pl
from jax.experimental.pallas import tpu as pltpu
from jax.sharding import PartitionSpec as P

HD = 128
F32 = jnp.float32
BF16 = jnp.bfloat16
LIMIT = 28 * 1024 * 1024
NT = (((1,), (1,)), ((), ()))


def attend(queries, cotangents, key_rows, value_rows, block_rows):
    score_scale = HD ** (-0.5)
    query_count = queries.shape[0]
    block_count = query_count // block_rows
    query_blocks = queries.reshape(block_count, block_rows, HD)
    grad_blocks = cotangents.reshape(block_count, block_rows, HD)

    def one_block(accumulated, pair_item):
        query_block, grad_block = pair_item
        scores = jnp.dot(query_block, key_rows.T, preferred_element_type=jnp.float32) * score_scale
        row_max = jnp.max(scores, axis=1, keepdims=True)
        probs = jnp.exp(scores - row_max)
        probs = probs / jnp.sum(probs, axis=1, keepdims=True)
        probs_low = probs.astype(jnp.bfloat16)
        out_rows = jnp.dot(probs_low, value_rows, preferred_element_type=jnp.float32).astype(
            jnp.bfloat16
        )
        prob_grad = jnp.dot(grad_block, value_rows.T, preferred_element_type=jnp.float32)
        row_dot = jnp.sum(
            grad_block.astype(jnp.float32) * out_rows.astype(jnp.float32), axis=1, keepdims=True
        )
        score_grad = (probs * (prob_grad - row_dot)).astype(jnp.bfloat16)
        query_grad = (
            jnp.dot(score_grad, key_rows, preferred_element_type=jnp.float32) * score_scale
        ).astype(jnp.bfloat16)
        key_grad = (
            accumulated[0]
            + jnp.dot(score_grad.T, query_block, preferred_element_type=jnp.float32) * score_scale
        )
        value_grad = accumulated[1] + jnp.dot(
            probs_low.T, grad_block, preferred_element_type=jnp.float32
        )
        return ((key_grad, value_grad), (query_grad, out_rows))

    empty = jnp.zeros((key_rows.shape[0], HD), jnp.float32)
    (key_grad, value_grad), (query_grad, out_rows) = lax.scan(
        one_block, (empty, empty), (query_blocks, grad_blocks)
    )
    return (
        query_grad.reshape(query_count, HD),
        out_rows.reshape(query_count, HD),
        key_grad,
        value_grad,
    )


def local_general(q_img, k_img, v_img, k_txt, v_txt, out_weight, d_out):
    rows_here = q_img.shape[0]
    heads_here = q_img.shape[1] // HD
    seq_count = lax.axis_size("seq")
    share_count = seq_count // heads_here
    part_rows = rows_here // share_count
    seq_index = lax.axis_index("seq")
    head_index = seq_index // share_count
    column_cut = d_out
    attn_grad = jnp.dot(
        column_cut,
        lax.all_gather(out_weight, "seq", axis=0, tiled=True),
        preferred_element_type=jnp.float32,
    ).astype(jnp.bfloat16)

    def to_heads(array_in):
        shaped = array_in.reshape(share_count, part_rows, heads_here, HD).transpose(2, 0, 1, 3)
        return shaped.reshape(seq_count, part_rows, HD)

    def whole_heads(array_in):
        shaped = array_in.reshape(rows_here, heads_here, HD).transpose(1, 0, 2)
        shaped = jnp.broadcast_to(shaped[:, None], (heads_here, share_count, rows_here, HD))
        return shaped.reshape(seq_count, rows_here, HD)

    def from_heads(array_in):
        shaped = array_in.reshape(heads_here, share_count, part_rows, HD).transpose(1, 2, 0, 3)
        return shaped.reshape(rows_here, heads_here * HD)

    text_keys = lax.dynamic_slice_in_dim(k_txt, head_index * HD, HD, 1)
    text_values = lax.dynamic_slice_in_dim(v_txt, head_index * HD, HD, 1)
    query_side = jnp.concatenate([to_heads(q_img), to_heads(attn_grad)], axis=2)
    key_side = jnp.concatenate([whole_heads(k_img), whole_heads(v_img)], axis=2)
    packed = jnp.concatenate([query_side, key_side], axis=1)
    received = lax.all_to_all(packed, "seq", split_axis=0, concat_axis=0, tiled=True)
    queries = received[:, :part_rows, :HD].reshape(seq_count * part_rows, HD)
    cotangents = received[:, :part_rows, HD:].reshape(seq_count * part_rows, HD)
    image_keys = received[:, part_rows:, :HD].reshape(seq_count * rows_here, HD)
    image_values = received[:, part_rows:, HD:].reshape(seq_count * rows_here, HD)
    key_rows = jnp.concatenate([image_keys, text_keys], axis=0)
    value_rows = jnp.concatenate([image_values, text_values], axis=0)
    query_grad, out_rows, key_grad, value_grad = attend(
        queries, cotangents, key_rows, value_rows, min(512, queries.shape[0])
    )
    image_count = image_keys.shape[0]
    query_part = (
        jnp.concatenate([query_grad, out_rows], axis=1)
        .astype(jnp.float32)
        .reshape(seq_count, part_rows, 2 * HD)
    )
    key_part = jnp.concatenate([key_grad[:image_count], value_grad[:image_count]], axis=1).reshape(
        seq_count, rows_here, 2 * HD
    )
    returned = lax.all_to_all(
        jnp.concatenate([query_part, key_part], axis=1).astype(jnp.bfloat16),
        "seq",
        split_axis=0,
        concat_axis=0,
        tiled=True,
    ).astype(jnp.float32)
    q_grad = from_heads(returned[:, :part_rows, :HD]).astype(jnp.bfloat16)
    out_tok = from_heads(returned[:, :part_rows, HD:]).astype(jnp.bfloat16)
    summed = jnp.sum(
        returned[:, part_rows:, :].reshape(heads_here, share_count, rows_here, 2 * HD), axis=1
    )
    summed = summed.transpose(1, 0, 2)
    k_grad = summed[:, :, :HD].reshape(rows_here, heads_here * HD).astype(jnp.bfloat16)
    v_grad = summed[:, :, HD:].reshape(rows_here, heads_here * HD).astype(jnp.bfloat16)
    column_cut = d_out
    d_weight = lax.psum_scatter(
        jnp.dot(column_cut.T, out_tok, preferred_element_type=jnp.float32).astype(jnp.bfloat16),
        "seq",
        scatter_dimension=0,
        tiled=True,
    ).astype(jnp.float32)
    return (q_grad, k_grad, v_grad, d_weight)


def call(kernel, outs, args, specs=None, scratch=(), scalars=0, out_specs=None, flops=0, moved=0, limit=LIMIT):
    vmem = pl.BlockSpec(memory_space=pltpu.VMEM)
    if specs is None:
        specs = [vmem] * (len(args) - scalars)
    if out_specs is None:
        out_specs = [vmem] * len(outs)
    return pl.pallas_call(
        kernel,
        out_shape=outs,
        grid_spec=pltpu.PrefetchScalarGridSpec(
            num_scalar_prefetch=scalars,
            grid=(1,),
            in_specs=specs,
            out_specs=out_specs,
            scratch_shapes=list(scratch),
        ),
        compiler_params=pltpu.CompilerParams(vmem_limit_bytes=limit),
        cost_estimate=pl.CostEstimate(flops=flops, bytes_accessed=moved, transcendentals=0),
    )(*args)


def halves():
    each = lax.axis_size("seq") // 2
    me = lax.axis_index("seq")
    return me // each, lax.rem(me, each)


def pack_kernel(q_ref, k_ref, v_ref, tok_ref):
    rows = q_ref.shape[0]
    for h in range(tok_ref.shape[0]):
        for i, ref in enumerate((q_ref, k_ref, v_ref)):
            tok_ref[h, i * rows : (i + 1) * rows, :] = ref[:, h * HD : (h + 1) * HD]


def pack_weight_kernel(w_ref, kt_ref, vt_ref, *refs):
    *wt_refs, text_ref = refs
    half, place = halves()
    each = len(wt_refs)
    text_ref[0] = kt_ref[...]
    text_ref[1] = vt_ref[...]
    for d, wt_ref in enumerate(wt_refs):
        to = jnp.bitwise_xor(place, d)
        for i, side in enumerate((half, 1 - half)):
            at = pl.multiple_of((side * each + to) * HD, HD)
            wt_ref[:, i * HD : (i + 1) * HD] = w_ref[:, pl.ds(at, HD)]


def forward_kernel(tok_ref, text_ref, probs_ref, out_ref, queries_ref, keys_t_ref, vals_ref, keys, vals_t, *, chunk):
    n, three, _ = tok_ref.shape
    rows = three // 3
    image = n * rows
    text = text_ref.shape[1]
    queries_ref[...] = tok_ref[:, 0:rows, :].reshape(image, HD)
    keys[0:image, :] = tok_ref[:, rows : 2 * rows, :].reshape(image, HD)
    keys[image : image + text, :] = text_ref[0]
    vals_ref[0:image, :] = tok_ref[:, 2 * rows : 3 * rows, :].reshape(image, HD)
    vals_ref[image : image + text, :] = text_ref[1]
    keys_t_ref[...] = keys[...].T
    vals_t[...] = vals_ref[...].T
    factor = HD ** (-0.5) * math.log2(math.e)
    for c in range(image // chunk):
        span = slice(c * chunk, (c + 1) * chunk)
        scores = lax.dot_general(keys[...], queries_ref[span, :], NT, preferred_element_type=F32)
        top = jnp.max(scores, axis=0, keepdims=True)
        weights = jnp.exp2((scores - top) * factor)
        total = jnp.sum(weights, axis=0, keepdims=True)
        low = (weights * (1.0 / total)).astype(BF16)
        probs_ref[:, span] = low
        out_ref[:, span] = jnp.dot(vals_t[...], low, preferred_element_type=F32).astype(BF16)


def partial_kernel(*refs, count):
    each = count // 2
    pieces, weights = refs[:count], refs[count : count + each]
    mine_ref, theirs_ref, cot_ref, weight = refs[count + each :]
    half, place = halves()
    core = lax.axis_index("fsdp")
    rows = pieces[0].shape[0]
    part = rows // 2
    for i, piece in enumerate(pieces):
        source = jnp.bitwise_xor(place, i % each)
        shift = (core if i < each else 1 - core) * part
        for j, side in enumerate((half, 1 - half)):
            at = pl.multiple_of((side * each + source) * rows + shift, 16)
            cot_ref[pl.ds(at, part), :] = piece[j * part : (j + 1) * part, :]
    for d, block in enumerate(weights):
        depth = block.shape[0]
        at = pl.multiple_of(jnp.bitwise_xor(place, d) * depth, 16)
        weight[pl.ds(at, depth), :] = block[...]
    step = 256

    @pl.loop(0, cot_ref.shape[0] // step)
    def _(i):
        at = pl.ds(pl.multiple_of(i * step, step), step)
        part = jnp.dot(cot_ref[at, :], weight[...], preferred_element_type=F32)
        mine_ref[at, :] = part[:, :HD]
        theirs_ref[at, :] = part[:, HD:].astype(BF16)


def weight_grad_kernel(cot_ref, mine_ref, theirs_ref, *refs):
    *dw_refs, outs = refs
    outs[0:HD, :] = mine_ref[...]
    outs[HD : 2 * HD, :] = theirs_ref[...]
    _, place = halves()
    for d, dw_ref in enumerate(dw_refs):
        depth = dw_ref.shape[1]
        at = pl.multiple_of(jnp.bitwise_xor(place, d) * depth, HD)
        dw_ref[...] = jnp.dot(outs[...], cot_ref[:, pl.ds(at, depth)], preferred_element_type=F32).astype(BF16)


def backward_kernel(
    queries_ref, keys_t_ref, vals_ref, probs_ref, out_ref, mine_ref, theirs_ref, send_ref, dk, dv, *, chunk
):
    n, three, _ = send_ref.shape
    rows = three // 3
    image = n * rows
    scale = HD ** (-0.5)
    per = chunk // rows
    for c in range(image // chunk):
        span = slice(c * chunk, (c + 1) * chunk)
        grads = (mine_ref[span, :] + theirs_ref[span, :].astype(F32)).astype(BF16)
        row_dot = jnp.sum(
            grads.astype(F32).T * out_ref[:, span].astype(F32), axis=0, keepdims=True
        )
        prob_grad = lax.dot_general(vals_ref[...], grads, NT, preferred_element_type=F32)
        low = probs_ref[:, span]
        score_grad = (low.astype(F32) * (prob_grad - row_dot)).astype(BF16)
        dq_t = jnp.dot(keys_t_ref[...], score_grad, preferred_element_type=F32) * scale
        send_ref[c * per : (c + 1) * per, 0:rows, :] = dq_t.T.astype(BF16).reshape(per, rows, HD)
        dk_part = jnp.dot(score_grad[0:image, :], queries_ref[span, :], preferred_element_type=F32)
        dv_part = jnp.dot(low[0:image, :], grads, preferred_element_type=F32)
        if c == 0:
            dk[...] = dk_part
            dv[...] = dv_part
        else:
            dk[...] += dk_part
            dv[...] += dv_part
    send_ref[:, rows : 2 * rows, :] = (dk[...] * scale).astype(BF16).reshape(n, rows, HD)
    send_ref[:, 2 * rows : 3 * rows, :] = dv[...].astype(BF16).reshape(n, rows, HD)


def unpack_kernel(tok_ref, q_ref, k_ref, v_ref):
    rows = q_ref.shape[0]
    for h in range(tok_ref.shape[0]):
        for i, ref in enumerate((q_ref, k_ref, v_ref)):
            ref[:, h * HD : (h + 1) * HD] = tok_ref[h, i * rows : (i + 1) * rows, :]


def unpack_weight_kernel(*refs):
    *dw_refs, w_ref = refs
    half, place = halves()
    each = len(dw_refs)
    for d, dw_ref in enumerate(dw_refs):
        source = jnp.bitwise_xor(place, d)
        for i, side in enumerate((half, 1 - half)):
            at = pl.multiple_of((side * each + source) * HD, HD)
            w_ref[:, pl.ds(at, HD)] = dw_ref[i * HD : (i + 1) * HD, :].astype(F32).T


def exchange(array, distance=0, cores=False):
    size = 2 * lax.axis_size("seq")
    pairs = [(i, i ^ (2 * distance + int(cores))) for i in range(size)]
    return lax.ppermute(array, ("seq", "fsdp"), pairs)


def cross_cotangents(d_out, n):
    rows, width = d_out.shape
    part, columns = rows // 2, width // 2
    half, _ = halves()
    first = lax.axis_index("fsdp") * part
    away = lax.dynamic_slice(d_out, (first, (1 - half) * columns), (part, columns))
    kept = lax.dynamic_slice(d_out, (first, half * columns), (part, columns))
    return kept, exchange(away, n // 2)


def gather_cotangents(kept, received, n):
    both = jnp.concatenate([kept, received], axis=0)
    pieces = [both] + [exchange(both, d) for d in range(1, n // 2)]
    return pieces + [exchange(piece, cores=True) for piece in pieces]


def local(q_img, k_img, v_img, k_txt, v_txt, out_weight, d_out):
    n = lax.axis_size("seq")
    rows, width = q_img.shape
    args = (q_img, k_img, v_img, k_txt, v_txt, out_weight, d_out)
    if width // HD != n or lax.axis_size("fsdp") != 2 or n < 4 or n & (n - 1) or rows % 32:
        return local_general(*args)
    depth = out_weight.shape[0]
    image = n * rows
    text = k_txt.shape[0]
    total = image + text
    chunk = 2 * rows
    shape = jax.ShapeDtypeStruct
    vmem = pl.BlockSpec(memory_space=pltpu.VMEM)

    kept, received = cross_cotangents(d_out, n)
    each = n // 2
    big = 60 * 1024 * 1024
    head = pl.BlockSpec((text, HD), lambda i, me_ref: (0, me_ref[0]))
    *w_out, text_head = call(
        lambda me_ref, *refs: pack_weight_kernel(*refs),
        [shape((depth, 2 * HD), BF16)] * each + [shape((2, text, HD), BF16)],
        [lax.axis_index("seq").astype(jnp.int32)[None], out_weight, k_txt, v_txt],
        specs=[vmem, head, head],
        scalars=1,
        moved=4 * depth * width,
        limit=big,
    )
    w_in = [w_out[0]] + [exchange(w_out[d], d) for d in range(1, each)]
    (tok_out,) = call(
        pack_kernel,
        [shape((n, 3 * rows, HD), BF16)],
        [q_img, k_img, v_img],
        moved=4 * 3 * rows * width,
        limit=big,
    )
    tok_out, received = lax.optimization_barrier((tok_out, received))
    received, w_in = lax.optimization_barrier((received, w_in))
    pieces = gather_cotangents(kept, received, n)
    tok_in = lax.all_to_all(tok_out, "seq", split_axis=0, concat_axis=0, tiled=True)

    probs, out_t, queries, keys_t, vals = call(
        functools.partial(forward_kernel, chunk=chunk),
        [shape(dims, BF16) for dims in ((total, image), (HD, image), (image, HD), (HD, total), (total, HD))],
        [tok_in, text_head],
        scratch=[pltpu.VMEM((total, HD), BF16), pltpu.VMEM((HD, total), BF16)],
        flops=4 * total * image * HD,
        moved=4 * total * image,
    )
    out_other = exchange(out_t, each)
    half_width = d_out.shape[1] // 2
    mine, theirs, cot = call(
        functools.partial(partial_kernel, count=len(pieces)),
        [shape((image, HD), F32), shape((image, HD), BF16), shape((image, half_width), BF16)],
        [*pieces, *w_in],
        scratch=[pltpu.VMEM((half_width, 2 * HD), BF16)],
        flops=4 * image * half_width * HD,
        moved=2 * image * half_width,
    )
    theirs = exchange(theirs, each)
    (grad_out,) = call(
        functools.partial(backward_kernel, chunk=chunk),
        [shape((n, 3 * rows, HD), BF16)],
        [queries, keys_t, vals, probs, out_t, mine, theirs],
        scratch=[pltpu.VMEM((image, HD), F32), pltpu.VMEM((image, HD), F32)],
        flops=8 * total * image * HD,
        moved=4 * total * image,
    )
    grad_out, out_other = lax.optimization_barrier((grad_out, out_other))
    grad_in = lax.all_to_all(grad_out, "seq", split_axis=0, concat_axis=0, tiled=True)
    dw_out = call(
        weight_grad_kernel,
        [shape((2 * HD, depth), BF16)] * each,
        [cot, out_t, out_other],
        scratch=[pltpu.VMEM((2 * HD, image), BF16)],
        flops=4 * image * half_width * HD,
        moved=2 * image * half_width,
    )
    dw_in = [dw_out[0]] + [exchange(dw_out[d], d) for d in range(1, each)]
    grads = call(
        unpack_kernel,
        [shape((rows, width), BF16)] * 3,
        [grad_in],
        moved=4 * 3 * rows * width,
    )
    (d_weight,) = call(
        unpack_weight_kernel,
        [shape((depth, width), F32)],
        dw_in,
        moved=6 * depth * width,
    )
    return (*grads, d_weight)


def solution(mesh):
    in_specs = (
        P(("group", "seq"), "fsdp"),
        P(("group", "seq"), "fsdp"),
        P(("group", "seq"), "fsdp"),
        P("group", "fsdp"),
        P("group", "fsdp"),
        P("seq", "fsdp"),
        P(("group", "seq"), None),
    )
    out_specs = (
        P(("group", "seq"), "fsdp"),
        P(("group", "seq"), "fsdp"),
        P(("group", "seq"), "fsdp"),
        P(("group", "seq"), "fsdp"),
    )
    return jax.shard_map(local, mesh=mesh, in_specs=in_specs, out_specs=out_specs, check_vma=False)
```

```python
import functools
import math

import jax
import jax.numpy as jnp
from jax import lax
from jax.experimental import pallas as pl
from jax.experimental.pallas import tpu as pltpu
from jax.sharding import PartitionSpec as P

HD = 128
F32 = jnp.float32
BF16 = jnp.bfloat16
LIMIT = 28 * 1024 * 1024
NT = (((1,), (1,)), ((), ()))


def attend(queries, cotangents, key_rows, value_rows, block_rows):
    score_scale = HD ** (-0.5)
    query_count = queries.shape[0]
    block_count = query_count // block_rows
    query_blocks = queries.reshape(block_count, block_rows, HD)
    grad_blocks = cotangents.reshape(block_count, block_rows, HD)

    def one_block(accumulated, pair_item):
        query_block, grad_block = pair_item
        scores = jnp.dot(query_block, key_rows.T, preferred_element_type=jnp.float32) * score_scale
        row_max = jnp.max(scores, axis=1, keepdims=True)
        probs = jnp.exp(scores - row_max)
        probs = probs / jnp.sum(probs, axis=1, keepdims=True)
        probs_low = probs.astype(jnp.bfloat16)
        out_rows = jnp.dot(probs_low, value_rows, preferred_element_type=jnp.float32).astype(
            jnp.bfloat16
        )
        prob_grad = jnp.dot(grad_block, value_rows.T, preferred_element_type=jnp.float32)
        row_dot = jnp.sum(
            grad_block.astype(jnp.float32) * out_rows.astype(jnp.float32), axis=1, keepdims=True
        )
        score_grad = (probs * (prob_grad - row_dot)).astype(jnp.bfloat16)
        query_grad = (
            jnp.dot(score_grad, key_rows, preferred_element_type=jnp.float32) * score_scale
        ).astype(jnp.bfloat16)
        key_grad = (
            accumulated[0]
            + jnp.dot(score_grad.T, query_block, preferred_element_type=jnp.float32) * score_scale
        )
        value_grad = accumulated[1] + jnp.dot(
            probs_low.T, grad_block, preferred_element_type=jnp.float32
        )
        return ((key_grad, value_grad), (query_grad, out_rows))

    empty = jnp.zeros((key_rows.shape[0], HD), jnp.float32)
    (key_grad, value_grad), (query_grad, out_rows) = lax.scan(
        one_block, (empty, empty), (query_blocks, grad_blocks)
    )
    return (
        query_grad.reshape(query_count, HD),
        out_rows.reshape(query_count, HD),
        key_grad,
        value_grad,
    )


def local_general(q_img, k_img, v_img, k_txt, v_txt, out_weight, d_out):
    rows_here = q_img.shape[0]
    heads_here = q_img.shape[1] // HD
    seq_count = lax.axis_size("seq")
    share_count = seq_count // heads_here
    part_rows = rows_here // share_count
    seq_index = lax.axis_index("seq")
    head_index = seq_index // share_count
    column_cut = d_out
    attn_grad = jnp.dot(
        column_cut,
        lax.all_gather(out_weight, "seq", axis=0, tiled=True),
        preferred_element_type=jnp.float32,
    ).astype(jnp.bfloat16)

    def to_heads(array_in):
        shaped = array_in.reshape(share_count, part_rows, heads_here, HD).transpose(2, 0, 1, 3)
        return shaped.reshape(seq_count, part_rows, HD)

    def whole_heads(array_in):
        shaped = array_in.reshape(rows_here, heads_here, HD).transpose(1, 0, 2)
        shaped = jnp.broadcast_to(shaped[:, None], (heads_here, share_count, rows_here, HD))
        return shaped.reshape(seq_count, rows_here, HD)

    def from_heads(array_in):
        shaped = array_in.reshape(heads_here, share_count, part_rows, HD).transpose(1, 2, 0, 3)
        return shaped.reshape(rows_here, heads_here * HD)

    text_keys = lax.dynamic_slice_in_dim(k_txt, head_index * HD, HD, 1)
    text_values = lax.dynamic_slice_in_dim(v_txt, head_index * HD, HD, 1)
    query_side = jnp.concatenate([to_heads(q_img), to_heads(attn_grad)], axis=2)
    key_side = jnp.concatenate([whole_heads(k_img), whole_heads(v_img)], axis=2)
    packed = jnp.concatenate([query_side, key_side], axis=1)
    received = lax.all_to_all(packed, "seq", split_axis=0, concat_axis=0, tiled=True)
    queries = received[:, :part_rows, :HD].reshape(seq_count * part_rows, HD)
    cotangents = received[:, :part_rows, HD:].reshape(seq_count * part_rows, HD)
    image_keys = received[:, part_rows:, :HD].reshape(seq_count * rows_here, HD)
    image_values = received[:, part_rows:, HD:].reshape(seq_count * rows_here, HD)
    key_rows = jnp.concatenate([image_keys, text_keys], axis=0)
    value_rows = jnp.concatenate([image_values, text_values], axis=0)
    query_grad, out_rows, key_grad, value_grad = attend(
        queries, cotangents, key_rows, value_rows, min(512, queries.shape[0])
    )
    image_count = image_keys.shape[0]
    query_part = (
        jnp.concatenate([query_grad, out_rows], axis=1)
        .astype(jnp.float32)
        .reshape(seq_count, part_rows, 2 * HD)
    )
    key_part = jnp.concatenate([key_grad[:image_count], value_grad[:image_count]], axis=1).reshape(
        seq_count, rows_here, 2 * HD
    )
    returned = lax.all_to_all(
        jnp.concatenate([query_part, key_part], axis=1).astype(jnp.bfloat16),
        "seq",
        split_axis=0,
        concat_axis=0,
        tiled=True,
    ).astype(jnp.float32)
    q_grad = from_heads(returned[:, :part_rows, :HD]).astype(jnp.bfloat16)
    out_tok = from_heads(returned[:, :part_rows, HD:]).astype(jnp.bfloat16)
    summed = jnp.sum(
        returned[:, part_rows:, :].reshape(heads_here, share_count, rows_here, 2 * HD), axis=1
    )
    summed = summed.transpose(1, 0, 2)
    k_grad = summed[:, :, :HD].reshape(rows_here, heads_here * HD).astype(jnp.bfloat16)
    v_grad = summed[:, :, HD:].reshape(rows_here, heads_here * HD).astype(jnp.bfloat16)
    column_cut = d_out
    d_weight = lax.psum_scatter(
        jnp.dot(column_cut.T, out_tok, preferred_element_type=jnp.float32).astype(jnp.bfloat16),
        "seq",
        scatter_dimension=0,
        tiled=True,
    ).astype(jnp.float32)
    return (q_grad, k_grad, v_grad, d_weight)


def call(kernel, outs, args, specs=None, scratch=(), scalars=0, out_specs=None, flops=0, moved=0, limit=LIMIT):
    vmem = pl.BlockSpec(memory_space=pltpu.VMEM)
    if specs is None:
        specs = [vmem] * (len(args) - scalars)
    if out_specs is None:
        out_specs = [vmem] * len(outs)
    return pl.pallas_call(
        kernel,
        out_shape=outs,
        grid_spec=pltpu.PrefetchScalarGridSpec(
            num_scalar_prefetch=scalars,
            grid=(1,),
            in_specs=specs,
            out_specs=out_specs,
            scratch_shapes=list(scratch),
        ),
        compiler_params=pltpu.CompilerParams(vmem_limit_bytes=limit),
        cost_estimate=pl.CostEstimate(flops=flops, bytes_accessed=moved, transcendentals=0),
    )(*args)


STEPS = (0, 2, 4, 6)


def head_columns(step, other_row):
    return pl.ds(pl.multiple_of(jnp.bitwise_xor(lax.axis_index("seq"), step + other_row) * HD, HD), HD)


def pack_kernel(me_ref, q_ref, k_ref, v_ref, w_ref, kt_ref, vt_ref, tok_ref, keep_ref, give_ref, text_ref):
    rows = q_ref.shape[0]
    for h in range(tok_ref.shape[0]):
        for i, ref in enumerate((q_ref, k_ref, v_ref)):
            tok_ref[h, i * rows : (i + 1) * rows, :] = ref[:, h * HD : (h + 1) * HD]
    for i, step in enumerate(STEPS):
        cols = slice(i * HD, (i + 1) * HD)
        keep_ref[:, cols] = w_ref[:, head_columns(step, 0)]
        give_ref[:, cols] = w_ref[:, head_columns(step, 1)]
    text_ref[0] = kt_ref[...]
    text_ref[1] = vt_ref[...]


def forward_kernel(tok_ref, text_ref, probs_ref, out_ref, queries_ref, keys_t_ref, vals_ref, keys, vals_t, *, chunk):
    n, three, _ = tok_ref.shape
    rows = three // 3
    image = n * rows
    text = text_ref.shape[1]
    queries_ref[...] = tok_ref[:, 0:rows, :].reshape(image, HD)
    keys[0:image, :] = tok_ref[:, rows : 2 * rows, :].reshape(image, HD)
    keys[image : image + text, :] = text_ref[0]
    vals_ref[0:image, :] = tok_ref[:, 2 * rows : 3 * rows, :].reshape(image, HD)
    vals_ref[image : image + text, :] = text_ref[1]
    keys_t_ref[...] = keys[...].T
    vals_t[...] = vals_ref[...].T
    factor = HD ** (-0.5) * math.log2(math.e)
    for c in range(image // chunk):
        span = slice(c * chunk, (c + 1) * chunk)
        scores = lax.dot_general(keys[...], queries_ref[span, :], NT, preferred_element_type=F32)
        top = jnp.max(scores, axis=0, keepdims=True)
        weights = jnp.exp2((scores - top) * factor)
        total = jnp.sum(weights, axis=0, keepdims=True)
        low = (weights * (1.0 / total)).astype(BF16)
        probs_ref[:, span] = low
        out_ref[:, span] = jnp.dot(vals_t[...], low, preferred_element_type=F32).astype(BF16)


def partial_kernel(*refs):
    *pieces, own_ref, other_ref, mine_ref, far_ref, near_ref, near_far_ref, cot_ref, weight = refs
    me = lax.axis_index("seq")
    core = lax.axis_index("fsdp")
    count = len(STEPS)
    part = pieces[0].shape[0] // count
    for p, piece in enumerate(pieces):
        row, swapped = p % 2, p // 2
        shift = jnp.bitwise_xor(core, swapped) * part
        for i, step in enumerate(STEPS):
            at = pl.multiple_of(jnp.bitwise_xor(me, step + row) * (2 * part) + shift, 16)
            cot_ref[pl.ds(at, part), :] = piece[i * part : (i + 1) * part, :]
    depth = own_ref.shape[0]
    y = lax.rem(me, 2)
    weight[pl.ds(pl.multiple_of(y * depth, 16), depth), :] = own_ref[...]
    weight[pl.ds(pl.multiple_of((1 - y) * depth, 16), depth), :] = other_ref[...]
    step = 256

    @pl.loop(0, cot_ref.shape[0] // step)
    def _(i):
        at = pl.ds(pl.multiple_of(i * step, step), step)
        part = jnp.dot(cot_ref[at, :], weight[...], preferred_element_type=F32)
        mine_ref[at, :] = part[:, :HD]
        near_ref[at, :] = part[:, HD : 2 * HD].astype(BF16)
        far_ref[at, :] = part[:, 2 * HD : 3 * HD]
        near_far_ref[at, :] = part[:, 3 * HD :].astype(BF16)


def weight_grad_kernel(cot_ref, *refs):
    *out_refs, own_ref, other_ref, outs = refs
    for i, ref in enumerate(out_refs):
        outs[i * HD : (i + 1) * HD, :] = ref[...]
    depth = own_ref.shape[1]
    y = lax.rem(lax.axis_index("seq"), 2)
    for ref, row in ((own_ref, y), (other_ref, 1 - y)):
        at = pl.multiple_of(row * depth, HD)
        ref[...] = jnp.dot(outs[...], cot_ref[:, pl.ds(at, depth)], preferred_element_type=F32).astype(BF16)


def backward_kernel(
    queries_ref, keys_t_ref, vals_ref, probs_ref, out_ref, mine_ref, near_ref, far_ref, send_ref, dk, dv, *, chunk
):
    n, three, _ = send_ref.shape
    rows = three // 3
    image = n * rows
    scale = HD ** (-0.5)
    per = chunk // rows
    for c in range(image // chunk):
        span = slice(c * chunk, (c + 1) * chunk)
        grads = mine_ref[span, :] + near_ref[span, :].astype(F32) + far_ref[span, :].astype(F32)
        grads = grads.astype(BF16)
        row_dot = jnp.sum(
            grads.astype(F32).T * out_ref[:, span].astype(F32), axis=0, keepdims=True
        )
        prob_grad = lax.dot_general(vals_ref[...], grads, NT, preferred_element_type=F32)
        low = probs_ref[:, span]
        score_grad = (low.astype(F32) * (prob_grad - row_dot)).astype(BF16)
        dq_t = jnp.dot(keys_t_ref[...], score_grad, preferred_element_type=F32) * scale
        send_ref[c * per : (c + 1) * per, 0:rows, :] = dq_t.T.astype(BF16).reshape(per, rows, HD)
        dk_part = jnp.dot(score_grad[0:image, :], queries_ref[span, :], preferred_element_type=F32)
        dv_part = jnp.dot(low[0:image, :], grads, preferred_element_type=F32)
        if c == 0:
            dk[...] = dk_part
            dv[...] = dv_part
        else:
            dk[...] += dk_part
            dv[...] += dv_part
    send_ref[:, rows : 2 * rows, :] = (dk[...] * scale).astype(BF16).reshape(n, rows, HD)
    send_ref[:, 2 * rows : 3 * rows, :] = dv[...].astype(BF16).reshape(n, rows, HD)


def unpack_kernel(tok_ref, q_ref, k_ref, v_ref):
    rows = q_ref.shape[0]
    for h in range(tok_ref.shape[0]):
        for i, ref in enumerate((q_ref, k_ref, v_ref)):
            ref[:, h * HD : (h + 1) * HD] = tok_ref[h, i * rows : (i + 1) * rows, :]


def unpack_weight_kernel(own_ref, other_ref, w_ref):
    for other_row, ref in enumerate((own_ref, other_ref)):
        for i, step in enumerate(STEPS):
            w_ref[:, head_columns(step, other_row)] = ref[i * HD : (i + 1) * HD, :].astype(F32).T


def exchange(array, distance=0, cores=False):
    if not distance and not cores:
        return array
    size = 2 * lax.axis_size("seq")
    pairs = [(i, i ^ (2 * distance + int(cores))) for i in range(size)]
    return lax.ppermute(array, ("seq", "fsdp"), pairs)


def gather_cotangents(d_out):
    rows, width = d_out.shape
    part, columns = rows // 2, width // len(STEPS)
    z = lax.axis_index("seq") // 2
    first = lax.axis_index("fsdp") * part
    along = [
        exchange(lax.dynamic_slice(d_out, (first, (z ^ (step // 2)) * columns), (part, columns)), step)
        for step in STEPS
    ]
    row = jnp.concatenate(along, axis=0)
    pieces = [row, exchange(row, 1)]
    return pieces + [exchange(piece, cores=True) for piece in pieces]


def local(q_img, k_img, v_img, k_txt, v_txt, out_weight, d_out):
    n = lax.axis_size("seq")
    rows, width = q_img.shape
    args = (q_img, k_img, v_img, k_txt, v_txt, out_weight, d_out)
    if n != 2 * len(STEPS) or width // HD != n or lax.axis_size("fsdp") != 2 or rows % 32:
        return local_general(*args)
    depth = out_weight.shape[0]
    image = n * rows
    text = k_txt.shape[0]
    total = image + text
    chunk = 2 * rows
    shape = jax.ShapeDtypeStruct
    vmem = pl.BlockSpec(memory_space=pltpu.VMEM)

    head = pl.BlockSpec((text, HD), lambda i, me_ref: (0, me_ref[0]))
    tok_out, keep, give, text_head = call(
        pack_kernel,
        [shape((n, 3 * rows, HD), BF16)] + [shape((depth, 4 * HD), BF16)] * 2 + [shape((2, text, HD), BF16)],
        [lax.axis_index("seq").astype(jnp.int32)[None], q_img, k_img, v_img, out_weight, k_txt, v_txt],
        specs=[vmem] * 4 + [head] * 2,
        scalars=1,
        moved=4 * (3 * rows + depth) * width,
        limit=60 * 1024 * 1024,
    )
    given = exchange(give, 1)
    pieces = gather_cotangents(d_out)
    tok_in = lax.all_to_all(tok_out, "seq", split_axis=0, concat_axis=0, tiled=True)

    probs, out_t, queries, keys_t, vals = call(
        functools.partial(forward_kernel, chunk=chunk),
        [shape(dims, BF16) for dims in ((total, image), (HD, image), (image, HD), (HD, total), (total, HD))],
        [tok_in, text_head],
        scratch=[pltpu.VMEM((total, HD), BF16), pltpu.VMEM((HD, total), BF16)],
        flops=4 * total * image * HD,
        moved=4 * total * image,
    )
    columns = pieces[0].shape[1]
    mine, far, near, near_far, cot = call(
        partial_kernel,
        [shape((image, HD), F32)] * 2 + [shape((image, HD), BF16)] * 2 + [shape((image, columns), BF16)],
        [*pieces, keep, given],
        scratch=[pltpu.VMEM((columns, 4 * HD), BF16)],
        flops=8 * image * columns * HD,
        moved=2 * image * columns,
    )
    near_far = exchange(near_far, 2)
    far = exchange((far + near_far.astype(F32)).astype(BF16), 4)
    near, _ = lax.optimization_barrier((near, near_far))
    near = exchange(near, 2)
    out_far = exchange(out_t, 4)
    outs = [out_t, exchange(out_t, 2), out_far, exchange(out_far, 2)]
    (grad_out,) = call(
        functools.partial(backward_kernel, chunk=chunk),
        [shape((n, 3 * rows, HD), BF16)],
        [queries, keys_t, vals, probs, out_t, mine, near, far],
        scratch=[pltpu.VMEM((image, HD), F32), pltpu.VMEM((image, HD), F32)],
        flops=8 * total * image * HD,
        moved=4 * total * image,
    )
    grad_in = lax.all_to_all(grad_out, "seq", split_axis=0, concat_axis=0, tiled=True)
    dw_own, dw_other = call(
        weight_grad_kernel,
        [shape((4 * HD, depth), BF16)] * 2,
        [cot, *outs],
        scratch=[pltpu.VMEM((4 * HD, image), BF16)],
        flops=8 * image * columns * HD,
        moved=2 * image * columns,
    )
    grads = call(
        unpack_kernel,
        [shape((rows, width), BF16)] * 3,
        [grad_in],
        moved=4 * 3 * rows * width,
    )
    (d_weight,) = call(
        unpack_weight_kernel,
        [shape((depth, width), F32)],
        [dw_own, exchange(dw_other, 1)],
        moved=6 * depth * width,
    )
    return (*grads, d_weight)


def solution(mesh):
    in_specs = (
        P(("group", "seq"), "fsdp"),
        P(("group", "seq"), "fsdp"),
        P(("group", "seq"), "fsdp"),
        P("group", "fsdp"),
        P("group", "fsdp"),
        P("seq", "fsdp"),
        P(("group", "seq"), None),
    )
    out_specs = (
        P(("group", "seq"), "fsdp"),
        P(("group", "seq"), "fsdp"),
        P(("group", "seq"), "fsdp"),
        P(("group", "seq"), "fsdp"),
    )
    return jax.shard_map(local, mesh=mesh, in_specs=in_specs, out_specs=out_specs, check_vma=False)
```

```python
import functools
import math

import jax
import jax.numpy as jnp
from jax import lax
from jax.experimental import pallas as pl
from jax.experimental.pallas import tpu as pltpu
from jax.sharding import PartitionSpec as P

HD = 128
F32 = jnp.float32
BF16 = jnp.bfloat16
LIMIT = 28 * 1024 * 1024
NT = (((1,), (1,)), ((), ()))


def attend(queries, cotangents, key_rows, value_rows, block_rows):
    score_scale = HD ** (-0.5)
    query_count = queries.shape[0]
    block_count = query_count // block_rows
    query_blocks = queries.reshape(block_count, block_rows, HD)
    grad_blocks = cotangents.reshape(block_count, block_rows, HD)

    def one_block(accumulated, pair_item):
        query_block, grad_block = pair_item
        scores = jnp.dot(query_block, key_rows.T, preferred_element_type=jnp.float32) * score_scale
        row_max = jnp.max(scores, axis=1, keepdims=True)
        probs = jnp.exp(scores - row_max)
        probs = probs / jnp.sum(probs, axis=1, keepdims=True)
        probs_low = probs.astype(jnp.bfloat16)
        out_rows = jnp.dot(probs_low, value_rows, preferred_element_type=jnp.float32).astype(
            jnp.bfloat16
        )
        prob_grad = jnp.dot(grad_block, value_rows.T, preferred_element_type=jnp.float32)
        row_dot = jnp.sum(
            grad_block.astype(jnp.float32) * out_rows.astype(jnp.float32), axis=1, keepdims=True
        )
        score_grad = (probs * (prob_grad - row_dot)).astype(jnp.bfloat16)
        query_grad = (
            jnp.dot(score_grad, key_rows, preferred_element_type=jnp.float32) * score_scale
        ).astype(jnp.bfloat16)
        key_grad = (
            accumulated[0]
            + jnp.dot(score_grad.T, query_block, preferred_element_type=jnp.float32) * score_scale
        )
        value_grad = accumulated[1] + jnp.dot(
            probs_low.T, grad_block, preferred_element_type=jnp.float32
        )
        return ((key_grad, value_grad), (query_grad, out_rows))

    empty = jnp.zeros((key_rows.shape[0], HD), jnp.float32)
    (key_grad, value_grad), (query_grad, out_rows) = lax.scan(
        one_block, (empty, empty), (query_blocks, grad_blocks)
    )
    return (
        query_grad.reshape(query_count, HD),
        out_rows.reshape(query_count, HD),
        key_grad,
        value_grad,
    )


def local_general(q_img, k_img, v_img, k_txt, v_txt, out_weight, d_out):
    rows_here = q_img.shape[0]
    heads_here = q_img.shape[1] // HD
    seq_count = lax.axis_size("seq")
    share_count = seq_count // heads_here
    part_rows = rows_here // share_count
    seq_index = lax.axis_index("seq")
    head_index = seq_index // share_count
    column_cut = d_out
    attn_grad = jnp.dot(
        column_cut,
        lax.all_gather(out_weight, "seq", axis=0, tiled=True),
        preferred_element_type=jnp.float32,
    ).astype(jnp.bfloat16)

    def to_heads(array_in):
        shaped = array_in.reshape(share_count, part_rows, heads_here, HD).transpose(2, 0, 1, 3)
        return shaped.reshape(seq_count, part_rows, HD)

    def whole_heads(array_in):
        shaped = array_in.reshape(rows_here, heads_here, HD).transpose(1, 0, 2)
        shaped = jnp.broadcast_to(shaped[:, None], (heads_here, share_count, rows_here, HD))
        return shaped.reshape(seq_count, rows_here, HD)

    def from_heads(array_in):
        shaped = array_in.reshape(heads_here, share_count, part_rows, HD).transpose(1, 2, 0, 3)
        return shaped.reshape(rows_here, heads_here * HD)

    text_keys = lax.dynamic_slice_in_dim(k_txt, head_index * HD, HD, 1)
    text_values = lax.dynamic_slice_in_dim(v_txt, head_index * HD, HD, 1)
    query_side = jnp.concatenate([to_heads(q_img), to_heads(attn_grad)], axis=2)
    key_side = jnp.concatenate([whole_heads(k_img), whole_heads(v_img)], axis=2)
    packed = jnp.concatenate([query_side, key_side], axis=1)
    received = lax.all_to_all(packed, "seq", split_axis=0, concat_axis=0, tiled=True)
    queries = received[:, :part_rows, :HD].reshape(seq_count * part_rows, HD)
    cotangents = received[:, :part_rows, HD:].reshape(seq_count * part_rows, HD)
    image_keys = received[:, part_rows:, :HD].reshape(seq_count * rows_here, HD)
    image_values = received[:, part_rows:, HD:].reshape(seq_count * rows_here, HD)
    key_rows = jnp.concatenate([image_keys, text_keys], axis=0)
    value_rows = jnp.concatenate([image_values, text_values], axis=0)
    query_grad, out_rows, key_grad, value_grad = attend(
        queries, cotangents, key_rows, value_rows, min(512, queries.shape[0])
    )
    image_count = image_keys.shape[0]
    query_part = (
        jnp.concatenate([query_grad, out_rows], axis=1)
        .astype(jnp.float32)
        .reshape(seq_count, part_rows, 2 * HD)
    )
    key_part = jnp.concatenate([key_grad[:image_count], value_grad[:image_count]], axis=1).reshape(
        seq_count, rows_here, 2 * HD
    )
    returned = lax.all_to_all(
        jnp.concatenate([query_part, key_part], axis=1).astype(jnp.bfloat16),
        "seq",
        split_axis=0,
        concat_axis=0,
        tiled=True,
    ).astype(jnp.float32)
    q_grad = from_heads(returned[:, :part_rows, :HD]).astype(jnp.bfloat16)
    out_tok = from_heads(returned[:, :part_rows, HD:]).astype(jnp.bfloat16)
    summed = jnp.sum(
        returned[:, part_rows:, :].reshape(heads_here, share_count, rows_here, 2 * HD), axis=1
    )
    summed = summed.transpose(1, 0, 2)
    k_grad = summed[:, :, :HD].reshape(rows_here, heads_here * HD).astype(jnp.bfloat16)
    v_grad = summed[:, :, HD:].reshape(rows_here, heads_here * HD).astype(jnp.bfloat16)
    column_cut = d_out
    d_weight = lax.psum_scatter(
        jnp.dot(column_cut.T, out_tok, preferred_element_type=jnp.float32).astype(jnp.bfloat16),
        "seq",
        scatter_dimension=0,
        tiled=True,
    ).astype(jnp.float32)
    return (q_grad, k_grad, v_grad, d_weight)


def call(kernel, outs, args, specs=None, scratch=(), scalars=0, out_specs=None, flops=0, moved=0, limit=LIMIT):
    vmem = pl.BlockSpec(memory_space=pltpu.VMEM)
    if specs is None:
        specs = [vmem] * (len(args) - scalars)
    if out_specs is None:
        out_specs = [vmem] * len(outs)
    return pl.pallas_call(
        kernel,
        out_shape=outs,
        grid_spec=pltpu.PrefetchScalarGridSpec(
            num_scalar_prefetch=scalars,
            grid=(1,),
            in_specs=specs,
            out_specs=out_specs,
            scratch_shapes=list(scratch),
        ),
        compiler_params=pltpu.CompilerParams(vmem_limit_bytes=limit),
        cost_estimate=pl.CostEstimate(flops=flops, bytes_accessed=moved, transcendentals=0),
    )(*args)


STEPS = (0, 2, 4, 6)


def head_columns(step, other_row):
    return pl.ds(pl.multiple_of(jnp.bitwise_xor(lax.axis_index("seq"), step + other_row) * HD, HD), HD)


def pack_kernel(q_ref, k_ref, v_ref, tok_ref):
    rows = q_ref.shape[0]
    for h in range(tok_ref.shape[0]):
        for i, ref in enumerate((q_ref, k_ref, v_ref)):
            tok_ref[h, i * rows : (i + 1) * rows, :] = ref[:, h * HD : (h + 1) * HD]


def pack_weight_kernel(me_ref, w_ref, kt_ref, vt_ref, keep_ref, give_ref, text_ref):
    for i, step in enumerate(STEPS):
        cols = slice(i * HD, (i + 1) * HD)
        keep_ref[:, cols] = w_ref[:, head_columns(step, 0)]
        give_ref[:, cols] = w_ref[:, head_columns(step, 1)]
    text_ref[0] = kt_ref[...]
    text_ref[1] = vt_ref[...]


def forward_kernel(tok_ref, text_ref, probs_ref, out_ref, queries_ref, keys_t_ref, vals_ref, keys, vals_t, *, chunk):
    n, three, _ = tok_ref.shape
    rows = three // 3
    image = n * rows
    text = text_ref.shape[1]
    queries_ref[...] = tok_ref[:, 0:rows, :].reshape(image, HD)
    keys[0:image, :] = tok_ref[:, rows : 2 * rows, :].reshape(image, HD)
    keys[image : image + text, :] = text_ref[0]
    vals_ref[0:image, :] = tok_ref[:, 2 * rows : 3 * rows, :].reshape(image, HD)
    vals_ref[image : image + text, :] = text_ref[1]
    keys_t_ref[...] = keys[...].T
    vals_t[...] = vals_ref[...].T
    factor = HD ** (-0.5) * math.log2(math.e)
    for c in range(image // chunk):
        span = slice(c * chunk, (c + 1) * chunk)
        scores = lax.dot_general(keys[...], queries_ref[span, :], NT, preferred_element_type=F32)
        top = jnp.max(scores, axis=0, keepdims=True)
        weights = jnp.exp2((scores - top) * factor)
        total = jnp.sum(weights, axis=0, keepdims=True)
        low = (weights * (1.0 / total)).astype(BF16)
        probs_ref[:, span] = low
        out_ref[:, span] = jnp.dot(vals_t[...], low, preferred_element_type=F32).astype(BF16)


def partial_kernel(*refs):
    *pieces, own_ref, other_ref, mine_ref, far_ref, near_ref, near_far_ref, cot_ref, weight = refs
    me = lax.axis_index("seq")
    core = lax.axis_index("fsdp")
    count = len(STEPS)
    part = pieces[0].shape[0] // count
    for p, piece in enumerate(pieces):
        row, swapped = p % 2, p // 2
        shift = jnp.bitwise_xor(core, swapped) * part
        for i, step in enumerate(STEPS):
            at = pl.multiple_of(jnp.bitwise_xor(me, step + row) * (2 * part) + shift, 16)
            cot_ref[pl.ds(at, part), :] = piece[i * part : (i + 1) * part, :]
    depth = own_ref.shape[0]
    y = lax.rem(me, 2)
    weight[pl.ds(pl.multiple_of(y * depth, 16), depth), :] = own_ref[...]
    weight[pl.ds(pl.multiple_of((1 - y) * depth, 16), depth), :] = other_ref[...]
    step = 256

    @pl.loop(0, cot_ref.shape[0] // step)
    def _(i):
        at = pl.ds(pl.multiple_of(i * step, step), step)
        part = jnp.dot(cot_ref[at, :], weight[...], preferred_element_type=F32)
        mine_ref[at, :] = part[:, :HD]
        near_ref[at, :] = part[:, HD : 2 * HD].astype(BF16)
        far_ref[at, :] = part[:, 2 * HD : 3 * HD]
        near_far_ref[at, :] = part[:, 3 * HD :].astype(BF16)


def weight_grad_kernel(cot_ref, *refs):
    *out_refs, own_ref, other_ref, outs = refs
    for i, ref in enumerate(out_refs):
        outs[i * HD : (i + 1) * HD, :] = ref[...]
    depth = own_ref.shape[1]
    y = lax.rem(lax.axis_index("seq"), 2)
    for ref, row in ((own_ref, y), (other_ref, 1 - y)):
        at = pl.multiple_of(row * depth, HD)
        ref[...] = jnp.dot(outs[...], cot_ref[:, pl.ds(at, depth)], preferred_element_type=F32).astype(BF16)


def backward_kernel(
    queries_ref, keys_t_ref, vals_ref, probs_ref, out_ref, mine_ref, near_ref, far_ref, send_ref, dk, dv, *, chunk
):
    n, three, _ = send_ref.shape
    rows = three // 3
    image = n * rows
    scale = HD ** (-0.5)
    per = chunk // rows
    for c in range(image // chunk):
        span = slice(c * chunk, (c + 1) * chunk)
        grads = mine_ref[span, :] + near_ref[span, :].astype(F32) + far_ref[span, :].astype(F32)
        grads = grads.astype(BF16)
        row_dot = jnp.sum(
            grads.astype(F32).T * out_ref[:, span].astype(F32), axis=0, keepdims=True
        )
        prob_grad = lax.dot_general(vals_ref[...], grads, NT, preferred_element_type=F32)
        low = probs_ref[:, span]
        score_grad = (low.astype(F32) * (prob_grad - row_dot)).astype(BF16)
        dq_t = jnp.dot(keys_t_ref[...], score_grad, preferred_element_type=F32) * scale
        send_ref[c * per : (c + 1) * per, 0:rows, :] = dq_t.T.astype(BF16).reshape(per, rows, HD)
        dk_part = jnp.dot(score_grad[0:image, :], queries_ref[span, :], preferred_element_type=F32)
        dv_part = jnp.dot(low[0:image, :], grads, preferred_element_type=F32)
        if c == 0:
            dk[...] = dk_part
            dv[...] = dv_part
        else:
            dk[...] += dk_part
            dv[...] += dv_part
    send_ref[:, rows : 2 * rows, :] = (dk[...] * scale).astype(BF16).reshape(n, rows, HD)
    send_ref[:, 2 * rows : 3 * rows, :] = dv[...].astype(BF16).reshape(n, rows, HD)


def unpack_kernel(tok_ref, q_ref, k_ref, v_ref):
    rows = q_ref.shape[0]
    for h in range(tok_ref.shape[0]):
        for i, ref in enumerate((q_ref, k_ref, v_ref)):
            ref[:, h * HD : (h + 1) * HD] = tok_ref[h, i * rows : (i + 1) * rows, :]


def unpack_weight_kernel(own_ref, other_ref, w_ref):
    for other_row, ref in enumerate((own_ref, other_ref)):
        for i, step in enumerate(STEPS):
            w_ref[:, head_columns(step, other_row)] = ref[i * HD : (i + 1) * HD, :].astype(F32).T


def exchange(array, distance=0, cores=False):
    if not distance and not cores:
        return array
    size = 2 * lax.axis_size("seq")
    pairs = [(i, i ^ (2 * distance + int(cores))) for i in range(size)]
    return lax.ppermute(array, ("seq", "fsdp"), pairs)


def gather_cotangents(d_out):
    rows, width = d_out.shape
    part, columns = rows // 2, width // len(STEPS)
    z = lax.axis_index("seq") // 2
    first = lax.axis_index("fsdp") * part
    along = [
        exchange(lax.dynamic_slice(d_out, (first, (z ^ (step // 2)) * columns), (part, columns)), step)
        for step in STEPS
    ]
    row = jnp.concatenate(along, axis=0)
    pieces = [row, exchange(row, 1)]
    return pieces + [exchange(piece, cores=True) for piece in pieces]


def local(q_img, k_img, v_img, k_txt, v_txt, out_weight, d_out):
    n = lax.axis_size("seq")
    rows, width = q_img.shape
    args = (q_img, k_img, v_img, k_txt, v_txt, out_weight, d_out)
    if n != 2 * len(STEPS) or width // HD != n or lax.axis_size("fsdp") != 2 or rows % 32:
        return local_general(*args)
    depth = out_weight.shape[0]
    image = n * rows
    text = k_txt.shape[0]
    total = image + text
    chunk = 2 * rows
    shape = jax.ShapeDtypeStruct
    vmem = pl.BlockSpec(memory_space=pltpu.VMEM)

    head = pl.BlockSpec((text, HD), lambda i, me_ref: (0, me_ref[0]))
    big = 60 * 1024 * 1024
    keep, give, text_head = call(
        pack_weight_kernel,
        [shape((depth, 4 * HD), BF16)] * 2 + [shape((2, text, HD), BF16)],
        [lax.axis_index("seq").astype(jnp.int32)[None], out_weight, k_txt, v_txt],
        specs=[vmem] + [head] * 2,
        scalars=1,
        moved=4 * depth * width,
        limit=big,
    )
    d_out, give = lax.optimization_barrier((d_out, give))
    given = exchange(give, 1)
    pieces = gather_cotangents(d_out)
    (tok_out,) = call(
        pack_kernel,
        [shape((n, 3 * rows, HD), BF16)],
        [q_img, k_img, v_img],
        moved=4 * 3 * rows * width,
        limit=big,
    )
    tok_out, given = lax.optimization_barrier((tok_out, given))
    tok_in = lax.all_to_all(tok_out, "seq", split_axis=0, concat_axis=0, tiled=True)

    probs, out_t, queries, keys_t, vals = call(
        functools.partial(forward_kernel, chunk=chunk),
        [shape(dims, BF16) for dims in ((total, image), (HD, image), (image, HD), (HD, total), (total, HD))],
        [tok_in, text_head],
        scratch=[pltpu.VMEM((total, HD), BF16), pltpu.VMEM((HD, total), BF16)],
        flops=4 * total * image * HD,
        moved=4 * total * image,
    )
    columns = pieces[0].shape[1]
    mine, far, near, near_far, cot = call(
        partial_kernel,
        [shape((image, HD), F32)] * 2 + [shape((image, HD), BF16)] * 2 + [shape((image, columns), BF16)],
        [*pieces, keep, given],
        scratch=[pltpu.VMEM((columns, 4 * HD), BF16)],
        flops=8 * image * columns * HD,
        moved=2 * image * columns,
    )
    near_far = exchange(near_far, 2)
    far = exchange((far + near_far.astype(F32)).astype(BF16), 4)
    near, _ = lax.optimization_barrier((near, near_far))
    near = exchange(near, 2)
    out_late, far = lax.optimization_barrier((out_t, far))
    out_far = exchange(out_late, 4)
    (grad_out,) = call(
        functools.partial(backward_kernel, chunk=chunk),
        [shape((n, 3 * rows, HD), BF16)],
        [queries, keys_t, vals, probs, out_t, mine, near, far],
        scratch=[pltpu.VMEM((image, HD), F32), pltpu.VMEM((image, HD), F32)],
        flops=8 * total * image * HD,
        moved=4 * total * image,
    )
    grad_out, out_far = lax.optimization_barrier((grad_out, out_far))
    grad_in = lax.all_to_all(grad_out, "seq", split_axis=0, concat_axis=0, tiled=True)
    outs = [out_t, exchange(out_t, 2), out_far, exchange(out_far, 2)]
    dw_own, dw_other = call(
        weight_grad_kernel,
        [shape((4 * HD, depth), BF16)] * 2,
        [cot, *outs],
        scratch=[pltpu.VMEM((4 * HD, image), BF16)],
        flops=8 * image * columns * HD,
        moved=2 * image * columns,
    )
    grads = call(
        unpack_kernel,
        [shape((rows, width), BF16)] * 3,
        [grad_in],
        moved=4 * 3 * rows * width,
    )
    (d_weight,) = call(
        unpack_weight_kernel,
        [shape((depth, width), F32)],
        [dw_own, exchange(dw_other, 1)],
        moved=6 * depth * width,
    )
    return (*grads, d_weight)


def solution(mesh):
    in_specs = (
        P(("group", "seq"), "fsdp"),
        P(("group", "seq"), "fsdp"),
        P(("group", "seq"), "fsdp"),
        P("group", "fsdp"),
        P("group", "fsdp"),
        P("seq", "fsdp"),
        P(("group", "seq"), None),
    )
    out_specs = (
        P(("group", "seq"), "fsdp"),
        P(("group", "seq"), "fsdp"),
        P(("group", "seq"), "fsdp"),
        P(("group", "seq"), "fsdp"),
    )
    return jax.shard_map(local, mesh=mesh, in_specs=in_specs, out_specs=out_specs, check_vma=False)
```

```python
import functools
import math

import jax
import jax.numpy as jnp
from jax import lax
from jax.experimental import pallas as pl
from jax.experimental.pallas import tpu as pltpu
from jax.sharding import PartitionSpec as P

HD = 128
F32 = jnp.float32
BF16 = jnp.bfloat16
LIMIT = 28 * 1024 * 1024
NT = (((1,), (1,)), ((), ()))


def attend(queries, cotangents, key_rows, value_rows, block_rows):
    score_scale = HD ** (-0.5)
    query_count = queries.shape[0]
    block_count = query_count // block_rows
    query_blocks = queries.reshape(block_count, block_rows, HD)
    grad_blocks = cotangents.reshape(block_count, block_rows, HD)

    def one_block(accumulated, pair_item):
        query_block, grad_block = pair_item
        scores = jnp.dot(query_block, key_rows.T, preferred_element_type=jnp.float32) * score_scale
        row_max = jnp.max(scores, axis=1, keepdims=True)
        probs = jnp.exp(scores - row_max)
        probs = probs / jnp.sum(probs, axis=1, keepdims=True)
        probs_low = probs.astype(jnp.bfloat16)
        out_rows = jnp.dot(probs_low, value_rows, preferred_element_type=jnp.float32).astype(
            jnp.bfloat16
        )
        prob_grad = jnp.dot(grad_block, value_rows.T, preferred_element_type=jnp.float32)
        row_dot = jnp.sum(
            grad_block.astype(jnp.float32) * out_rows.astype(jnp.float32), axis=1, keepdims=True
        )
        score_grad = (probs * (prob_grad - row_dot)).astype(jnp.bfloat16)
        query_grad = (
            jnp.dot(score_grad, key_rows, preferred_element_type=jnp.float32) * score_scale
        ).astype(jnp.bfloat16)
        key_grad = (
            accumulated[0]
            + jnp.dot(score_grad.T, query_block, preferred_element_type=jnp.float32) * score_scale
        )
        value_grad = accumulated[1] + jnp.dot(
            probs_low.T, grad_block, preferred_element_type=jnp.float32
        )
        return ((key_grad, value_grad), (query_grad, out_rows))

    empty = jnp.zeros((key_rows.shape[0], HD), jnp.float32)
    (key_grad, value_grad), (query_grad, out_rows) = lax.scan(
        one_block, (empty, empty), (query_blocks, grad_blocks)
    )
    return (
        query_grad.reshape(query_count, HD),
        out_rows.reshape(query_count, HD),
        key_grad,
        value_grad,
    )


def local_general(q_img, k_img, v_img, k_txt, v_txt, out_weight, d_out):
    rows_here = q_img.shape[0]
    heads_here = q_img.shape[1] // HD
    seq_count = lax.axis_size("seq")
    share_count = seq_count // heads_here
    part_rows = rows_here // share_count
    seq_index = lax.axis_index("seq")
    head_index = seq_index // share_count
    column_cut = d_out
    attn_grad = jnp.dot(
        column_cut,
        lax.all_gather(out_weight, "seq", axis=0, tiled=True),
        preferred_element_type=jnp.float32,
    ).astype(jnp.bfloat16)

    def to_heads(array_in):
        shaped = array_in.reshape(share_count, part_rows, heads_here, HD).transpose(2, 0, 1, 3)
        return shaped.reshape(seq_count, part_rows, HD)

    def whole_heads(array_in):
        shaped = array_in.reshape(rows_here, heads_here, HD).transpose(1, 0, 2)
        shaped = jnp.broadcast_to(shaped[:, None], (heads_here, share_count, rows_here, HD))
        return shaped.reshape(seq_count, rows_here, HD)

    def from_heads(array_in):
        shaped = array_in.reshape(heads_here, share_count, part_rows, HD).transpose(1, 2, 0, 3)
        return shaped.reshape(rows_here, heads_here * HD)

    text_keys = lax.dynamic_slice_in_dim(k_txt, head_index * HD, HD, 1)
    text_values = lax.dynamic_slice_in_dim(v_txt, head_index * HD, HD, 1)
    query_side = jnp.concatenate([to_heads(q_img), to_heads(attn_grad)], axis=2)
    key_side = jnp.concatenate([whole_heads(k_img), whole_heads(v_img)], axis=2)
    packed = jnp.concatenate([query_side, key_side], axis=1)
    received = lax.all_to_all(packed, "seq", split_axis=0, concat_axis=0, tiled=True)
    queries = received[:, :part_rows, :HD].reshape(seq_count * part_rows, HD)
    cotangents = received[:, :part_rows, HD:].reshape(seq_count * part_rows, HD)
    image_keys = received[:, part_rows:, :HD].reshape(seq_count * rows_here, HD)
    image_values = received[:, part_rows:, HD:].reshape(seq_count * rows_here, HD)
    key_rows = jnp.concatenate([image_keys, text_keys], axis=0)
    value_rows = jnp.concatenate([image_values, text_values], axis=0)
    query_grad, out_rows, key_grad, value_grad = attend(
        queries, cotangents, key_rows, value_rows, min(512, queries.shape[0])
    )
    image_count = image_keys.shape[0]
    query_part = (
        jnp.concatenate([query_grad, out_rows], axis=1)
        .astype(jnp.float32)
        .reshape(seq_count, part_rows, 2 * HD)
    )
    key_part = jnp.concatenate([key_grad[:image_count], value_grad[:image_count]], axis=1).reshape(
        seq_count, rows_here, 2 * HD
    )
    returned = lax.all_to_all(
        jnp.concatenate([query_part, key_part], axis=1).astype(jnp.bfloat16),
        "seq",
        split_axis=0,
        concat_axis=0,
        tiled=True,
    ).astype(jnp.float32)
    q_grad = from_heads(returned[:, :part_rows, :HD]).astype(jnp.bfloat16)
    out_tok = from_heads(returned[:, :part_rows, HD:]).astype(jnp.bfloat16)
    summed = jnp.sum(
        returned[:, part_rows:, :].reshape(heads_here, share_count, rows_here, 2 * HD), axis=1
    )
    summed = summed.transpose(1, 0, 2)
    k_grad = summed[:, :, :HD].reshape(rows_here, heads_here * HD).astype(jnp.bfloat16)
    v_grad = summed[:, :, HD:].reshape(rows_here, heads_here * HD).astype(jnp.bfloat16)
    column_cut = d_out
    d_weight = lax.psum_scatter(
        jnp.dot(column_cut.T, out_tok, preferred_element_type=jnp.float32).astype(jnp.bfloat16),
        "seq",
        scatter_dimension=0,
        tiled=True,
    ).astype(jnp.float32)
    return (q_grad, k_grad, v_grad, d_weight)


def call(kernel, outs, args, specs=None, scratch=(), scalars=0, out_specs=None, flops=0, moved=0, limit=LIMIT):
    vmem = pl.BlockSpec(memory_space=pltpu.VMEM)
    if specs is None:
        specs = [vmem] * (len(args) - scalars)
    if out_specs is None:
        out_specs = [vmem] * len(outs)
    return pl.pallas_call(
        kernel,
        out_shape=outs,
        grid_spec=pltpu.PrefetchScalarGridSpec(
            num_scalar_prefetch=scalars,
            grid=(1,),
            in_specs=specs,
            out_specs=out_specs,
            scratch_shapes=list(scratch),
        ),
        compiler_params=pltpu.CompilerParams(vmem_limit_bytes=limit),
        cost_estimate=pl.CostEstimate(flops=flops, bytes_accessed=moved, transcendentals=0),
    )(*args)


STEPS = (0, 2, 4, 6)


def head_columns(step, other_row):
    return pl.ds(pl.multiple_of(jnp.bitwise_xor(lax.axis_index("seq"), step + other_row) * HD, HD), HD)


def pack_kernel(me_ref, q_ref, k_ref, v_ref, w_ref, kt_ref, vt_ref, tok_ref, keep_ref, give_ref, text_ref):
    rows = q_ref.shape[0]
    for h in range(tok_ref.shape[0]):
        for i, ref in enumerate((q_ref, k_ref, v_ref)):
            tok_ref[h, i * rows : (i + 1) * rows, :] = ref[:, h * HD : (h + 1) * HD]
    for i, step in enumerate(STEPS):
        cols = slice(i * HD, (i + 1) * HD)
        keep_ref[:, cols] = w_ref[:, head_columns(step, 0)]
        give_ref[:, cols] = w_ref[:, head_columns(step, 1)]
    text_ref[0] = kt_ref[...]
    text_ref[1] = vt_ref[...]


def forward_kernel(tok_ref, text_ref, probs_ref, out_ref, queries_ref, keys_t_ref, vals_ref, keys, vals_t, *, chunk):
    n, three, _ = tok_ref.shape
    rows = three // 3
    image = n * rows
    text = text_ref.shape[1]
    queries_ref[...] = tok_ref[:, 0:rows, :].reshape(image, HD)
    keys[0:image, :] = tok_ref[:, rows : 2 * rows, :].reshape(image, HD)
    keys[image : image + text, :] = text_ref[0]
    vals_ref[0:image, :] = tok_ref[:, 2 * rows : 3 * rows, :].reshape(image, HD)
    vals_ref[image : image + text, :] = text_ref[1]
    keys_t_ref[...] = keys[...].T
    vals_t[...] = vals_ref[...].T
    factor = HD ** (-0.5) * math.log2(math.e)
    for c in range(image // chunk):
        span = slice(c * chunk, (c + 1) * chunk)
        scores = lax.dot_general(keys[...], queries_ref[span, :], NT, preferred_element_type=F32)
        top = jnp.max(scores, axis=0, keepdims=True)
        weights = jnp.exp2((scores - top) * factor)
        total = jnp.sum(weights, axis=0, keepdims=True)
        low = (weights * (1.0 / total)).astype(BF16)
        probs_ref[:, span] = low
        out_ref[:, span] = jnp.dot(vals_t[...], low, preferred_element_type=F32).astype(BF16)


def partial_kernel(*refs):
    *pieces, own_ref, other_ref, mine_ref, far_ref, near_ref, near_far_ref, cot_ref, weight = refs
    me = lax.axis_index("seq")
    core = lax.axis_index("fsdp")
    count = len(STEPS)
    part = pieces[0].shape[0] // count
    for p, piece in enumerate(pieces):
        row, swapped = p % 2, p // 2
        shift = jnp.bitwise_xor(core, swapped) * part
        for i, step in enumerate(STEPS):
            at = pl.multiple_of(jnp.bitwise_xor(me, step + row) * (2 * part) + shift, 16)
            cot_ref[pl.ds(at, part), :] = piece[i * part : (i + 1) * part, :]
    depth = own_ref.shape[0]
    y = lax.rem(me, 2)
    weight[pl.ds(pl.multiple_of(y * depth, 16), depth), :] = own_ref[...]
    weight[pl.ds(pl.multiple_of((1 - y) * depth, 16), depth), :] = other_ref[...]
    step = 256

    @pl.loop(0, cot_ref.shape[0] // step)
    def _(i):
        at = pl.ds(pl.multiple_of(i * step, step), step)
        part = jnp.dot(cot_ref[at, :], weight[...], preferred_element_type=F32)
        mine_ref[at, :] = part[:, :HD]
        near_ref[at, :] = part[:, HD : 2 * HD].astype(BF16)
        far_ref[at, :] = part[:, 2 * HD : 3 * HD]
        near_far_ref[at, :] = part[:, 3 * HD :].astype(BF16)


def weight_grad_kernel(cot_ref, *refs):
    *out_refs, own_ref, other_ref, outs = refs
    for i, ref in enumerate(out_refs):
        outs[i * HD : (i + 1) * HD, :] = ref[...]
    depth = own_ref.shape[1]
    y = lax.rem(lax.axis_index("seq"), 2)
    for ref, row in ((own_ref, y), (other_ref, 1 - y)):
        at = pl.multiple_of(row * depth, HD)
        ref[...] = jnp.dot(outs[...], cot_ref[:, pl.ds(at, depth)], preferred_element_type=F32).astype(BF16)


def backward_kernel(
    queries_ref, keys_t_ref, vals_ref, probs_ref, out_ref, mine_ref, near_ref, far_ref, send_ref, dk, dv, *, chunk
):
    n, three, _ = send_ref.shape
    rows = three // 3
    image = n * rows
    scale = HD ** (-0.5)
    per = chunk // rows
    for c in range(image // chunk):
        span = slice(c * chunk, (c + 1) * chunk)
        grads = mine_ref[span, :] + near_ref[span, :].astype(F32) + far_ref[span, :].astype(F32)
        grads = grads.astype(BF16)
        row_dot = jnp.sum(
            grads.astype(F32).T * out_ref[:, span].astype(F32), axis=0, keepdims=True
        )
        prob_grad = lax.dot_general(vals_ref[...], grads, NT, preferred_element_type=F32)
        low = probs_ref[:, span]
        score_grad = (low.astype(F32) * (prob_grad - row_dot)).astype(BF16)
        dq_t = jnp.dot(keys_t_ref[...], score_grad, preferred_element_type=F32) * scale
        send_ref[c * per : (c + 1) * per, 0:rows, :] = dq_t.T.astype(BF16).reshape(per, rows, HD)
        dk_part = jnp.dot(score_grad[0:image, :], queries_ref[span, :], preferred_element_type=F32)
        dv_part = jnp.dot(low[0:image, :], grads, preferred_element_type=F32)
        if c == 0:
            dk[...] = dk_part
            dv[...] = dv_part
        else:
            dk[...] += dk_part
            dv[...] += dv_part
    send_ref[:, rows : 2 * rows, :] = (dk[...] * scale).astype(BF16).reshape(n, rows, HD)
    send_ref[:, 2 * rows : 3 * rows, :] = dv[...].astype(BF16).reshape(n, rows, HD)


def unpack_kernel(tok_ref, q_ref, k_ref, v_ref):
    rows = q_ref.shape[0]
    for h in range(tok_ref.shape[0]):
        for i, ref in enumerate((q_ref, k_ref, v_ref)):
            ref[:, h * HD : (h + 1) * HD] = tok_ref[h, i * rows : (i + 1) * rows, :]


def unpack_weight_kernel(own_ref, other_ref, w_ref):
    for other_row, ref in enumerate((own_ref, other_ref)):
        for i, step in enumerate(STEPS):
            w_ref[:, head_columns(step, other_row)] = ref[i * HD : (i + 1) * HD, :].astype(F32).T


def exchange(array, distance=0, cores=False):
    if not distance and not cores:
        return array
    size = 2 * lax.axis_size("seq")
    pairs = [(i, i ^ (2 * distance + int(cores))) for i in range(size)]
    return lax.ppermute(array, ("seq", "fsdp"), pairs)


def gather_cotangents(d_out):
    rows, width = d_out.shape
    part, columns = rows // 2, width // len(STEPS)
    z = lax.axis_index("seq") // 2
    first = lax.axis_index("fsdp") * part
    along = [
        exchange(lax.dynamic_slice(d_out, (first, (z ^ (step // 2)) * columns), (part, columns)), step)
        for step in STEPS
    ]
    row = jnp.concatenate(along, axis=0)
    pieces = [row, exchange(row, 1)]
    return pieces + [exchange(piece, cores=True) for piece in pieces]


def local(q_img, k_img, v_img, k_txt, v_txt, out_weight, d_out):
    n = lax.axis_size("seq")
    rows, width = q_img.shape
    args = (q_img, k_img, v_img, k_txt, v_txt, out_weight, d_out)
    if n != 2 * len(STEPS) or width // HD != n or lax.axis_size("fsdp") != 2 or rows % 32:
        return local_general(*args)
    depth = out_weight.shape[0]
    image = n * rows
    text = k_txt.shape[0]
    total = image + text
    chunk = 2 * rows
    shape = jax.ShapeDtypeStruct
    vmem = pl.BlockSpec(memory_space=pltpu.VMEM)

    head = pl.BlockSpec((text, HD), lambda i, me_ref: (0, me_ref[0]))
    tok_out, keep, give, text_head = call(
        pack_kernel,
        [shape((n, 3 * rows, HD), BF16)] + [shape((depth, 4 * HD), BF16)] * 2 + [shape((2, text, HD), BF16)],
        [lax.axis_index("seq").astype(jnp.int32)[None], q_img, k_img, v_img, out_weight, k_txt, v_txt],
        specs=[vmem] * 4 + [head] * 2,
        scalars=1,
        moved=4 * (3 * rows + depth) * width,
        limit=60 * 1024 * 1024,
    )
    given = exchange(give, 1)
    d_out, _ = lax.optimization_barrier((d_out, give))
    pieces = gather_cotangents(d_out)
    tok_in = lax.all_to_all(tok_out, "seq", split_axis=0, concat_axis=0, tiled=True)

    probs, out_t, queries, keys_t, vals = call(
        functools.partial(forward_kernel, chunk=chunk),
        [shape(dims, BF16) for dims in ((total, image), (HD, image), (image, HD), (HD, total), (total, HD))],
        [tok_in, text_head],
        scratch=[pltpu.VMEM((total, HD), BF16), pltpu.VMEM((HD, total), BF16)],
        flops=4 * total * image * HD,
        moved=4 * total * image,
    )
    out_far = exchange(out_t, 4)
    outs = [out_t, exchange(out_t, 2), out_far, exchange(out_far, 2)]
    columns = pieces[0].shape[1]
    keep, _ = lax.optimization_barrier((keep, out_t))
    mine, far, near, near_far, cot = call(
        partial_kernel,
        [shape((image, HD), F32)] * 2 + [shape((image, HD), BF16)] * 2 + [shape((image, columns), BF16)],
        [*pieces, keep, given],
        scratch=[pltpu.VMEM((columns, 4 * HD), BF16)],
        flops=8 * image * columns * HD,
        moved=2 * image * columns,
    )
    near_far = exchange(near_far, 2)
    far = exchange((far + near_far.astype(F32)).astype(BF16), 4)
    near, _ = lax.optimization_barrier((near, near_far))
    near = exchange(near, 2)
    dw_own, dw_other = call(
        weight_grad_kernel,
        [shape((4 * HD, depth), BF16)] * 2,
        [cot, *outs],
        scratch=[pltpu.VMEM((4 * HD, image), BF16)],
        flops=8 * image * columns * HD,
        moved=2 * image * columns,
    )
    mine, _ = lax.optimization_barrier((mine, dw_own))
    (grad_out,) = call(
        functools.partial(backward_kernel, chunk=chunk),
        [shape((n, 3 * rows, HD), BF16)],
        [queries, keys_t, vals, probs, out_t, mine, near, far],
        scratch=[pltpu.VMEM((image, HD), F32), pltpu.VMEM((image, HD), F32)],
        flops=8 * total * image * HD,
        moved=4 * total * image,
    )
    grad_in = lax.all_to_all(grad_out, "seq", split_axis=0, concat_axis=0, tiled=True)
    grads = call(
        unpack_kernel,
        [shape((rows, width), BF16)] * 3,
        [grad_in],
        moved=4 * 3 * rows * width,
    )
    (d_weight,) = call(
        unpack_weight_kernel,
        [shape((depth, width), F32)],
        [dw_own, exchange(dw_other, 1)],
        moved=6 * depth * width,
    )
    return (*grads, d_weight)


def solution(mesh):
    in_specs = (
        P(("group", "seq"), "fsdp"),
        P(("group", "seq"), "fsdp"),
        P(("group", "seq"), "fsdp"),
        P("group", "fsdp"),
        P("group", "fsdp"),
        P("seq", "fsdp"),
        P(("group", "seq"), None),
    )
    out_specs = (
        P(("group", "seq"), "fsdp"),
        P(("group", "seq"), "fsdp"),
        P(("group", "seq"), "fsdp"),
        P(("group", "seq"), "fsdp"),
    )
    return jax.shard_map(local, mesh=mesh, in_specs=in_specs, out_specs=out_specs, check_vma=False)
```

```python
import functools
import math

import jax
import jax.numpy as jnp
from jax import lax
from jax.experimental import pallas as pl
from jax.experimental.pallas import tpu as pltpu
from jax.sharding import PartitionSpec as P

HD = 128
F32 = jnp.float32
BF16 = jnp.bfloat16
LIMIT = 28 * 1024 * 1024
NT = (((1,), (1,)), ((), ()))


def attend(queries, cotangents, key_rows, value_rows, block_rows):
    score_scale = HD ** (-0.5)
    query_count = queries.shape[0]
    block_count = query_count // block_rows
    query_blocks = queries.reshape(block_count, block_rows, HD)
    grad_blocks = cotangents.reshape(block_count, block_rows, HD)

    def one_block(accumulated, pair_item):
        query_block, grad_block = pair_item
        scores = jnp.dot(query_block, key_rows.T, preferred_element_type=jnp.float32) * score_scale
        row_max = jnp.max(scores, axis=1, keepdims=True)
        probs = jnp.exp(scores - row_max)
        probs = probs / jnp.sum(probs, axis=1, keepdims=True)
        probs_low = probs.astype(jnp.bfloat16)
        out_rows = jnp.dot(probs_low, value_rows, preferred_element_type=jnp.float32).astype(
            jnp.bfloat16
        )
        prob_grad = jnp.dot(grad_block, value_rows.T, preferred_element_type=jnp.float32)
        row_dot = jnp.sum(
            grad_block.astype(jnp.float32) * out_rows.astype(jnp.float32), axis=1, keepdims=True
        )
        score_grad = (probs * (prob_grad - row_dot)).astype(jnp.bfloat16)
        query_grad = (
            jnp.dot(score_grad, key_rows, preferred_element_type=jnp.float32) * score_scale
        ).astype(jnp.bfloat16)
        key_grad = (
            accumulated[0]
            + jnp.dot(score_grad.T, query_block, preferred_element_type=jnp.float32) * score_scale
        )
        value_grad = accumulated[1] + jnp.dot(
            probs_low.T, grad_block, preferred_element_type=jnp.float32
        )
        return ((key_grad, value_grad), (query_grad, out_rows))

    empty = jnp.zeros((key_rows.shape[0], HD), jnp.float32)
    (key_grad, value_grad), (query_grad, out_rows) = lax.scan(
        one_block, (empty, empty), (query_blocks, grad_blocks)
    )
    return (
        query_grad.reshape(query_count, HD),
        out_rows.reshape(query_count, HD),
        key_grad,
        value_grad,
    )


def local_general(q_img, k_img, v_img, k_txt, v_txt, out_weight, d_out):
    rows_here = q_img.shape[0]
    heads_here = q_img.shape[1] // HD
    seq_count = lax.axis_size("seq")
    share_count = seq_count // heads_here
    part_rows = rows_here // share_count
    seq_index = lax.axis_index("seq")
    head_index = seq_index // share_count
    column_cut = d_out
    attn_grad = jnp.dot(
        column_cut,
        lax.all_gather(out_weight, "seq", axis=0, tiled=True),
        preferred_element_type=jnp.float32,
    ).astype(jnp.bfloat16)

    def to_heads(array_in):
        shaped = array_in.reshape(share_count, part_rows, heads_here, HD).transpose(2, 0, 1, 3)
        return shaped.reshape(seq_count, part_rows, HD)

    def whole_heads(array_in):
        shaped = array_in.reshape(rows_here, heads_here, HD).transpose(1, 0, 2)
        shaped = jnp.broadcast_to(shaped[:, None], (heads_here, share_count, rows_here, HD))
        return shaped.reshape(seq_count, rows_here, HD)

    def from_heads(array_in):
        shaped = array_in.reshape(heads_here, share_count, part_rows, HD).transpose(1, 2, 0, 3)
        return shaped.reshape(rows_here, heads_here * HD)

    text_keys = lax.dynamic_slice_in_dim(k_txt, head_index * HD, HD, 1)
    text_values = lax.dynamic_slice_in_dim(v_txt, head_index * HD, HD, 1)
    query_side = jnp.concatenate([to_heads(q_img), to_heads(attn_grad)], axis=2)
    key_side = jnp.concatenate([whole_heads(k_img), whole_heads(v_img)], axis=2)
    packed = jnp.concatenate([query_side, key_side], axis=1)
    received = lax.all_to_all(packed, "seq", split_axis=0, concat_axis=0, tiled=True)
    queries = received[:, :part_rows, :HD].reshape(seq_count * part_rows, HD)
    cotangents = received[:, :part_rows, HD:].reshape(seq_count * part_rows, HD)
    image_keys = received[:, part_rows:, :HD].reshape(seq_count * rows_here, HD)
    image_values = received[:, part_rows:, HD:].reshape(seq_count * rows_here, HD)
    key_rows = jnp.concatenate([image_keys, text_keys], axis=0)
    value_rows = jnp.concatenate([image_values, text_values], axis=0)
    query_grad, out_rows, key_grad, value_grad = attend(
        queries, cotangents, key_rows, value_rows, min(512, queries.shape[0])
    )
    image_count = image_keys.shape[0]
    query_part = (
        jnp.concatenate([query_grad, out_rows], axis=1)
        .astype(jnp.float32)
        .reshape(seq_count, part_rows, 2 * HD)
    )
    key_part = jnp.concatenate([key_grad[:image_count], value_grad[:image_count]], axis=1).reshape(
        seq_count, rows_here, 2 * HD
    )
    returned = lax.all_to_all(
        jnp.concatenate([query_part, key_part], axis=1).astype(jnp.bfloat16),
        "seq",
        split_axis=0,
        concat_axis=0,
        tiled=True,
    ).astype(jnp.float32)
    q_grad = from_heads(returned[:, :part_rows, :HD]).astype(jnp.bfloat16)
    out_tok = from_heads(returned[:, :part_rows, HD:]).astype(jnp.bfloat16)
    summed = jnp.sum(
        returned[:, part_rows:, :].reshape(heads_here, share_count, rows_here, 2 * HD), axis=1
    )
    summed = summed.transpose(1, 0, 2)
    k_grad = summed[:, :, :HD].reshape(rows_here, heads_here * HD).astype(jnp.bfloat16)
    v_grad = summed[:, :, HD:].reshape(rows_here, heads_here * HD).astype(jnp.bfloat16)
    column_cut = d_out
    d_weight = lax.psum_scatter(
        jnp.dot(column_cut.T, out_tok, preferred_element_type=jnp.float32).astype(jnp.bfloat16),
        "seq",
        scatter_dimension=0,
        tiled=True,
    ).astype(jnp.float32)
    return (q_grad, k_grad, v_grad, d_weight)


def call(kernel, outs, args, specs=None, scratch=(), scalars=0, out_specs=None, flops=0, moved=0, limit=LIMIT):
    vmem = pl.BlockSpec(memory_space=pltpu.VMEM)
    if specs is None:
        specs = [vmem] * (len(args) - scalars)
    if out_specs is None:
        out_specs = [vmem] * len(outs)
    return pl.pallas_call(
        kernel,
        out_shape=outs,
        grid_spec=pltpu.PrefetchScalarGridSpec(
            num_scalar_prefetch=scalars,
            grid=(1,),
            in_specs=specs,
            out_specs=out_specs,
            scratch_shapes=list(scratch),
        ),
        compiler_params=pltpu.CompilerParams(vmem_limit_bytes=limit),
        cost_estimate=pl.CostEstimate(flops=flops, bytes_accessed=moved, transcendentals=0),
    )(*args)


STEPS = (0, 2, 4, 6)


def head_columns(step, other_row):
    return pl.ds(pl.multiple_of(jnp.bitwise_xor(lax.axis_index("seq"), step + other_row) * HD, HD), HD)


def pack_kernel(q_ref, k_ref, v_ref, tok_ref):
    rows = q_ref.shape[0]
    for h in range(tok_ref.shape[0]):
        for i, ref in enumerate((q_ref, k_ref, v_ref)):
            tok_ref[h, i * rows : (i + 1) * rows, :] = ref[:, h * HD : (h + 1) * HD]


def pack_weight_kernel(me_ref, w_ref, kt_ref, vt_ref, keep_ref, give_ref, text_ref):
    for i, step in enumerate(STEPS):
        cols = slice(i * HD, (i + 1) * HD)
        keep_ref[:, cols] = w_ref[:, head_columns(step, 0)]
        give_ref[:, cols] = w_ref[:, head_columns(step, 1)]
    text_ref[0] = kt_ref[...]
    text_ref[1] = vt_ref[...]


def forward_kernel(tok_ref, text_ref, probs_ref, out_ref, queries_ref, keys_t_ref, vals_ref, keys, vals_t, *, chunk):
    n, three, _ = tok_ref.shape
    rows = three // 3
    image = n * rows
    text = text_ref.shape[1]
    queries_ref[...] = tok_ref[:, 0:rows, :].reshape(image, HD)
    keys[0:image, :] = tok_ref[:, rows : 2 * rows, :].reshape(image, HD)
    keys[image : image + text, :] = text_ref[0]
    vals_ref[0:image, :] = tok_ref[:, 2 * rows : 3 * rows, :].reshape(image, HD)
    vals_ref[image : image + text, :] = text_ref[1]
    keys_t_ref[...] = keys[...].T
    vals_t[...] = vals_ref[...].T
    factor = HD ** (-0.5) * math.log2(math.e)
    for c in range(image // chunk):
        span = slice(c * chunk, (c + 1) * chunk)
        scores = lax.dot_general(keys[...], queries_ref[span, :], NT, preferred_element_type=F32)
        top = jnp.max(scores, axis=0, keepdims=True)
        weights = jnp.exp2((scores - top) * factor)
        total = jnp.sum(weights, axis=0, keepdims=True)
        low = (weights * (1.0 / total)).astype(BF16)
        probs_ref[:, span] = low
        out_ref[:, span] = jnp.dot(vals_t[...], low, preferred_element_type=F32).astype(BF16)


def partial_kernel(*refs):
    *pieces, own_ref, other_ref, mine_ref, far_ref, near_ref, near_far_ref, cot_ref, weight = refs
    me = lax.axis_index("seq")
    core = lax.axis_index("fsdp")
    count = len(STEPS)
    part = pieces[0].shape[0] // count
    for p, piece in enumerate(pieces):
        row, swapped = p % 2, p // 2
        shift = jnp.bitwise_xor(core, swapped) * part
        for i, step in enumerate(STEPS):
            at = pl.multiple_of(jnp.bitwise_xor(me, step + row) * (2 * part) + shift, 16)
            cot_ref[pl.ds(at, part), :] = piece[i * part : (i + 1) * part, :]
    depth = own_ref.shape[0]
    y = lax.rem(me, 2)
    weight[pl.ds(pl.multiple_of(y * depth, 16), depth), :] = own_ref[...]
    weight[pl.ds(pl.multiple_of((1 - y) * depth, 16), depth), :] = other_ref[...]
    step = 256

    @pl.loop(0, cot_ref.shape[0] // step)
    def _(i):
        at = pl.ds(pl.multiple_of(i * step, step), step)
        part = jnp.dot(cot_ref[at, :], weight[...], preferred_element_type=F32)
        mine_ref[at, :] = part[:, :HD]
        near_ref[at, :] = part[:, HD : 2 * HD].astype(BF16)
        far_ref[at, :] = part[:, 2 * HD : 3 * HD]
        near_far_ref[at, :] = part[:, 3 * HD :].astype(BF16)


def weight_grad_kernel(cot_ref, *refs):
    *out_refs, own_ref, other_ref, outs = refs
    first = 0
    for ref in out_refs:
        outs[first : first + ref.shape[0], :] = ref[...]
        first += ref.shape[0]
    depth = own_ref.shape[1]
    y = lax.rem(lax.axis_index("seq"), 2)
    for ref, row in ((own_ref, y), (other_ref, 1 - y)):
        at = pl.multiple_of(row * depth, HD)
        ref[...] = jnp.dot(outs[...], cot_ref[:, pl.ds(at, depth)], preferred_element_type=F32).astype(BF16)


def backward_kernel(
    queries_ref, keys_t_ref, vals_ref, probs_ref, out_ref, mine_ref, near_ref, far_ref, send_ref, dk, dv, *, chunk
):
    n, three, _ = send_ref.shape
    rows = three // 3
    image = n * rows
    scale = HD ** (-0.5)
    per = chunk // rows
    for c in range(image // chunk):
        span = slice(c * chunk, (c + 1) * chunk)
        grads = mine_ref[span, :] + near_ref[span, :].astype(F32) + far_ref[span, :].astype(F32)
        grads = grads.astype(BF16)
        row_dot = jnp.sum(
            grads.astype(F32).T * out_ref[:, span].astype(F32), axis=0, keepdims=True
        )
        prob_grad = lax.dot_general(vals_ref[...], grads, NT, preferred_element_type=F32)
        low = probs_ref[:, span]
        score_grad = (low.astype(F32) * (prob_grad - row_dot)).astype(BF16)
        dq_t = jnp.dot(keys_t_ref[...], score_grad, preferred_element_type=F32) * scale
        send_ref[c * per : (c + 1) * per, 0:rows, :] = dq_t.T.astype(BF16).reshape(per, rows, HD)
        dk_part = jnp.dot(score_grad[0:image, :], queries_ref[span, :], preferred_element_type=F32)
        dv_part = jnp.dot(low[0:image, :], grads, preferred_element_type=F32)
        if c == 0:
            dk[...] = dk_part
            dv[...] = dv_part
        else:
            dk[...] += dk_part
            dv[...] += dv_part
    send_ref[:, rows : 2 * rows, :] = (dk[...] * scale).astype(BF16).reshape(n, rows, HD)
    send_ref[:, 2 * rows : 3 * rows, :] = dv[...].astype(BF16).reshape(n, rows, HD)


def unpack_kernel(tok_ref, q_ref, k_ref, v_ref):
    rows = q_ref.shape[0]
    for h in range(tok_ref.shape[0]):
        for i, ref in enumerate((q_ref, k_ref, v_ref)):
            ref[:, h * HD : (h + 1) * HD] = tok_ref[h, i * rows : (i + 1) * rows, :]


def unpack_weight_kernel(own_ref, other_ref, w_ref):
    for other_row, ref in enumerate((own_ref, other_ref)):
        for i, step in enumerate(STEPS):
            w_ref[:, head_columns(step, other_row)] = ref[i * HD : (i + 1) * HD, :].astype(F32).T


def exchange(array, distance=0, cores=False):
    if not distance and not cores:
        return array
    size = 2 * lax.axis_size("seq")
    pairs = [(i, i ^ (2 * distance + int(cores))) for i in range(size)]
    return lax.ppermute(array, ("seq", "fsdp"), pairs)


def send_cotangents(d_out):
    rows, width = d_out.shape
    part, columns = rows // 2, width // len(STEPS)
    z = lax.axis_index("seq") // 2
    first = lax.axis_index("fsdp") * part
    return [
        exchange(lax.dynamic_slice(d_out, (first, (z ^ (step // 2)) * columns), (part, columns)), step)
        for step in STEPS
    ]


def gather_cotangents(along):
    row = jnp.concatenate(along, axis=0)
    pieces = [row, exchange(row, 1)]
    return pieces + [exchange(piece, cores=True) for piece in pieces]


def local(q_img, k_img, v_img, k_txt, v_txt, out_weight, d_out):
    n = lax.axis_size("seq")
    rows, width = q_img.shape
    args = (q_img, k_img, v_img, k_txt, v_txt, out_weight, d_out)
    if n != 2 * len(STEPS) or width // HD != n or lax.axis_size("fsdp") != 2 or rows % 32:
        return local_general(*args)
    depth = out_weight.shape[0]
    image = n * rows
    text = k_txt.shape[0]
    total = image + text
    chunk = 2 * rows
    shape = jax.ShapeDtypeStruct
    vmem = pl.BlockSpec(memory_space=pltpu.VMEM)

    head = pl.BlockSpec((text, HD), lambda i, me_ref: (0, me_ref[0]))
    big = 60 * 1024 * 1024
    keep, give, text_head = call(
        pack_weight_kernel,
        [shape((depth, 4 * HD), BF16)] * 2 + [shape((2, text, HD), BF16)],
        [lax.axis_index("seq").astype(jnp.int32)[None], out_weight, k_txt, v_txt],
        specs=[vmem] + [head] * 2,
        scalars=1,
        moved=4 * depth * width,
        limit=big,
    )
    d_out, give = lax.optimization_barrier((d_out, give))
    given = exchange(give, 1)
    along = send_cotangents(d_out)
    (tok_out,) = call(
        pack_kernel,
        [shape((n, 3 * rows, HD), BF16)],
        [q_img, k_img, v_img],
        moved=4 * 3 * rows * width,
        limit=big,
    )
    tok_out, along[1] = lax.optimization_barrier((tok_out, along[1]))
    pieces = gather_cotangents(along)
    tok_in = lax.all_to_all(tok_out, "seq", split_axis=0, concat_axis=0, tiled=True)

    probs, out_t, queries, keys_t, vals = call(
        functools.partial(forward_kernel, chunk=chunk),
        [shape(dims, BF16) for dims in ((total, image), (HD, image), (image, HD), (HD, total), (total, HD))],
        [tok_in, text_head],
        scratch=[pltpu.VMEM((total, HD), BF16), pltpu.VMEM((HD, total), BF16)],
        flops=4 * total * image * HD,
        moved=4 * total * image,
    )
    columns = pieces[0].shape[1]
    mine, far, near, near_far, cot = call(
        partial_kernel,
        [shape((image, HD), F32)] * 2 + [shape((image, HD), BF16)] * 2 + [shape((image, columns), BF16)],
        [*pieces, keep, given],
        scratch=[pltpu.VMEM((columns, 4 * HD), BF16)],
        flops=8 * image * columns * HD,
        moved=2 * image * columns,
    )
    near_far = exchange(near_far, 2)
    far, out_t = lax.optimization_barrier(((far + near_far.astype(F32)).astype(BF16), out_t))
    far = exchange(far, 4)
    near, _ = lax.optimization_barrier((near, near_far))
    near = exchange(near, 2)
    out_near = exchange(out_t, 2)
    half = HD // 2
    out_late, far = lax.optimization_barrier((out_t, far))
    out_far = [exchange(out_late[:half], 4), exchange(out_late[half:], 4)]
    (grad_out,) = call(
        functools.partial(backward_kernel, chunk=chunk),
        [shape((n, 3 * rows, HD), BF16)],
        [queries, keys_t, vals, probs, out_t, mine, near, far],
        scratch=[pltpu.VMEM((image, HD), F32), pltpu.VMEM((image, HD), F32)],
        flops=8 * total * image * HD,
        moved=4 * total * image,
    )
    grad_out, out_far[0] = lax.optimization_barrier((grad_out, out_far[0]))
    grad_in = lax.all_to_all(grad_out, "seq", split_axis=0, concat_axis=0, tiled=True)
    outs = [out_t, out_near, *out_far, *(exchange(part, 2) for part in out_far)]
    dw_own, dw_other = call(
        weight_grad_kernel,
        [shape((4 * HD, depth), BF16)] * 2,
        [cot, *outs],
        scratch=[pltpu.VMEM((4 * HD, image), BF16)],
        flops=8 * image * columns * HD,
        moved=2 * image * columns,
    )
    grads = call(
        unpack_kernel,
        [shape((rows, width), BF16)] * 3,
        [grad_in],
        moved=4 * 3 * rows * width,
    )
    (d_weight,) = call(
        unpack_weight_kernel,
        [shape((depth, width), F32)],
        [dw_own, exchange(dw_other, 1)],
        moved=6 * depth * width,
    )
    return (*grads, d_weight)


def solution(mesh):
    in_specs = (
        P(("group", "seq"), "fsdp"),
        P(("group", "seq"), "fsdp"),
        P(("group", "seq"), "fsdp"),
        P("group", "fsdp"),
        P("group", "fsdp"),
        P("seq", "fsdp"),
        P(("group", "seq"), None),
    )
    out_specs = (
        P(("group", "seq"), "fsdp"),
        P(("group", "seq"), "fsdp"),
        P(("group", "seq"), "fsdp"),
        P(("group", "seq"), "fsdp"),
    )
    return jax.shard_map(local, mesh=mesh, in_specs=in_specs, out_specs=out_specs, check_vma=False)
```

```python
import functools
import math

import jax
import jax.numpy as jnp
from jax import lax
from jax.experimental import pallas as pl
from jax.experimental.pallas import tpu as pltpu
from jax.sharding import PartitionSpec as P

HD = 128
F32 = jnp.float32
BF16 = jnp.bfloat16
LIMIT = 28 * 1024 * 1024
NT = (((1,), (1,)), ((), ()))


def attend(queries, cotangents, key_rows, value_rows, block_rows):
    score_scale = HD ** (-0.5)
    query_count = queries.shape[0]
    block_count = query_count // block_rows
    query_blocks = queries.reshape(block_count, block_rows, HD)
    grad_blocks = cotangents.reshape(block_count, block_rows, HD)

    def one_block(accumulated, pair_item):
        query_block, grad_block = pair_item
        scores = jnp.dot(query_block, key_rows.T, preferred_element_type=jnp.float32) * score_scale
        row_max = jnp.max(scores, axis=1, keepdims=True)
        probs = jnp.exp(scores - row_max)
        probs = probs / jnp.sum(probs, axis=1, keepdims=True)
        probs_low = probs.astype(jnp.bfloat16)
        out_rows = jnp.dot(probs_low, value_rows, preferred_element_type=jnp.float32).astype(
            jnp.bfloat16
        )
        prob_grad = jnp.dot(grad_block, value_rows.T, preferred_element_type=jnp.float32)
        row_dot = jnp.sum(
            grad_block.astype(jnp.float32) * out_rows.astype(jnp.float32), axis=1, keepdims=True
        )
        score_grad = (probs * (prob_grad - row_dot)).astype(jnp.bfloat16)
        query_grad = (
            jnp.dot(score_grad, key_rows, preferred_element_type=jnp.float32) * score_scale
        ).astype(jnp.bfloat16)
        key_grad = (
            accumulated[0]
            + jnp.dot(score_grad.T, query_block, preferred_element_type=jnp.float32) * score_scale
        )
        value_grad = accumulated[1] + jnp.dot(
            probs_low.T, grad_block, preferred_element_type=jnp.float32
        )
        return ((key_grad, value_grad), (query_grad, out_rows))

    empty = jnp.zeros((key_rows.shape[0], HD), jnp.float32)
    (key_grad, value_grad), (query_grad, out_rows) = lax.scan(
        one_block, (empty, empty), (query_blocks, grad_blocks)
    )
    return (
        query_grad.reshape(query_count, HD),
        out_rows.reshape(query_count, HD),
        key_grad,
        value_grad,
    )


def local_general(q_img, k_img, v_img, k_txt, v_txt, out_weight, d_out):
    rows_here = q_img.shape[0]
    heads_here = q_img.shape[1] // HD
    seq_count = lax.axis_size("seq")
    share_count = seq_count // heads_here
    part_rows = rows_here // share_count
    seq_index = lax.axis_index("seq")
    head_index = seq_index // share_count
    column_cut = d_out
    attn_grad = jnp.dot(
        column_cut,
        lax.all_gather(out_weight, "seq", axis=0, tiled=True),
        preferred_element_type=jnp.float32,
    ).astype(jnp.bfloat16)

    def to_heads(array_in):
        shaped = array_in.reshape(share_count, part_rows, heads_here, HD).transpose(2, 0, 1, 3)
        return shaped.reshape(seq_count, part_rows, HD)

    def whole_heads(array_in):
        shaped = array_in.reshape(rows_here, heads_here, HD).transpose(1, 0, 2)
        shaped = jnp.broadcast_to(shaped[:, None], (heads_here, share_count, rows_here, HD))
        return shaped.reshape(seq_count, rows_here, HD)

    def from_heads(array_in):
        shaped = array_in.reshape(heads_here, share_count, part_rows, HD).transpose(1, 2, 0, 3)
        return shaped.reshape(rows_here, heads_here * HD)

    text_keys = lax.dynamic_slice_in_dim(k_txt, head_index * HD, HD, 1)
    text_values = lax.dynamic_slice_in_dim(v_txt, head_index * HD, HD, 1)
    query_side = jnp.concatenate([to_heads(q_img), to_heads(attn_grad)], axis=2)
    key_side = jnp.concatenate([whole_heads(k_img), whole_heads(v_img)], axis=2)
    packed = jnp.concatenate([query_side, key_side], axis=1)
    received = lax.all_to_all(packed, "seq", split_axis=0, concat_axis=0, tiled=True)
    queries = received[:, :part_rows, :HD].reshape(seq_count * part_rows, HD)
    cotangents = received[:, :part_rows, HD:].reshape(seq_count * part_rows, HD)
    image_keys = received[:, part_rows:, :HD].reshape(seq_count * rows_here, HD)
    image_values = received[:, part_rows:, HD:].reshape(seq_count * rows_here, HD)
    key_rows = jnp.concatenate([image_keys, text_keys], axis=0)
    value_rows = jnp.concatenate([image_values, text_values], axis=0)
    query_grad, out_rows, key_grad, value_grad = attend(
        queries, cotangents, key_rows, value_rows, min(512, queries.shape[0])
    )
    image_count = image_keys.shape[0]
    query_part = (
        jnp.concatenate([query_grad, out_rows], axis=1)
        .astype(jnp.float32)
        .reshape(seq_count, part_rows, 2 * HD)
    )
    key_part = jnp.concatenate([key_grad[:image_count], value_grad[:image_count]], axis=1).reshape(
        seq_count, rows_here, 2 * HD
    )
    returned = lax.all_to_all(
        jnp.concatenate([query_part, key_part], axis=1).astype(jnp.bfloat16),
        "seq",
        split_axis=0,
        concat_axis=0,
        tiled=True,
    ).astype(jnp.float32)
    q_grad = from_heads(returned[:, :part_rows, :HD]).astype(jnp.bfloat16)
    out_tok = from_heads(returned[:, :part_rows, HD:]).astype(jnp.bfloat16)
    summed = jnp.sum(
        returned[:, part_rows:, :].reshape(heads_here, share_count, rows_here, 2 * HD), axis=1
    )
    summed = summed.transpose(1, 0, 2)
    k_grad = summed[:, :, :HD].reshape(rows_here, heads_here * HD).astype(jnp.bfloat16)
    v_grad = summed[:, :, HD:].reshape(rows_here, heads_here * HD).astype(jnp.bfloat16)
    column_cut = d_out
    d_weight = lax.psum_scatter(
        jnp.dot(column_cut.T, out_tok, preferred_element_type=jnp.float32).astype(jnp.bfloat16),
        "seq",
        scatter_dimension=0,
        tiled=True,
    ).astype(jnp.float32)
    return (q_grad, k_grad, v_grad, d_weight)


def call(kernel, outs, args, specs=None, scratch=(), scalars=0, out_specs=None, flops=0, moved=0, limit=LIMIT):
    vmem = pl.BlockSpec(memory_space=pltpu.VMEM)
    if specs is None:
        specs = [vmem] * (len(args) - scalars)
    if out_specs is None:
        out_specs = [vmem] * len(outs)
    return pl.pallas_call(
        kernel,
        out_shape=outs,
        grid_spec=pltpu.PrefetchScalarGridSpec(
            num_scalar_prefetch=scalars,
            grid=(1,),
            in_specs=specs,
            out_specs=out_specs,
            scratch_shapes=list(scratch),
        ),
        compiler_params=pltpu.CompilerParams(vmem_limit_bytes=limit),
        cost_estimate=pl.CostEstimate(flops=flops, bytes_accessed=moved, transcendentals=0),
    )(*args)


STEPS = (0, 2, 4, 6)


def head_columns(step, other_row):
    return pl.ds(pl.multiple_of(jnp.bitwise_xor(lax.axis_index("seq"), step + other_row) * HD, HD), HD)


def pack_kernel(q_ref, k_ref, v_ref, tok_ref):
    rows = q_ref.shape[0]
    for h in range(tok_ref.shape[0]):
        for i, ref in enumerate((q_ref, k_ref, v_ref)):
            tok_ref[h, i * rows : (i + 1) * rows, :] = ref[:, h * HD : (h + 1) * HD]


def pack_weight_kernel(me_ref, w_ref, kt_ref, vt_ref, keep_ref, give_ref, text_ref):
    for i, step in enumerate(STEPS):
        cols = slice(i * HD, (i + 1) * HD)
        keep_ref[:, cols] = w_ref[:, head_columns(step, 0)]
        give_ref[:, cols] = w_ref[:, head_columns(step, 1)]
    text_ref[0] = kt_ref[...]
    text_ref[1] = vt_ref[...]


def forward_kernel(tok_ref, text_ref, probs_ref, out_ref, queries_ref, keys_t_ref, vals_ref, keys, vals_t, *, chunk):
    n, three, _ = tok_ref.shape
    rows = three // 3
    image = n * rows
    text = text_ref.shape[1]
    queries_ref[...] = tok_ref[:, 0:rows, :].reshape(image, HD)
    keys[0:image, :] = tok_ref[:, rows : 2 * rows, :].reshape(image, HD)
    keys[image : image + text, :] = text_ref[0]
    vals_ref[0:image, :] = tok_ref[:, 2 * rows : 3 * rows, :].reshape(image, HD)
    vals_ref[image : image + text, :] = text_ref[1]
    keys_t_ref[...] = keys[...].T
    vals_t[...] = vals_ref[...].T
    factor = HD ** (-0.5) * math.log2(math.e)
    for c in range(image // chunk):
        span = slice(c * chunk, (c + 1) * chunk)
        scores = lax.dot_general(keys[...], queries_ref[span, :], NT, preferred_element_type=F32)
        top = jnp.max(scores, axis=0, keepdims=True)
        weights = jnp.exp2((scores - top) * factor)
        total = jnp.sum(weights, axis=0, keepdims=True)
        low = (weights * (1.0 / total)).astype(BF16)
        probs_ref[:, span] = low
        out_ref[:, span] = jnp.dot(vals_t[...], low, preferred_element_type=F32).astype(BF16)


def partial_kernel(*refs):
    *pieces, own_ref, other_ref, mine_ref, far_ref, near_ref, near_far_ref, cot_ref, weight = refs
    me = lax.axis_index("seq")
    core = lax.axis_index("fsdp")
    count = len(STEPS)
    part = pieces[0].shape[0] // count
    for p, piece in enumerate(pieces):
        row, swapped = p % 2, p // 2
        shift = jnp.bitwise_xor(core, swapped) * part
        for i, step in enumerate(STEPS):
            at = pl.multiple_of(jnp.bitwise_xor(me, step + row) * (2 * part) + shift, 16)
            cot_ref[pl.ds(at, part), :] = piece[i * part : (i + 1) * part, :]
    depth = own_ref.shape[0]
    y = lax.rem(me, 2)
    weight[pl.ds(pl.multiple_of(y * depth, 16), depth), :] = own_ref[...]
    weight[pl.ds(pl.multiple_of((1 - y) * depth, 16), depth), :] = other_ref[...]
    step = 256

    @pl.loop(0, cot_ref.shape[0] // step)
    def _(i):
        at = pl.ds(pl.multiple_of(i * step, step), step)
        part = jnp.dot(cot_ref[at, :], weight[...], preferred_element_type=F32)
        mine_ref[at, :] = part[:, :HD]
        near_ref[at, :] = part[:, HD : 2 * HD].astype(BF16)
        far_ref[at, :] = part[:, 2 * HD : 3 * HD]
        near_far_ref[at, :] = part[:, 3 * HD :].astype(BF16)


def weight_grad_kernel(cot_ref, *refs):
    *out_refs, own_ref, other_ref, outs = refs
    first = 0
    for ref in out_refs:
        outs[first : first + ref.shape[0], :] = ref[...]
        first += ref.shape[0]
    depth = own_ref.shape[1]
    y = lax.rem(lax.axis_index("seq"), 2)
    for ref, row in ((own_ref, y), (other_ref, 1 - y)):
        at = pl.multiple_of(row * depth, HD)
        ref[...] = jnp.dot(outs[...], cot_ref[:, pl.ds(at, depth)], preferred_element_type=F32).astype(BF16)


def backward_kernel(
    queries_ref, keys_t_ref, vals_ref, probs_ref, out_ref, mine_ref, near_ref, far_ref, send_ref, dk, dv, *, chunk
):
    n, three, _ = send_ref.shape
    rows = three // 3
    image = n * rows
    scale = HD ** (-0.5)
    per = chunk // rows
    for c in range(image // chunk):
        span = slice(c * chunk, (c + 1) * chunk)
        grads = mine_ref[span, :] + near_ref[span, :].astype(F32) + far_ref[span, :].astype(F32)
        grads = grads.astype(BF16)
        row_dot = jnp.sum(
            grads.astype(F32).T * out_ref[:, span].astype(F32), axis=0, keepdims=True
        )
        prob_grad = lax.dot_general(vals_ref[...], grads, NT, preferred_element_type=F32)
        low = probs_ref[:, span]
        score_grad = (low.astype(F32) * (prob_grad - row_dot)).astype(BF16)
        dq_t = jnp.dot(keys_t_ref[...], score_grad, preferred_element_type=F32) * scale
        send_ref[c * per : (c + 1) * per, 0:rows, :] = dq_t.T.astype(BF16).reshape(per, rows, HD)
        dk_part = jnp.dot(score_grad[0:image, :], queries_ref[span, :], preferred_element_type=F32)
        dv_part = jnp.dot(low[0:image, :], grads, preferred_element_type=F32)
        if c == 0:
            dk[...] = dk_part
            dv[...] = dv_part
        else:
            dk[...] += dk_part
            dv[...] += dv_part
    send_ref[:, rows : 2 * rows, :] = (dk[...] * scale).astype(BF16).reshape(n, rows, HD)
    send_ref[:, 2 * rows : 3 * rows, :] = dv[...].astype(BF16).reshape(n, rows, HD)


def unpack_kernel(tok_ref, q_ref, k_ref, v_ref):
    rows = q_ref.shape[0]
    for h in range(tok_ref.shape[0]):
        for i, ref in enumerate((q_ref, k_ref, v_ref)):
            ref[:, h * HD : (h + 1) * HD] = tok_ref[h, i * rows : (i + 1) * rows, :]


def unpack_weight_kernel(own_ref, other_ref, w_ref):
    for other_row, ref in enumerate((own_ref, other_ref)):
        for i, step in enumerate(STEPS):
            w_ref[:, head_columns(step, other_row)] = ref[i * HD : (i + 1) * HD, :].astype(F32).T


def exchange(array, distance=0, cores=False):
    if not distance and not cores:
        return array
    size = 2 * lax.axis_size("seq")
    pairs = [(i, i ^ (2 * distance + int(cores))) for i in range(size)]
    return lax.ppermute(array, ("seq", "fsdp"), pairs)


def send_cotangents(d_out):
    rows, width = d_out.shape
    part, columns = rows // 2, width // len(STEPS)
    z = lax.axis_index("seq") // 2
    first = lax.axis_index("fsdp") * part
    return [
        exchange(lax.dynamic_slice(d_out, (first, (z ^ (step // 2)) * columns), (part, columns)), step)
        for step in STEPS
    ]


def gather_cotangents(along):
    row = jnp.concatenate(along, axis=0)
    pieces = [row, exchange(row, 1)]
    return pieces + [exchange(piece, cores=True) for piece in pieces]


def local(q_img, k_img, v_img, k_txt, v_txt, out_weight, d_out):
    n = lax.axis_size("seq")
    rows, width = q_img.shape
    args = (q_img, k_img, v_img, k_txt, v_txt, out_weight, d_out)
    if n != 2 * len(STEPS) or width // HD != n or lax.axis_size("fsdp") != 2 or rows % 32:
        return local_general(*args)
    depth = out_weight.shape[0]
    image = n * rows
    text = k_txt.shape[0]
    total = image + text
    chunk = 2 * rows
    shape = jax.ShapeDtypeStruct
    vmem = pl.BlockSpec(memory_space=pltpu.VMEM)

    head = pl.BlockSpec((text, HD), lambda i, me_ref: (0, me_ref[0]))
    big = 60 * 1024 * 1024
    keep, give, text_head = call(
        pack_weight_kernel,
        [shape((depth, 4 * HD), BF16)] * 2 + [shape((2, text, HD), BF16)],
        [lax.axis_index("seq").astype(jnp.int32)[None], out_weight, k_txt, v_txt],
        specs=[vmem] + [head] * 2,
        scalars=1,
        moved=4 * depth * width,
        limit=big,
    )
    d_out, give = lax.optimization_barrier((d_out, give))
    given = exchange(give, 1)
    along = send_cotangents(d_out)
    (tok_out,) = call(
        pack_kernel,
        [shape((n, 3 * rows, HD), BF16)],
        [q_img, k_img, v_img],
        moved=4 * 3 * rows * width,
        limit=big,
    )
    tok_out, along[1] = lax.optimization_barrier((tok_out, along[1]))
    along, given = lax.optimization_barrier((along, given))
    pieces = gather_cotangents(along)
    tok_in = lax.all_to_all(tok_out, "seq", split_axis=0, concat_axis=0, tiled=True)

    probs, out_t, queries, keys_t, vals = call(
        functools.partial(forward_kernel, chunk=chunk),
        [shape(dims, BF16) for dims in ((total, image), (HD, image), (image, HD), (HD, total), (total, HD))],
        [tok_in, text_head],
        scratch=[pltpu.VMEM((total, HD), BF16), pltpu.VMEM((HD, total), BF16)],
        flops=4 * total * image * HD,
        moved=4 * total * image,
    )
    columns = pieces[0].shape[1]
    mine, far, near, near_far, cot = call(
        partial_kernel,
        [shape((image, HD), F32)] * 2 + [shape((image, HD), BF16)] * 2 + [shape((image, columns), BF16)],
        [*pieces, keep, given],
        scratch=[pltpu.VMEM((columns, 4 * HD), BF16)],
        flops=8 * image * columns * HD,
        moved=2 * image * columns,
    )
    near_far = exchange(near_far, 2)
    far, out_t = lax.optimization_barrier(((far + near_far.astype(F32)).astype(BF16), out_t))
    far = exchange(far, 4)
    near, _ = lax.optimization_barrier((near, near_far))
    near = exchange(near, 2)
    out_near = exchange(out_t, 2)
    out_late, far, out_near = lax.optimization_barrier((out_t, far, out_near))
    out_far = exchange(out_late, 4)
    (grad_out,) = call(
        functools.partial(backward_kernel, chunk=chunk),
        [shape((n, 3 * rows, HD), BF16)],
        [queries, keys_t, vals, probs, out_t, mine, near, far],
        scratch=[pltpu.VMEM((image, HD), F32), pltpu.VMEM((image, HD), F32)],
        flops=8 * total * image * HD,
        moved=4 * total * image,
    )
    grad_in = lax.all_to_all(grad_out, "seq", split_axis=0, concat_axis=0, tiled=True)
    outs = [out_t, out_near, out_far, exchange(out_far, 2)]
    dw_own, dw_other = call(
        weight_grad_kernel,
        [shape((4 * HD, depth), BF16)] * 2,
        [cot, *outs],
        scratch=[pltpu.VMEM((4 * HD, image), BF16)],
        flops=256 * image * columns * HD,
        moved=2 * image * columns,
    )
    grads = call(
        unpack_kernel,
        [shape((rows, width), BF16)] * 3,
        [grad_in],
        moved=4 * 3 * rows * width,
    )
    (d_weight,) = call(
        unpack_weight_kernel,
        [shape((depth, width), F32)],
        [dw_own, exchange(dw_other, 1)],
        moved=6 * depth * width,
    )
    return (*grads, d_weight)


def solution(mesh):
    in_specs = (
        P(("group", "seq"), "fsdp"),
        P(("group", "seq"), "fsdp"),
        P(("group", "seq"), "fsdp"),
        P("group", "fsdp"),
        P("group", "fsdp"),
        P("seq", "fsdp"),
        P(("group", "seq"), None),
    )
    out_specs = (
        P(("group", "seq"), "fsdp"),
        P(("group", "seq"), "fsdp"),
        P(("group", "seq"), "fsdp"),
        P(("group", "seq"), "fsdp"),
    )
    return jax.shard_map(local, mesh=mesh, in_specs=in_specs, out_specs=out_specs, check_vma=False)
```

```python
import functools
import math

import jax
import jax.numpy as jnp
from jax import lax
from jax.experimental import pallas as pl
from jax.experimental.pallas import tpu as pltpu
from jax.sharding import PartitionSpec as P

HD = 128
F32 = jnp.float32
BF16 = jnp.bfloat16
LIMIT = 28 * 1024 * 1024
NT = (((1,), (1,)), ((), ()))


def attend(queries, cotangents, key_rows, value_rows, block_rows):
    score_scale = HD ** (-0.5)
    query_count = queries.shape[0]
    block_count = query_count // block_rows
    query_blocks = queries.reshape(block_count, block_rows, HD)
    grad_blocks = cotangents.reshape(block_count, block_rows, HD)

    def one_block(accumulated, pair_item):
        query_block, grad_block = pair_item
        scores = jnp.dot(query_block, key_rows.T, preferred_element_type=jnp.float32) * score_scale
        row_max = jnp.max(scores, axis=1, keepdims=True)
        probs = jnp.exp(scores - row_max)
        probs = probs / jnp.sum(probs, axis=1, keepdims=True)
        probs_low = probs.astype(jnp.bfloat16)
        out_rows = jnp.dot(probs_low, value_rows, preferred_element_type=jnp.float32).astype(
            jnp.bfloat16
        )
        prob_grad = jnp.dot(grad_block, value_rows.T, preferred_element_type=jnp.float32)
        row_dot = jnp.sum(
            grad_block.astype(jnp.float32) * out_rows.astype(jnp.float32), axis=1, keepdims=True
        )
        score_grad = (probs * (prob_grad - row_dot)).astype(jnp.bfloat16)
        query_grad = (
            jnp.dot(score_grad, key_rows, preferred_element_type=jnp.float32) * score_scale
        ).astype(jnp.bfloat16)
        key_grad = (
            accumulated[0]
            + jnp.dot(score_grad.T, query_block, preferred_element_type=jnp.float32) * score_scale
        )
        value_grad = accumulated[1] + jnp.dot(
            probs_low.T, grad_block, preferred_element_type=jnp.float32
        )
        return ((key_grad, value_grad), (query_grad, out_rows))

    empty = jnp.zeros((key_rows.shape[0], HD), jnp.float32)
    (key_grad, value_grad), (query_grad, out_rows) = lax.scan(
        one_block, (empty, empty), (query_blocks, grad_blocks)
    )
    return (
        query_grad.reshape(query_count, HD),
        out_rows.reshape(query_count, HD),
        key_grad,
        value_grad,
    )


def local_general(q_img, k_img, v_img, k_txt, v_txt, out_weight, d_out):
    rows_here = q_img.shape[0]
    heads_here = q_img.shape[1] // HD
    seq_count = lax.axis_size("seq")
    share_count = seq_count // heads_here
    part_rows = rows_here // share_count
    seq_index = lax.axis_index("seq")
    head_index = seq_index // share_count
    column_cut = d_out
    attn_grad = jnp.dot(
        column_cut,
        lax.all_gather(out_weight, "seq", axis=0, tiled=True),
        preferred_element_type=jnp.float32,
    ).astype(jnp.bfloat16)

    def to_heads(array_in):
        shaped = array_in.reshape(share_count, part_rows, heads_here, HD).transpose(2, 0, 1, 3)
        return shaped.reshape(seq_count, part_rows, HD)

    def whole_heads(array_in):
        shaped = array_in.reshape(rows_here, heads_here, HD).transpose(1, 0, 2)
        shaped = jnp.broadcast_to(shaped[:, None], (heads_here, share_count, rows_here, HD))
        return shaped.reshape(seq_count, rows_here, HD)

    def from_heads(array_in):
        shaped = array_in.reshape(heads_here, share_count, part_rows, HD).transpose(1, 2, 0, 3)
        return shaped.reshape(rows_here, heads_here * HD)

    text_keys = lax.dynamic_slice_in_dim(k_txt, head_index * HD, HD, 1)
    text_values = lax.dynamic_slice_in_dim(v_txt, head_index * HD, HD, 1)
    query_side = jnp.concatenate([to_heads(q_img), to_heads(attn_grad)], axis=2)
    key_side = jnp.concatenate([whole_heads(k_img), whole_heads(v_img)], axis=2)
    packed = jnp.concatenate([query_side, key_side], axis=1)
    received = lax.all_to_all(packed, "seq", split_axis=0, concat_axis=0, tiled=True)
    queries = received[:, :part_rows, :HD].reshape(seq_count * part_rows, HD)
    cotangents = received[:, :part_rows, HD:].reshape(seq_count * part_rows, HD)
    image_keys = received[:, part_rows:, :HD].reshape(seq_count * rows_here, HD)
    image_values = received[:, part_rows:, HD:].reshape(seq_count * rows_here, HD)
    key_rows = jnp.concatenate([image_keys, text_keys], axis=0)
    value_rows = jnp.concatenate([image_values, text_values], axis=0)
    query_grad, out_rows, key_grad, value_grad = attend(
        queries, cotangents, key_rows, value_rows, min(512, queries.shape[0])
    )
    image_count = image_keys.shape[0]
    query_part = (
        jnp.concatenate([query_grad, out_rows], axis=1)
        .astype(jnp.float32)
        .reshape(seq_count, part_rows, 2 * HD)
    )
    key_part = jnp.concatenate([key_grad[:image_count], value_grad[:image_count]], axis=1).reshape(
        seq_count, rows_here, 2 * HD
    )
    returned = lax.all_to_all(
        jnp.concatenate([query_part, key_part], axis=1).astype(jnp.bfloat16),
        "seq",
        split_axis=0,
        concat_axis=0,
        tiled=True,
    ).astype(jnp.float32)
    q_grad = from_heads(returned[:, :part_rows, :HD]).astype(jnp.bfloat16)
    out_tok = from_heads(returned[:, :part_rows, HD:]).astype(jnp.bfloat16)
    summed = jnp.sum(
        returned[:, part_rows:, :].reshape(heads_here, share_count, rows_here, 2 * HD), axis=1
    )
    summed = summed.transpose(1, 0, 2)
    k_grad = summed[:, :, :HD].reshape(rows_here, heads_here * HD).astype(jnp.bfloat16)
    v_grad = summed[:, :, HD:].reshape(rows_here, heads_here * HD).astype(jnp.bfloat16)
    column_cut = d_out
    d_weight = lax.psum_scatter(
        jnp.dot(column_cut.T, out_tok, preferred_element_type=jnp.float32).astype(jnp.bfloat16),
        "seq",
        scatter_dimension=0,
        tiled=True,
    ).astype(jnp.float32)
    return (q_grad, k_grad, v_grad, d_weight)


def call(kernel, outs, args, specs=None, scratch=(), scalars=0, out_specs=None, flops=0, moved=0, limit=LIMIT):
    vmem = pl.BlockSpec(memory_space=pltpu.VMEM)
    if specs is None:
        specs = [vmem] * (len(args) - scalars)
    if out_specs is None:
        out_specs = [vmem] * len(outs)
    return pl.pallas_call(
        kernel,
        out_shape=outs,
        grid_spec=pltpu.PrefetchScalarGridSpec(
            num_scalar_prefetch=scalars,
            grid=(1,),
            in_specs=specs,
            out_specs=out_specs,
            scratch_shapes=list(scratch),
        ),
        compiler_params=pltpu.CompilerParams(vmem_limit_bytes=limit),
        cost_estimate=pl.CostEstimate(flops=flops, bytes_accessed=moved, transcendentals=0),
    )(*args)


STEPS = (0, 2, 4, 6)


def head_columns(step, other_row):
    return pl.ds(pl.multiple_of(jnp.bitwise_xor(lax.axis_index("seq"), step + other_row) * HD, HD), HD)


def pack_kernel(q_ref, k_ref, v_ref, tok_ref):
    rows = q_ref.shape[0]
    for h in range(tok_ref.shape[0]):
        for i, ref in enumerate((q_ref, k_ref, v_ref)):
            tok_ref[h, i * rows : (i + 1) * rows, :] = ref[:, h * HD : (h + 1) * HD]


def pack_weight_kernel(me_ref, w_ref, kt_ref, vt_ref, keep_ref, give_ref, text_ref):
    for i, step in enumerate(STEPS):
        cols = slice(i * HD, (i + 1) * HD)
        keep_ref[:, cols] = w_ref[:, head_columns(step, 0)]
        give_ref[:, cols] = w_ref[:, head_columns(step, 1)]
    text_ref[0] = kt_ref[...]
    text_ref[1] = vt_ref[...]


def forward_kernel(tok_ref, text_ref, probs_ref, out_ref, queries_ref, keys_t_ref, vals_ref, keys, vals_t, *, chunk):
    n, three, _ = tok_ref.shape
    rows = three // 3
    image = n * rows
    text = text_ref.shape[1]
    queries_ref[...] = tok_ref[:, 0:rows, :].reshape(image, HD)
    keys[0:image, :] = tok_ref[:, rows : 2 * rows, :].reshape(image, HD)
    keys[image : image + text, :] = text_ref[0]
    vals_ref[0:image, :] = tok_ref[:, 2 * rows : 3 * rows, :].reshape(image, HD)
    vals_ref[image : image + text, :] = text_ref[1]
    keys_t_ref[...] = keys[...].T
    vals_t[...] = vals_ref[...].T
    factor = HD ** (-0.5) * math.log2(math.e)
    for c in range(image // chunk):
        span = slice(c * chunk, (c + 1) * chunk)
        scores = lax.dot_general(keys[...], queries_ref[span, :], NT, preferred_element_type=F32)
        top = jnp.max(scores, axis=0, keepdims=True)
        weights = jnp.exp2((scores - top) * factor)
        total = jnp.sum(weights, axis=0, keepdims=True)
        low = (weights * (1.0 / total)).astype(BF16)
        probs_ref[:, span] = low
        out_ref[:, span] = jnp.dot(vals_t[...], low, preferred_element_type=F32).astype(BF16)


def partial_kernel(*refs):
    *pieces, own_ref, other_ref, mine_ref, far_ref, near_ref, near_far_ref, cot_ref, weight = refs
    me = lax.axis_index("seq")
    core = lax.axis_index("fsdp")
    count = len(STEPS)
    part = pieces[0].shape[0] // count
    for p, piece in enumerate(pieces):
        row, swapped = p % 2, p // 2
        shift = jnp.bitwise_xor(core, swapped) * part
        for i, step in enumerate(STEPS):
            at = pl.multiple_of(jnp.bitwise_xor(me, step + row) * (2 * part) + shift, 16)
            cot_ref[pl.ds(at, part), :] = piece[i * part : (i + 1) * part, :]
    depth = own_ref.shape[0]
    y = lax.rem(me, 2)
    weight[pl.ds(pl.multiple_of(y * depth, 16), depth), :] = own_ref[...]
    weight[pl.ds(pl.multiple_of((1 - y) * depth, 16), depth), :] = other_ref[...]
    step = 256

    @pl.loop(0, cot_ref.shape[0] // step)
    def _(i):
        at = pl.ds(pl.multiple_of(i * step, step), step)
        part = jnp.dot(cot_ref[at, :], weight[...], preferred_element_type=F32)
        mine_ref[at, :] = part[:, :HD]
        near_ref[at, :] = part[:, HD : 2 * HD].astype(BF16)
        far_ref[at, :] = part[:, 2 * HD : 3 * HD]
        near_far_ref[at, :] = part[:, 3 * HD :].astype(BF16)


def weight_grad_kernel(cot_ref, *refs):
    *out_refs, own_ref, other_ref, outs = refs
    first = 0
    for ref in out_refs:
        outs[first : first + ref.shape[0], :] = ref[...]
        first += ref.shape[0]
    depth = own_ref.shape[1]
    y = lax.rem(lax.axis_index("seq"), 2)
    for ref, row in ((own_ref, y), (other_ref, 1 - y)):
        at = pl.multiple_of(row * depth, HD)
        ref[...] = jnp.dot(outs[...], cot_ref[:, pl.ds(at, depth)], preferred_element_type=F32).astype(BF16)


def backward_kernel(
    queries_ref, keys_t_ref, vals_ref, probs_ref, out_ref, mine_ref, near_ref, far_ref, send_ref, dk, dv, *, chunk
):
    n, three, _ = send_ref.shape
    rows = three // 3
    image = n * rows
    scale = HD ** (-0.5)
    per = chunk // rows
    for c in range(image // chunk):
        span = slice(c * chunk, (c + 1) * chunk)
        grads = mine_ref[span, :] + near_ref[span, :].astype(F32) + far_ref[span, :].astype(F32)
        grads = grads.astype(BF16)
        row_dot = jnp.sum(
            grads.astype(F32).T * out_ref[:, span].astype(F32), axis=0, keepdims=True
        )
        prob_grad = lax.dot_general(vals_ref[...], grads, NT, preferred_element_type=F32)
        low = probs_ref[:, span]
        score_grad = (low.astype(F32) * (prob_grad - row_dot)).astype(BF16)
        dq_t = jnp.dot(keys_t_ref[...], score_grad, preferred_element_type=F32) * scale
        send_ref[c * per : (c + 1) * per, 0:rows, :] = dq_t.T.astype(BF16).reshape(per, rows, HD)
        dk_part = jnp.dot(score_grad[0:image, :], queries_ref[span, :], preferred_element_type=F32)
        dv_part = jnp.dot(low[0:image, :], grads, preferred_element_type=F32)
        if c == 0:
            dk[...] = dk_part
            dv[...] = dv_part
        else:
            dk[...] += dk_part
            dv[...] += dv_part
    send_ref[:, rows : 2 * rows, :] = (dk[...] * scale).astype(BF16).reshape(n, rows, HD)
    send_ref[:, 2 * rows : 3 * rows, :] = dv[...].astype(BF16).reshape(n, rows, HD)


def unpack_kernel(tok_ref, q_ref, k_ref, v_ref):
    rows = q_ref.shape[0]
    for h in range(tok_ref.shape[0]):
        for i, ref in enumerate((q_ref, k_ref, v_ref)):
            ref[:, h * HD : (h + 1) * HD] = tok_ref[h, i * rows : (i + 1) * rows, :]


def unpack_weight_kernel(own_ref, other_ref, w_ref):
    for other_row, ref in enumerate((own_ref, other_ref)):
        for i, step in enumerate(STEPS):
            w_ref[:, head_columns(step, other_row)] = ref[i * HD : (i + 1) * HD, :].astype(F32).T


def exchange(array, distance=0, cores=False):
    if not distance and not cores:
        return array
    size = 2 * lax.axis_size("seq")
    pairs = [(i, i ^ (2 * distance + int(cores))) for i in range(size)]
    return lax.ppermute(array, ("seq", "fsdp"), pairs)


def send_cotangents(d_out):
    rows, width = d_out.shape
    part, columns = rows // 2, width // len(STEPS)
    z = lax.axis_index("seq") // 2
    first = lax.axis_index("fsdp") * part
    return [
        exchange(lax.dynamic_slice(d_out, (first, (z ^ (step // 2)) * columns), (part, columns)), step)
        for step in STEPS
    ]


def gather_cotangents(along):
    row = jnp.concatenate(along, axis=0)
    pieces = [row, exchange(row, 1)]
    return pieces + [exchange(piece, cores=True) for piece in pieces]


def local(q_img, k_img, v_img, k_txt, v_txt, out_weight, d_out):
    n = lax.axis_size("seq")
    rows, width = q_img.shape
    args = (q_img, k_img, v_img, k_txt, v_txt, out_weight, d_out)
    if n != 2 * len(STEPS) or width // HD != n or lax.axis_size("fsdp") != 2 or rows % 32:
        return local_general(*args)
    depth = out_weight.shape[0]
    image = n * rows
    text = k_txt.shape[0]
    total = image + text
    chunk = 2 * rows
    shape = jax.ShapeDtypeStruct
    vmem = pl.BlockSpec(memory_space=pltpu.VMEM)

    head = pl.BlockSpec((text, HD), lambda i, me_ref: (0, me_ref[0]))
    big = 60 * 1024 * 1024
    keep, give, text_head = call(
        pack_weight_kernel,
        [shape((depth, 4 * HD), BF16)] * 2 + [shape((2, text, HD), BF16)],
        [lax.axis_index("seq").astype(jnp.int32)[None], out_weight, k_txt, v_txt],
        specs=[vmem] + [head] * 2,
        scalars=1,
        moved=4 * depth * width,
        limit=big,
    )
    d_out, give = lax.optimization_barrier((d_out, give))
    given = exchange(give, 1)
    along = send_cotangents(d_out)
    (tok_out,) = call(
        pack_kernel,
        [shape((n, 3 * rows, HD), BF16)],
        [q_img, k_img, v_img],
        moved=4 * 3 * rows * width,
        limit=big,
    )
    tok_out, along[1] = lax.optimization_barrier((tok_out, along[1]))
    along, given = lax.optimization_barrier((along, given))
    pieces = gather_cotangents(along)
    tok_in = lax.all_to_all(tok_out, "seq", split_axis=0, concat_axis=0, tiled=True)

    probs, out_t, queries, keys_t, vals = call(
        functools.partial(forward_kernel, chunk=chunk),
        [shape(dims, BF16) for dims in ((total, image), (HD, image), (image, HD), (HD, total), (total, HD))],
        [tok_in, text_head],
        scratch=[pltpu.VMEM((total, HD), BF16), pltpu.VMEM((HD, total), BF16)],
        flops=4 * total * image * HD,
        moved=4 * total * image,
    )
    columns = pieces[0].shape[1]
    mine, far, near, near_far, cot = call(
        partial_kernel,
        [shape((image, HD), F32)] * 2 + [shape((image, HD), BF16)] * 2 + [shape((image, columns), BF16)],
        [*pieces, keep, given],
        scratch=[pltpu.VMEM((columns, 4 * HD), BF16)],
        flops=8 * image * columns * HD,
        moved=2 * image * columns,
    )
    out_near, out_far = exchange(out_t, 2), exchange(out_t, 4)
    near_far, _ = lax.optimization_barrier((near_far, out_t))
    near_far = exchange(near_far, 2)
    far, out_far = lax.optimization_barrier(((far + near_far.astype(F32)).astype(BF16), out_far))
    far = exchange(far, 4)
    near, _ = lax.optimization_barrier((near, near_far))
    near = exchange(near, 2)
    outs = [out_t, out_near, out_far, exchange(out_far, 2)]
    dw_own, dw_other = call(
        weight_grad_kernel,
        [shape((4 * HD, depth), BF16)] * 2,
        [cot, *outs],
        scratch=[pltpu.VMEM((4 * HD, image), BF16)],
        flops=8 * image * columns * HD,
        moved=2 * image * columns,
    )
    mine, _ = lax.optimization_barrier((mine, dw_own))
    (grad_out,) = call(
        functools.partial(backward_kernel, chunk=chunk),
        [shape((n, 3 * rows, HD), BF16)],
        [queries, keys_t, vals, probs, out_t, mine, near, far],
        scratch=[pltpu.VMEM((image, HD), F32), pltpu.VMEM((image, HD), F32)],
        flops=8 * total * image * HD,
        moved=4 * total * image,
    )
    grad_in = lax.all_to_all(grad_out, "seq", split_axis=0, concat_axis=0, tiled=True)
    grads = call(
        unpack_kernel,
        [shape((rows, width), BF16)] * 3,
        [grad_in],
        moved=4 * 3 * rows * width,
    )
    (d_weight,) = call(
        unpack_weight_kernel,
        [shape((depth, width), F32)],
        [dw_own, exchange(dw_other, 1)],
        moved=6 * depth * width,
    )
    return (*grads, d_weight)


def solution(mesh):
    in_specs = (
        P(("group", "seq"), "fsdp"),
        P(("group", "seq"), "fsdp"),
        P(("group", "seq"), "fsdp"),
        P("group", "fsdp"),
        P("group", "fsdp"),
        P("seq", "fsdp"),
        P(("group", "seq"), None),
    )
    out_specs = (
        P(("group", "seq"), "fsdp"),
        P(("group", "seq"), "fsdp"),
        P(("group", "seq"), "fsdp"),
        P(("group", "seq"), "fsdp"),
    )
    return jax.shard_map(local, mesh=mesh, in_specs=in_specs, out_specs=out_specs, check_vma=False)
```

```python
import functools
import math

import jax
import jax.numpy as jnp
from jax import lax
from jax.experimental import pallas as pl
from jax.experimental.pallas import tpu as pltpu
from jax.sharding import PartitionSpec as P

HD = 128
F32 = jnp.float32
BF16 = jnp.bfloat16
LIMIT = 28 * 1024 * 1024
NT = (((1,), (1,)), ((), ()))


def attend(queries, cotangents, key_rows, value_rows, block_rows):
    score_scale = HD ** (-0.5)
    query_count = queries.shape[0]
    block_count = query_count // block_rows
    query_blocks = queries.reshape(block_count, block_rows, HD)
    grad_blocks = cotangents.reshape(block_count, block_rows, HD)

    def one_block(accumulated, pair_item):
        query_block, grad_block = pair_item
        scores = jnp.dot(query_block, key_rows.T, preferred_element_type=jnp.float32) * score_scale
        row_max = jnp.max(scores, axis=1, keepdims=True)
        probs = jnp.exp(scores - row_max)
        probs = probs / jnp.sum(probs, axis=1, keepdims=True)
        probs_low = probs.astype(jnp.bfloat16)
        out_rows = jnp.dot(probs_low, value_rows, preferred_element_type=jnp.float32).astype(
            jnp.bfloat16
        )
        prob_grad = jnp.dot(grad_block, value_rows.T, preferred_element_type=jnp.float32)
        row_dot = jnp.sum(
            grad_block.astype(jnp.float32) * out_rows.astype(jnp.float32), axis=1, keepdims=True
        )
        score_grad = (probs * (prob_grad - row_dot)).astype(jnp.bfloat16)
        query_grad = (
            jnp.dot(score_grad, key_rows, preferred_element_type=jnp.float32) * score_scale
        ).astype(jnp.bfloat16)
        key_grad = (
            accumulated[0]
            + jnp.dot(score_grad.T, query_block, preferred_element_type=jnp.float32) * score_scale
        )
        value_grad = accumulated[1] + jnp.dot(
            probs_low.T, grad_block, preferred_element_type=jnp.float32
        )
        return ((key_grad, value_grad), (query_grad, out_rows))

    empty = jnp.zeros((key_rows.shape[0], HD), jnp.float32)
    (key_grad, value_grad), (query_grad, out_rows) = lax.scan(
        one_block, (empty, empty), (query_blocks, grad_blocks)
    )
    return (
        query_grad.reshape(query_count, HD),
        out_rows.reshape(query_count, HD),
        key_grad,
        value_grad,
    )


def local_general(q_img, k_img, v_img, k_txt, v_txt, out_weight, d_out):
    rows_here = q_img.shape[0]
    heads_here = q_img.shape[1] // HD
    seq_count = lax.axis_size("seq")
    share_count = seq_count // heads_here
    part_rows = rows_here // share_count
    seq_index = lax.axis_index("seq")
    head_index = seq_index // share_count
    column_cut = d_out
    attn_grad = jnp.dot(
        column_cut,
        lax.all_gather(out_weight, "seq", axis=0, tiled=True),
        preferred_element_type=jnp.float32,
    ).astype(jnp.bfloat16)

    def to_heads(array_in):
        shaped = array_in.reshape(share_count, part_rows, heads_here, HD).transpose(2, 0, 1, 3)
        return shaped.reshape(seq_count, part_rows, HD)

    def whole_heads(array_in):
        shaped = array_in.reshape(rows_here, heads_here, HD).transpose(1, 0, 2)
        shaped = jnp.broadcast_to(shaped[:, None], (heads_here, share_count, rows_here, HD))
        return shaped.reshape(seq_count, rows_here, HD)

    def from_heads(array_in):
        shaped = array_in.reshape(heads_here, share_count, part_rows, HD).transpose(1, 2, 0, 3)
        return shaped.reshape(rows_here, heads_here * HD)

    text_keys = lax.dynamic_slice_in_dim(k_txt, head_index * HD, HD, 1)
    text_values = lax.dynamic_slice_in_dim(v_txt, head_index * HD, HD, 1)
    query_side = jnp.concatenate([to_heads(q_img), to_heads(attn_grad)], axis=2)
    key_side = jnp.concatenate([whole_heads(k_img), whole_heads(v_img)], axis=2)
    packed = jnp.concatenate([query_side, key_side], axis=1)
    received = lax.all_to_all(packed, "seq", split_axis=0, concat_axis=0, tiled=True)
    queries = received[:, :part_rows, :HD].reshape(seq_count * part_rows, HD)
    cotangents = received[:, :part_rows, HD:].reshape(seq_count * part_rows, HD)
    image_keys = received[:, part_rows:, :HD].reshape(seq_count * rows_here, HD)
    image_values = received[:, part_rows:, HD:].reshape(seq_count * rows_here, HD)
    key_rows = jnp.concatenate([image_keys, text_keys], axis=0)
    value_rows = jnp.concatenate([image_values, text_values], axis=0)
    query_grad, out_rows, key_grad, value_grad = attend(
        queries, cotangents, key_rows, value_rows, min(512, queries.shape[0])
    )
    image_count = image_keys.shape[0]
    query_part = (
        jnp.concatenate([query_grad, out_rows], axis=1)
        .astype(jnp.float32)
        .reshape(seq_count, part_rows, 2 * HD)
    )
    key_part = jnp.concatenate([key_grad[:image_count], value_grad[:image_count]], axis=1).reshape(
        seq_count, rows_here, 2 * HD
    )
    returned = lax.all_to_all(
        jnp.concatenate([query_part, key_part], axis=1).astype(jnp.bfloat16),
        "seq",
        split_axis=0,
        concat_axis=0,
        tiled=True,
    ).astype(jnp.float32)
    q_grad = from_heads(returned[:, :part_rows, :HD]).astype(jnp.bfloat16)
    out_tok = from_heads(returned[:, :part_rows, HD:]).astype(jnp.bfloat16)
    summed = jnp.sum(
        returned[:, part_rows:, :].reshape(heads_here, share_count, rows_here, 2 * HD), axis=1
    )
    summed = summed.transpose(1, 0, 2)
    k_grad = summed[:, :, :HD].reshape(rows_here, heads_here * HD).astype(jnp.bfloat16)
    v_grad = summed[:, :, HD:].reshape(rows_here, heads_here * HD).astype(jnp.bfloat16)
    column_cut = d_out
    d_weight = lax.psum_scatter(
        jnp.dot(column_cut.T, out_tok, preferred_element_type=jnp.float32).astype(jnp.bfloat16),
        "seq",
        scatter_dimension=0,
        tiled=True,
    ).astype(jnp.float32)
    return (q_grad, k_grad, v_grad, d_weight)


def call(kernel, outs, args, specs=None, scratch=(), scalars=0, out_specs=None, flops=0, moved=0, limit=LIMIT):
    vmem = pl.BlockSpec(memory_space=pltpu.VMEM)
    if specs is None:
        specs = [vmem] * (len(args) - scalars)
    if out_specs is None:
        out_specs = [vmem] * len(outs)
    return pl.pallas_call(
        kernel,
        out_shape=outs,
        grid_spec=pltpu.PrefetchScalarGridSpec(
            num_scalar_prefetch=scalars,
            grid=(1,),
            in_specs=specs,
            out_specs=out_specs,
            scratch_shapes=list(scratch),
        ),
        compiler_params=pltpu.CompilerParams(vmem_limit_bytes=limit),
        cost_estimate=pl.CostEstimate(flops=flops, bytes_accessed=moved, transcendentals=0),
    )(*args)


STEPS = (0, 2, 4, 6)


def head_columns(step, other_row):
    return pl.ds(pl.multiple_of(jnp.bitwise_xor(lax.axis_index("seq"), step + other_row) * HD, HD), HD)


def pack_kernel(q_ref, k_ref, v_ref, tok_ref):
    rows = q_ref.shape[0]
    for h in range(tok_ref.shape[0]):
        for i, ref in enumerate((q_ref, k_ref, v_ref)):
            tok_ref[h, i * rows : (i + 1) * rows, :] = ref[:, h * HD : (h + 1) * HD]


def pack_weight_kernel(me_ref, w_ref, kt_ref, vt_ref, keep_ref, give_ref, text_ref):
    for i, step in enumerate(STEPS):
        cols = slice(i * HD, (i + 1) * HD)
        keep_ref[:, cols] = w_ref[:, head_columns(step, 0)]
        give_ref[:, cols] = w_ref[:, head_columns(step, 1)]
    text_ref[0] = kt_ref[...]
    text_ref[1] = vt_ref[...]


def forward_kernel(tok_ref, text_ref, probs_ref, out_ref, queries_ref, keys_t_ref, vals_ref, keys, vals_t, *, chunk):
    n, three, _ = tok_ref.shape
    rows = three // 3
    image = n * rows
    text = text_ref.shape[1]
    queries_ref[...] = tok_ref[:, 0:rows, :].reshape(image, HD)
    keys[0:image, :] = tok_ref[:, rows : 2 * rows, :].reshape(image, HD)
    keys[image : image + text, :] = text_ref[0]
    vals_ref[0:image, :] = tok_ref[:, 2 * rows : 3 * rows, :].reshape(image, HD)
    vals_ref[image : image + text, :] = text_ref[1]
    keys_t_ref[...] = keys[...].T
    vals_t[...] = vals_ref[...].T
    factor = HD ** (-0.5) * math.log2(math.e)
    for c in range(image // chunk):
        span = slice(c * chunk, (c + 1) * chunk)
        scores = lax.dot_general(keys[...], queries_ref[span, :], NT, preferred_element_type=F32)
        top = jnp.max(scores, axis=0, keepdims=True)
        weights = jnp.exp2((scores - top) * factor)
        total = jnp.sum(weights, axis=0, keepdims=True)
        low = (weights * (1.0 / total)).astype(BF16)
        probs_ref[:, span] = low
        out_ref[:, span] = jnp.dot(vals_t[...], low, preferred_element_type=F32).astype(BF16)


def partial_kernel(*refs):
    *pieces, own_ref, other_ref, mine_ref, far_ref, near_ref, near_far_ref, cot_ref, weight = refs
    me = lax.axis_index("seq")
    core = lax.axis_index("fsdp")
    count = len(STEPS)
    part = pieces[0].shape[0] // count
    for p, piece in enumerate(pieces):
        row, swapped = p % 2, p // 2
        shift = jnp.bitwise_xor(core, swapped) * part
        for i, step in enumerate(STEPS):
            at = pl.multiple_of(jnp.bitwise_xor(me, step + row) * (2 * part) + shift, 16)
            cot_ref[pl.ds(at, part), :] = piece[i * part : (i + 1) * part, :]
    depth = own_ref.shape[0]
    y = lax.rem(me, 2)
    weight[pl.ds(pl.multiple_of(y * depth, 16), depth), :] = own_ref[...]
    weight[pl.ds(pl.multiple_of((1 - y) * depth, 16), depth), :] = other_ref[...]
    step = 256

    @pl.loop(0, cot_ref.shape[0] // step)
    def _(i):
        at = pl.ds(pl.multiple_of(i * step, step), step)
        part = jnp.dot(cot_ref[at, :], weight[...], preferred_element_type=F32)
        mine_ref[at, :] = part[:, :HD]
        near_ref[at, :] = part[:, HD : 2 * HD].astype(BF16)
        far_ref[at, :] = part[:, 2 * HD : 3 * HD]
        near_far_ref[at, :] = part[:, 3 * HD :].astype(BF16)


def weight_grad_kernel(cot_ref, *refs):
    *out_refs, own_ref, other_ref, outs = refs
    first = 0
    for ref in out_refs:
        outs[first : first + ref.shape[0], :] = ref[...]
        first += ref.shape[0]
    depth = own_ref.shape[1]
    y = lax.rem(lax.axis_index("seq"), 2)
    for ref, row in ((own_ref, y), (other_ref, 1 - y)):
        at = pl.multiple_of(row * depth, HD)
        ref[...] = jnp.dot(outs[...], cot_ref[:, pl.ds(at, depth)], preferred_element_type=F32).astype(BF16)


def backward_kernel(
    queries_ref, keys_t_ref, vals_ref, probs_ref, out_ref, mine_ref, near_ref, far_ref, send_ref, dk, dv, *, chunk
):
    n, three, _ = send_ref.shape
    rows = three // 3
    image = n * rows
    scale = HD ** (-0.5)
    per = chunk // rows
    for c in range(image // chunk):
        span = slice(c * chunk, (c + 1) * chunk)
        grads = mine_ref[span, :] + near_ref[span, :].astype(F32) + far_ref[span, :].astype(F32)
        grads = grads.astype(BF16)
        row_dot = jnp.sum(
            grads.astype(F32).T * out_ref[:, span].astype(F32), axis=0, keepdims=True
        )
        prob_grad = lax.dot_general(vals_ref[...], grads, NT, preferred_element_type=F32)
        low = probs_ref[:, span]
        score_grad = (low.astype(F32) * (prob_grad - row_dot)).astype(BF16)
        dq_t = jnp.dot(keys_t_ref[...], score_grad, preferred_element_type=F32) * scale
        send_ref[c * per : (c + 1) * per, 0:rows, :] = dq_t.T.astype(BF16).reshape(per, rows, HD)
        dk_part = jnp.dot(score_grad[0:image, :], queries_ref[span, :], preferred_element_type=F32)
        dv_part = jnp.dot(low[0:image, :], grads, preferred_element_type=F32)
        if c == 0:
            dk[...] = dk_part
            dv[...] = dv_part
        else:
            dk[...] += dk_part
            dv[...] += dv_part
    send_ref[:, rows : 2 * rows, :] = (dk[...] * scale).astype(BF16).reshape(n, rows, HD)
    send_ref[:, 2 * rows : 3 * rows, :] = dv[...].astype(BF16).reshape(n, rows, HD)


def unpack_kernel(tok_ref, q_ref, k_ref, v_ref):
    rows = q_ref.shape[0]
    for h in range(tok_ref.shape[0]):
        for i, ref in enumerate((q_ref, k_ref, v_ref)):
            ref[:, h * HD : (h + 1) * HD] = tok_ref[h, i * rows : (i + 1) * rows, :]


def unpack_weight_kernel(own_ref, other_ref, w_ref):
    for other_row, ref in enumerate((own_ref, other_ref)):
        for i, step in enumerate(STEPS):
            w_ref[:, head_columns(step, other_row)] = ref[i * HD : (i + 1) * HD, :].astype(F32).T


def exchange(array, distance=0, cores=False):
    if not distance and not cores:
        return array
    size = 2 * lax.axis_size("seq")
    pairs = [(i, i ^ (2 * distance + int(cores))) for i in range(size)]
    return lax.ppermute(array, ("seq", "fsdp"), pairs)


def send_cotangents(d_out):
    rows, width = d_out.shape
    part, columns = rows // 2, width // len(STEPS)
    z = lax.axis_index("seq") // 2
    first = lax.axis_index("fsdp") * part
    return [
        exchange(lax.dynamic_slice(d_out, (first, (z ^ (step // 2)) * columns), (part, columns)), step)
        for step in STEPS
    ]


def gather_cotangents(along):
    row = jnp.concatenate(along, axis=0)
    pieces = [row, exchange(row, 1)]
    return pieces + [exchange(piece, cores=True) for piece in pieces]


def local(q_img, k_img, v_img, k_txt, v_txt, out_weight, d_out):
    n = lax.axis_size("seq")
    rows, width = q_img.shape
    args = (q_img, k_img, v_img, k_txt, v_txt, out_weight, d_out)
    if n != 2 * len(STEPS) or width // HD != n or lax.axis_size("fsdp") != 2 or rows % 32:
        return local_general(*args)
    depth = out_weight.shape[0]
    image = n * rows
    text = k_txt.shape[0]
    total = image + text
    chunk = 2 * rows
    shape = jax.ShapeDtypeStruct
    vmem = pl.BlockSpec(memory_space=pltpu.VMEM)

    head = pl.BlockSpec((text, HD), lambda i, me_ref: (0, me_ref[0]))
    big = 60 * 1024 * 1024
    keep, give, text_head = call(
        pack_weight_kernel,
        [shape((depth, 4 * HD), BF16)] * 2 + [shape((2, text, HD), BF16)],
        [lax.axis_index("seq").astype(jnp.int32)[None], out_weight, k_txt, v_txt],
        specs=[vmem] + [head] * 2,
        scalars=1,
        moved=4 * depth * width,
        limit=big,
    )
    d_out, give = lax.optimization_barrier((d_out, give))
    given = exchange(give, 1)
    along = send_cotangents(d_out)
    (tok_out,) = call(
        pack_kernel,
        [shape((n, 3 * rows, HD), BF16)],
        [q_img, k_img, v_img],
        moved=4 * 3 * rows * width,
        limit=big,
    )
    tok_out, along[1] = lax.optimization_barrier((tok_out, along[1]))
    along, given = lax.optimization_barrier((along, given))
    pieces = gather_cotangents(along)
    tok_in = lax.all_to_all(tok_out, "seq", split_axis=0, concat_axis=0, tiled=True)

    probs, out_t, queries, keys_t, vals = call(
        functools.partial(forward_kernel, chunk=chunk),
        [shape(dims, BF16) for dims in ((total, image), (HD, image), (image, HD), (HD, total), (total, HD))],
        [tok_in, text_head],
        scratch=[pltpu.VMEM((total, HD), BF16), pltpu.VMEM((HD, total), BF16)],
        flops=4 * total * image * HD,
        moved=4 * total * image,
    )
    columns = pieces[0].shape[1]
    mine, far, near, near_far, cot = call(
        partial_kernel,
        [shape((image, HD), F32)] * 2 + [shape((image, HD), BF16)] * 2 + [shape((image, columns), BF16)],
        [*pieces, keep, given],
        scratch=[pltpu.VMEM((columns, 4 * HD), BF16)],
        flops=8 * image * columns * HD,
        moved=2 * image * columns,
    )
    near_far = exchange(near_far, 2)
    far = exchange((far + near_far.astype(F32)).astype(BF16), 4)
    near, _ = lax.optimization_barrier((near, near_far))
    near = exchange(near, 2)
    out_near = exchange(out_t, 2)
    out_late, far, out_near = lax.optimization_barrier((out_t, far, out_near))
    out_far = exchange(out_late, 4)
    (grad_out,) = call(
        functools.partial(backward_kernel, chunk=chunk),
        [shape((n, 3 * rows, HD), BF16)],
        [queries, keys_t, vals, probs, out_t, mine, near, far],
        scratch=[pltpu.VMEM((image, HD), F32), pltpu.VMEM((image, HD), F32)],
        flops=8 * total * image * HD,
        moved=4 * total * image,
    )
    grad_in = lax.all_to_all(grad_out, "seq", split_axis=0, concat_axis=0, tiled=True)
    out_far, _ = lax.optimization_barrier((out_far, grad_out))
    outs = [out_t, out_near, out_far, exchange(out_far, 2)]
    dw_own, dw_other = call(
        weight_grad_kernel,
        [shape((4 * HD, depth), BF16)] * 2,
        [cot, *outs],
        scratch=[pltpu.VMEM((4 * HD, image), BF16)],
        flops=96 * image * columns * HD,
        moved=2 * image * columns,
    )
    grads = call(
        unpack_kernel,
        [shape((rows, width), BF16)] * 3,
        [grad_in],
        moved=4 * 3 * rows * width,
    )
    (d_weight,) = call(
        unpack_weight_kernel,
        [shape((depth, width), F32)],
        [dw_own, exchange(dw_other, 1)],
        moved=6 * depth * width,
    )
    return (*grads, d_weight)


def solution(mesh):
    in_specs = (
        P(("group", "seq"), "fsdp"),
        P(("group", "seq"), "fsdp"),
        P(("group", "seq"), "fsdp"),
        P("group", "fsdp"),
        P("group", "fsdp"),
        P("seq", "fsdp"),
        P(("group", "seq"), None),
    )
    out_specs = (
        P(("group", "seq"), "fsdp"),
        P(("group", "seq"), "fsdp"),
        P(("group", "seq"), "fsdp"),
        P(("group", "seq"), "fsdp"),
    )
    return jax.shard_map(local, mesh=mesh, in_specs=in_specs, out_specs=out_specs, check_vma=False)
```

```python
import functools
import math

import jax
import jax.numpy as jnp
from jax import lax
from jax.experimental import pallas as pl
from jax.experimental.pallas import tpu as pltpu
from jax.sharding import PartitionSpec as P

HD = 128
F32 = jnp.float32
BF16 = jnp.bfloat16
LIMIT = 28 * 1024 * 1024
NT = (((1,), (1,)), ((), ()))


def attend(queries, cotangents, key_rows, value_rows, block_rows):
    score_scale = HD ** (-0.5)
    query_count = queries.shape[0]
    block_count = query_count // block_rows
    query_blocks = queries.reshape(block_count, block_rows, HD)
    grad_blocks = cotangents.reshape(block_count, block_rows, HD)

    def one_block(accumulated, pair_item):
        query_block, grad_block = pair_item
        scores = jnp.dot(query_block, key_rows.T, preferred_element_type=jnp.float32) * score_scale
        row_max = jnp.max(scores, axis=1, keepdims=True)
        probs = jnp.exp(scores - row_max)
        probs = probs / jnp.sum(probs, axis=1, keepdims=True)
        probs_low = probs.astype(jnp.bfloat16)
        out_rows = jnp.dot(probs_low, value_rows, preferred_element_type=jnp.float32).astype(
            jnp.bfloat16
        )
        prob_grad = jnp.dot(grad_block, value_rows.T, preferred_element_type=jnp.float32)
        row_dot = jnp.sum(
            grad_block.astype(jnp.float32) * out_rows.astype(jnp.float32), axis=1, keepdims=True
        )
        score_grad = (probs * (prob_grad - row_dot)).astype(jnp.bfloat16)
        query_grad = (
            jnp.dot(score_grad, key_rows, preferred_element_type=jnp.float32) * score_scale
        ).astype(jnp.bfloat16)
        key_grad = (
            accumulated[0]
            + jnp.dot(score_grad.T, query_block, preferred_element_type=jnp.float32) * score_scale
        )
        value_grad = accumulated[1] + jnp.dot(
            probs_low.T, grad_block, preferred_element_type=jnp.float32
        )
        return ((key_grad, value_grad), (query_grad, out_rows))

    empty = jnp.zeros((key_rows.shape[0], HD), jnp.float32)
    (key_grad, value_grad), (query_grad, out_rows) = lax.scan(
        one_block, (empty, empty), (query_blocks, grad_blocks)
    )
    return (
        query_grad.reshape(query_count, HD),
        out_rows.reshape(query_count, HD),
        key_grad,
        value_grad,
    )


def local_general(q_img, k_img, v_img, k_txt, v_txt, out_weight, d_out):
    rows_here = q_img.shape[0]
    heads_here = q_img.shape[1] // HD
    seq_count = lax.axis_size("seq")
    share_count = seq_count // heads_here
    part_rows = rows_here // share_count
    seq_index = lax.axis_index("seq")
    head_index = seq_index // share_count
    column_cut = d_out
    attn_grad = jnp.dot(
        column_cut,
        lax.all_gather(out_weight, "seq", axis=0, tiled=True),
        preferred_element_type=jnp.float32,
    ).astype(jnp.bfloat16)

    def to_heads(array_in):
        shaped = array_in.reshape(share_count, part_rows, heads_here, HD).transpose(2, 0, 1, 3)
        return shaped.reshape(seq_count, part_rows, HD)

    def whole_heads(array_in):
        shaped = array_in.reshape(rows_here, heads_here, HD).transpose(1, 0, 2)
        shaped = jnp.broadcast_to(shaped[:, None], (heads_here, share_count, rows_here, HD))
        return shaped.reshape(seq_count, rows_here, HD)

    def from_heads(array_in):
        shaped = array_in.reshape(heads_here, share_count, part_rows, HD).transpose(1, 2, 0, 3)
        return shaped.reshape(rows_here, heads_here * HD)

    text_keys = lax.dynamic_slice_in_dim(k_txt, head_index * HD, HD, 1)
    text_values = lax.dynamic_slice_in_dim(v_txt, head_index * HD, HD, 1)
    query_side = jnp.concatenate([to_heads(q_img), to_heads(attn_grad)], axis=2)
    key_side = jnp.concatenate([whole_heads(k_img), whole_heads(v_img)], axis=2)
    packed = jnp.concatenate([query_side, key_side], axis=1)
    received = lax.all_to_all(packed, "seq", split_axis=0, concat_axis=0, tiled=True)
    queries = received[:, :part_rows, :HD].reshape(seq_count * part_rows, HD)
    cotangents = received[:, :part_rows, HD:].reshape(seq_count * part_rows, HD)
    image_keys = received[:, part_rows:, :HD].reshape(seq_count * rows_here, HD)
    image_values = received[:, part_rows:, HD:].reshape(seq_count * rows_here, HD)
    key_rows = jnp.concatenate([image_keys, text_keys], axis=0)
    value_rows = jnp.concatenate([image_values, text_values], axis=0)
    query_grad, out_rows, key_grad, value_grad = attend(
        queries, cotangents, key_rows, value_rows, min(512, queries.shape[0])
    )
    image_count = image_keys.shape[0]
    query_part = (
        jnp.concatenate([query_grad, out_rows], axis=1)
        .astype(jnp.float32)
        .reshape(seq_count, part_rows, 2 * HD)
    )
    key_part = jnp.concatenate([key_grad[:image_count], value_grad[:image_count]], axis=1).reshape(
        seq_count, rows_here, 2 * HD
    )
    returned = lax.all_to_all(
        jnp.concatenate([query_part, key_part], axis=1).astype(jnp.bfloat16),
        "seq",
        split_axis=0,
        concat_axis=0,
        tiled=True,
    ).astype(jnp.float32)
    q_grad = from_heads(returned[:, :part_rows, :HD]).astype(jnp.bfloat16)
    out_tok = from_heads(returned[:, :part_rows, HD:]).astype(jnp.bfloat16)
    summed = jnp.sum(
        returned[:, part_rows:, :].reshape(heads_here, share_count, rows_here, 2 * HD), axis=1
    )
    summed = summed.transpose(1, 0, 2)
    k_grad = summed[:, :, :HD].reshape(rows_here, heads_here * HD).astype(jnp.bfloat16)
    v_grad = summed[:, :, HD:].reshape(rows_here, heads_here * HD).astype(jnp.bfloat16)
    column_cut = d_out
    d_weight = lax.psum_scatter(
        jnp.dot(column_cut.T, out_tok, preferred_element_type=jnp.float32).astype(jnp.bfloat16),
        "seq",
        scatter_dimension=0,
        tiled=True,
    ).astype(jnp.float32)
    return (q_grad, k_grad, v_grad, d_weight)


def call(kernel, outs, args, specs=None, scratch=(), scalars=0, out_specs=None, flops=0, moved=0, limit=LIMIT):
    vmem = pl.BlockSpec(memory_space=pltpu.VMEM)
    if specs is None:
        specs = [vmem] * (len(args) - scalars)
    if out_specs is None:
        out_specs = [vmem] * len(outs)
    return pl.pallas_call(
        kernel,
        out_shape=outs,
        grid_spec=pltpu.PrefetchScalarGridSpec(
            num_scalar_prefetch=scalars,
            grid=(1,),
            in_specs=specs,
            out_specs=out_specs,
            scratch_shapes=list(scratch),
        ),
        compiler_params=pltpu.CompilerParams(vmem_limit_bytes=limit),
        cost_estimate=pl.CostEstimate(flops=flops, bytes_accessed=moved, transcendentals=0),
    )(*args)


STEPS = (0, 2, 4, 6)


def head_columns(step, other_row):
    return pl.ds(pl.multiple_of(jnp.bitwise_xor(lax.axis_index("seq"), step + other_row) * HD, HD), HD)


def pack_kernel(q_ref, k_ref, v_ref, tok_ref):
    rows = q_ref.shape[0]
    for h in range(tok_ref.shape[0]):
        for i, ref in enumerate((q_ref, k_ref, v_ref)):
            tok_ref[h, i * rows : (i + 1) * rows, :] = ref[:, h * HD : (h + 1) * HD]


def pack_weight_kernel(me_ref, w_ref, kt_ref, vt_ref, keep_ref, give_ref, text_ref):
    for i, step in enumerate(STEPS):
        cols = slice(i * HD, (i + 1) * HD)
        keep_ref[:, cols] = w_ref[:, head_columns(step, 0)]
        give_ref[:, cols] = w_ref[:, head_columns(step, 1)]
    text_ref[0] = kt_ref[...]
    text_ref[1] = vt_ref[...]


def forward_kernel(tok_ref, text_ref, probs_ref, out_ref, queries_ref, keys_t_ref, vals_ref, keys, vals_t, *, chunk):
    n, three, _ = tok_ref.shape
    rows = three // 3
    image = n * rows
    text = text_ref.shape[1]
    queries_ref[...] = tok_ref[:, 0:rows, :].reshape(image, HD)
    keys[0:image, :] = tok_ref[:, rows : 2 * rows, :].reshape(image, HD)
    keys[image : image + text, :] = text_ref[0]
    vals_ref[0:image, :] = tok_ref[:, 2 * rows : 3 * rows, :].reshape(image, HD)
    vals_ref[image : image + text, :] = text_ref[1]
    keys_t_ref[...] = keys[...].T
    vals_t[...] = vals_ref[...].T
    factor = HD ** (-0.5) * math.log2(math.e)
    for c in range(image // chunk):
        span = slice(c * chunk, (c + 1) * chunk)
        scores = lax.dot_general(keys[...], queries_ref[span, :], NT, preferred_element_type=F32)
        top = jnp.max(scores, axis=0, keepdims=True)
        weights = jnp.exp2((scores - top) * factor)
        total = jnp.sum(weights, axis=0, keepdims=True)
        low = (weights * (1.0 / total)).astype(BF16)
        probs_ref[:, span] = low
        out_ref[:, span] = jnp.dot(vals_t[...], low, preferred_element_type=F32).astype(BF16)


def partial_kernel(*refs):
    *pieces, own_ref, other_ref, mine_ref, far_ref, near_ref, near_far_ref, cot_ref, weight = refs
    me = lax.axis_index("seq")
    core = lax.axis_index("fsdp")
    count = len(STEPS)
    part = pieces[0].shape[0] // count
    for p, piece in enumerate(pieces):
        row, swapped = p % 2, p // 2
        shift = jnp.bitwise_xor(core, swapped) * part
        for i, step in enumerate(STEPS):
            at = pl.multiple_of(jnp.bitwise_xor(me, step + row) * (2 * part) + shift, 16)
            cot_ref[pl.ds(at, part), :] = piece[i * part : (i + 1) * part, :]
    depth = own_ref.shape[0]
    y = lax.rem(me, 2)
    weight[pl.ds(pl.multiple_of(y * depth, 16), depth), :] = own_ref[...]
    weight[pl.ds(pl.multiple_of((1 - y) * depth, 16), depth), :] = other_ref[...]
    step = 256

    @pl.loop(0, cot_ref.shape[0] // step)
    def _(i):
        at = pl.ds(pl.multiple_of(i * step, step), step)
        part = jnp.dot(cot_ref[at, :], weight[...], preferred_element_type=F32)
        mine_ref[at, :] = part[:, :HD]
        near_ref[at, :] = part[:, HD : 2 * HD].astype(BF16)
        far_ref[at, :] = part[:, 2 * HD : 3 * HD]
        near_far_ref[at, :] = part[:, 3 * HD :].astype(BF16)


def weight_grad_kernel(cot_ref, *refs):
    *out_refs, own_ref, other_ref, outs = refs
    first = 0
    for ref in out_refs:
        outs[first : first + ref.shape[0], :] = ref[...]
        first += ref.shape[0]
    depth = own_ref.shape[1]
    y = lax.rem(lax.axis_index("seq"), 2)
    for ref, row in ((own_ref, y), (other_ref, 1 - y)):
        at = pl.multiple_of(row * depth, HD)
        ref[...] = jnp.dot(outs[...], cot_ref[:, pl.ds(at, depth)], preferred_element_type=F32).astype(BF16)


def backward_kernel(
    queries_ref, keys_t_ref, vals_ref, probs_ref, out_ref, mine_ref, near_ref, far_ref, send_ref, dk, dv, *, chunk
):
    n, three, _ = send_ref.shape
    rows = three // 3
    image = n * rows
    scale = HD ** (-0.5)
    per = chunk // rows
    for c in range(image // chunk):
        span = slice(c * chunk, (c + 1) * chunk)
        grads = mine_ref[span, :] + near_ref[span, :].astype(F32) + far_ref[span, :].astype(F32)
        grads = grads.astype(BF16)
        row_dot = jnp.sum(
            grads.astype(F32).T * out_ref[:, span].astype(F32), axis=0, keepdims=True
        )
        prob_grad = lax.dot_general(vals_ref[...], grads, NT, preferred_element_type=F32)
        low = probs_ref[:, span]
        score_grad = (low.astype(F32) * (prob_grad - row_dot)).astype(BF16)
        dq_t = jnp.dot(keys_t_ref[...], score_grad, preferred_element_type=F32) * scale
        send_ref[c * per : (c + 1) * per, 0:rows, :] = dq_t.T.astype(BF16).reshape(per, rows, HD)
        dk_part = jnp.dot(score_grad[0:image, :], queries_ref[span, :], preferred_element_type=F32)
        dv_part = jnp.dot(low[0:image, :], grads, preferred_element_type=F32)
        if c == 0:
            dk[...] = dk_part
            dv[...] = dv_part
        else:
            dk[...] += dk_part
            dv[...] += dv_part
    send_ref[:, rows : 2 * rows, :] = (dk[...] * scale).astype(BF16).reshape(n, rows, HD)
    send_ref[:, 2 * rows : 3 * rows, :] = dv[...].astype(BF16).reshape(n, rows, HD)


def unpack_kernel(tok_ref, q_ref, k_ref, v_ref):
    rows = q_ref.shape[0]
    for h in range(tok_ref.shape[0]):
        for i, ref in enumerate((q_ref, k_ref, v_ref)):
            ref[:, h * HD : (h + 1) * HD] = tok_ref[h, i * rows : (i + 1) * rows, :]


def unpack_weight_kernel(own_ref, other_ref, w_ref):
    for other_row, ref in enumerate((own_ref, other_ref)):
        for i, step in enumerate(STEPS):
            w_ref[:, head_columns(step, other_row)] = ref[i * HD : (i + 1) * HD, :].astype(F32).T


def exchange(array, distance=0, cores=False):
    if not distance and not cores:
        return array
    size = 2 * lax.axis_size("seq")
    pairs = [(i, i ^ (2 * distance + int(cores))) for i in range(size)]
    return lax.ppermute(array, ("seq", "fsdp"), pairs)


def send_cotangents(d_out):
    rows, width = d_out.shape
    part, columns = rows // 2, width // len(STEPS)
    z = lax.axis_index("seq") // 2
    first = lax.axis_index("fsdp") * part
    return [
        exchange(lax.dynamic_slice(d_out, (first, (z ^ (step // 2)) * columns), (part, columns)), step)
        for step in STEPS
    ]


def gather_cotangents(along):
    row = jnp.concatenate(along, axis=0)
    pieces = [row, exchange(row, 1)]
    return pieces + [exchange(piece, cores=True) for piece in pieces]


def local(q_img, k_img, v_img, k_txt, v_txt, out_weight, d_out):
    n = lax.axis_size("seq")
    rows, width = q_img.shape
    args = (q_img, k_img, v_img, k_txt, v_txt, out_weight, d_out)
    if n != 2 * len(STEPS) or width // HD != n or lax.axis_size("fsdp") != 2 or rows % 32:
        return local_general(*args)
    depth = out_weight.shape[0]
    image = n * rows
    text = k_txt.shape[0]
    total = image + text
    chunk = 2 * rows
    shape = jax.ShapeDtypeStruct
    vmem = pl.BlockSpec(memory_space=pltpu.VMEM)

    head = pl.BlockSpec((text, HD), lambda i, me_ref: (0, me_ref[0]))
    big = 60 * 1024 * 1024
    keep, give, text_head = call(
        pack_weight_kernel,
        [shape((depth, 4 * HD), BF16)] * 2 + [shape((2, text, HD), BF16)],
        [lax.axis_index("seq").astype(jnp.int32)[None], out_weight, k_txt, v_txt],
        specs=[vmem] + [head] * 2,
        scalars=1,
        moved=4 * depth * width,
        limit=big,
    )
    d_out, give = lax.optimization_barrier((d_out, give))
    given = exchange(give, 1)
    along = send_cotangents(d_out)
    (tok_out,) = call(
        pack_kernel,
        [shape((n, 3 * rows, HD), BF16)],
        [q_img, k_img, v_img],
        moved=4 * 3 * rows * width,
        limit=big,
    )
    tok_out, along[1] = lax.optimization_barrier((tok_out, along[1]))
    along, given = lax.optimization_barrier((along, given))
    pieces = gather_cotangents(along)
    tok_in = lax.all_to_all(tok_out, "seq", split_axis=0, concat_axis=0, tiled=True)

    probs, out_t, queries, keys_t, vals = call(
        functools.partial(forward_kernel, chunk=chunk),
        [shape(dims, BF16) for dims in ((total, image), (HD, image), (image, HD), (HD, total), (total, HD))],
        [tok_in, text_head],
        scratch=[pltpu.VMEM((total, HD), BF16), pltpu.VMEM((HD, total), BF16)],
        flops=4 * total * image * HD,
        moved=4 * total * image,
    )
    columns = pieces[0].shape[1]
    mine, far, near, near_far, cot = call(
        partial_kernel,
        [shape((image, HD), F32)] * 2 + [shape((image, HD), BF16)] * 2 + [shape((image, columns), BF16)],
        [*pieces, keep, given],
        scratch=[pltpu.VMEM((columns, 4 * HD), BF16)],
        flops=8 * image * columns * HD,
        moved=2 * image * columns,
    )
    near_far = exchange(near_far, 2)
    near_far, out_t, near = lax.optimization_barrier((near_far, out_t, near))
    far = exchange((far + near_far.astype(F32)).astype(BF16), 4)
    near = exchange(near, 2)
    out_late, far, near = lax.optimization_barrier((out_t, far, near))
    out_near, out_far = exchange(out_late, 2), exchange(out_late, 4)
    (grad_out,) = call(
        functools.partial(backward_kernel, chunk=chunk),
        [shape((n, 3 * rows, HD), BF16)],
        [queries, keys_t, vals, probs, out_t, mine, near, far],
        scratch=[pltpu.VMEM((image, HD), F32), pltpu.VMEM((image, HD), F32)],
        flops=8 * total * image * HD,
        moved=4 * total * image,
    )
    grad_in = lax.all_to_all(grad_out, "seq", split_axis=0, concat_axis=0, tiled=True)
    out_far, out_near, _ = lax.optimization_barrier((out_far, out_near, grad_out))
    outs = [out_t, out_near, out_far, exchange(out_far, 2)]
    dw_own, dw_other = call(
        weight_grad_kernel,
        [shape((4 * HD, depth), BF16)] * 2,
        [cot, *outs],
        scratch=[pltpu.VMEM((4 * HD, image), BF16)],
        flops=96 * image * columns * HD,
        moved=2 * image * columns,
    )
    grads = call(
        unpack_kernel,
        [shape((rows, width), BF16)] * 3,
        [grad_in],
        moved=4 * 3 * rows * width,
    )
    (d_weight,) = call(
        unpack_weight_kernel,
        [shape((depth, width), F32)],
        [dw_own, exchange(dw_other, 1)],
        moved=6 * depth * width,
    )
    return (*grads, d_weight)


def solution(mesh):
    in_specs = (
        P(("group", "seq"), "fsdp"),
        P(("group", "seq"), "fsdp"),
        P(("group", "seq"), "fsdp"),
        P("group", "fsdp"),
        P("group", "fsdp"),
        P("seq", "fsdp"),
        P(("group", "seq"), None),
    )
    out_specs = (
        P(("group", "seq"), "fsdp"),
        P(("group", "seq"), "fsdp"),
        P(("group", "seq"), "fsdp"),
        P(("group", "seq"), "fsdp"),
    )
    return jax.shard_map(local, mesh=mesh, in_specs=in_specs, out_specs=out_specs, check_vma=False)
```

```python
import functools
import math

import jax
import jax.numpy as jnp
from jax import lax
from jax.experimental import pallas as pl
from jax.experimental.pallas import tpu as pltpu
from jax.sharding import PartitionSpec as P

HD = 128
F32 = jnp.float32
BF16 = jnp.bfloat16
LIMIT = 16 * 1024 * 1024
NT = (((1,), (1,)), ((), ()))


def attend(queries, cotangents, key_rows, value_rows, block_rows):
    score_scale = HD ** (-0.5)
    query_count = queries.shape[0]
    block_count = query_count // block_rows
    query_blocks = queries.reshape(block_count, block_rows, HD)
    grad_blocks = cotangents.reshape(block_count, block_rows, HD)

    def one_block(accumulated, pair_item):
        query_block, grad_block = pair_item
        scores = jnp.dot(query_block, key_rows.T, preferred_element_type=jnp.float32) * score_scale
        row_max = jnp.max(scores, axis=1, keepdims=True)
        probs = jnp.exp(scores - row_max)
        probs = probs / jnp.sum(probs, axis=1, keepdims=True)
        probs_low = probs.astype(jnp.bfloat16)
        out_rows = jnp.dot(probs_low, value_rows, preferred_element_type=jnp.float32).astype(
            jnp.bfloat16
        )
        prob_grad = jnp.dot(grad_block, value_rows.T, preferred_element_type=jnp.float32)
        row_dot = jnp.sum(
            grad_block.astype(jnp.float32) * out_rows.astype(jnp.float32), axis=1, keepdims=True
        )
        score_grad = (probs * (prob_grad - row_dot)).astype(jnp.bfloat16)
        query_grad = (
            jnp.dot(score_grad, key_rows, preferred_element_type=jnp.float32) * score_scale
        ).astype(jnp.bfloat16)
        key_grad = (
            accumulated[0]
            + jnp.dot(score_grad.T, query_block, preferred_element_type=jnp.float32) * score_scale
        )
        value_grad = accumulated[1] + jnp.dot(
            probs_low.T, grad_block, preferred_element_type=jnp.float32
        )
        return ((key_grad, value_grad), (query_grad, out_rows))

    empty = jnp.zeros((key_rows.shape[0], HD), jnp.float32)
    (key_grad, value_grad), (query_grad, out_rows) = lax.scan(
        one_block, (empty, empty), (query_blocks, grad_blocks)
    )
    return (
        query_grad.reshape(query_count, HD),
        out_rows.reshape(query_count, HD),
        key_grad,
        value_grad,
    )


def local_general(q_img, k_img, v_img, k_txt, v_txt, out_weight, d_out):
    rows_here = q_img.shape[0]
    heads_here = q_img.shape[1] // HD
    seq_count = lax.axis_size("seq")
    share_count = seq_count // heads_here
    part_rows = rows_here // share_count
    seq_index = lax.axis_index("seq")
    head_index = seq_index // share_count
    column_cut = d_out
    attn_grad = jnp.dot(
        column_cut,
        lax.all_gather(out_weight, "seq", axis=0, tiled=True),
        preferred_element_type=jnp.float32,
    ).astype(jnp.bfloat16)

    def to_heads(array_in):
        shaped = array_in.reshape(share_count, part_rows, heads_here, HD).transpose(2, 0, 1, 3)
        return shaped.reshape(seq_count, part_rows, HD)

    def whole_heads(array_in):
        shaped = array_in.reshape(rows_here, heads_here, HD).transpose(1, 0, 2)
        shaped = jnp.broadcast_to(shaped[:, None], (heads_here, share_count, rows_here, HD))
        return shaped.reshape(seq_count, rows_here, HD)

    def from_heads(array_in):
        shaped = array_in.reshape(heads_here, share_count, part_rows, HD).transpose(1, 2, 0, 3)
        return shaped.reshape(rows_here, heads_here * HD)

    text_keys = lax.dynamic_slice_in_dim(k_txt, head_index * HD, HD, 1)
    text_values = lax.dynamic_slice_in_dim(v_txt, head_index * HD, HD, 1)
    query_side = jnp.concatenate([to_heads(q_img), to_heads(attn_grad)], axis=2)
    key_side = jnp.concatenate([whole_heads(k_img), whole_heads(v_img)], axis=2)
    packed = jnp.concatenate([query_side, key_side], axis=1)
    received = lax.all_to_all(packed, "seq", split_axis=0, concat_axis=0, tiled=True)
    queries = received[:, :part_rows, :HD].reshape(seq_count * part_rows, HD)
    cotangents = received[:, :part_rows, HD:].reshape(seq_count * part_rows, HD)
    image_keys = received[:, part_rows:, :HD].reshape(seq_count * rows_here, HD)
    image_values = received[:, part_rows:, HD:].reshape(seq_count * rows_here, HD)
    key_rows = jnp.concatenate([image_keys, text_keys], axis=0)
    value_rows = jnp.concatenate([image_values, text_values], axis=0)
    query_grad, out_rows, key_grad, value_grad = attend(
        queries, cotangents, key_rows, value_rows, min(512, queries.shape[0])
    )
    image_count = image_keys.shape[0]
    query_part = (
        jnp.concatenate([query_grad, out_rows], axis=1)
        .astype(jnp.float32)
        .reshape(seq_count, part_rows, 2 * HD)
    )
    key_part = jnp.concatenate([key_grad[:image_count], value_grad[:image_count]], axis=1).reshape(
        seq_count, rows_here, 2 * HD
    )
    returned = lax.all_to_all(
        jnp.concatenate([query_part, key_part], axis=1).astype(jnp.bfloat16),
        "seq",
        split_axis=0,
        concat_axis=0,
        tiled=True,
    ).astype(jnp.float32)
    q_grad = from_heads(returned[:, :part_rows, :HD]).astype(jnp.bfloat16)
    out_tok = from_heads(returned[:, :part_rows, HD:]).astype(jnp.bfloat16)
    summed = jnp.sum(
        returned[:, part_rows:, :].reshape(heads_here, share_count, rows_here, 2 * HD), axis=1
    )
    summed = summed.transpose(1, 0, 2)
    k_grad = summed[:, :, :HD].reshape(rows_here, heads_here * HD).astype(jnp.bfloat16)
    v_grad = summed[:, :, HD:].reshape(rows_here, heads_here * HD).astype(jnp.bfloat16)
    column_cut = d_out
    d_weight = lax.psum_scatter(
        jnp.dot(column_cut.T, out_tok, preferred_element_type=jnp.float32).astype(jnp.bfloat16),
        "seq",
        scatter_dimension=0,
        tiled=True,
    ).astype(jnp.float32)
    return (q_grad, k_grad, v_grad, d_weight)


def call(kernel, outs, args, specs=None, scratch=(), scalars=0, out_specs=None, flops=0, moved=0, limit=LIMIT):
    vmem = pl.BlockSpec(memory_space=pltpu.VMEM)
    if specs is None:
        specs = [vmem] * (len(args) - scalars)
    if out_specs is None:
        out_specs = [vmem] * len(outs)
    return pl.pallas_call(
        kernel,
        out_shape=outs,
        grid_spec=pltpu.PrefetchScalarGridSpec(
            num_scalar_prefetch=scalars,
            grid=(1,),
            in_specs=specs,
            out_specs=out_specs,
            scratch_shapes=list(scratch),
        ),
        compiler_params=pltpu.CompilerParams(vmem_limit_bytes=limit),
        cost_estimate=pl.CostEstimate(flops=flops, bytes_accessed=moved, transcendentals=0),
    )(*args)


STEPS = (0, 2, 4, 6)


def head_columns(step, other_row):
    return pl.ds(pl.multiple_of(jnp.bitwise_xor(lax.axis_index("seq"), step + other_row) * HD, HD), HD)


def pack_kernel(q_ref, k_ref, v_ref, tok_ref):
    rows = q_ref.shape[0]
    for h in range(tok_ref.shape[0]):
        for i, ref in enumerate((q_ref, k_ref, v_ref)):
            tok_ref[h, i * rows : (i + 1) * rows, :] = ref[:, h * HD : (h + 1) * HD]


def pack_weight_kernel(me_ref, w_ref, kt_ref, vt_ref, keep_ref, give_ref, text_ref):
    for i, step in enumerate(STEPS):
        cols = slice(i * HD, (i + 1) * HD)
        keep_ref[:, cols] = w_ref[:, head_columns(step, 0)]
        give_ref[:, cols] = w_ref[:, head_columns(step, 1)]
    text_ref[0] = kt_ref[...]
    text_ref[1] = vt_ref[...]


def forward_kernel(tok_ref, text_ref, probs_ref, out_ref, queries_ref, keys_t_ref, vals_ref, keys, vals_t, *, chunk):
    n, three, _ = tok_ref.shape
    rows = three // 3
    image = n * rows
    text = text_ref.shape[1]
    queries_ref[...] = tok_ref[:, 0:rows, :].reshape(image, HD)
    keys[0:image, :] = tok_ref[:, rows : 2 * rows, :].reshape(image, HD)
    keys[image : image + text, :] = text_ref[0]
    vals_ref[0:image, :] = tok_ref[:, 2 * rows : 3 * rows, :].reshape(image, HD)
    vals_ref[image : image + text, :] = text_ref[1]
    keys_t_ref[...] = keys[...].T
    vals_t[...] = vals_ref[...].T
    factor = HD ** (-0.5) * math.log2(math.e)
    for c in range(image // chunk):
        span = slice(c * chunk, (c + 1) * chunk)
        scores = lax.dot_general(keys[...], queries_ref[span, :], NT, preferred_element_type=F32)
        top = jnp.max(scores, axis=0, keepdims=True)
        weights = jnp.exp2((scores - top) * factor)
        total = jnp.sum(weights, axis=0, keepdims=True)
        low = (weights * (1.0 / total)).astype(BF16)
        probs_ref[:, span] = low
        out_ref[:, span] = jnp.dot(vals_t[...], low, preferred_element_type=F32).astype(BF16)


def partial_kernel(*refs, kinds):
    *pieces, own_ref, other_ref, mine_ref, far0_ref, far1_ref, near_ref, send0_ref, send1_ref, cot_ref, weight = refs
    me = lax.axis_index("seq")
    core = lax.axis_index("fsdp")
    part = pieces[0].shape[0]
    for piece, (first, row, swapped) in zip(pieces, kinds):
        shift = jnp.bitwise_xor(core, swapped) * part
        for i in range(piece.shape[0] // part):
            at = pl.multiple_of(jnp.bitwise_xor(me, STEPS[first + i] + row) * (2 * part) + shift, 16)
            cot_ref[pl.ds(at, part), :] = piece[i * part : (i + 1) * part, :]
    depth = own_ref.shape[0]
    y = lax.rem(me, 2)
    weight[pl.ds(pl.multiple_of(y * depth, 16), depth), :] = own_ref[...]
    weight[pl.ds(pl.multiple_of((1 - y) * depth, 16), depth), :] = other_ref[...]
    step = 256
    half = far0_ref.shape[0] // step
    for h, (far_ref, send_ref) in enumerate(((far0_ref, send0_ref), (far1_ref, send1_ref))):

        @pl.loop(0, half)
        def _(i):
            at = pl.ds(pl.multiple_of((h * half + i) * step, step), step)
            within = pl.ds(pl.multiple_of(i * step, step), step)
            part = jnp.dot(cot_ref[at, :], weight[...], preferred_element_type=F32)
            mine_ref[at, :] = part[:, :HD]
            near_ref[at, :] = part[:, HD : 2 * HD].astype(BF16)
            far_ref[within, :] = part[:, 2 * HD : 3 * HD]
            send_ref[within, :] = part[:, 3 * HD :].astype(BF16)


def weight_grad_kernel(cot_ref, *refs):
    *out_refs, own_ref, other_ref, outs = refs
    first = 0
    for ref in out_refs:
        outs[first : first + ref.shape[0], :] = ref[...]
        first += ref.shape[0]
    depth = own_ref.shape[1]
    y = lax.rem(lax.axis_index("seq"), 2)
    for ref, row in ((own_ref, y), (other_ref, 1 - y)):
        at = pl.multiple_of(row * depth, HD)
        ref[...] = jnp.dot(outs[...], cot_ref[:, pl.ds(at, depth)], preferred_element_type=F32).astype(BF16)


def backward_kernel(
    queries_ref, keys_t_ref, vals_ref, probs_ref, out_ref, mine_ref, near_ref, far0_ref, far1_ref, send_ref, dk, dv, *, chunk
):
    n, three, _ = send_ref.shape
    rows = three // 3
    image = n * rows
    scale = HD ** (-0.5)
    per = chunk // rows
    for c in range(image // chunk):
        span = slice(c * chunk, (c + 1) * chunk)
        far_ref, within = (far0_ref, c) if 2 * c * chunk < image else (far1_ref, c - image // chunk // 2)
        far = far_ref[within * chunk : (within + 1) * chunk, :].astype(F32)
        grads = mine_ref[span, :] + near_ref[span, :].astype(F32) + far
        grads = grads.astype(BF16)
        row_dot = jnp.sum(
            grads.astype(F32).T * out_ref[:, span].astype(F32), axis=0, keepdims=True
        )
        prob_grad = lax.dot_general(vals_ref[...], grads, NT, preferred_element_type=F32)
        low = probs_ref[:, span]
        score_grad = (low.astype(F32) * (prob_grad - row_dot)).astype(BF16)
        dq_t = jnp.dot(keys_t_ref[...], score_grad, preferred_element_type=F32) * scale
        send_ref[c * per : (c + 1) * per, 0:rows, :] = dq_t.T.astype(BF16).reshape(per, rows, HD)
        dk_part = jnp.dot(score_grad[0:image, :], queries_ref[span, :], preferred_element_type=F32)
        dv_part = jnp.dot(low[0:image, :], grads, preferred_element_type=F32)
        if c == 0:
            dk[...] = dk_part
            dv[...] = dv_part
        else:
            dk[...] += dk_part
            dv[...] += dv_part
    send_ref[:, rows : 2 * rows, :] = (dk[...] * scale).astype(BF16).reshape(n, rows, HD)
    send_ref[:, 2 * rows : 3 * rows, :] = dv[...].astype(BF16).reshape(n, rows, HD)


def unpack_kernel(tok_ref, q_ref, k_ref, v_ref):
    rows = q_ref.shape[0]
    for h in range(tok_ref.shape[0]):
        for i, ref in enumerate((q_ref, k_ref, v_ref)):
            ref[:, h * HD : (h + 1) * HD] = tok_ref[h, i * rows : (i + 1) * rows, :]


def unpack_weight_kernel(own_ref, other_ref, w_ref):
    for other_row, ref in enumerate((own_ref, other_ref)):
        for i, step in enumerate(STEPS):
            w_ref[:, head_columns(step, other_row)] = ref[i * HD : (i + 1) * HD, :].astype(F32).T


def exchange(array, distance=0, cores=False):
    if not distance and not cores:
        return array
    size = 2 * lax.axis_size("seq")
    pairs = [(i, i ^ (2 * distance + int(cores))) for i in range(size)]
    return lax.ppermute(array, ("seq", "fsdp"), pairs)


def send_cotangents(d_out):
    rows, width = d_out.shape
    part, columns = rows // 2, width // len(STEPS)
    z = lax.axis_index("seq") // 2
    first = lax.axis_index("fsdp") * part
    along = [
        exchange(lax.dynamic_slice(d_out, (first, (z ^ (step // 2)) * columns), (part, columns)), step)
        for step in STEPS
    ]
    return along, lax.dynamic_slice(d_out, (part - first, z * columns), (part, columns))


def gather_cotangents(own, own_swapped, own_y, rest):
    rest = jnp.concatenate(rest, axis=0)
    rest_y = exchange(rest, 1)
    swapped = [exchange(piece, cores=True) for piece in (own_y, rest, rest_y)]
    pieces = [own, own_swapped, own_y, rest, rest_y, *swapped]
    return pieces, [(0, 0, 0), (0, 0, 1), (0, 1, 0), (1, 0, 0), (1, 1, 0), (0, 1, 1), (1, 0, 1), (1, 1, 1)]


def local(q_img, k_img, v_img, k_txt, v_txt, out_weight, d_out):
    n = lax.axis_size("seq")
    rows, width = q_img.shape
    args = (q_img, k_img, v_img, k_txt, v_txt, out_weight, d_out)
    if n != 2 * len(STEPS) or width // HD != n or lax.axis_size("fsdp") != 2 or rows % 32:
        return local_general(*args)
    depth = out_weight.shape[0]
    image = n * rows
    text = k_txt.shape[0]
    total = image + text
    chunk = 2 * rows
    shape = jax.ShapeDtypeStruct
    vmem = pl.BlockSpec(memory_space=pltpu.VMEM)

    head = pl.BlockSpec((text, HD), lambda i, me_ref: (0, me_ref[0]))
    big = 60 * 1024 * 1024
    keep, give, text_head = call(
        pack_weight_kernel,
        [shape((depth, 4 * HD), BF16)] * 2 + [shape((2, text, HD), BF16)],
        [lax.axis_index("seq").astype(jnp.int32)[None], out_weight, k_txt, v_txt],
        specs=[vmem] + [head] * 2,
        scalars=1,
        moved=4 * depth * width,
        limit=big,
    )
    d_out, give = lax.optimization_barrier((d_out, give))
    given = exchange(give, 1)
    (own, *rest), own_swapped = send_cotangents(d_out)
    own_y = exchange(own, 1)
    (tok_out,) = call(
        pack_kernel,
        [shape((n, 3 * rows, HD), BF16)],
        [q_img, k_img, v_img],
        moved=4 * 3 * rows * width,
        limit=big,
    )
    tok_out, rest[0] = lax.optimization_barrier((tok_out, rest[0]))
    rest, given = lax.optimization_barrier((rest, given))
    pieces, kinds = gather_cotangents(own, own_swapped, own_y, rest)
    tok_in = lax.all_to_all(tok_out, "seq", split_axis=0, concat_axis=0, tiled=True)

    probs, out_t, queries, keys_t, vals = call(
        functools.partial(forward_kernel, chunk=chunk),
        [shape(dims, BF16) for dims in ((total, image), (HD, image), (image, HD), (HD, total), (total, HD))],
        [tok_in, text_head],
        scratch=[pltpu.VMEM((total, HD), BF16), pltpu.VMEM((HD, total), BF16)],
        flops=4 * total * image * HD,
        moved=4 * total * image,
    )
    columns = pieces[0].shape[1]
    mine, *far, near, send0, send1, cot = call(
        functools.partial(partial_kernel, kinds=kinds),
        [shape((image, HD), F32)]
        + [shape((image // 2, HD), F32)] * 2
        + [shape((image, HD), BF16)]
        + [shape((image // 2, HD), BF16)] * 2
        + [shape((image, columns), BF16)],
        [*pieces, keep, given],
        scratch=[pltpu.VMEM((columns, 4 * HD), BF16)],
        flops=8 * image * columns * HD,
        moved=2 * image * columns,
    )
    near_far = [exchange(send0, 2), exchange(send1, 2)]
    near_far, out_t, near = lax.optimization_barrier((near_far, out_t, near))
    far = [exchange((f + r.astype(F32)).astype(BF16), 4) for f, r in zip(far, near_far)]
    near = exchange(near, 2)
    out_late, far, near = lax.optimization_barrier((out_t, far, near))
    out_near, out_far = exchange(out_late, 2), exchange(out_late, 4)
    (grad_out,) = call(
        functools.partial(backward_kernel, chunk=chunk),
        [shape((n, 3 * rows, HD), BF16)],
        [queries, keys_t, vals, probs, out_t, mine, near, *far],
        scratch=[pltpu.VMEM((image, HD), F32), pltpu.VMEM((image, HD), F32)],
        flops=8 * total * image * HD,
        moved=4 * total * image,
    )
    grad_in = lax.all_to_all(grad_out, "seq", split_axis=0, concat_axis=0, tiled=True)
    out_far, out_near, _ = lax.optimization_barrier((out_far, out_near, grad_out))
    outs = [out_t, out_near, out_far, exchange(out_far, 2)]
    dw_own, dw_other = call(
        weight_grad_kernel,
        [shape((4 * HD, depth), BF16)] * 2,
        [cot, *outs],
        scratch=[pltpu.VMEM((4 * HD, image), BF16)],
        flops=40 * image * columns * HD,
        moved=2 * image * columns,
    )
    grads = call(
        unpack_kernel,
        [shape((rows, width), BF16)] * 3,
        [grad_in],
        moved=4 * 3 * rows * width,
    )
    (d_weight,) = call(
        unpack_weight_kernel,
        [shape((depth, width), F32)],
        [dw_own, exchange(dw_other, 1)],
        moved=6 * depth * width,
    )
    return (*grads, d_weight)


def solution(mesh):
    in_specs = (
        P(("group", "seq"), "fsdp"),
        P(("group", "seq"), "fsdp"),
        P(("group", "seq"), "fsdp"),
        P("group", "fsdp"),
        P("group", "fsdp"),
        P("seq", "fsdp"),
        P(("group", "seq"), None),
    )
    out_specs = (
        P(("group", "seq"), "fsdp"),
        P(("group", "seq"), "fsdp"),
        P(("group", "seq"), "fsdp"),
        P(("group", "seq"), "fsdp"),
    )
    return jax.shard_map(local, mesh=mesh, in_specs=in_specs, out_specs=out_specs, check_vma=False)
```

```python
import functools
import math

import jax
import jax.numpy as jnp
from jax import lax
from jax.experimental import pallas as pl
from jax.experimental.pallas import tpu as pltpu
from jax.sharding import PartitionSpec as P

HD = 128
F32 = jnp.float32
BF16 = jnp.bfloat16
LIMIT = 28 * 1024 * 1024
NT = (((1,), (1,)), ((), ()))


def attend(queries, cotangents, key_rows, value_rows, block_rows):
    score_scale = HD ** (-0.5)
    query_count = queries.shape[0]
    block_count = query_count // block_rows
    query_blocks = queries.reshape(block_count, block_rows, HD)
    grad_blocks = cotangents.reshape(block_count, block_rows, HD)

    def one_block(accumulated, pair_item):
        query_block, grad_block = pair_item
        scores = jnp.dot(query_block, key_rows.T, preferred_element_type=jnp.float32) * score_scale
        row_max = jnp.max(scores, axis=1, keepdims=True)
        probs = jnp.exp(scores - row_max)
        probs = probs / jnp.sum(probs, axis=1, keepdims=True)
        probs_low = probs.astype(jnp.bfloat16)
        out_rows = jnp.dot(probs_low, value_rows, preferred_element_type=jnp.float32).astype(
            jnp.bfloat16
        )
        prob_grad = jnp.dot(grad_block, value_rows.T, preferred_element_type=jnp.float32)
        row_dot = jnp.sum(
            grad_block.astype(jnp.float32) * out_rows.astype(jnp.float32), axis=1, keepdims=True
        )
        score_grad = (probs * (prob_grad - row_dot)).astype(jnp.bfloat16)
        query_grad = (
            jnp.dot(score_grad, key_rows, preferred_element_type=jnp.float32) * score_scale
        ).astype(jnp.bfloat16)
        key_grad = (
            accumulated[0]
            + jnp.dot(score_grad.T, query_block, preferred_element_type=jnp.float32) * score_scale
        )
        value_grad = accumulated[1] + jnp.dot(
            probs_low.T, grad_block, preferred_element_type=jnp.float32
        )
        return ((key_grad, value_grad), (query_grad, out_rows))

    empty = jnp.zeros((key_rows.shape[0], HD), jnp.float32)
    (key_grad, value_grad), (query_grad, out_rows) = lax.scan(
        one_block, (empty, empty), (query_blocks, grad_blocks)
    )
    return (
        query_grad.reshape(query_count, HD),
        out_rows.reshape(query_count, HD),
        key_grad,
        value_grad,
    )


def local_general(q_img, k_img, v_img, k_txt, v_txt, out_weight, d_out):
    rows_here = q_img.shape[0]
    heads_here = q_img.shape[1] // HD
    seq_count = lax.axis_size("seq")
    share_count = seq_count // heads_here
    part_rows = rows_here // share_count
    seq_index = lax.axis_index("seq")
    head_index = seq_index // share_count
    column_cut = d_out
    attn_grad = jnp.dot(
        column_cut,
        lax.all_gather(out_weight, "seq", axis=0, tiled=True),
        preferred_element_type=jnp.float32,
    ).astype(jnp.bfloat16)

    def to_heads(array_in):
        shaped = array_in.reshape(share_count, part_rows, heads_here, HD).transpose(2, 0, 1, 3)
        return shaped.reshape(seq_count, part_rows, HD)

    def whole_heads(array_in):
        shaped = array_in.reshape(rows_here, heads_here, HD).transpose(1, 0, 2)
        shaped = jnp.broadcast_to(shaped[:, None], (heads_here, share_count, rows_here, HD))
        return shaped.reshape(seq_count, rows_here, HD)

    def from_heads(array_in):
        shaped = array_in.reshape(heads_here, share_count, part_rows, HD).transpose(1, 2, 0, 3)
        return shaped.reshape(rows_here, heads_here * HD)

    text_keys = lax.dynamic_slice_in_dim(k_txt, head_index * HD, HD, 1)
    text_values = lax.dynamic_slice_in_dim(v_txt, head_index * HD, HD, 1)
    query_side = jnp.concatenate([to_heads(q_img), to_heads(attn_grad)], axis=2)
    key_side = jnp.concatenate([whole_heads(k_img), whole_heads(v_img)], axis=2)
    packed = jnp.concatenate([query_side, key_side], axis=1)
    received = lax.all_to_all(packed, "seq", split_axis=0, concat_axis=0, tiled=True)
    queries = received[:, :part_rows, :HD].reshape(seq_count * part_rows, HD)
    cotangents = received[:, :part_rows, HD:].reshape(seq_count * part_rows, HD)
    image_keys = received[:, part_rows:, :HD].reshape(seq_count * rows_here, HD)
    image_values = received[:, part_rows:, HD:].reshape(seq_count * rows_here, HD)
    key_rows = jnp.concatenate([image_keys, text_keys], axis=0)
    value_rows = jnp.concatenate([image_values, text_values], axis=0)
    query_grad, out_rows, key_grad, value_grad = attend(
        queries, cotangents, key_rows, value_rows, min(512, queries.shape[0])
    )
    image_count = image_keys.shape[0]
    query_part = (
        jnp.concatenate([query_grad, out_rows], axis=1)
        .astype(jnp.float32)
        .reshape(seq_count, part_rows, 2 * HD)
    )
    key_part = jnp.concatenate([key_grad[:image_count], value_grad[:image_count]], axis=1).reshape(
        seq_count, rows_here, 2 * HD
    )
    returned = lax.all_to_all(
        jnp.concatenate([query_part, key_part], axis=1).astype(jnp.bfloat16),
        "seq",
        split_axis=0,
        concat_axis=0,
        tiled=True,
    ).astype(jnp.float32)
    q_grad = from_heads(returned[:, :part_rows, :HD]).astype(jnp.bfloat16)
    out_tok = from_heads(returned[:, :part_rows, HD:]).astype(jnp.bfloat16)
    summed = jnp.sum(
        returned[:, part_rows:, :].reshape(heads_here, share_count, rows_here, 2 * HD), axis=1
    )
    summed = summed.transpose(1, 0, 2)
    k_grad = summed[:, :, :HD].reshape(rows_here, heads_here * HD).astype(jnp.bfloat16)
    v_grad = summed[:, :, HD:].reshape(rows_here, heads_here * HD).astype(jnp.bfloat16)
    column_cut = d_out
    d_weight = lax.psum_scatter(
        jnp.dot(column_cut.T, out_tok, preferred_element_type=jnp.float32).astype(jnp.bfloat16),
        "seq",
        scatter_dimension=0,
        tiled=True,
    ).astype(jnp.float32)
    return (q_grad, k_grad, v_grad, d_weight)


def call(kernel, outs, args, specs=None, scratch=(), scalars=0, out_specs=None, flops=0, moved=0, limit=LIMIT):
    vmem = pl.BlockSpec(memory_space=pltpu.VMEM)
    if specs is None:
        specs = [vmem] * (len(args) - scalars)
    if out_specs is None:
        out_specs = [vmem] * len(outs)
    return pl.pallas_call(
        kernel,
        out_shape=outs,
        grid_spec=pltpu.PrefetchScalarGridSpec(
            num_scalar_prefetch=scalars,
            grid=(1,),
            in_specs=specs,
            out_specs=out_specs,
            scratch_shapes=list(scratch),
        ),
        compiler_params=pltpu.CompilerParams(vmem_limit_bytes=limit),
        cost_estimate=pl.CostEstimate(flops=flops, bytes_accessed=moved, transcendentals=0),
    )(*args)


STEPS = (0, 2, 4, 6)


def head_columns(step, other_row):
    return pl.ds(pl.multiple_of(jnp.bitwise_xor(lax.axis_index("seq"), step + other_row) * HD, HD), HD)


def pack_kernel(q_ref, k_ref, v_ref, tok_ref):
    rows = q_ref.shape[0]
    for h in range(tok_ref.shape[0]):
        for i, ref in enumerate((q_ref, k_ref, v_ref)):
            tok_ref[h, i * rows : (i + 1) * rows, :] = ref[:, h * HD : (h + 1) * HD]


def pack_weight_kernel(me_ref, w_ref, kt_ref, vt_ref, keep_ref, give_ref, text_ref):
    for i, step in enumerate(STEPS):
        cols = slice(i * HD, (i + 1) * HD)
        keep_ref[:, cols] = w_ref[:, head_columns(step, 0)]
        give_ref[:, cols] = w_ref[:, head_columns(step, 1)]
    text_ref[0] = kt_ref[...]
    text_ref[1] = vt_ref[...]


def query_order(n):
    y = lax.rem(lax.axis_index("seq"), 2)
    return [2 * z + y for z in range(n // 2)] + [2 * z + 1 - y for z in range(n // 2)]


def forward_kernel(tok_ref, text_ref, probs_ref, out_ref, queries_ref, keys_t_ref, vals_ref, keys, vals_t, *, chunk):
    n, three, _ = tok_ref.shape
    rows = three // 3
    image = n * rows
    text = text_ref.shape[1]
    for i, source in enumerate(query_order(n)):
        queries_ref[i * rows : (i + 1) * rows, :] = tok_ref[source, 0:rows, :]
    keys[0:image, :] = tok_ref[:, rows : 2 * rows, :].reshape(image, HD)
    keys[image : image + text, :] = text_ref[0]
    vals_ref[0:image, :] = tok_ref[:, 2 * rows : 3 * rows, :].reshape(image, HD)
    vals_ref[image : image + text, :] = text_ref[1]
    keys_t_ref[...] = keys[...].T
    vals_t[...] = vals_ref[...].T
    factor = HD ** (-0.5) * math.log2(math.e)
    for c in range(image // chunk):
        span = slice(c * chunk, (c + 1) * chunk)
        scores = lax.dot_general(keys[...], queries_ref[span, :], NT, preferred_element_type=F32)
        top = jnp.max(scores, axis=0, keepdims=True)
        weights = jnp.exp2((scores - top) * factor)
        total = jnp.sum(weights, axis=0, keepdims=True)
        low = (weights * (1.0 / total)).astype(BF16)
        probs_ref[:, span] = low
        out_ref[:, span] = jnp.dot(vals_t[...], low, preferred_element_type=F32).astype(BF16)


def partial_kernel(piece_ref, swapped_ref, own_ref, other_ref, *refs):
    mine_ref, far_ref, near_ref, send_ref, cot_ref, weight = refs
    me = lax.axis_index("seq")
    core = lax.axis_index("fsdp")
    part = piece_ref.shape[0] // len(STEPS)
    for piece, shift in ((piece_ref, core), (swapped_ref, 1 - core)):
        for i, step in enumerate(STEPS):
            z = jnp.bitwise_xor(me, step) // 2
            at = pl.multiple_of(z * (2 * part) + shift * part, 16)
            cot_ref[pl.ds(at, part), :] = piece[i * part : (i + 1) * part, :]
    depth = own_ref.shape[0]
    y = lax.rem(me, 2)
    weight[pl.ds(pl.multiple_of(y * depth, 16), depth), :] = own_ref[...]
    weight[pl.ds(pl.multiple_of((1 - y) * depth, 16), depth), :] = other_ref[...]
    step = 256

    @pl.loop(0, cot_ref.shape[0] // step)
    def _(i):
        at = pl.ds(pl.multiple_of(i * step, step), step)
        part = jnp.dot(cot_ref[at, :], weight[...], preferred_element_type=F32)
        mine_ref[at, :] = part[:, :HD]
        near_ref[at, :] = part[:, HD : 2 * HD].astype(BF16)
        far_ref[at, :] = part[:, 2 * HD : 3 * HD]
        send_ref[at, :] = part[:, 3 * HD :].astype(BF16)


def weight_grad_kernel(cot0_ref, cot1_ref, *refs):
    *out_refs, own_ref, other_ref, outs = refs
    for i, ref in enumerate(out_refs):
        outs[i * HD : (i + 1) * HD, :] = ref[...]
    depth = own_ref.shape[1]
    tokens = cot0_ref.shape[0]
    y = lax.rem(lax.axis_index("seq"), 2)
    for ref, row in ((own_ref, y), (other_ref, 1 - y)):
        cols = pl.ds(pl.multiple_of(row * depth, HD), depth)
        total = jnp.dot(outs[:, :tokens], cot0_ref[:, cols], preferred_element_type=F32)
        total += jnp.dot(outs[:, tokens:], cot1_ref[:, cols], preferred_element_type=F32)
        ref[...] = total.astype(BF16)


def backward_kernel(queries_ref, keys_t_ref, vals_ref, probs_ref, out_ref, *refs, chunk):
    *grad_refs, send_ref, dk, dv = refs
    n, three, _ = send_ref.shape
    rows = three // 3
    image = n * rows
    scale = HD ** (-0.5)
    per = chunk // rows
    order = query_order(n)
    half = image // chunk // 2
    for c in range(image // chunk):
        span = slice(c * chunk, (c + 1) * chunk)
        within = slice(c % half * chunk, (c % half + 1) * chunk)
        mine_ref, near_ref, far_ref = grad_refs[c // half :: 2]
        grads = mine_ref[within, :] + near_ref[within, :].astype(F32) + far_ref[within, :].astype(F32)
        grads = grads.astype(BF16)
        row_dot = jnp.sum(
            grads.astype(F32).T * out_ref[:, span].astype(F32), axis=0, keepdims=True
        )
        prob_grad = lax.dot_general(vals_ref[...], grads, NT, preferred_element_type=F32)
        low = probs_ref[:, span]
        score_grad = (low.astype(F32) * (prob_grad - row_dot)).astype(BF16)
        dq = (jnp.dot(keys_t_ref[...], score_grad, preferred_element_type=F32) * scale).T.astype(BF16)
        for i in range(per):
            send_ref[order[c * per + i], 0:rows, :] = dq[i * rows : (i + 1) * rows, :]
        dk_part = jnp.dot(score_grad[0:image, :], queries_ref[span, :], preferred_element_type=F32)
        dv_part = jnp.dot(low[0:image, :], grads, preferred_element_type=F32)
        if c == 0:
            dk[...] = dk_part
            dv[...] = dv_part
        else:
            dk[...] += dk_part
            dv[...] += dv_part
    send_ref[:, rows : 2 * rows, :] = (dk[...] * scale).astype(BF16).reshape(n, rows, HD)
    send_ref[:, 2 * rows : 3 * rows, :] = dv[...].astype(BF16).reshape(n, rows, HD)


def unpack_kernel(tok_ref, q_ref, k_ref, v_ref):
    rows = q_ref.shape[0]
    for h in range(tok_ref.shape[0]):
        for i, ref in enumerate((q_ref, k_ref, v_ref)):
            ref[:, h * HD : (h + 1) * HD] = tok_ref[h, i * rows : (i + 1) * rows, :]


def unpack_weight_kernel(own_ref, other_ref, w_ref):
    for other_row, ref in enumerate((own_ref, other_ref)):
        for i, step in enumerate(STEPS):
            w_ref[:, head_columns(step, other_row)] = ref[i * HD : (i + 1) * HD, :].astype(F32).T


def exchange(array, distance=0, cores=False):
    if not distance and not cores:
        return array
    size = 2 * lax.axis_size("seq")
    pairs = [(i, i ^ (2 * distance + int(cores))) for i in range(size)]
    return lax.ppermute(array, ("seq", "fsdp"), pairs)


def send_cotangents(d_out):
    rows, width = d_out.shape
    part, columns = rows // 2, width // len(STEPS)
    z = lax.axis_index("seq") // 2
    first = lax.axis_index("fsdp") * part
    return [
        exchange(lax.dynamic_slice(d_out, (first, (z ^ (step // 2)) * columns), (part, columns)), step)
        for step in STEPS
    ]


def local(q_img, k_img, v_img, k_txt, v_txt, out_weight, d_out):
    n = lax.axis_size("seq")
    rows, width = q_img.shape
    args = (q_img, k_img, v_img, k_txt, v_txt, out_weight, d_out)
    if n != 2 * len(STEPS) or width // HD != n or lax.axis_size("fsdp") != 2 or rows % 32:
        return local_general(*args)
    depth = out_weight.shape[0]
    image = n * rows
    text = k_txt.shape[0]
    total = image + text
    chunk = 2 * rows
    shape = jax.ShapeDtypeStruct
    vmem = pl.BlockSpec(memory_space=pltpu.VMEM)

    head = pl.BlockSpec((text, HD), lambda i, me_ref: (0, me_ref[0]))
    big = 60 * 1024 * 1024
    keep, give, text_head = call(
        pack_weight_kernel,
        [shape((depth, 4 * HD), BF16)] * 2 + [shape((2, text, HD), BF16)],
        [lax.axis_index("seq").astype(jnp.int32)[None], out_weight, k_txt, v_txt],
        specs=[vmem] + [head] * 2,
        scalars=1,
        moved=4 * depth * width,
        limit=big,
    )
    d_out, give = lax.optimization_barrier((d_out, give))
    given = exchange(give, 1)
    along = send_cotangents(d_out)
    (tok_out,) = call(
        pack_kernel,
        [shape((n, 3 * rows, HD), BF16)],
        [q_img, k_img, v_img],
        moved=4 * 3 * rows * width,
        limit=big,
    )
    tok_out, along[1] = lax.optimization_barrier((tok_out, along[1]))
    along, given = lax.optimization_barrier((along, given))
    row = jnp.concatenate(along, axis=0)
    row_swapped = exchange(row, cores=True)
    other_row = exchange(row, 1)
    other_swapped = exchange(other_row, cores=True)
    tok_in = lax.all_to_all(tok_out, "seq", split_axis=0, concat_axis=0, tiled=True)

    probs, out_t, queries, keys_t, vals = call(
        functools.partial(forward_kernel, chunk=chunk),
        [shape(dims, BF16) for dims in ((total, image), (HD, image), (image, HD), (HD, total), (total, HD))],
        [tok_in, text_head],
        scratch=[pltpu.VMEM((total, HD), BF16), pltpu.VMEM((HD, total), BF16)],
        flops=4 * total * image * HD,
        moved=4 * total * image,
    )
    columns = row.shape[1]

    def partial(*operands):
        return call(
            partial_kernel,
            [shape((image // 2, HD), F32)] * 2
            + [shape((image // 2, HD), BF16)] * 2
            + [shape((image // 2, columns), BF16)],
            [*operands, keep, given],
            scratch=[pltpu.VMEM((columns, 4 * HD), BF16)],
            flops=4 * image * columns * HD,
            moved=image * columns,
        )

    def add(kept, received):
        return (kept + received.astype(F32)).astype(BF16)

    mine0, kept0, near0, send0, cot0 = partial(row, row_swapped)
    far0 = exchange(add(kept0, exchange(send0, 2)), 4)
    near0 = exchange(near0, 2)
    other_row, far0, near0 = lax.optimization_barrier((other_row, far0, near0))
    mine1, kept1, near1, send1, cot1 = partial(other_row, other_swapped)
    send1, out_t, near1 = lax.optimization_barrier((exchange(send1, 2), out_t, near1))
    far1 = exchange(add(kept1, send1), 4)
    near1 = exchange(near1, 2)
    out_late, far1, near1 = lax.optimization_barrier((out_t, far1, near1))
    out_near, out_far = exchange(out_late, 2), exchange(out_late, 4)
    (grad_out,) = call(
        functools.partial(backward_kernel, chunk=chunk),
        [shape((n, 3 * rows, HD), BF16)],
        [queries, keys_t, vals, probs, out_t, mine0, mine1, near0, near1, far0, far1],
        scratch=[pltpu.VMEM((image, HD), F32), pltpu.VMEM((image, HD), F32)],
        flops=8 * total * image * HD,
        moved=4 * total * image,
    )
    grad_in = lax.all_to_all(grad_out, "seq", split_axis=0, concat_axis=0, tiled=True)
    out_far, out_near, _ = lax.optimization_barrier((out_far, out_near, grad_out))
    outs = [out_t, out_near, out_far, exchange(out_far, 2)]
    dw_own, dw_other = call(
        weight_grad_kernel,
        [shape((4 * HD, depth), BF16)] * 2,
        [cot0, cot1, *outs],
        scratch=[pltpu.VMEM((4 * HD, image), BF16)],
        flops=96 * image * columns * HD,
        moved=2 * image * columns,
    )
    grads = call(
        unpack_kernel,
        [shape((rows, width), BF16)] * 3,
        [grad_in],
        moved=4 * 3 * rows * width,
    )
    (d_weight,) = call(
        unpack_weight_kernel,
        [shape((depth, width), F32)],
        [dw_own, exchange(dw_other, 1)],
        moved=6 * depth * width,
    )
    return (*grads, d_weight)


def solution(mesh):
    in_specs = (
        P(("group", "seq"), "fsdp"),
        P(("group", "seq"), "fsdp"),
        P(("group", "seq"), "fsdp"),
        P("group", "fsdp"),
        P("group", "fsdp"),
        P("seq", "fsdp"),
        P(("group", "seq"), None),
    )
    out_specs = (
        P(("group", "seq"), "fsdp"),
        P(("group", "seq"), "fsdp"),
        P(("group", "seq"), "fsdp"),
        P(("group", "seq"), "fsdp"),
    )
    return jax.shard_map(local, mesh=mesh, in_specs=in_specs, out_specs=out_specs, check_vma=False)
```

```python
import functools
import math

import jax
import jax.numpy as jnp
from jax import lax
from jax.experimental import pallas as pl
from jax.experimental.pallas import tpu as pltpu
from jax.sharding import PartitionSpec as P

HD = 128
F32 = jnp.float32
BF16 = jnp.bfloat16
LIMIT = 28 * 1024 * 1024
NT = (((1,), (1,)), ((), ()))


def attend(queries, cotangents, key_rows, value_rows, block_rows):
    score_scale = HD ** (-0.5)
    query_count = queries.shape[0]
    block_count = query_count // block_rows
    query_blocks = queries.reshape(block_count, block_rows, HD)
    grad_blocks = cotangents.reshape(block_count, block_rows, HD)

    def one_block(accumulated, pair_item):
        query_block, grad_block = pair_item
        scores = jnp.dot(query_block, key_rows.T, preferred_element_type=jnp.float32) * score_scale
        row_max = jnp.max(scores, axis=1, keepdims=True)
        probs = jnp.exp(scores - row_max)
        probs = probs / jnp.sum(probs, axis=1, keepdims=True)
        probs_low = probs.astype(jnp.bfloat16)
        out_rows = jnp.dot(probs_low, value_rows, preferred_element_type=jnp.float32).astype(
            jnp.bfloat16
        )
        prob_grad = jnp.dot(grad_block, value_rows.T, preferred_element_type=jnp.float32)
        row_dot = jnp.sum(
            grad_block.astype(jnp.float32) * out_rows.astype(jnp.float32), axis=1, keepdims=True
        )
        score_grad = (probs * (prob_grad - row_dot)).astype(jnp.bfloat16)
        query_grad = (
            jnp.dot(score_grad, key_rows, preferred_element_type=jnp.float32) * score_scale
        ).astype(jnp.bfloat16)
        key_grad = (
            accumulated[0]
            + jnp.dot(score_grad.T, query_block, preferred_element_type=jnp.float32) * score_scale
        )
        value_grad = accumulated[1] + jnp.dot(
            probs_low.T, grad_block, preferred_element_type=jnp.float32
        )
        return ((key_grad, value_grad), (query_grad, out_rows))

    empty = jnp.zeros((key_rows.shape[0], HD), jnp.float32)
    (key_grad, value_grad), (query_grad, out_rows) = lax.scan(
        one_block, (empty, empty), (query_blocks, grad_blocks)
    )
    return (
        query_grad.reshape(query_count, HD),
        out_rows.reshape(query_count, HD),
        key_grad,
        value_grad,
    )


def local_general(q_img, k_img, v_img, k_txt, v_txt, out_weight, d_out):
    rows_here = q_img.shape[0]
    heads_here = q_img.shape[1] // HD
    seq_count = lax.axis_size("seq")
    share_count = seq_count // heads_here
    part_rows = rows_here // share_count
    seq_index = lax.axis_index("seq")
    head_index = seq_index // share_count
    column_cut = d_out
    attn_grad = jnp.dot(
        column_cut,
        lax.all_gather(out_weight, "seq", axis=0, tiled=True),
        preferred_element_type=jnp.float32,
    ).astype(jnp.bfloat16)

    def to_heads(array_in):
        shaped = array_in.reshape(share_count, part_rows, heads_here, HD).transpose(2, 0, 1, 3)
        return shaped.reshape(seq_count, part_rows, HD)

    def whole_heads(array_in):
        shaped = array_in.reshape(rows_here, heads_here, HD).transpose(1, 0, 2)
        shaped = jnp.broadcast_to(shaped[:, None], (heads_here, share_count, rows_here, HD))
        return shaped.reshape(seq_count, rows_here, HD)

    def from_heads(array_in):
        shaped = array_in.reshape(heads_here, share_count, part_rows, HD).transpose(1, 2, 0, 3)
        return shaped.reshape(rows_here, heads_here * HD)

    text_keys = lax.dynamic_slice_in_dim(k_txt, head_index * HD, HD, 1)
    text_values = lax.dynamic_slice_in_dim(v_txt, head_index * HD, HD, 1)
    query_side = jnp.concatenate([to_heads(q_img), to_heads(attn_grad)], axis=2)
    key_side = jnp.concatenate([whole_heads(k_img), whole_heads(v_img)], axis=2)
    packed = jnp.concatenate([query_side, key_side], axis=1)
    received = lax.all_to_all(packed, "seq", split_axis=0, concat_axis=0, tiled=True)
    queries = received[:, :part_rows, :HD].reshape(seq_count * part_rows, HD)
    cotangents = received[:, :part_rows, HD:].reshape(seq_count * part_rows, HD)
    image_keys = received[:, part_rows:, :HD].reshape(seq_count * rows_here, HD)
    image_values = received[:, part_rows:, HD:].reshape(seq_count * rows_here, HD)
    key_rows = jnp.concatenate([image_keys, text_keys], axis=0)
    value_rows = jnp.concatenate([image_values, text_values], axis=0)
    query_grad, out_rows, key_grad, value_grad = attend(
        queries, cotangents, key_rows, value_rows, min(512, queries.shape[0])
    )
    image_count = image_keys.shape[0]
    query_part = (
        jnp.concatenate([query_grad, out_rows], axis=1)
        .astype(jnp.float32)
        .reshape(seq_count, part_rows, 2 * HD)
    )
    key_part = jnp.concatenate([key_grad[:image_count], value_grad[:image_count]], axis=1).reshape(
        seq_count, rows_here, 2 * HD
    )
    returned = lax.all_to_all(
        jnp.concatenate([query_part, key_part], axis=1).astype(jnp.bfloat16),
        "seq",
        split_axis=0,
        concat_axis=0,
        tiled=True,
    ).astype(jnp.float32)
    q_grad = from_heads(returned[:, :part_rows, :HD]).astype(jnp.bfloat16)
    out_tok = from_heads(returned[:, :part_rows, HD:]).astype(jnp.bfloat16)
    summed = jnp.sum(
        returned[:, part_rows:, :].reshape(heads_here, share_count, rows_here, 2 * HD), axis=1
    )
    summed = summed.transpose(1, 0, 2)
    k_grad = summed[:, :, :HD].reshape(rows_here, heads_here * HD).astype(jnp.bfloat16)
    v_grad = summed[:, :, HD:].reshape(rows_here, heads_here * HD).astype(jnp.bfloat16)
    column_cut = d_out
    d_weight = lax.psum_scatter(
        jnp.dot(column_cut.T, out_tok, preferred_element_type=jnp.float32).astype(jnp.bfloat16),
        "seq",
        scatter_dimension=0,
        tiled=True,
    ).astype(jnp.float32)
    return (q_grad, k_grad, v_grad, d_weight)


def call(kernel, outs, args, specs=None, scratch=(), scalars=0, out_specs=None, flops=0, moved=0, limit=LIMIT):
    vmem = pl.BlockSpec(memory_space=pltpu.VMEM)
    if specs is None:
        specs = [vmem] * (len(args) - scalars)
    if out_specs is None:
        out_specs = [vmem] * len(outs)
    return pl.pallas_call(
        kernel,
        out_shape=outs,
        grid_spec=pltpu.PrefetchScalarGridSpec(
            num_scalar_prefetch=scalars,
            grid=(1,),
            in_specs=specs,
            out_specs=out_specs,
            scratch_shapes=list(scratch),
        ),
        compiler_params=pltpu.CompilerParams(vmem_limit_bytes=limit),
        cost_estimate=pl.CostEstimate(flops=flops, bytes_accessed=moved, transcendentals=0),
    )(*args)


STEPS = (0, 2, 4, 6)


def head_columns(step, other_row):
    return pl.ds(pl.multiple_of(jnp.bitwise_xor(lax.axis_index("seq"), step + other_row) * HD, HD), HD)


def pack_kernel(q_ref, k_ref, v_ref, tok_ref):
    rows = q_ref.shape[0]
    for h in range(tok_ref.shape[0]):
        for i, ref in enumerate((q_ref, k_ref, v_ref)):
            tok_ref[h, i * rows : (i + 1) * rows, :] = ref[:, h * HD : (h + 1) * HD]


def pack_weight_kernel(me_ref, w_ref, kt_ref, vt_ref, keep_ref, give_ref, text_ref):
    for i, step in enumerate(STEPS):
        cols = slice(i * HD, (i + 1) * HD)
        keep_ref[:, cols] = w_ref[:, head_columns(step, 0)]
        give_ref[:, cols] = w_ref[:, head_columns(step, 1)]
    text_ref[0] = kt_ref[...]
    text_ref[1] = vt_ref[...]


def query_order(n):
    y = lax.rem(lax.axis_index("seq"), 2)
    return [2 * z + y for z in range(n // 2)] + [2 * z + 1 - y for z in range(n // 2)]


def forward_kernel(tok_ref, text_ref, probs_ref, out_ref, queries_ref, keys_t_ref, vals_ref, keys, vals_t, *, chunk):
    n, three, _ = tok_ref.shape
    rows = three // 3
    image = n * rows
    text = text_ref.shape[1]
    for i, source in enumerate(query_order(n)):
        queries_ref[i * rows : (i + 1) * rows, :] = tok_ref[source, 0:rows, :]
    keys[0:image, :] = tok_ref[:, rows : 2 * rows, :].reshape(image, HD)
    keys[image : image + text, :] = text_ref[0]
    vals_ref[0:image, :] = tok_ref[:, 2 * rows : 3 * rows, :].reshape(image, HD)
    vals_ref[image : image + text, :] = text_ref[1]
    keys_t_ref[...] = keys[...].T
    vals_t[...] = vals_ref[...].T
    factor = HD ** (-0.5) * math.log2(math.e)
    for c in range(image // chunk):
        span = slice(c * chunk, (c + 1) * chunk)
        scores = lax.dot_general(keys[...], queries_ref[span, :], NT, preferred_element_type=F32)
        top = jnp.max(scores, axis=0, keepdims=True)
        weights = jnp.exp2((scores - top) * factor)
        total = jnp.sum(weights, axis=0, keepdims=True)
        low = (weights * (1.0 / total)).astype(BF16)
        probs_ref[:, span] = low
        out_ref[:, span] = jnp.dot(vals_t[...], low, preferred_element_type=F32).astype(BF16)


def partial_kernel(piece_ref, swapped_ref, own_ref, other_ref, *refs):
    mine_ref, far_ref, near_ref, send_ref, cot_ref, weight = refs
    me = lax.axis_index("seq")
    core = lax.axis_index("fsdp")
    part = piece_ref.shape[0] // len(STEPS)
    for piece, shift in ((piece_ref, core), (swapped_ref, 1 - core)):
        for i, step in enumerate(STEPS):
            z = jnp.bitwise_xor(me, step) // 2
            at = pl.multiple_of(z * (2 * part) + shift * part, 16)
            cot_ref[pl.ds(at, part), :] = piece[i * part : (i + 1) * part, :]
    depth = own_ref.shape[0]
    y = lax.rem(me, 2)
    weight[pl.ds(pl.multiple_of(y * depth, 16), depth), :] = own_ref[...]
    weight[pl.ds(pl.multiple_of((1 - y) * depth, 16), depth), :] = other_ref[...]
    step = 256

    @pl.loop(0, cot_ref.shape[0] // step)
    def _(i):
        at = pl.ds(pl.multiple_of(i * step, step), step)
        part = jnp.dot(cot_ref[at, :], weight[...], preferred_element_type=F32)
        mine_ref[at, :] = part[:, :HD]
        near_ref[at, :] = part[:, HD : 2 * HD].astype(BF16)
        far_ref[at, :] = part[:, 2 * HD : 3 * HD]
        send_ref[at, :] = part[:, 3 * HD :].astype(BF16)


def weight_grad_kernel(cot0_ref, cot1_ref, *refs):
    *out_refs, own_ref, other_ref, outs = refs
    for i, ref in enumerate(out_refs):
        outs[i * HD : (i + 1) * HD, :] = ref[...]
    depth = own_ref.shape[1]
    tokens = cot0_ref.shape[0]
    y = lax.rem(lax.axis_index("seq"), 2)
    for ref, row in ((own_ref, y), (other_ref, 1 - y)):
        cols = pl.ds(pl.multiple_of(row * depth, HD), depth)
        total = jnp.dot(outs[:, :tokens], cot0_ref[:, cols], preferred_element_type=F32)
        total += jnp.dot(outs[:, tokens:], cot1_ref[:, cols], preferred_element_type=F32)
        ref[...] = total.astype(BF16)


def backward_kernel(queries_ref, keys_t_ref, vals_ref, probs_ref, out_ref, *refs, chunk):
    *grad_refs, send_ref, dk, dv = refs
    n, three, _ = send_ref.shape
    rows = three // 3
    image = n * rows
    scale = HD ** (-0.5)
    per = chunk // rows
    order = query_order(n)
    half = image // chunk // 2
    for c in range(image // chunk):
        span = slice(c * chunk, (c + 1) * chunk)
        within = slice(c % half * chunk, (c % half + 1) * chunk)
        mine_ref, near_ref, far_ref = grad_refs[c // half :: 2]
        grads = mine_ref[within, :] + near_ref[within, :].astype(F32) + far_ref[within, :].astype(F32)
        grads = grads.astype(BF16)
        row_dot = jnp.sum(
            grads.astype(F32).T * out_ref[:, span].astype(F32), axis=0, keepdims=True
        )
        prob_grad = lax.dot_general(vals_ref[...], grads, NT, preferred_element_type=F32)
        low = probs_ref[:, span]
        score_grad = (low.astype(F32) * (prob_grad - row_dot)).astype(BF16)
        dq = (jnp.dot(keys_t_ref[...], score_grad, preferred_element_type=F32) * scale).T.astype(BF16)
        for i in range(per):
            send_ref[order[c * per + i], 0:rows, :] = dq[i * rows : (i + 1) * rows, :]
        dk_part = jnp.dot(score_grad[0:image, :], queries_ref[span, :], preferred_element_type=F32)
        dv_part = jnp.dot(low[0:image, :], grads, preferred_element_type=F32)
        if c == 0:
            dk[...] = dk_part
            dv[...] = dv_part
        else:
            dk[...] += dk_part
            dv[...] += dv_part
    send_ref[:, rows : 2 * rows, :] = (dk[...] * scale).astype(BF16).reshape(n, rows, HD)
    send_ref[:, 2 * rows : 3 * rows, :] = dv[...].astype(BF16).reshape(n, rows, HD)


def unpack_kernel(tok_ref, q_ref, k_ref, v_ref):
    rows = q_ref.shape[0]
    for h in range(tok_ref.shape[0]):
        for i, ref in enumerate((q_ref, k_ref, v_ref)):
            ref[:, h * HD : (h + 1) * HD] = tok_ref[h, i * rows : (i + 1) * rows, :]


def unpack_weight_kernel(own_ref, other_ref, w_ref):
    for other_row, ref in enumerate((own_ref, other_ref)):
        for i, step in enumerate(STEPS):
            w_ref[:, head_columns(step, other_row)] = ref[i * HD : (i + 1) * HD, :].astype(F32).T


def exchange(array, distance=0, cores=False):
    if not distance and not cores:
        return array
    size = 2 * lax.axis_size("seq")
    pairs = [(i, i ^ (2 * distance + int(cores))) for i in range(size)]
    return lax.ppermute(array, ("seq", "fsdp"), pairs)


def send_cotangents(d_out):
    rows, width = d_out.shape
    part, columns = rows // 2, width // len(STEPS)
    z = lax.axis_index("seq") // 2
    first = lax.axis_index("fsdp") * part
    return [
        exchange(lax.dynamic_slice(d_out, (first, (z ^ (step // 2)) * columns), (part, columns)), step)
        for step in STEPS
    ]


def local(q_img, k_img, v_img, k_txt, v_txt, out_weight, d_out):
    n = lax.axis_size("seq")
    rows, width = q_img.shape
    args = (q_img, k_img, v_img, k_txt, v_txt, out_weight, d_out)
    if n != 2 * len(STEPS) or width // HD != n or lax.axis_size("fsdp") != 2 or rows % 32:
        return local_general(*args)
    depth = out_weight.shape[0]
    image = n * rows
    text = k_txt.shape[0]
    total = image + text
    chunk = 2 * rows
    shape = jax.ShapeDtypeStruct
    vmem = pl.BlockSpec(memory_space=pltpu.VMEM)

    head = pl.BlockSpec((text, HD), lambda i, me_ref: (0, me_ref[0]))
    big = 60 * 1024 * 1024
    keep, give, text_head = call(
        pack_weight_kernel,
        [shape((depth, 4 * HD), BF16)] * 2 + [shape((2, text, HD), BF16)],
        [lax.axis_index("seq").astype(jnp.int32)[None], out_weight, k_txt, v_txt],
        specs=[vmem] + [head] * 2,
        scalars=1,
        moved=4 * depth * width,
        limit=big,
    )
    d_out, give = lax.optimization_barrier((d_out, give))
    given = exchange(give, 1)
    along = send_cotangents(d_out)
    (tok_out,) = call(
        pack_kernel,
        [shape((n, 3 * rows, HD), BF16)],
        [q_img, k_img, v_img],
        moved=4 * 3 * rows * width,
        limit=big,
    )
    tok_out, along[1] = lax.optimization_barrier((tok_out, along[1]))
    along, given = lax.optimization_barrier((along, given))
    row = jnp.concatenate(along, axis=0)
    row_swapped = exchange(row, cores=True)
    other_row = exchange(row, 1)
    tok_in = lax.all_to_all(tok_out, "seq", split_axis=0, concat_axis=0, tiled=True)

    probs, out_t, queries, keys_t, vals = call(
        functools.partial(forward_kernel, chunk=chunk),
        [shape(dims, BF16) for dims in ((total, image), (HD, image), (image, HD), (HD, total), (total, HD))],
        [tok_in, text_head],
        scratch=[pltpu.VMEM((total, HD), BF16), pltpu.VMEM((HD, total), BF16)],
        flops=4 * total * image * HD,
        moved=4 * total * image,
    )
    columns = row.shape[1]

    def partial(*operands):
        return call(
            partial_kernel,
            [shape((image // 2, HD), F32)] * 2
            + [shape((image // 2, HD), BF16)] * 2
            + [shape((image // 2, columns), BF16)],
            [*operands, keep, given],
            scratch=[pltpu.VMEM((columns, 4 * HD), BF16)],
            flops=4 * image * columns * HD,
            moved=image * columns,
        )

    def add(kept, received):
        return (kept + received.astype(F32)).astype(BF16)

    mine0, kept0, near0, send0, cot0 = partial(row, row_swapped)
    far0 = exchange(add(kept0, exchange(send0, 2)), 4)
    near0 = exchange(near0, 2)
    other_row, far0, near0 = lax.optimization_barrier((other_row, far0, near0))
    other_swapped = exchange(other_row, cores=True)
    mine1, kept1, near1, send1, cot1 = partial(other_row, other_swapped)
    send1, out_t, near1 = lax.optimization_barrier((exchange(send1, 2), out_t, near1))
    far1 = exchange(add(kept1, send1), 4)
    near1 = exchange(near1, 2)
    out_late, far1, near1 = lax.optimization_barrier((out_t, far1, near1))
    out_near, out_far = exchange(out_late, 2), exchange(out_late, 4)
    (grad_out,) = call(
        functools.partial(backward_kernel, chunk=chunk),
        [shape((n, 3 * rows, HD), BF16)],
        [queries, keys_t, vals, probs, out_t, mine0, mine1, near0, near1, far0, far1],
        scratch=[pltpu.VMEM((image, HD), F32), pltpu.VMEM((image, HD), F32)],
        flops=8 * total * image * HD,
        moved=4 * total * image,
    )
    grad_in = lax.all_to_all(grad_out, "seq", split_axis=0, concat_axis=0, tiled=True)
    out_far, out_near, _ = lax.optimization_barrier((out_far, out_near, grad_out))
    outs = [out_t, out_near, out_far, exchange(out_far, 2)]
    dw_own, dw_other = call(
        weight_grad_kernel,
        [shape((4 * HD, depth), BF16)] * 2,
        [cot0, cot1, *outs],
        scratch=[pltpu.VMEM((4 * HD, image), BF16)],
        flops=72 * image * columns * HD,
        moved=2 * image * columns,
    )
    grads = call(
        unpack_kernel,
        [shape((rows, width), BF16)] * 3,
        [grad_in],
        moved=4 * 3 * rows * width,
    )
    (d_weight,) = call(
        unpack_weight_kernel,
        [shape((depth, width), F32)],
        [dw_own, exchange(dw_other, 1)],
        moved=6 * depth * width,
    )
    return (*grads, d_weight)


def solution(mesh):
    in_specs = (
        P(("group", "seq"), "fsdp"),
        P(("group", "seq"), "fsdp"),
        P(("group", "seq"), "fsdp"),
        P("group", "fsdp"),
        P("group", "fsdp"),
        P("seq", "fsdp"),
        P(("group", "seq"), None),
    )
    out_specs = (
        P(("group", "seq"), "fsdp"),
        P(("group", "seq"), "fsdp"),
        P(("group", "seq"), "fsdp"),
        P(("group", "seq"), "fsdp"),
    )
    return jax.shard_map(local, mesh=mesh, in_specs=in_specs, out_specs=out_specs, check_vma=False)
```

```python
import functools
import math

import jax
import jax.numpy as jnp
from jax import lax
from jax.experimental import pallas as pl
from jax.experimental.pallas import tpu as pltpu
from jax.sharding import PartitionSpec as P

HD = 128
F32 = jnp.float32
BF16 = jnp.bfloat16
LIMIT = 28 * 1024 * 1024
NT = (((1,), (1,)), ((), ()))


def attend(queries, cotangents, key_rows, value_rows, block_rows):
    score_scale = HD ** (-0.5)
    query_count = queries.shape[0]
    block_count = query_count // block_rows
    query_blocks = queries.reshape(block_count, block_rows, HD)
    grad_blocks = cotangents.reshape(block_count, block_rows, HD)

    def one_block(accumulated, pair_item):
        query_block, grad_block = pair_item
        scores = jnp.dot(query_block, key_rows.T, preferred_element_type=jnp.float32) * score_scale
        row_max = jnp.max(scores, axis=1, keepdims=True)
        probs = jnp.exp(scores - row_max)
        probs = probs / jnp.sum(probs, axis=1, keepdims=True)
        probs_low = probs.astype(jnp.bfloat16)
        out_rows = jnp.dot(probs_low, value_rows, preferred_element_type=jnp.float32).astype(
            jnp.bfloat16
        )
        prob_grad = jnp.dot(grad_block, value_rows.T, preferred_element_type=jnp.float32)
        row_dot = jnp.sum(
            grad_block.astype(jnp.float32) * out_rows.astype(jnp.float32), axis=1, keepdims=True
        )
        score_grad = (probs * (prob_grad - row_dot)).astype(jnp.bfloat16)
        query_grad = (
            jnp.dot(score_grad, key_rows, preferred_element_type=jnp.float32) * score_scale
        ).astype(jnp.bfloat16)
        key_grad = (
            accumulated[0]
            + jnp.dot(score_grad.T, query_block, preferred_element_type=jnp.float32) * score_scale
        )
        value_grad = accumulated[1] + jnp.dot(
            probs_low.T, grad_block, preferred_element_type=jnp.float32
        )
        return ((key_grad, value_grad), (query_grad, out_rows))

    empty = jnp.zeros((key_rows.shape[0], HD), jnp.float32)
    (key_grad, value_grad), (query_grad, out_rows) = lax.scan(
        one_block, (empty, empty), (query_blocks, grad_blocks)
    )
    return (
        query_grad.reshape(query_count, HD),
        out_rows.reshape(query_count, HD),
        key_grad,
        value_grad,
    )


def local_general(q_img, k_img, v_img, k_txt, v_txt, out_weight, d_out):
    rows_here = q_img.shape[0]
    heads_here = q_img.shape[1] // HD
    seq_count = lax.axis_size("seq")
    share_count = seq_count // heads_here
    part_rows = rows_here // share_count
    seq_index = lax.axis_index("seq")
    head_index = seq_index // share_count
    column_cut = d_out
    attn_grad = jnp.dot(
        column_cut,
        lax.all_gather(out_weight, "seq", axis=0, tiled=True),
        preferred_element_type=jnp.float32,
    ).astype(jnp.bfloat16)

    def to_heads(array_in):
        shaped = array_in.reshape(share_count, part_rows, heads_here, HD).transpose(2, 0, 1, 3)
        return shaped.reshape(seq_count, part_rows, HD)

    def whole_heads(array_in):
        shaped = array_in.reshape(rows_here, heads_here, HD).transpose(1, 0, 2)
        shaped = jnp.broadcast_to(shaped[:, None], (heads_here, share_count, rows_here, HD))
        return shaped.reshape(seq_count, rows_here, HD)

    def from_heads(array_in):
        shaped = array_in.reshape(heads_here, share_count, part_rows, HD).transpose(1, 2, 0, 3)
        return shaped.reshape(rows_here, heads_here * HD)

    text_keys = lax.dynamic_slice_in_dim(k_txt, head_index * HD, HD, 1)
    text_values = lax.dynamic_slice_in_dim(v_txt, head_index * HD, HD, 1)
    query_side = jnp.concatenate([to_heads(q_img), to_heads(attn_grad)], axis=2)
    key_side = jnp.concatenate([whole_heads(k_img), whole_heads(v_img)], axis=2)
    packed = jnp.concatenate([query_side, key_side], axis=1)
    received = lax.all_to_all(packed, "seq", split_axis=0, concat_axis=0, tiled=True)
    queries = received[:, :part_rows, :HD].reshape(seq_count * part_rows, HD)
    cotangents = received[:, :part_rows, HD:].reshape(seq_count * part_rows, HD)
    image_keys = received[:, part_rows:, :HD].reshape(seq_count * rows_here, HD)
    image_values = received[:, part_rows:, HD:].reshape(seq_count * rows_here, HD)
    key_rows = jnp.concatenate([image_keys, text_keys], axis=0)
    value_rows = jnp.concatenate([image_values, text_values], axis=0)
    query_grad, out_rows, key_grad, value_grad = attend(
        queries, cotangents, key_rows, value_rows, min(512, queries.shape[0])
    )
    image_count = image_keys.shape[0]
    query_part = (
        jnp.concatenate([query_grad, out_rows], axis=1)
        .astype(jnp.float32)
        .reshape(seq_count, part_rows, 2 * HD)
    )
    key_part = jnp.concatenate([key_grad[:image_count], value_grad[:image_count]], axis=1).reshape(
        seq_count, rows_here, 2 * HD
    )
    returned = lax.all_to_all(
        jnp.concatenate([query_part, key_part], axis=1).astype(jnp.bfloat16),
        "seq",
        split_axis=0,
        concat_axis=0,
        tiled=True,
    ).astype(jnp.float32)
    q_grad = from_heads(returned[:, :part_rows, :HD]).astype(jnp.bfloat16)
    out_tok = from_heads(returned[:, :part_rows, HD:]).astype(jnp.bfloat16)
    summed = jnp.sum(
        returned[:, part_rows:, :].reshape(heads_here, share_count, rows_here, 2 * HD), axis=1
    )
    summed = summed.transpose(1, 0, 2)
    k_grad = summed[:, :, :HD].reshape(rows_here, heads_here * HD).astype(jnp.bfloat16)
    v_grad = summed[:, :, HD:].reshape(rows_here, heads_here * HD).astype(jnp.bfloat16)
    column_cut = d_out
    d_weight = lax.psum_scatter(
        jnp.dot(column_cut.T, out_tok, preferred_element_type=jnp.float32).astype(jnp.bfloat16),
        "seq",
        scatter_dimension=0,
        tiled=True,
    ).astype(jnp.float32)
    return (q_grad, k_grad, v_grad, d_weight)


def call(kernel, outs, args, specs=None, scratch=(), scalars=0, out_specs=None, flops=0, moved=0, limit=LIMIT):
    vmem = pl.BlockSpec(memory_space=pltpu.VMEM)
    if specs is None:
        specs = [vmem] * (len(args) - scalars)
    if out_specs is None:
        out_specs = [vmem] * len(outs)
    return pl.pallas_call(
        kernel,
        out_shape=outs,
        grid_spec=pltpu.PrefetchScalarGridSpec(
            num_scalar_prefetch=scalars,
            grid=(1,),
            in_specs=specs,
            out_specs=out_specs,
            scratch_shapes=list(scratch),
        ),
        compiler_params=pltpu.CompilerParams(vmem_limit_bytes=limit),
        cost_estimate=pl.CostEstimate(flops=flops, bytes_accessed=moved, transcendentals=0),
    )(*args)


STEPS = (0, 2, 4, 6)


def head_columns(step, other_row):
    return pl.ds(pl.multiple_of(jnp.bitwise_xor(lax.axis_index("seq"), step + other_row) * HD, HD), HD)


def pack_kernel(q_ref, k_ref, v_ref, tok_ref):
    rows = q_ref.shape[0]
    for h in range(tok_ref.shape[0]):
        for i, ref in enumerate((q_ref, k_ref, v_ref)):
            tok_ref[h, i * rows : (i + 1) * rows, :] = ref[:, h * HD : (h + 1) * HD]


def pack_weight_kernel(me_ref, w_ref, kt_ref, vt_ref, keep_ref, give_ref, text_ref):
    for i, step in enumerate(STEPS):
        cols = slice(i * HD, (i + 1) * HD)
        keep_ref[:, cols] = w_ref[:, head_columns(step, 0)]
        give_ref[:, cols] = w_ref[:, head_columns(step, 1)]
    text_ref[0] = kt_ref[...]
    text_ref[1] = vt_ref[...]


def query_order(n):
    y = lax.rem(lax.axis_index("seq"), 2)
    return [2 * z + y for z in range(n // 2)] + [2 * z + 1 - y for z in range(n // 2)]


def forward_kernel(tok_ref, text_ref, probs_ref, out_ref, queries_ref, keys_t_ref, vals_ref, keys, vals_t, *, chunk):
    n, three, _ = tok_ref.shape
    rows = three // 3
    image = n * rows
    text = text_ref.shape[1]
    for i, source in enumerate(query_order(n)):
        queries_ref[i * rows : (i + 1) * rows, :] = tok_ref[source, 0:rows, :]
    keys[0:image, :] = tok_ref[:, rows : 2 * rows, :].reshape(image, HD)
    keys[image : image + text, :] = text_ref[0]
    vals_ref[0:image, :] = tok_ref[:, 2 * rows : 3 * rows, :].reshape(image, HD)
    vals_ref[image : image + text, :] = text_ref[1]
    keys_t_ref[...] = keys[...].T
    vals_t[...] = vals_ref[...].T
    factor = HD ** (-0.5) * math.log2(math.e)
    for c in range(image // chunk):
        span = slice(c * chunk, (c + 1) * chunk)
        scores = lax.dot_general(keys[...], queries_ref[span, :], NT, preferred_element_type=F32)
        top = jnp.max(scores, axis=0, keepdims=True)
        weights = jnp.exp2((scores - top) * factor)
        total = jnp.sum(weights, axis=0, keepdims=True)
        low = (weights * (1.0 / total)).astype(BF16)
        probs_ref[:, span] = low
        out_ref[:, span] = jnp.dot(vals_t[...], low, preferred_element_type=F32).astype(BF16)


def partial_kernel(piece_ref, swapped_ref, own_ref, other_ref, *refs):
    mine_ref, far_ref, near_ref, send_ref, cot_ref, weight = refs
    me = lax.axis_index("seq")
    core = lax.axis_index("fsdp")
    part = piece_ref.shape[0] // len(STEPS)
    for piece, shift in ((piece_ref, core), (swapped_ref, 1 - core)):
        for i, step in enumerate(STEPS):
            z = jnp.bitwise_xor(me, step) // 2
            at = pl.multiple_of(z * (2 * part) + shift * part, 16)
            cot_ref[pl.ds(at, part), :] = piece[i * part : (i + 1) * part, :]
    depth = own_ref.shape[0]
    y = lax.rem(me, 2)
    weight[pl.ds(pl.multiple_of(y * depth, 16), depth), :] = own_ref[...]
    weight[pl.ds(pl.multiple_of((1 - y) * depth, 16), depth), :] = other_ref[...]
    step = 256

    @pl.loop(0, cot_ref.shape[0] // step)
    def _(i):
        at = pl.ds(pl.multiple_of(i * step, step), step)
        part = jnp.dot(cot_ref[at, :], weight[...], preferred_element_type=F32)
        mine_ref[at, :] = part[:, :HD]
        near_ref[at, :] = part[:, HD : 2 * HD].astype(BF16)
        far_ref[at, :] = part[:, 2 * HD : 3 * HD]
        send_ref[at, :] = part[:, 3 * HD :].astype(BF16)


def weight_grad_kernel(cot0_ref, cot1_ref, *refs):
    *out_refs, own_ref, other_ref, outs = refs
    for i, ref in enumerate(out_refs):
        outs[i * HD : (i + 1) * HD, :] = ref[...]
    depth = own_ref.shape[1]
    tokens = cot0_ref.shape[0]
    y = lax.rem(lax.axis_index("seq"), 2)
    for ref, row in ((own_ref, y), (other_ref, 1 - y)):
        cols = pl.ds(pl.multiple_of(row * depth, HD), depth)
        total = jnp.dot(outs[:, :tokens], cot0_ref[:, cols], preferred_element_type=F32)
        total += jnp.dot(outs[:, tokens:], cot1_ref[:, cols], preferred_element_type=F32)
        ref[...] = total.astype(BF16)


def backward_kernel(queries_ref, keys_t_ref, vals_ref, probs_ref, out_ref, *refs, chunk):
    *grad_refs, send_ref, dk, dv = refs
    n, three, _ = send_ref.shape
    rows = three // 3
    image = n * rows
    scale = HD ** (-0.5)
    per = chunk // rows
    order = query_order(n)
    half = image // chunk // 2
    for c in range(image // chunk):
        span = slice(c * chunk, (c + 1) * chunk)
        within = slice(c % half * chunk, (c % half + 1) * chunk)
        mine_ref, near_ref, far_ref = grad_refs[c // half :: 2]
        grads = mine_ref[within, :] + near_ref[within, :].astype(F32) + far_ref[within, :].astype(F32)
        grads = grads.astype(BF16)
        row_dot = jnp.sum(
            grads.astype(F32).T * out_ref[:, span].astype(F32), axis=0, keepdims=True
        )
        prob_grad = lax.dot_general(vals_ref[...], grads, NT, preferred_element_type=F32)
        low = probs_ref[:, span]
        score_grad = (low.astype(F32) * (prob_grad - row_dot)).astype(BF16)
        dq = (jnp.dot(keys_t_ref[...], score_grad, preferred_element_type=F32) * scale).T.astype(BF16)
        for i in range(per):
            send_ref[order[c * per + i], 0:rows, :] = dq[i * rows : (i + 1) * rows, :]
        dk_part = jnp.dot(score_grad[0:image, :], queries_ref[span, :], preferred_element_type=F32)
        dv_part = jnp.dot(low[0:image, :], grads, preferred_element_type=F32)
        if c == 0:
            dk[...] = dk_part
            dv[...] = dv_part
        else:
            dk[...] += dk_part
            dv[...] += dv_part
    send_ref[:, rows : 2 * rows, :] = (dk[...] * scale).astype(BF16).reshape(n, rows, HD)
    send_ref[:, 2 * rows : 3 * rows, :] = dv[...].astype(BF16).reshape(n, rows, HD)


def unpack_kernel(tok_ref, q_ref, k_ref, v_ref):
    rows = q_ref.shape[0]
    for h in range(tok_ref.shape[0]):
        for i, ref in enumerate((q_ref, k_ref, v_ref)):
            ref[:, h * HD : (h + 1) * HD] = tok_ref[h, i * rows : (i + 1) * rows, :]


def unpack_weight_kernel(own_ref, other_ref, w_ref):
    for other_row, ref in enumerate((own_ref, other_ref)):
        for i, step in enumerate(STEPS):
            w_ref[:, head_columns(step, other_row)] = ref[i * HD : (i + 1) * HD, :].astype(F32).T


def exchange(array, distance=0, cores=False):
    if not distance and not cores:
        return array
    size = 2 * lax.axis_size("seq")
    pairs = [(i, i ^ (2 * distance + int(cores))) for i in range(size)]
    return lax.ppermute(array, ("seq", "fsdp"), pairs)


def send_cotangents(d_out):
    rows, width = d_out.shape
    part, columns = rows // 2, width // len(STEPS)
    z = lax.axis_index("seq") // 2
    first = lax.axis_index("fsdp") * part
    return [
        exchange(lax.dynamic_slice(d_out, (first, (z ^ (step // 2)) * columns), (part, columns)), step)
        for step in STEPS
    ]


def local(q_img, k_img, v_img, k_txt, v_txt, out_weight, d_out):
    n = lax.axis_size("seq")
    rows, width = q_img.shape
    args = (q_img, k_img, v_img, k_txt, v_txt, out_weight, d_out)
    if n != 2 * len(STEPS) or width // HD != n or lax.axis_size("fsdp") != 2 or rows % 32:
        return local_general(*args)
    depth = out_weight.shape[0]
    image = n * rows
    text = k_txt.shape[0]
    total = image + text
    chunk = 2 * rows
    shape = jax.ShapeDtypeStruct
    vmem = pl.BlockSpec(memory_space=pltpu.VMEM)

    head = pl.BlockSpec((text, HD), lambda i, me_ref: (0, me_ref[0]))
    big = 60 * 1024 * 1024
    keep, give, text_head = call(
        pack_weight_kernel,
        [shape((depth, 4 * HD), BF16)] * 2 + [shape((2, text, HD), BF16)],
        [lax.axis_index("seq").astype(jnp.int32)[None], out_weight, k_txt, v_txt],
        specs=[vmem] + [head] * 2,
        scalars=1,
        moved=4 * depth * width,
        limit=big,
    )
    d_out, give = lax.optimization_barrier((d_out, give))
    given = exchange(give, 1)
    along = send_cotangents(d_out)
    (tok_out,) = call(
        pack_kernel,
        [shape((n, 3 * rows, HD), BF16)],
        [q_img, k_img, v_img],
        moved=4 * 3 * rows * width,
        limit=big,
    )
    tok_out, along[1] = lax.optimization_barrier((tok_out, along[1]))
    along, given = lax.optimization_barrier((along, given))
    row = jnp.concatenate(along, axis=0)
    row_swapped = exchange(row, cores=True)
    other_row = exchange(row, 1)
    other_swapped = exchange(other_row, cores=True)
    tok_in = lax.all_to_all(tok_out, "seq", split_axis=0, concat_axis=0, tiled=True)

    probs, out_t, queries, keys_t, vals = call(
        functools.partial(forward_kernel, chunk=chunk),
        [shape(dims, BF16) for dims in ((total, image), (HD, image), (image, HD), (HD, total), (total, HD))],
        [tok_in, text_head],
        scratch=[pltpu.VMEM((total, HD), BF16), pltpu.VMEM((HD, total), BF16)],
        flops=4 * total * image * HD,
        moved=4 * total * image,
    )
    columns = row.shape[1]

    def partial(*operands):
        return call(
            partial_kernel,
            [shape((image // 2, HD), F32)] * 2
            + [shape((image // 2, HD), BF16)] * 2
            + [shape((image // 2, columns), BF16)],
            [*operands, keep, given],
            scratch=[pltpu.VMEM((columns, 4 * HD), BF16)],
            flops=4 * image * columns * HD,
            moved=image * columns,
        )

    def add(kept, received):
        return (kept + received.astype(F32)).astype(BF16)

    mine0, kept0, near0, send0, cot0 = partial(row, row_swapped)
    other_row, send0 = lax.optimization_barrier((other_row, exchange(send0, 2)))
    mine1, kept1, near1, send1, cot1 = partial(other_row, other_swapped)
    send1, sum0, near0 = lax.optimization_barrier((send1, add(kept0, send0), near0))
    far0, near0, send1 = exchange(sum0, 4), exchange(near0, 2), exchange(send1, 2)
    send1, out_t, near1, far0, near0 = lax.optimization_barrier((send1, out_t, near1, far0, near0))
    far1 = exchange(add(kept1, send1), 4)
    near1 = exchange(near1, 2)
    out_late, far1, near1 = lax.optimization_barrier((out_t, far1, near1))
    out_near, out_far = exchange(out_late, 2), exchange(out_late, 4)
    (grad_out,) = call(
        functools.partial(backward_kernel, chunk=chunk),
        [shape((n, 3 * rows, HD), BF16)],
        [queries, keys_t, vals, probs, out_t, mine0, mine1, near0, near1, far0, far1],
        scratch=[pltpu.VMEM((image, HD), F32), pltpu.VMEM((image, HD), F32)],
        flops=8 * total * image * HD,
        moved=4 * total * image,
    )
    grad_in = lax.all_to_all(grad_out, "seq", split_axis=0, concat_axis=0, tiled=True)
    out_far, out_near, _ = lax.optimization_barrier((out_far, out_near, grad_out))
    outs = [out_t, out_near, out_far, exchange(out_far, 2)]
    dw_own, dw_other = call(
        weight_grad_kernel,
        [shape((4 * HD, depth), BF16)] * 2,
        [cot0, cot1, *outs],
        scratch=[pltpu.VMEM((4 * HD, image), BF16)],
        flops=96 * image * columns * HD,
        moved=2 * image * columns,
    )
    grads = call(
        unpack_kernel,
        [shape((rows, width), BF16)] * 3,
        [grad_in],
        moved=4 * 3 * rows * width,
    )
    (d_weight,) = call(
        unpack_weight_kernel,
        [shape((depth, width), F32)],
        [dw_own, exchange(dw_other, 1)],
        moved=6 * depth * width,
    )
    return (*grads, d_weight)


def solution(mesh):
    in_specs = (
        P(("group", "seq"), "fsdp"),
        P(("group", "seq"), "fsdp"),
        P(("group", "seq"), "fsdp"),
        P("group", "fsdp"),
        P("group", "fsdp"),
        P("seq", "fsdp"),
        P(("group", "seq"), None),
    )
    out_specs = (
        P(("group", "seq"), "fsdp"),
        P(("group", "seq"), "fsdp"),
        P(("group", "seq"), "fsdp"),
        P(("group", "seq"), "fsdp"),
    )
    return jax.shard_map(local, mesh=mesh, in_specs=in_specs, out_specs=out_specs, check_vma=False)
```

```python
import functools
import math

import jax
import jax.numpy as jnp
from jax import lax
from jax.experimental import pallas as pl
from jax.experimental.pallas import tpu as pltpu
from jax.sharding import PartitionSpec as P

HD = 128
F32 = jnp.float32
BF16 = jnp.bfloat16
LIMIT = 28 * 1024 * 1024
NT = (((1,), (1,)), ((), ()))


def attend(queries, cotangents, key_rows, value_rows, block_rows):
    score_scale = HD ** (-0.5)
    query_count = queries.shape[0]
    block_count = query_count // block_rows
    query_blocks = queries.reshape(block_count, block_rows, HD)
    grad_blocks = cotangents.reshape(block_count, block_rows, HD)

    def one_block(accumulated, pair_item):
        query_block, grad_block = pair_item
        scores = jnp.dot(query_block, key_rows.T, preferred_element_type=jnp.float32) * score_scale
        row_max = jnp.max(scores, axis=1, keepdims=True)
        probs = jnp.exp(scores - row_max)
        probs = probs / jnp.sum(probs, axis=1, keepdims=True)
        probs_low = probs.astype(jnp.bfloat16)
        out_rows = jnp.dot(probs_low, value_rows, preferred_element_type=jnp.float32).astype(
            jnp.bfloat16
        )
        prob_grad = jnp.dot(grad_block, value_rows.T, preferred_element_type=jnp.float32)
        row_dot = jnp.sum(
            grad_block.astype(jnp.float32) * out_rows.astype(jnp.float32), axis=1, keepdims=True
        )
        score_grad = (probs * (prob_grad - row_dot)).astype(jnp.bfloat16)
        query_grad = (
            jnp.dot(score_grad, key_rows, preferred_element_type=jnp.float32) * score_scale
        ).astype(jnp.bfloat16)
        key_grad = (
            accumulated[0]
            + jnp.dot(score_grad.T, query_block, preferred_element_type=jnp.float32) * score_scale
        )
        value_grad = accumulated[1] + jnp.dot(
            probs_low.T, grad_block, preferred_element_type=jnp.float32
        )
        return ((key_grad, value_grad), (query_grad, out_rows))

    empty = jnp.zeros((key_rows.shape[0], HD), jnp.float32)
    (key_grad, value_grad), (query_grad, out_rows) = lax.scan(
        one_block, (empty, empty), (query_blocks, grad_blocks)
    )
    return (
        query_grad.reshape(query_count, HD),
        out_rows.reshape(query_count, HD),
        key_grad,
        value_grad,
    )


def local_general(q_img, k_img, v_img, k_txt, v_txt, out_weight, d_out):
    rows_here = q_img.shape[0]
    heads_here = q_img.shape[1] // HD
    seq_count = lax.axis_size("seq")
    share_count = seq_count // heads_here
    part_rows = rows_here // share_count
    seq_index = lax.axis_index("seq")
    head_index = seq_index // share_count
    column_cut = d_out
    attn_grad = jnp.dot(
        column_cut,
        lax.all_gather(out_weight, "seq", axis=0, tiled=True),
        preferred_element_type=jnp.float32,
    ).astype(jnp.bfloat16)

    def to_heads(array_in):
        shaped = array_in.reshape(share_count, part_rows, heads_here, HD).transpose(2, 0, 1, 3)
        return shaped.reshape(seq_count, part_rows, HD)

    def whole_heads(array_in):
        shaped = array_in.reshape(rows_here, heads_here, HD).transpose(1, 0, 2)
        shaped = jnp.broadcast_to(shaped[:, None], (heads_here, share_count, rows_here, HD))
        return shaped.reshape(seq_count, rows_here, HD)

    def from_heads(array_in):
        shaped = array_in.reshape(heads_here, share_count, part_rows, HD).transpose(1, 2, 0, 3)
        return shaped.reshape(rows_here, heads_here * HD)

    text_keys = lax.dynamic_slice_in_dim(k_txt, head_index * HD, HD, 1)
    text_values = lax.dynamic_slice_in_dim(v_txt, head_index * HD, HD, 1)
    query_side = jnp.concatenate([to_heads(q_img), to_heads(attn_grad)], axis=2)
    key_side = jnp.concatenate([whole_heads(k_img), whole_heads(v_img)], axis=2)
    packed = jnp.concatenate([query_side, key_side], axis=1)
    received = lax.all_to_all(packed, "seq", split_axis=0, concat_axis=0, tiled=True)
    queries = received[:, :part_rows, :HD].reshape(seq_count * part_rows, HD)
    cotangents = received[:, :part_rows, HD:].reshape(seq_count * part_rows, HD)
    image_keys = received[:, part_rows:, :HD].reshape(seq_count * rows_here, HD)
    image_values = received[:, part_rows:, HD:].reshape(seq_count * rows_here, HD)
    key_rows = jnp.concatenate([image_keys, text_keys], axis=0)
    value_rows = jnp.concatenate([image_values, text_values], axis=0)
    query_grad, out_rows, key_grad, value_grad = attend(
        queries, cotangents, key_rows, value_rows, min(512, queries.shape[0])
    )
    image_count = image_keys.shape[0]
    query_part = (
        jnp.concatenate([query_grad, out_rows], axis=1)
        .astype(jnp.float32)
        .reshape(seq_count, part_rows, 2 * HD)
    )
    key_part = jnp.concatenate([key_grad[:image_count], value_grad[:image_count]], axis=1).reshape(
        seq_count, rows_here, 2 * HD
    )
    returned = lax.all_to_all(
        jnp.concatenate([query_part, key_part], axis=1).astype(jnp.bfloat16),
        "seq",
        split_axis=0,
        concat_axis=0,
        tiled=True,
    ).astype(jnp.float32)
    q_grad = from_heads(returned[:, :part_rows, :HD]).astype(jnp.bfloat16)
    out_tok = from_heads(returned[:, :part_rows, HD:]).astype(jnp.bfloat16)
    summed = jnp.sum(
        returned[:, part_rows:, :].reshape(heads_here, share_count, rows_here, 2 * HD), axis=1
    )
    summed = summed.transpose(1, 0, 2)
    k_grad = summed[:, :, :HD].reshape(rows_here, heads_here * HD).astype(jnp.bfloat16)
    v_grad = summed[:, :, HD:].reshape(rows_here, heads_here * HD).astype(jnp.bfloat16)
    column_cut = d_out
    d_weight = lax.psum_scatter(
        jnp.dot(column_cut.T, out_tok, preferred_element_type=jnp.float32).astype(jnp.bfloat16),
        "seq",
        scatter_dimension=0,
        tiled=True,
    ).astype(jnp.float32)
    return (q_grad, k_grad, v_grad, d_weight)


def call(kernel, outs, args, specs=None, scratch=(), scalars=0, out_specs=None, flops=0, moved=0, limit=LIMIT):
    vmem = pl.BlockSpec(memory_space=pltpu.VMEM)
    if specs is None:
        specs = [vmem] * (len(args) - scalars)
    if out_specs is None:
        out_specs = [vmem] * len(outs)
    return pl.pallas_call(
        kernel,
        out_shape=outs,
        grid_spec=pltpu.PrefetchScalarGridSpec(
            num_scalar_prefetch=scalars,
            grid=(1,),
            in_specs=specs,
            out_specs=out_specs,
            scratch_shapes=list(scratch),
        ),
        compiler_params=pltpu.CompilerParams(vmem_limit_bytes=limit),
        cost_estimate=pl.CostEstimate(flops=flops, bytes_accessed=moved, transcendentals=0),
    )(*args)


STEPS = (0, 2, 4, 6)


def head_columns(step, other_row):
    return pl.ds(pl.multiple_of(jnp.bitwise_xor(lax.axis_index("seq"), step + other_row) * HD, HD), HD)


def pack_kernel(q_ref, k_ref, v_ref, tok_ref):
    rows = q_ref.shape[0]
    for h in range(tok_ref.shape[0]):
        for i, ref in enumerate((q_ref, k_ref, v_ref)):
            tok_ref[h, i * rows : (i + 1) * rows, :] = ref[:, h * HD : (h + 1) * HD]


def pack_weight_kernel(me_ref, w_ref, kt_ref, vt_ref, keep_ref, give_ref, text_ref):
    for i, step in enumerate(STEPS):
        cols = slice(i * HD, (i + 1) * HD)
        keep_ref[:, cols] = w_ref[:, head_columns(step, 0)]
        give_ref[:, cols] = w_ref[:, head_columns(step, 1)]
    text_ref[0] = kt_ref[...]
    text_ref[1] = vt_ref[...]


def query_order(n):
    y = lax.rem(lax.axis_index("seq"), 2)
    return [2 * z + y for z in range(n // 2)] + [2 * z + 1 - y for z in range(n // 2)]


def forward_kernel(tok_ref, text_ref, probs_ref, out_ref, queries_ref, keys_t_ref, vals_ref, keys, vals_t, *, chunk):
    n, three, _ = tok_ref.shape
    rows = three // 3
    image = n * rows
    text = text_ref.shape[1]
    for i, source in enumerate(query_order(n)):
        queries_ref[i * rows : (i + 1) * rows, :] = tok_ref[source, 0:rows, :]
    keys[0:image, :] = tok_ref[:, rows : 2 * rows, :].reshape(image, HD)
    keys[image : image + text, :] = text_ref[0]
    vals_ref[0:image, :] = tok_ref[:, 2 * rows : 3 * rows, :].reshape(image, HD)
    vals_ref[image : image + text, :] = text_ref[1]
    keys_t_ref[...] = keys[...].T
    vals_t[...] = vals_ref[...].T
    factor = HD ** (-0.5) * math.log2(math.e)
    for c in range(image // chunk):
        span = slice(c * chunk, (c + 1) * chunk)
        scores = lax.dot_general(keys[...], queries_ref[span, :], NT, preferred_element_type=F32)
        top = jnp.max(scores, axis=0, keepdims=True)
        weights = jnp.exp2((scores - top) * factor)
        total = jnp.sum(weights, axis=0, keepdims=True)
        low = (weights * (1.0 / total)).astype(BF16)
        probs_ref[:, span] = low
        out_ref[:, span] = jnp.dot(vals_t[...], low, preferred_element_type=F32).astype(BF16)


def partial_kernel(piece_ref, swapped_ref, own_ref, other_ref, *refs):
    mine_ref, far_ref, near_ref, send_ref, cot_ref, weight = refs
    me = lax.axis_index("seq")
    core = lax.axis_index("fsdp")
    part = piece_ref.shape[0] // len(STEPS)
    for piece, shift in ((piece_ref, core), (swapped_ref, 1 - core)):
        for i, step in enumerate(STEPS):
            z = jnp.bitwise_xor(me, step) // 2
            at = pl.multiple_of(z * (2 * part) + shift * part, 16)
            cot_ref[pl.ds(at, part), :] = piece[i * part : (i + 1) * part, :]
    depth = own_ref.shape[0]
    y = lax.rem(me, 2)
    weight[pl.ds(pl.multiple_of(y * depth, 16), depth), :] = own_ref[...]
    weight[pl.ds(pl.multiple_of((1 - y) * depth, 16), depth), :] = other_ref[...]
    step = 256

    @pl.loop(0, cot_ref.shape[0] // step)
    def _(i):
        at = pl.ds(pl.multiple_of(i * step, step), step)
        part = jnp.dot(cot_ref[at, :], weight[...], preferred_element_type=F32)
        mine_ref[at, :] = part[:, :HD]
        near_ref[at, :] = part[:, HD : 2 * HD].astype(BF16)
        far_ref[at, :] = part[:, 2 * HD : 3 * HD]
        send_ref[at, :] = part[:, 3 * HD :].astype(BF16)


def weight_grad_kernel(cot0_ref, cot1_ref, *refs):
    *out_refs, own_ref, other_ref, outs = refs
    for i, ref in enumerate(out_refs):
        outs[i * HD : (i + 1) * HD, :] = ref[...]
    depth = own_ref.shape[1]
    tokens = cot0_ref.shape[0]
    y = lax.rem(lax.axis_index("seq"), 2)
    for ref, row in ((own_ref, y), (other_ref, 1 - y)):
        cols = pl.ds(pl.multiple_of(row * depth, HD), depth)
        total = jnp.dot(outs[:, :tokens], cot0_ref[:, cols], preferred_element_type=F32)
        total += jnp.dot(outs[:, tokens:], cot1_ref[:, cols], preferred_element_type=F32)
        ref[...] = total.astype(BF16)


def backward_kernel(queries_ref, keys_t_ref, vals_ref, probs_ref, out_ref, *refs, chunk):
    *grad_refs, send_ref, dk, dv = refs
    n, three, _ = send_ref.shape
    rows = three // 3
    image = n * rows
    scale = HD ** (-0.5)
    per = chunk // rows
    order = query_order(n)
    half = image // chunk // 2
    for c in range(image // chunk):
        span = slice(c * chunk, (c + 1) * chunk)
        within = slice(c % half * chunk, (c % half + 1) * chunk)
        mine_ref, near_ref, far_ref = grad_refs[c // half :: 2]
        grads = mine_ref[within, :] + near_ref[within, :].astype(F32) + far_ref[within, :].astype(F32)
        grads = grads.astype(BF16)
        row_dot = jnp.sum(
            grads.astype(F32).T * out_ref[:, span].astype(F32), axis=0, keepdims=True
        )
        prob_grad = lax.dot_general(vals_ref[...], grads, NT, preferred_element_type=F32)
        low = probs_ref[:, span]
        score_grad = (low.astype(F32) * (prob_grad - row_dot)).astype(BF16)
        dq = (jnp.dot(keys_t_ref[...], score_grad, preferred_element_type=F32) * scale).T.astype(BF16)
        for i in range(per):
            send_ref[order[c * per + i], 0:rows, :] = dq[i * rows : (i + 1) * rows, :]
        dk_part = jnp.dot(score_grad[0:image, :], queries_ref[span, :], preferred_element_type=F32)
        dv_part = jnp.dot(low[0:image, :], grads, preferred_element_type=F32)
        if c == 0:
            dk[...] = dk_part
            dv[...] = dv_part
        else:
            dk[...] += dk_part
            dv[...] += dv_part
    send_ref[:, rows : 2 * rows, :] = (dk[...] * scale).astype(BF16).reshape(n, rows, HD)
    send_ref[:, 2 * rows : 3 * rows, :] = dv[...].astype(BF16).reshape(n, rows, HD)


def unpack_kernel(tok_ref, q_ref, k_ref, v_ref):
    rows = q_ref.shape[0]
    for h in range(tok_ref.shape[0]):
        for i, ref in enumerate((q_ref, k_ref, v_ref)):
            ref[:, h * HD : (h + 1) * HD] = tok_ref[h, i * rows : (i + 1) * rows, :]


def unpack_weight_kernel(own_ref, other_ref, w_ref):
    for other_row, ref in enumerate((own_ref, other_ref)):
        for i, step in enumerate(STEPS):
            w_ref[:, head_columns(step, other_row)] = ref[i * HD : (i + 1) * HD, :].astype(F32).T


def exchange(array, distance=0, cores=False):
    if not distance and not cores:
        return array
    size = 2 * lax.axis_size("seq")
    pairs = [(i, i ^ (2 * distance + int(cores))) for i in range(size)]
    return lax.ppermute(array, ("seq", "fsdp"), pairs)


def send_cotangents(d_out):
    rows, width = d_out.shape
    part, columns = rows // 2, width // len(STEPS)
    z = lax.axis_index("seq") // 2
    first = lax.axis_index("fsdp") * part
    return [
        exchange(lax.dynamic_slice(d_out, (first, (z ^ (step // 2)) * columns), (part, columns)), step)
        for step in STEPS
    ]


def local(q_img, k_img, v_img, k_txt, v_txt, out_weight, d_out):
    n = lax.axis_size("seq")
    rows, width = q_img.shape
    args = (q_img, k_img, v_img, k_txt, v_txt, out_weight, d_out)
    if n != 2 * len(STEPS) or width // HD != n or lax.axis_size("fsdp") != 2 or rows % 32:
        return local_general(*args)
    depth = out_weight.shape[0]
    image = n * rows
    text = k_txt.shape[0]
    total = image + text
    chunk = 2 * rows
    shape = jax.ShapeDtypeStruct
    vmem = pl.BlockSpec(memory_space=pltpu.VMEM)

    head = pl.BlockSpec((text, HD), lambda i, me_ref: (0, me_ref[0]))
    big = 60 * 1024 * 1024
    keep, give, text_head = call(
        pack_weight_kernel,
        [shape((depth, 4 * HD), BF16)] * 2 + [shape((2, text, HD), BF16)],
        [lax.axis_index("seq").astype(jnp.int32)[None], out_weight, k_txt, v_txt],
        specs=[vmem] + [head] * 2,
        scalars=1,
        moved=4 * depth * width,
        limit=big,
    )
    d_out, give = lax.optimization_barrier((d_out, give))
    given = exchange(give, 1)
    along = send_cotangents(d_out)
    (tok_out,) = call(
        pack_kernel,
        [shape((n, 3 * rows, HD), BF16)],
        [q_img, k_img, v_img],
        moved=4 * 3 * rows * width,
        limit=big,
    )
    tok_out, along[1] = lax.optimization_barrier((tok_out, along[1]))
    along, given = lax.optimization_barrier((along, given))
    row = jnp.concatenate(along, axis=0)
    row_swapped = exchange(row, cores=True)
    other_row = exchange(row, 1)
    other_swapped = exchange(other_row, cores=True)
    tok_in = lax.all_to_all(tok_out, "seq", split_axis=0, concat_axis=0, tiled=True)

    probs, out_t, queries, keys_t, vals = call(
        functools.partial(forward_kernel, chunk=chunk),
        [shape(dims, BF16) for dims in ((total, image), (HD, image), (image, HD), (HD, total), (total, HD))],
        [tok_in, text_head],
        scratch=[pltpu.VMEM((total, HD), BF16), pltpu.VMEM((HD, total), BF16)],
        flops=4 * total * image * HD,
        moved=4 * total * image,
    )
    columns = row.shape[1]

    def partial(*operands):
        return call(
            partial_kernel,
            [shape((image // 2, HD), F32)] * 2
            + [shape((image // 2, HD), BF16)] * 2
            + [shape((image // 2, columns), BF16)],
            [*operands, keep, given],
            scratch=[pltpu.VMEM((columns, 4 * HD), BF16)],
            flops=4 * image * columns * HD,
            moved=image * columns,
        )

    def add(kept, received):
        return (kept + received.astype(F32)).astype(BF16)

    mine0, kept0, near0, send0, cot0 = partial(row, row_swapped)
    far0 = exchange(add(kept0, exchange(send0, 2)), 4)
    near0 = exchange(near0, 2)
    mine1, kept1, near1, send1, cot1 = partial(other_row, other_swapped)
    send1, far0, near0, out_t = lax.optimization_barrier((send1, far0, near0, out_t))
    out_far = exchange(out_t, 4)
    send1, near1 = lax.optimization_barrier((exchange(send1, 2), near1))
    far1 = exchange(add(kept1, send1), 4)
    near1 = exchange(near1, 2)
    out_late, far1, near1, out_far = lax.optimization_barrier((out_t, far1, near1, out_far))
    out_near = exchange(out_late, 2)
    (grad_out,) = call(
        functools.partial(backward_kernel, chunk=chunk),
        [shape((n, 3 * rows, HD), BF16)],
        [queries, keys_t, vals, probs, out_t, mine0, mine1, near0, near1, far0, far1],
        scratch=[pltpu.VMEM((image, HD), F32), pltpu.VMEM((image, HD), F32)],
        flops=8 * total * image * HD,
        moved=4 * total * image,
    )
    grad_in = lax.all_to_all(grad_out, "seq", split_axis=0, concat_axis=0, tiled=True)
    out_far, out_near, _ = lax.optimization_barrier((out_far, out_near, grad_out))
    outs = [out_t, out_near, out_far, exchange(out_far, 2)]
    dw_own, dw_other = call(
        weight_grad_kernel,
        [shape((4 * HD, depth), BF16)] * 2,
        [cot0, cot1, *outs],
        scratch=[pltpu.VMEM((4 * HD, image), BF16)],
        flops=96 * image * columns * HD,
        moved=2 * image * columns,
    )
    grads = call(
        unpack_kernel,
        [shape((rows, width), BF16)] * 3,
        [grad_in],
        moved=4 * 3 * rows * width,
    )
    (d_weight,) = call(
        unpack_weight_kernel,
        [shape((depth, width), F32)],
        [dw_own, exchange(dw_other, 1)],
        moved=6 * depth * width,
    )
    return (*grads, d_weight)


def solution(mesh):
    in_specs = (
        P(("group", "seq"), "fsdp"),
        P(("group", "seq"), "fsdp"),
        P(("group", "seq"), "fsdp"),
        P("group", "fsdp"),
        P("group", "fsdp"),
        P("seq", "fsdp"),
        P(("group", "seq"), None),
    )
    out_specs = (
        P(("group", "seq"), "fsdp"),
        P(("group", "seq"), "fsdp"),
        P(("group", "seq"), "fsdp"),
        P(("group", "seq"), "fsdp"),
    )
    return jax.shard_map(local, mesh=mesh, in_specs=in_specs, out_specs=out_specs, check_vma=False)
```

```python
import functools
import math

import jax
import jax.numpy as jnp
from jax import lax
from jax.experimental import pallas as pl
from jax.experimental.pallas import tpu as pltpu
from jax.sharding import PartitionSpec as P

HD = 128
F32 = jnp.float32
BF16 = jnp.bfloat16
LIMIT = 28 * 1024 * 1024
NT = (((1,), (1,)), ((), ()))


def attend(queries, cotangents, key_rows, value_rows, block_rows):
    score_scale = HD ** (-0.5)
    query_count = queries.shape[0]
    block_count = query_count // block_rows
    query_blocks = queries.reshape(block_count, block_rows, HD)
    grad_blocks = cotangents.reshape(block_count, block_rows, HD)

    def one_block(accumulated, pair_item):
        query_block, grad_block = pair_item
        scores = jnp.dot(query_block, key_rows.T, preferred_element_type=jnp.float32) * score_scale
        row_max = jnp.max(scores, axis=1, keepdims=True)
        probs = jnp.exp(scores - row_max)
        probs = probs / jnp.sum(probs, axis=1, keepdims=True)
        probs_low = probs.astype(jnp.bfloat16)
        out_rows = jnp.dot(probs_low, value_rows, preferred_element_type=jnp.float32).astype(
            jnp.bfloat16
        )
        prob_grad = jnp.dot(grad_block, value_rows.T, preferred_element_type=jnp.float32)
        row_dot = jnp.sum(
            grad_block.astype(jnp.float32) * out_rows.astype(jnp.float32), axis=1, keepdims=True
        )
        score_grad = (probs * (prob_grad - row_dot)).astype(jnp.bfloat16)
        query_grad = (
            jnp.dot(score_grad, key_rows, preferred_element_type=jnp.float32) * score_scale
        ).astype(jnp.bfloat16)
        key_grad = (
            accumulated[0]
            + jnp.dot(score_grad.T, query_block, preferred_element_type=jnp.float32) * score_scale
        )
        value_grad = accumulated[1] + jnp.dot(
            probs_low.T, grad_block, preferred_element_type=jnp.float32
        )
        return ((key_grad, value_grad), (query_grad, out_rows))

    empty = jnp.zeros((key_rows.shape[0], HD), jnp.float32)
    (key_grad, value_grad), (query_grad, out_rows) = lax.scan(
        one_block, (empty, empty), (query_blocks, grad_blocks)
    )
    return (
        query_grad.reshape(query_count, HD),
        out_rows.reshape(query_count, HD),
        key_grad,
        value_grad,
    )


def local_general(q_img, k_img, v_img, k_txt, v_txt, out_weight, d_out):
    rows_here = q_img.shape[0]
    heads_here = q_img.shape[1] // HD
    seq_count = lax.axis_size("seq")
    share_count = seq_count // heads_here
    part_rows = rows_here // share_count
    seq_index = lax.axis_index("seq")
    head_index = seq_index // share_count
    column_cut = d_out
    attn_grad = jnp.dot(
        column_cut,
        lax.all_gather(out_weight, "seq", axis=0, tiled=True),
        preferred_element_type=jnp.float32,
    ).astype(jnp.bfloat16)

    def to_heads(array_in):
        shaped = array_in.reshape(share_count, part_rows, heads_here, HD).transpose(2, 0, 1, 3)
        return shaped.reshape(seq_count, part_rows, HD)

    def whole_heads(array_in):
        shaped = array_in.reshape(rows_here, heads_here, HD).transpose(1, 0, 2)
        shaped = jnp.broadcast_to(shaped[:, None], (heads_here, share_count, rows_here, HD))
        return shaped.reshape(seq_count, rows_here, HD)

    def from_heads(array_in):
        shaped = array_in.reshape(heads_here, share_count, part_rows, HD).transpose(1, 2, 0, 3)
        return shaped.reshape(rows_here, heads_here * HD)

    text_keys = lax.dynamic_slice_in_dim(k_txt, head_index * HD, HD, 1)
    text_values = lax.dynamic_slice_in_dim(v_txt, head_index * HD, HD, 1)
    query_side = jnp.concatenate([to_heads(q_img), to_heads(attn_grad)], axis=2)
    key_side = jnp.concatenate([whole_heads(k_img), whole_heads(v_img)], axis=2)
    packed = jnp.concatenate([query_side, key_side], axis=1)
    received = lax.all_to_all(packed, "seq", split_axis=0, concat_axis=0, tiled=True)
    queries = received[:, :part_rows, :HD].reshape(seq_count * part_rows, HD)
    cotangents = received[:, :part_rows, HD:].reshape(seq_count * part_rows, HD)
    image_keys = received[:, part_rows:, :HD].reshape(seq_count * rows_here, HD)
    image_values = received[:, part_rows:, HD:].reshape(seq_count * rows_here, HD)
    key_rows = jnp.concatenate([image_keys, text_keys], axis=0)
    value_rows = jnp.concatenate([image_values, text_values], axis=0)
    query_grad, out_rows, key_grad, value_grad = attend(
        queries, cotangents, key_rows, value_rows, min(512, queries.shape[0])
    )
    image_count = image_keys.shape[0]
    query_part = (
        jnp.concatenate([query_grad, out_rows], axis=1)
        .astype(jnp.float32)
        .reshape(seq_count, part_rows, 2 * HD)
    )
    key_part = jnp.concatenate([key_grad[:image_count], value_grad[:image_count]], axis=1).reshape(
        seq_count, rows_here, 2 * HD
    )
    returned = lax.all_to_all(
        jnp.concatenate([query_part, key_part], axis=1).astype(jnp.bfloat16),
        "seq",
        split_axis=0,
        concat_axis=0,
        tiled=True,
    ).astype(jnp.float32)
    q_grad = from_heads(returned[:, :part_rows, :HD]).astype(jnp.bfloat16)
    out_tok = from_heads(returned[:, :part_rows, HD:]).astype(jnp.bfloat16)
    summed = jnp.sum(
        returned[:, part_rows:, :].reshape(heads_here, share_count, rows_here, 2 * HD), axis=1
    )
    summed = summed.transpose(1, 0, 2)
    k_grad = summed[:, :, :HD].reshape(rows_here, heads_here * HD).astype(jnp.bfloat16)
    v_grad = summed[:, :, HD:].reshape(rows_here, heads_here * HD).astype(jnp.bfloat16)
    column_cut = d_out
    d_weight = lax.psum_scatter(
        jnp.dot(column_cut.T, out_tok, preferred_element_type=jnp.float32).astype(jnp.bfloat16),
        "seq",
        scatter_dimension=0,
        tiled=True,
    ).astype(jnp.float32)
    return (q_grad, k_grad, v_grad, d_weight)


def call(kernel, outs, args, specs=None, scratch=(), scalars=0, out_specs=None, flops=0, moved=0, limit=LIMIT):
    vmem = pl.BlockSpec(memory_space=pltpu.VMEM)
    if specs is None:
        specs = [vmem] * (len(args) - scalars)
    if out_specs is None:
        out_specs = [vmem] * len(outs)
    return pl.pallas_call(
        kernel,
        out_shape=outs,
        grid_spec=pltpu.PrefetchScalarGridSpec(
            num_scalar_prefetch=scalars,
            grid=(1,),
            in_specs=specs,
            out_specs=out_specs,
            scratch_shapes=list(scratch),
        ),
        compiler_params=pltpu.CompilerParams(vmem_limit_bytes=limit),
        cost_estimate=pl.CostEstimate(flops=flops, bytes_accessed=moved, transcendentals=0),
    )(*args)


STEPS = (0, 2, 4, 6)


def head_columns(step, other_row):
    return pl.ds(pl.multiple_of(jnp.bitwise_xor(lax.axis_index("seq"), step + other_row) * HD, HD), HD)


def pack_kernel(me_ref, q_ref, k_ref, v_ref, kt_ref, vt_ref, tok_ref, text_ref):
    rows = q_ref.shape[0]
    for h in range(tok_ref.shape[0]):
        for i, ref in enumerate((q_ref, k_ref, v_ref)):
            tok_ref[h, i * rows : (i + 1) * rows, :] = ref[:, h * HD : (h + 1) * HD]
    text_ref[0] = kt_ref[...]
    text_ref[1] = vt_ref[...]


def query_order(n):
    y = lax.rem(lax.axis_index("seq"), 2)
    return [2 * z + y for z in range(n // 2)] + [2 * z + 1 - y for z in range(n // 2)]


def forward_kernel(tok_ref, text_ref, probs_ref, out_ref, queries_ref, keys_t_ref, vals_ref, keys, vals_t, *, chunk):
    n, three, _ = tok_ref.shape
    rows = three // 3
    image = n * rows
    text = text_ref.shape[1]
    for i, source in enumerate(query_order(n)):
        queries_ref[i * rows : (i + 1) * rows, :] = tok_ref[source, 0:rows, :]
    keys[0:image, :] = tok_ref[:, rows : 2 * rows, :].reshape(image, HD)
    keys[image : image + text, :] = text_ref[0]
    vals_ref[0:image, :] = tok_ref[:, 2 * rows : 3 * rows, :].reshape(image, HD)
    vals_ref[image : image + text, :] = text_ref[1]
    keys_t_ref[...] = keys[...].T
    vals_t[...] = vals_ref[...].T
    factor = HD ** (-0.5) * math.log2(math.e)
    for c in range(image // chunk):
        span = slice(c * chunk, (c + 1) * chunk)
        scores = lax.dot_general(keys[...], queries_ref[span, :], NT, preferred_element_type=F32)
        top = jnp.max(scores, axis=0, keepdims=True)
        weights = jnp.exp2((scores - top) * factor)
        total = jnp.sum(weights, axis=0, keepdims=True)
        low = (weights * (1.0 / total)).astype(BF16)
        probs_ref[:, span] = low
        out_ref[:, span] = jnp.dot(vals_t[...], low, preferred_element_type=F32).astype(BF16)


def place_rows(piece_ref, swapped_ref, cot, start):
    me = lax.axis_index("seq")
    core = lax.axis_index("fsdp")
    part = piece_ref.shape[0] // len(STEPS)
    for piece, shift in ((piece_ref, core), (swapped_ref, 1 - core)):
        for i, step in enumerate(STEPS):
            z = jnp.bitwise_xor(me, step) // 2
            at = pl.multiple_of(start + z * (2 * part) + shift * part, 16)
            cot[pl.ds(at, part), :] = piece[i * part : (i + 1) * part, :]


def partial_kernel(piece_ref, swapped_ref, own_ref, other_ref, mine_ref, near_ref, far_ref, send_ref, cot, weight):
    place_rows(piece_ref, swapped_ref, cot, 0)
    me = lax.axis_index("seq")
    depth = own_ref.shape[0]
    y = lax.rem(me, 2)
    weight[pl.ds(pl.multiple_of(y * depth, 16), depth), :] = own_ref[...]
    weight[pl.ds(pl.multiple_of((1 - y) * depth, 16), depth), :] = other_ref[...]
    for step, ref in zip(STEPS, (mine_ref, near_ref, far_ref, send_ref)):
        z = jnp.bitwise_xor(me, step) // 2
        cols = pl.ds(pl.multiple_of(z * 2 * HD, 2 * HD), 2 * HD)
        ref[...] = jnp.dot(cot[...], weight[:, cols], preferred_element_type=F32).astype(ref.dtype)


def weight_grad_kernel(*refs):
    *pieces, out0, out1, out2, out3, own_ref, other_ref, cot, outs = refs
    tokens = cot.shape[0]
    place_rows(pieces[0], pieces[1], cot, 0)
    place_rows(pieces[2], pieces[3], cot, tokens // 2)
    for i, ref in enumerate((out0, out1, out2, out3)):
        outs[i * HD : (i + 1) * HD, :] = ref[...]
    depth = own_ref.shape[1]
    y = lax.rem(lax.axis_index("seq"), 2)
    for ref, row in ((own_ref, y), (other_ref, 1 - y)):
        cols = pl.ds(pl.multiple_of(row * depth, HD), depth)
        ref[...] = jnp.dot(outs[...], cot[:, cols], preferred_element_type=F32).astype(BF16)


def backward_kernel(queries_ref, keys_t_ref, vals_ref, probs_ref, out_ref, *refs, chunk):
    *grad_refs, send_ref, dk, dv = refs
    n, three, _ = send_ref.shape
    rows = three // 3
    image = n * rows
    scale = HD ** (-0.5)
    per = chunk // rows
    order = query_order(n)
    half = image // chunk // 2
    for c in range(image // chunk):
        span = slice(c * chunk, (c + 1) * chunk)
        within = slice(c % half * chunk, (c % half + 1) * chunk)
        grads = grad_refs[c // half][within, :]
        row_dot = jnp.sum(
            grads.astype(F32).T * out_ref[:, span].astype(F32), axis=0, keepdims=True
        )
        prob_grad = lax.dot_general(vals_ref[...], grads, NT, preferred_element_type=F32)
        low = probs_ref[:, span]
        score_grad = (low.astype(F32) * (prob_grad - row_dot)).astype(BF16)
        dq = (jnp.dot(keys_t_ref[...], score_grad, preferred_element_type=F32) * scale).T.astype(BF16)
        for i in range(per):
            send_ref[order[c * per + i], 0:rows, :] = dq[i * rows : (i + 1) * rows, :]
        dk_part = jnp.dot(score_grad[0:image, :], queries_ref[span, :], preferred_element_type=F32)
        dv_part = jnp.dot(low[0:image, :], grads, preferred_element_type=F32)
        if c == 0:
            dk[...] = dk_part
            dv[...] = dv_part
        else:
            dk[...] += dk_part
            dv[...] += dv_part
    send_ref[:, rows : 2 * rows, :] = (dk[...] * scale).astype(BF16).reshape(n, rows, HD)
    send_ref[:, 2 * rows : 3 * rows, :] = dv[...].astype(BF16).reshape(n, rows, HD)


def unpack_kernel(tok_ref, q_ref, k_ref, v_ref):
    rows = q_ref.shape[0]
    for h in range(tok_ref.shape[0]):
        for i, ref in enumerate((q_ref, k_ref, v_ref)):
            ref[:, h * HD : (h + 1) * HD] = tok_ref[h, i * rows : (i + 1) * rows, :]


def unpack_weight_kernel(own_ref, other_ref, w_ref):
    for other_row, ref in enumerate((own_ref, other_ref)):
        for i, step in enumerate(STEPS):
            w_ref[:, head_columns(step, other_row)] = ref[i * HD : (i + 1) * HD, :].astype(F32).T


def exchange(array, distance=0, cores=False):
    if not distance and not cores:
        return array
    size = 2 * lax.axis_size("seq")
    pairs = [(i, i ^ (2 * distance + int(cores))) for i in range(size)]
    return lax.ppermute(array, ("seq", "fsdp"), pairs)


def send_cotangents(d_out):
    rows, width = d_out.shape
    part, columns = rows // 2, width // len(STEPS)
    z = lax.axis_index("seq") // 2
    first = lax.axis_index("fsdp") * part
    return [
        exchange(lax.dynamic_slice(d_out, (first, (z ^ (step // 2)) * columns), (part, columns)), step)
        for step in STEPS
    ]


def local(q_img, k_img, v_img, k_txt, v_txt, out_weight, d_out):
    n = lax.axis_size("seq")
    rows, width = q_img.shape
    args = (q_img, k_img, v_img, k_txt, v_txt, out_weight, d_out)
    if n != 2 * len(STEPS) or width // HD != n or lax.axis_size("fsdp") != 2 or rows % 32:
        return local_general(*args)
    depth = out_weight.shape[0]
    image = n * rows
    text = k_txt.shape[0]
    total = image + text
    chunk = 2 * rows
    shape = jax.ShapeDtypeStruct
    vmem = pl.BlockSpec(memory_space=pltpu.VMEM)

    head = pl.BlockSpec((text, HD), lambda i, me_ref: (0, me_ref[0]))
    given = exchange(out_weight, 1)
    along = send_cotangents(d_out)
    tok_out, text_head = call(
        pack_kernel,
        [shape((n, 3 * rows, HD), BF16), shape((2, text, HD), BF16)],
        [lax.axis_index("seq").astype(jnp.int32)[None], q_img, k_img, v_img, k_txt, v_txt],
        specs=[vmem] * 3 + [head] * 2,
        scalars=1,
        moved=4 * 3 * rows * width,
        limit=60 * 1024 * 1024,
    )
    tok_out, along[1] = lax.optimization_barrier((tok_out, along[1]))
    along, given = lax.optimization_barrier((along, given))
    row = jnp.concatenate(along, axis=0)
    row_swapped = exchange(row, cores=True)
    tok_in = lax.all_to_all(tok_out, "seq", split_axis=0, concat_axis=0, tiled=True)

    probs, out_t, queries, keys_t, vals = call(
        functools.partial(forward_kernel, chunk=chunk),
        [shape(dims, BF16) for dims in ((total, image), (HD, image), (image, HD), (HD, total), (total, HD))],
        [tok_in, text_head],
        scratch=[pltpu.VMEM((total, HD), BF16), pltpu.VMEM((HD, total), BF16)],
        flops=4 * total * image * HD,
        moved=4 * total * image,
    )
    columns = row.shape[1]
    mine, near, far, send = call(
        partial_kernel,
        [shape((image // 2, 2 * HD), kind) for kind in (F32, BF16, F32, BF16)],
        [row, row_swapped, out_weight, given],
        scratch=[pltpu.VMEM((image // 2, columns), BF16), pltpu.VMEM((columns, width), BF16)],
        flops=8 * image * columns * HD,
        moved=2 * image * columns,
    )
    send, out_t, near = lax.optimization_barrier((exchange(send, 2), out_t, near))
    far = exchange((far + send.astype(F32)).astype(BF16), 4)
    near = exchange(near, 2)
    heads = mine + near.astype(F32) + far.astype(F32)
    first_row = lax.axis_index("seq") % 2 == 0
    kept = jnp.where(first_row, heads[:, :HD], heads[:, HD:]).astype(BF16)
    got = exchange(jnp.where(first_row, heads[:, HD:], heads[:, :HD]).astype(BF16), 1)
    row, _ = lax.optimization_barrier((row, out_t))
    other_row = exchange(row, 1)
    out_late, got, other_row = lax.optimization_barrier((out_t, got, other_row))
    other_swapped = exchange(other_row, cores=True)
    out_near, out_far = exchange(out_late, 2), exchange(out_late, 4)
    (grad_out,) = call(
        functools.partial(backward_kernel, chunk=chunk),
        [shape((n, 3 * rows, HD), BF16)],
        [queries, keys_t, vals, probs, out_t, kept, got],
        scratch=[pltpu.VMEM((image, HD), F32), pltpu.VMEM((image, HD), F32)],
        flops=8 * total * image * HD,
        moved=4 * total * image,
    )
    grad_in = lax.all_to_all(grad_out, "seq", split_axis=0, concat_axis=0, tiled=True)
    out_far, out_near, _ = lax.optimization_barrier((out_far, out_near, grad_out))
    outs = [out_t, out_near, out_far, exchange(out_far, 2)]
    dw_own, dw_other = call(
        weight_grad_kernel,
        [shape((4 * HD, depth), BF16)] * 2,
        [row, row_swapped, other_row, other_swapped, *outs],
        scratch=[pltpu.VMEM((image, columns), BF16), pltpu.VMEM((4 * HD, image), BF16)],
        flops=96 * image * columns * HD,
        moved=2 * image * columns,
    )
    grads = call(
        unpack_kernel,
        [shape((rows, width), BF16)] * 3,
        [grad_in],
        moved=4 * 3 * rows * width,
    )
    (d_weight,) = call(
        unpack_weight_kernel,
        [shape((depth, width), F32)],
        [dw_own, exchange(dw_other, 1)],
        moved=6 * depth * width,
    )
    return (*grads, d_weight)


def solution(mesh):
    in_specs = (
        P(("group", "seq"), "fsdp"),
        P(("group", "seq"), "fsdp"),
        P(("group", "seq"), "fsdp"),
        P("group", "fsdp"),
        P("group", "fsdp"),
        P("seq", "fsdp"),
        P(("group", "seq"), None),
    )
    out_specs = (
        P(("group", "seq"), "fsdp"),
        P(("group", "seq"), "fsdp"),
        P(("group", "seq"), "fsdp"),
        P(("group", "seq"), "fsdp"),
    )
    return jax.shard_map(local, mesh=mesh, in_specs=in_specs, out_specs=out_specs, check_vma=False)
```

```python
import functools
import math

import jax
import jax.numpy as jnp
from jax import lax
from jax.experimental import pallas as pl
from jax.experimental.pallas import tpu as pltpu
from jax.sharding import PartitionSpec as P

HD = 128
F32 = jnp.float32
BF16 = jnp.bfloat16
LIMIT = 16 * 1024 * 1024
NT = (((1,), (1,)), ((), ()))


def attend(queries, cotangents, key_rows, value_rows, block_rows):
    score_scale = HD ** (-0.5)
    query_count = queries.shape[0]
    block_count = query_count // block_rows
    query_blocks = queries.reshape(block_count, block_rows, HD)
    grad_blocks = cotangents.reshape(block_count, block_rows, HD)

    def one_block(accumulated, pair_item):
        query_block, grad_block = pair_item
        scores = jnp.dot(query_block, key_rows.T, preferred_element_type=jnp.float32) * score_scale
        row_max = jnp.max(scores, axis=1, keepdims=True)
        probs = jnp.exp(scores - row_max)
        probs = probs / jnp.sum(probs, axis=1, keepdims=True)
        probs_low = probs.astype(jnp.bfloat16)
        out_rows = jnp.dot(probs_low, value_rows, preferred_element_type=jnp.float32).astype(
            jnp.bfloat16
        )
        prob_grad = jnp.dot(grad_block, value_rows.T, preferred_element_type=jnp.float32)
        row_dot = jnp.sum(
            grad_block.astype(jnp.float32) * out_rows.astype(jnp.float32), axis=1, keepdims=True
        )
        score_grad = (probs * (prob_grad - row_dot)).astype(jnp.bfloat16)
        query_grad = (
            jnp.dot(score_grad, key_rows, preferred_element_type=jnp.float32) * score_scale
        ).astype(jnp.bfloat16)
        key_grad = (
            accumulated[0]
            + jnp.dot(score_grad.T, query_block, preferred_element_type=jnp.float32) * score_scale
        )
        value_grad = accumulated[1] + jnp.dot(
            probs_low.T, grad_block, preferred_element_type=jnp.float32
        )
        return ((key_grad, value_grad), (query_grad, out_rows))

    empty = jnp.zeros((key_rows.shape[0], HD), jnp.float32)
    (key_grad, value_grad), (query_grad, out_rows) = lax.scan(
        one_block, (empty, empty), (query_blocks, grad_blocks)
    )
    return (
        query_grad.reshape(query_count, HD),
        out_rows.reshape(query_count, HD),
        key_grad,
        value_grad,
    )


def local_general(q_img, k_img, v_img, k_txt, v_txt, out_weight, d_out):
    rows_here = q_img.shape[0]
    heads_here = q_img.shape[1] // HD
    seq_count = lax.axis_size("seq")
    share_count = seq_count // heads_here
    part_rows = rows_here // share_count
    seq_index = lax.axis_index("seq")
    head_index = seq_index // share_count
    column_cut = d_out
    attn_grad = jnp.dot(
        column_cut,
        lax.all_gather(out_weight, "seq", axis=0, tiled=True),
        preferred_element_type=jnp.float32,
    ).astype(jnp.bfloat16)

    def to_heads(array_in):
        shaped = array_in.reshape(share_count, part_rows, heads_here, HD).transpose(2, 0, 1, 3)
        return shaped.reshape(seq_count, part_rows, HD)

    def whole_heads(array_in):
        shaped = array_in.reshape(rows_here, heads_here, HD).transpose(1, 0, 2)
        shaped = jnp.broadcast_to(shaped[:, None], (heads_here, share_count, rows_here, HD))
        return shaped.reshape(seq_count, rows_here, HD)

    def from_heads(array_in):
        shaped = array_in.reshape(heads_here, share_count, part_rows, HD).transpose(1, 2, 0, 3)
        return shaped.reshape(rows_here, heads_here * HD)

    text_keys = lax.dynamic_slice_in_dim(k_txt, head_index * HD, HD, 1)
    text_values = lax.dynamic_slice_in_dim(v_txt, head_index * HD, HD, 1)
    query_side = jnp.concatenate([to_heads(q_img), to_heads(attn_grad)], axis=2)
    key_side = jnp.concatenate([whole_heads(k_img), whole_heads(v_img)], axis=2)
    packed = jnp.concatenate([query_side, key_side], axis=1)
    received = lax.all_to_all(packed, "seq", split_axis=0, concat_axis=0, tiled=True)
    queries = received[:, :part_rows, :HD].reshape(seq_count * part_rows, HD)
    cotangents = received[:, :part_rows, HD:].reshape(seq_count * part_rows, HD)
    image_keys = received[:, part_rows:, :HD].reshape(seq_count * rows_here, HD)
    image_values = received[:, part_rows:, HD:].reshape(seq_count * rows_here, HD)
    key_rows = jnp.concatenate([image_keys, text_keys], axis=0)
    value_rows = jnp.concatenate([image_values, text_values], axis=0)
    query_grad, out_rows, key_grad, value_grad = attend(
        queries, cotangents, key_rows, value_rows, min(512, queries.shape[0])
    )
    image_count = image_keys.shape[0]
    query_part = (
        jnp.concatenate([query_grad, out_rows], axis=1)
        .astype(jnp.float32)
        .reshape(seq_count, part_rows, 2 * HD)
    )
    key_part = jnp.concatenate([key_grad[:image_count], value_grad[:image_count]], axis=1).reshape(
        seq_count, rows_here, 2 * HD
    )
    returned = lax.all_to_all(
        jnp.concatenate([query_part, key_part], axis=1).astype(jnp.bfloat16),
        "seq",
        split_axis=0,
        concat_axis=0,
        tiled=True,
    ).astype(jnp.float32)
    q_grad = from_heads(returned[:, :part_rows, :HD]).astype(jnp.bfloat16)
    out_tok = from_heads(returned[:, :part_rows, HD:]).astype(jnp.bfloat16)
    summed = jnp.sum(
        returned[:, part_rows:, :].reshape(heads_here, share_count, rows_here, 2 * HD), axis=1
    )
    summed = summed.transpose(1, 0, 2)
    k_grad = summed[:, :, :HD].reshape(rows_here, heads_here * HD).astype(jnp.bfloat16)
    v_grad = summed[:, :, HD:].reshape(rows_here, heads_here * HD).astype(jnp.bfloat16)
    column_cut = d_out
    d_weight = lax.psum_scatter(
        jnp.dot(column_cut.T, out_tok, preferred_element_type=jnp.float32).astype(jnp.bfloat16),
        "seq",
        scatter_dimension=0,
        tiled=True,
    ).astype(jnp.float32)
    return (q_grad, k_grad, v_grad, d_weight)


def call(kernel, outs, args, specs=None, scratch=(), scalars=0, out_specs=None, flops=0, moved=0, limit=LIMIT):
    vmem = pl.BlockSpec(memory_space=pltpu.VMEM)
    if specs is None:
        specs = [vmem] * (len(args) - scalars)
    if out_specs is None:
        out_specs = [vmem] * len(outs)
    return pl.pallas_call(
        kernel,
        out_shape=outs,
        grid_spec=pltpu.PrefetchScalarGridSpec(
            num_scalar_prefetch=scalars,
            grid=(1,),
            in_specs=specs,
            out_specs=out_specs,
            scratch_shapes=list(scratch),
        ),
        compiler_params=pltpu.CompilerParams(vmem_limit_bytes=limit),
        cost_estimate=pl.CostEstimate(flops=flops, bytes_accessed=moved, transcendentals=0),
    )(*args)


STEPS = (0, 2, 4, 6)


def head_columns(step, other_row):
    return pl.ds(pl.multiple_of(jnp.bitwise_xor(lax.axis_index("seq"), step + other_row) * HD, HD), HD)


def pack_kernel(me_ref, q_ref, k_ref, v_ref, kt_ref, vt_ref, tok_ref, text_ref):
    rows = q_ref.shape[0]
    for h in range(tok_ref.shape[0]):
        for i, ref in enumerate((q_ref, k_ref, v_ref)):
            tok_ref[h, i * rows : (i + 1) * rows, :] = ref[:, h * HD : (h + 1) * HD]
    text_ref[0] = kt_ref[...]
    text_ref[1] = vt_ref[...]


def query_order(n):
    y = lax.rem(lax.axis_index("seq"), 2)
    return [2 * z + y for z in range(n // 2)] + [2 * z + 1 - y for z in range(n // 2)]


def forward_kernel(tok_ref, text_ref, probs_ref, out_ref, queries_ref, keys_t_ref, vals_ref, keys, vals_t, *, chunk):
    n, three, _ = tok_ref.shape
    rows = three // 3
    image = n * rows
    text = text_ref.shape[1]
    for i, source in enumerate(query_order(n)):
        queries_ref[i * rows : (i + 1) * rows, :] = tok_ref[source, 0:rows, :]
    keys[0:image, :] = tok_ref[:, rows : 2 * rows, :].reshape(image, HD)
    keys[image : image + text, :] = text_ref[0]
    vals_ref[0:image, :] = tok_ref[:, 2 * rows : 3 * rows, :].reshape(image, HD)
    vals_ref[image : image + text, :] = text_ref[1]
    keys_t_ref[...] = keys[...].T
    vals_t[...] = vals_ref[...].T
    factor = HD ** (-0.5) * math.log2(math.e)
    for c in range(image // chunk):
        span = slice(c * chunk, (c + 1) * chunk)
        scores = lax.dot_general(keys[...], queries_ref[span, :], NT, preferred_element_type=F32)
        top = jnp.max(scores, axis=0, keepdims=True)
        weights = jnp.exp2((scores - top) * factor)
        total = jnp.sum(weights, axis=0, keepdims=True)
        low = (weights * (1.0 / total)).astype(BF16)
        probs_ref[:, span] = low
        out_ref[:, span] = jnp.dot(vals_t[...], low, preferred_element_type=F32).astype(BF16)


def place_rows(piece_ref, swapped_ref, cot, start):
    me = lax.axis_index("seq")
    core = lax.axis_index("fsdp")
    part = piece_ref.shape[0] // len(STEPS)
    for piece, shift in ((piece_ref, core), (swapped_ref, 1 - core)):
        for i, step in enumerate(STEPS):
            z = jnp.bitwise_xor(me, step) // 2
            at = pl.multiple_of(start + z * (2 * part) + shift * part, 16)
            cot[pl.ds(at, part), :] = piece[i * part : (i + 1) * part, :]


def partial_kernel(piece_ref, swapped_ref, own_ref, other_ref, mine_ref, near_ref, far_ref, send_ref, cot, weight):
    place_rows(piece_ref, swapped_ref, cot, 0)
    me = lax.axis_index("seq")
    depth = own_ref.shape[0]
    y = lax.rem(me, 2)
    weight[pl.ds(pl.multiple_of(y * depth, 16), depth), :] = own_ref[...]
    weight[pl.ds(pl.multiple_of((1 - y) * depth, 16), depth), :] = other_ref[...]
    for step, ref in zip(STEPS, (mine_ref, near_ref, far_ref, send_ref)):
        z = jnp.bitwise_xor(me, step) // 2
        cols = pl.ds(pl.multiple_of(z * 2 * HD, 2 * HD), 2 * HD)
        ref[...] = jnp.dot(cot[...], weight[:, cols], preferred_element_type=F32).astype(ref.dtype)


def weight_grad_kernel(*refs):
    *pieces, out0, out1, out2, out3, own_ref, other_ref, cot, outs = refs
    tokens = cot.shape[0]
    place_rows(pieces[0], pieces[1], cot, 0)
    place_rows(pieces[2], pieces[3], cot, tokens // 2)
    for i, ref in enumerate((out0, out1, out2, out3)):
        outs[i * HD : (i + 1) * HD, :] = ref[...]
    depth = own_ref.shape[1]
    y = lax.rem(lax.axis_index("seq"), 2)
    for ref, row in ((own_ref, y), (other_ref, 1 - y)):
        cols = pl.ds(pl.multiple_of(row * depth, HD), depth)
        ref[...] = jnp.dot(outs[...], cot[:, cols], preferred_element_type=F32).astype(BF16)


def backward_kernel(queries_ref, keys_t_ref, vals_ref, probs_ref, out_ref, *refs, chunk):
    *grad_refs, send_ref, dk, dv = refs
    n, three, _ = send_ref.shape
    rows = three // 3
    image = n * rows
    scale = HD ** (-0.5)
    per = chunk // rows
    order = query_order(n)
    half = image // chunk // 2
    for c in range(image // chunk):
        span = slice(c * chunk, (c + 1) * chunk)
        within = slice(c % half * chunk, (c % half + 1) * chunk)
        grads = grad_refs[c // half][within, :]
        row_dot = jnp.sum(
            grads.astype(F32).T * out_ref[:, span].astype(F32), axis=0, keepdims=True
        )
        prob_grad = lax.dot_general(vals_ref[...], grads, NT, preferred_element_type=F32)
        low = probs_ref[:, span]
        score_grad = (low.astype(F32) * (prob_grad - row_dot)).astype(BF16)
        dq = (jnp.dot(keys_t_ref[...], score_grad, preferred_element_type=F32) * scale).T.astype(BF16)
        for i in range(per):
            send_ref[order[c * per + i], 0:rows, :] = dq[i * rows : (i + 1) * rows, :]
        dk_part = jnp.dot(score_grad[0:image, :], queries_ref[span, :], preferred_element_type=F32)
        dv_part = jnp.dot(low[0:image, :], grads, preferred_element_type=F32)
        if c == 0:
            dk[...] = dk_part
            dv[...] = dv_part
        else:
            dk[...] += dk_part
            dv[...] += dv_part
    send_ref[:, rows : 2 * rows, :] = (dk[...] * scale).astype(BF16).reshape(n, rows, HD)
    send_ref[:, 2 * rows : 3 * rows, :] = dv[...].astype(BF16).reshape(n, rows, HD)


def unpack_kernel(tok_ref, q_ref, k_ref, v_ref):
    rows = q_ref.shape[0]
    for h in range(tok_ref.shape[0]):
        for i, ref in enumerate((q_ref, k_ref, v_ref)):
            ref[:, h * HD : (h + 1) * HD] = tok_ref[h, i * rows : (i + 1) * rows, :]


def unpack_weight_kernel(own_ref, other_ref, w_ref):
    for other_row, ref in enumerate((own_ref, other_ref)):
        for i, step in enumerate(STEPS):
            w_ref[:, head_columns(step, other_row)] = ref[i * HD : (i + 1) * HD, :].astype(F32).T


def exchange(array, distance=0, cores=False):
    if not distance and not cores:
        return array
    size = 2 * lax.axis_size("seq")
    pairs = [(i, i ^ (2 * distance + int(cores))) for i in range(size)]
    return lax.ppermute(array, ("seq", "fsdp"), pairs)


def send_cotangents(d_out):
    rows, width = d_out.shape
    part, columns = rows // 2, width // len(STEPS)
    z = lax.axis_index("seq") // 2
    first = lax.axis_index("fsdp") * part
    return [
        exchange(lax.dynamic_slice(d_out, (first, (z ^ (step // 2)) * columns), (part, columns)), step)
        for step in STEPS
    ]


def local(q_img, k_img, v_img, k_txt, v_txt, out_weight, d_out):
    n = lax.axis_size("seq")
    rows, width = q_img.shape
    args = (q_img, k_img, v_img, k_txt, v_txt, out_weight, d_out)
    if n != 2 * len(STEPS) or width // HD != n or lax.axis_size("fsdp") != 2 or rows % 32:
        return local_general(*args)
    depth = out_weight.shape[0]
    image = n * rows
    text = k_txt.shape[0]
    total = image + text
    chunk = 2 * rows
    shape = jax.ShapeDtypeStruct
    vmem = pl.BlockSpec(memory_space=pltpu.VMEM)

    head = pl.BlockSpec((text, HD), lambda i, me_ref: (0, me_ref[0]))
    given = exchange(out_weight, 1)
    along = send_cotangents(d_out)
    tok_out, text_head = call(
        pack_kernel,
        [shape((n, 3 * rows, HD), BF16), shape((2, text, HD), BF16)],
        [lax.axis_index("seq").astype(jnp.int32)[None], q_img, k_img, v_img, k_txt, v_txt],
        specs=[vmem] * 3 + [head] * 2,
        scalars=1,
        moved=4 * 3 * rows * width,
        limit=60 * 1024 * 1024,
    )
    tok_out, along = lax.optimization_barrier((tok_out, along))
    along, given = lax.optimization_barrier((along, given))
    row = jnp.concatenate(along, axis=0)
    row_swapped = exchange(row, cores=True)
    tok_in = lax.all_to_all(tok_out, "seq", split_axis=0, concat_axis=0, tiled=True)

    probs, out_t, queries, keys_t, vals = call(
        functools.partial(forward_kernel, chunk=chunk),
        [shape(dims, BF16) for dims in ((total, image), (HD, image), (image, HD), (HD, total), (total, HD))],
        [tok_in, text_head],
        scratch=[pltpu.VMEM((total, HD), BF16), pltpu.VMEM((HD, total), BF16)],
        flops=4 * total * image * HD,
        moved=4 * total * image,
    )
    columns = row.shape[1]
    mine, near, far, send = call(
        partial_kernel,
        [shape((image // 2, 2 * HD), kind) for kind in (F32, BF16, F32, BF16)],
        [row, row_swapped, out_weight, given],
        scratch=[pltpu.VMEM((image // 2, columns), BF16), pltpu.VMEM((columns, width), BF16)],
        flops=8 * image * columns * HD,
        moved=2 * image * columns,
    )
    send, out_t, near = lax.optimization_barrier((exchange(send, 2), out_t, near))
    far = exchange((far + send.astype(F32)).astype(BF16), 4)
    near = exchange(near, 2)
    heads = mine + near.astype(F32) + far.astype(F32)
    first_row = lax.axis_index("seq") % 2 == 0
    kept = jnp.where(first_row, heads[:, :HD], heads[:, HD:]).astype(BF16)
    got = exchange(jnp.where(first_row, heads[:, HD:], heads[:, :HD]).astype(BF16), 1)
    row, _ = lax.optimization_barrier((row, out_t))
    other_row = exchange(row, 1)
    out_late, got, other_row = lax.optimization_barrier((out_t, got, other_row))
    other_swapped = exchange(other_row, cores=True)
    out_near, out_far = exchange(out_late, 2), exchange(out_late, 4)
    (grad_out,) = call(
        functools.partial(backward_kernel, chunk=chunk),
        [shape((n, 3 * rows, HD), BF16)],
        [queries, keys_t, vals, probs, out_t, kept, got],
        scratch=[pltpu.VMEM((image, HD), F32), pltpu.VMEM((image, HD), F32)],
        flops=8 * total * image * HD,
        moved=4 * total * image,
    )
    grad_in = lax.all_to_all(grad_out, "seq", split_axis=0, concat_axis=0, tiled=True)
    out_far, out_near, _ = lax.optimization_barrier((out_far, out_near, grad_out))
    outs = [out_t, out_near, out_far, exchange(out_far, 2)]
    dw_own, dw_other = call(
        weight_grad_kernel,
        [shape((4 * HD, depth), BF16)] * 2,
        [row, row_swapped, other_row, other_swapped, *outs],
        scratch=[pltpu.VMEM((image, columns), BF16), pltpu.VMEM((4 * HD, image), BF16)],
        flops=96 * image * columns * HD,
        moved=2 * image * columns,
    )
    grads = call(
        unpack_kernel,
        [shape((rows, width), BF16)] * 3,
        [grad_in],
        moved=4 * 3 * rows * width,
    )
    (d_weight,) = call(
        unpack_weight_kernel,
        [shape((depth, width), F32)],
        [dw_own, exchange(dw_other, 1)],
        moved=6 * depth * width,
    )
    return (*grads, d_weight)


def solution(mesh):
    in_specs = (
        P(("group", "seq"), "fsdp"),
        P(("group", "seq"), "fsdp"),
        P(("group", "seq"), "fsdp"),
        P("group", "fsdp"),
        P("group", "fsdp"),
        P("seq", "fsdp"),
        P(("group", "seq"), None),
    )
    out_specs = (
        P(("group", "seq"), "fsdp"),
        P(("group", "seq"), "fsdp"),
        P(("group", "seq"), "fsdp"),
        P(("group", "seq"), "fsdp"),
    )
    return jax.shard_map(local, mesh=mesh, in_specs=in_specs, out_specs=out_specs, check_vma=False)
```

```python
import functools
import math

import jax
import jax.numpy as jnp
from jax import lax
from jax.experimental import pallas as pl
from jax.experimental.pallas import tpu as pltpu
from jax.sharding import PartitionSpec as P

HD = 128
F32 = jnp.float32
BF16 = jnp.bfloat16
LIMIT = 16 * 1024 * 1024
NT = (((1,), (1,)), ((), ()))


def attend(queries, cotangents, key_rows, value_rows, block_rows):
    score_scale = HD ** (-0.5)
    query_count = queries.shape[0]
    block_count = query_count // block_rows
    query_blocks = queries.reshape(block_count, block_rows, HD)
    grad_blocks = cotangents.reshape(block_count, block_rows, HD)

    def one_block(accumulated, pair_item):
        query_block, grad_block = pair_item
        scores = jnp.dot(query_block, key_rows.T, preferred_element_type=jnp.float32) * score_scale
        row_max = jnp.max(scores, axis=1, keepdims=True)
        probs = jnp.exp(scores - row_max)
        probs = probs / jnp.sum(probs, axis=1, keepdims=True)
        probs_low = probs.astype(jnp.bfloat16)
        out_rows = jnp.dot(probs_low, value_rows, preferred_element_type=jnp.float32).astype(
            jnp.bfloat16
        )
        prob_grad = jnp.dot(grad_block, value_rows.T, preferred_element_type=jnp.float32)
        row_dot = jnp.sum(
            grad_block.astype(jnp.float32) * out_rows.astype(jnp.float32), axis=1, keepdims=True
        )
        score_grad = (probs * (prob_grad - row_dot)).astype(jnp.bfloat16)
        query_grad = (
            jnp.dot(score_grad, key_rows, preferred_element_type=jnp.float32) * score_scale
        ).astype(jnp.bfloat16)
        key_grad = (
            accumulated[0]
            + jnp.dot(score_grad.T, query_block, preferred_element_type=jnp.float32) * score_scale
        )
        value_grad = accumulated[1] + jnp.dot(
            probs_low.T, grad_block, preferred_element_type=jnp.float32
        )
        return ((key_grad, value_grad), (query_grad, out_rows))

    empty = jnp.zeros((key_rows.shape[0], HD), jnp.float32)
    (key_grad, value_grad), (query_grad, out_rows) = lax.scan(
        one_block, (empty, empty), (query_blocks, grad_blocks)
    )
    return (
        query_grad.reshape(query_count, HD),
        out_rows.reshape(query_count, HD),
        key_grad,
        value_grad,
    )


def local_general(q_img, k_img, v_img, k_txt, v_txt, out_weight, d_out):
    rows_here = q_img.shape[0]
    heads_here = q_img.shape[1] // HD
    seq_count = lax.axis_size("seq")
    share_count = seq_count // heads_here
    part_rows = rows_here // share_count
    seq_index = lax.axis_index("seq")
    head_index = seq_index // share_count
    column_cut = d_out
    attn_grad = jnp.dot(
        column_cut,
        lax.all_gather(out_weight, "seq", axis=0, tiled=True),
        preferred_element_type=jnp.float32,
    ).astype(jnp.bfloat16)

    def to_heads(array_in):
        shaped = array_in.reshape(share_count, part_rows, heads_here, HD).transpose(2, 0, 1, 3)
        return shaped.reshape(seq_count, part_rows, HD)

    def whole_heads(array_in):
        shaped = array_in.reshape(rows_here, heads_here, HD).transpose(1, 0, 2)
        shaped = jnp.broadcast_to(shaped[:, None], (heads_here, share_count, rows_here, HD))
        return shaped.reshape(seq_count, rows_here, HD)

    def from_heads(array_in):
        shaped = array_in.reshape(heads_here, share_count, part_rows, HD).transpose(1, 2, 0, 3)
        return shaped.reshape(rows_here, heads_here * HD)

    text_keys = lax.dynamic_slice_in_dim(k_txt, head_index * HD, HD, 1)
    text_values = lax.dynamic_slice_in_dim(v_txt, head_index * HD, HD, 1)
    query_side = jnp.concatenate([to_heads(q_img), to_heads(attn_grad)], axis=2)
    key_side = jnp.concatenate([whole_heads(k_img), whole_heads(v_img)], axis=2)
    packed = jnp.concatenate([query_side, key_side], axis=1)
    received = lax.all_to_all(packed, "seq", split_axis=0, concat_axis=0, tiled=True)
    queries = received[:, :part_rows, :HD].reshape(seq_count * part_rows, HD)
    cotangents = received[:, :part_rows, HD:].reshape(seq_count * part_rows, HD)
    image_keys = received[:, part_rows:, :HD].reshape(seq_count * rows_here, HD)
    image_values = received[:, part_rows:, HD:].reshape(seq_count * rows_here, HD)
    key_rows = jnp.concatenate([image_keys, text_keys], axis=0)
    value_rows = jnp.concatenate([image_values, text_values], axis=0)
    query_grad, out_rows, key_grad, value_grad = attend(
        queries, cotangents, key_rows, value_rows, min(512, queries.shape[0])
    )
    image_count = image_keys.shape[0]
    query_part = (
        jnp.concatenate([query_grad, out_rows], axis=1)
        .astype(jnp.float32)
        .reshape(seq_count, part_rows, 2 * HD)
    )
    key_part = jnp.concatenate([key_grad[:image_count], value_grad[:image_count]], axis=1).reshape(
        seq_count, rows_here, 2 * HD
    )
    returned = lax.all_to_all(
        jnp.concatenate([query_part, key_part], axis=1).astype(jnp.bfloat16),
        "seq",
        split_axis=0,
        concat_axis=0,
        tiled=True,
    ).astype(jnp.float32)
    q_grad = from_heads(returned[:, :part_rows, :HD]).astype(jnp.bfloat16)
    out_tok = from_heads(returned[:, :part_rows, HD:]).astype(jnp.bfloat16)
    summed = jnp.sum(
        returned[:, part_rows:, :].reshape(heads_here, share_count, rows_here, 2 * HD), axis=1
    )
    summed = summed.transpose(1, 0, 2)
    k_grad = summed[:, :, :HD].reshape(rows_here, heads_here * HD).astype(jnp.bfloat16)
    v_grad = summed[:, :, HD:].reshape(rows_here, heads_here * HD).astype(jnp.bfloat16)
    column_cut = d_out
    d_weight = lax.psum_scatter(
        jnp.dot(column_cut.T, out_tok, preferred_element_type=jnp.float32).astype(jnp.bfloat16),
        "seq",
        scatter_dimension=0,
        tiled=True,
    ).astype(jnp.float32)
    return (q_grad, k_grad, v_grad, d_weight)


def call(kernel, outs, args, specs=None, scratch=(), scalars=0, out_specs=None, flops=0, moved=0, limit=LIMIT):
    vmem = pl.BlockSpec(memory_space=pltpu.VMEM)
    if specs is None:
        specs = [vmem] * (len(args) - scalars)
    if out_specs is None:
        out_specs = [vmem] * len(outs)
    return pl.pallas_call(
        kernel,
        out_shape=outs,
        grid_spec=pltpu.PrefetchScalarGridSpec(
            num_scalar_prefetch=scalars,
            grid=(1,),
            in_specs=specs,
            out_specs=out_specs,
            scratch_shapes=list(scratch),
        ),
        compiler_params=pltpu.CompilerParams(vmem_limit_bytes=limit),
        cost_estimate=pl.CostEstimate(flops=flops, bytes_accessed=moved, transcendentals=0),
    )(*args)


STEPS = (0, 2, 4, 6)


def head_columns(step, other_row):
    return pl.ds(pl.multiple_of(jnp.bitwise_xor(lax.axis_index("seq"), step + other_row) * HD, HD), HD)


def pack_kernel(me_ref, q_ref, k_ref, v_ref, kt_ref, vt_ref, tok_ref, text_ref):
    rows = q_ref.shape[0]
    for h in range(tok_ref.shape[0]):
        for i, ref in enumerate((q_ref, k_ref, v_ref)):
            tok_ref[h, i * rows : (i + 1) * rows, :] = ref[:, h * HD : (h + 1) * HD]
    text_ref[0] = kt_ref[...]
    text_ref[1] = vt_ref[...]


def query_order(n):
    y = lax.rem(lax.axis_index("seq"), 2)
    return [2 * z + y for z in range(n // 2)] + [2 * z + 1 - y for z in range(n // 2)]


def forward_kernel(tok_ref, text_ref, probs_ref, out_ref, queries_ref, keys_t_ref, vals_ref, keys, vals_t, *, chunk):
    n, three, _ = tok_ref.shape
    rows = three // 3
    image = n * rows
    text = text_ref.shape[1]
    for i, source in enumerate(query_order(n)):
        queries_ref[i * rows : (i + 1) * rows, :] = tok_ref[source, 0:rows, :]
    keys[0:image, :] = tok_ref[:, rows : 2 * rows, :].reshape(image, HD)
    keys[image : image + text, :] = text_ref[0]
    vals_ref[0:image, :] = tok_ref[:, 2 * rows : 3 * rows, :].reshape(image, HD)
    vals_ref[image : image + text, :] = text_ref[1]
    keys_t_ref[...] = keys[...].T
    vals_t[...] = vals_ref[...].T
    factor = HD ** (-0.5) * math.log2(math.e)
    for c in range(image // chunk):
        span = slice(c * chunk, (c + 1) * chunk)
        scores = lax.dot_general(keys[...], queries_ref[span, :], NT, preferred_element_type=F32)
        top = jnp.max(scores, axis=0, keepdims=True)
        weights = jnp.exp2((scores - top) * factor)
        total = jnp.sum(weights, axis=0, keepdims=True)
        low = (weights * (1.0 / total)).astype(BF16)
        probs_ref[:, span] = low
        out_ref[:, span] = jnp.dot(vals_t[...], low, preferred_element_type=F32).astype(BF16)


def place_rows(piece_ref, swapped_ref, cot, start):
    me = lax.axis_index("seq")
    core = lax.axis_index("fsdp")
    part = piece_ref.shape[0] // len(STEPS)
    for piece, shift in ((piece_ref, core), (swapped_ref, 1 - core)):
        for i, step in enumerate(STEPS):
            z = jnp.bitwise_xor(me, step) // 2
            at = pl.multiple_of(start + z * (2 * part) + shift * part, 16)
            cot[pl.ds(at, part), :] = piece[i * part : (i + 1) * part, :]


def partial_kernel(piece_ref, swapped_ref, own_ref, other_ref, mine_ref, near_ref, far_ref, send_ref, cot, weight):
    place_rows(piece_ref, swapped_ref, cot, 0)
    me = lax.axis_index("seq")
    depth = own_ref.shape[0]
    y = lax.rem(me, 2)
    weight[pl.ds(pl.multiple_of(y * depth, 16), depth), :] = own_ref[...]
    weight[pl.ds(pl.multiple_of((1 - y) * depth, 16), depth), :] = other_ref[...]
    for step, ref in zip(STEPS, (mine_ref, near_ref, far_ref, send_ref)):
        z = jnp.bitwise_xor(me, step) // 2
        cols = pl.ds(pl.multiple_of(z * 2 * HD, 2 * HD), 2 * HD)
        ref[...] = jnp.dot(cot[...], weight[:, cols], preferred_element_type=F32).astype(ref.dtype)


def concat_kernel(*refs):
    *pieces, out_ref = refs
    part = pieces[0].shape[0]
    for i, piece in enumerate(pieces):
        out_ref[i * part : (i + 1) * part, :] = piece[...]


def add_kernel(kept_ref, received_ref, out_ref):
    out_ref[...] = (kept_ref[...] + received_ref[...].astype(F32)).astype(BF16)


def finish_kernel(mine_ref, near_ref, far_ref, kept_ref, give_ref):
    heads = mine_ref[...] + near_ref[...].astype(F32) + far_ref[...].astype(F32)
    first, second = heads[:, :HD].astype(BF16), heads[:, HD:].astype(BF16)
    first_row = lax.rem(lax.axis_index("seq"), 2) == 0
    kept_ref[...] = jnp.where(first_row, first, second)
    give_ref[...] = jnp.where(first_row, second, first)


def weight_grad_kernel(*refs):
    *pieces, out0, out1, out2, out3, own_ref, other_ref, cot, outs = refs
    tokens = cot.shape[0]
    place_rows(pieces[0], pieces[1], cot, 0)
    place_rows(pieces[2], pieces[3], cot, tokens // 2)
    for i, ref in enumerate((out0, out1, out2, out3)):
        outs[i * HD : (i + 1) * HD, :] = ref[...]
    depth = own_ref.shape[1]
    y = lax.rem(lax.axis_index("seq"), 2)
    for ref, row in ((own_ref, y), (other_ref, 1 - y)):
        cols = pl.ds(pl.multiple_of(row * depth, HD), depth)
        ref[...] = jnp.dot(outs[...], cot[:, cols], preferred_element_type=F32).astype(BF16)


def backward_kernel(queries_ref, keys_t_ref, vals_ref, probs_ref, out_ref, *refs, chunk):
    *grad_refs, send_ref, dk, dv = refs
    n, three, _ = send_ref.shape
    rows = three // 3
    image = n * rows
    scale = HD ** (-0.5)
    per = chunk // rows
    order = query_order(n)
    half = image // chunk // 2
    for c in range(image // chunk):
        span = slice(c * chunk, (c + 1) * chunk)
        within = slice(c % half * chunk, (c % half + 1) * chunk)
        grads = grad_refs[c // half][within, :]
        row_dot = jnp.sum(
            grads.astype(F32).T * out_ref[:, span].astype(F32), axis=0, keepdims=True
        )
        prob_grad = lax.dot_general(vals_ref[...], grads, NT, preferred_element_type=F32)
        low = probs_ref[:, span]
        score_grad = (low.astype(F32) * (prob_grad - row_dot)).astype(BF16)
        dq = (jnp.dot(keys_t_ref[...], score_grad, preferred_element_type=F32) * scale).T.astype(BF16)
        for i in range(per):
            send_ref[order[c * per + i], 0:rows, :] = dq[i * rows : (i + 1) * rows, :]
        dk_part = jnp.dot(score_grad[0:image, :], queries_ref[span, :], preferred_element_type=F32)
        dv_part = jnp.dot(low[0:image, :], grads, preferred_element_type=F32)
        if c == 0:
            dk[...] = dk_part
            dv[...] = dv_part
        else:
            dk[...] += dk_part
            dv[...] += dv_part
    send_ref[:, rows : 2 * rows, :] = (dk[...] * scale).astype(BF16).reshape(n, rows, HD)
    send_ref[:, 2 * rows : 3 * rows, :] = dv[...].astype(BF16).reshape(n, rows, HD)


def unpack_kernel(tok_ref, q_ref, k_ref, v_ref):
    rows = q_ref.shape[0]
    for h in range(tok_ref.shape[0]):
        for i, ref in enumerate((q_ref, k_ref, v_ref)):
            ref[:, h * HD : (h + 1) * HD] = tok_ref[h, i * rows : (i + 1) * rows, :]


def unpack_weight_kernel(own_ref, other_ref, w_ref):
    for other_row, ref in enumerate((own_ref, other_ref)):
        for i, step in enumerate(STEPS):
            w_ref[:, head_columns(step, other_row)] = ref[i * HD : (i + 1) * HD, :].astype(F32).T


def exchange(array, distance=0, cores=False):
    if not distance and not cores:
        return array
    size = 2 * lax.axis_size("seq")
    pairs = [(i, i ^ (2 * distance + int(cores))) for i in range(size)]
    return lax.ppermute(array, ("seq", "fsdp"), pairs)


def send_cotangents(d_out):
    rows, width = d_out.shape
    part, columns = rows // 2, width // len(STEPS)
    z = lax.axis_index("seq") // 2
    first = lax.axis_index("fsdp") * part
    return [
        exchange(lax.dynamic_slice(d_out, (first, (z ^ (step // 2)) * columns), (part, columns)), step)
        for step in STEPS
    ]


def local(q_img, k_img, v_img, k_txt, v_txt, out_weight, d_out):
    n = lax.axis_size("seq")
    rows, width = q_img.shape
    args = (q_img, k_img, v_img, k_txt, v_txt, out_weight, d_out)
    if n != 2 * len(STEPS) or width // HD != n or lax.axis_size("fsdp") != 2 or rows % 32:
        return local_general(*args)
    depth = out_weight.shape[0]
    image = n * rows
    text = k_txt.shape[0]
    total = image + text
    chunk = 2 * rows
    shape = jax.ShapeDtypeStruct
    vmem = pl.BlockSpec(memory_space=pltpu.VMEM)

    head = pl.BlockSpec((text, HD), lambda i, me_ref: (0, me_ref[0]))
    given = exchange(out_weight, 1)
    along = send_cotangents(d_out)
    tok_out, text_head = call(
        pack_kernel,
        [shape((n, 3 * rows, HD), BF16), shape((2, text, HD), BF16)],
        [lax.axis_index("seq").astype(jnp.int32)[None], q_img, k_img, v_img, k_txt, v_txt],
        specs=[vmem] * 3 + [head] * 2,
        scalars=1,
        moved=4 * 3 * rows * width,
        limit=60 * 1024 * 1024,
    )
    tok_out, along = lax.optimization_barrier((tok_out, along))
    along, given = lax.optimization_barrier((along, given))
    (row,) = call(concat_kernel, [shape((4 * along[0].shape[0], along[0].shape[1]), BF16)], along)
    row_swapped = exchange(row, cores=True)
    tok_in = lax.all_to_all(tok_out, "seq", split_axis=0, concat_axis=0, tiled=True)

    probs, out_t, queries, keys_t, vals = call(
        functools.partial(forward_kernel, chunk=chunk),
        [shape(dims, BF16) for dims in ((total, image), (HD, image), (image, HD), (HD, total), (total, HD))],
        [tok_in, text_head],
        scratch=[pltpu.VMEM((total, HD), BF16), pltpu.VMEM((HD, total), BF16)],
        flops=4 * total * image * HD,
        moved=4 * total * image,
    )
    columns = row.shape[1]
    mine, near, far, send = call(
        partial_kernel,
        [shape((image // 2, 2 * HD), kind) for kind in (F32, BF16, F32, BF16)],
        [row, row_swapped, out_weight, given],
        scratch=[pltpu.VMEM((image // 2, columns), BF16), pltpu.VMEM((columns, width), BF16)],
        flops=8 * image * columns * HD,
        moved=2 * image * columns,
    )
    send, out_t, near = lax.optimization_barrier((exchange(send, 2), out_t, near))
    (far,) = call(add_kernel, [shape(far.shape, BF16)], [far, send])
    far = exchange(far, 4)
    near = exchange(near, 2)
    kept, give = call(finish_kernel, [shape((image // 2, HD), BF16)] * 2, [mine, near, far])
    got = exchange(give, 1)
    row, _ = lax.optimization_barrier((row, out_t))
    other_row = exchange(row, 1)
    out_late, got, other_row = lax.optimization_barrier((out_t, got, other_row))
    other_swapped = exchange(other_row, cores=True)
    out_near, out_far = exchange(out_late, 2), exchange(out_late, 4)
    (grad_out,) = call(
        functools.partial(backward_kernel, chunk=chunk),
        [shape((n, 3 * rows, HD), BF16)],
        [queries, keys_t, vals, probs, out_t, kept, got],
        scratch=[pltpu.VMEM((image, HD), F32), pltpu.VMEM((image, HD), F32)],
        flops=8 * total * image * HD,
        moved=4 * total * image,
    )
    grad_in = lax.all_to_all(grad_out, "seq", split_axis=0, concat_axis=0, tiled=True)
    out_far, out_near, _ = lax.optimization_barrier((out_far, out_near, grad_out))
    outs = [out_t, out_near, out_far, exchange(out_far, 2)]
    dw_own, dw_other = call(
        weight_grad_kernel,
        [shape((4 * HD, depth), BF16)] * 2,
        [row, row_swapped, other_row, other_swapped, *outs],
        scratch=[pltpu.VMEM((image, columns), BF16), pltpu.VMEM((4 * HD, image), BF16)],
        flops=96 * image * columns * HD,
        moved=2 * image * columns,
    )
    grads = call(
        unpack_kernel,
        [shape((rows, width), BF16)] * 3,
        [grad_in],
        moved=4 * 3 * rows * width,
    )
    (d_weight,) = call(
        unpack_weight_kernel,
        [shape((depth, width), F32)],
        [dw_own, exchange(dw_other, 1)],
        moved=6 * depth * width,
    )
    return (*grads, d_weight)


def solution(mesh):
    in_specs = (
        P(("group", "seq"), "fsdp"),
        P(("group", "seq"), "fsdp"),
        P(("group", "seq"), "fsdp"),
        P("group", "fsdp"),
        P("group", "fsdp"),
        P("seq", "fsdp"),
        P(("group", "seq"), None),
    )
    out_specs = (
        P(("group", "seq"), "fsdp"),
        P(("group", "seq"), "fsdp"),
        P(("group", "seq"), "fsdp"),
        P(("group", "seq"), "fsdp"),
    )
    return jax.shard_map(local, mesh=mesh, in_specs=in_specs, out_specs=out_specs, check_vma=False)
```

```python
import functools
import math

import jax
import jax.numpy as jnp
from jax import lax
from jax.experimental import pallas as pl
from jax.experimental.pallas import tpu as pltpu
from jax.sharding import PartitionSpec as P

HD = 128
F32 = jnp.float32
BF16 = jnp.bfloat16
LIMIT = 16 * 1024 * 1024
NT = (((1,), (1,)), ((), ()))


def attend(queries, cotangents, key_rows, value_rows, block_rows):
    score_scale = HD ** (-0.5)
    query_count = queries.shape[0]
    block_count = query_count // block_rows
    query_blocks = queries.reshape(block_count, block_rows, HD)
    grad_blocks = cotangents.reshape(block_count, block_rows, HD)

    def one_block(accumulated, pair_item):
        query_block, grad_block = pair_item
        scores = jnp.dot(query_block, key_rows.T, preferred_element_type=jnp.float32) * score_scale
        row_max = jnp.max(scores, axis=1, keepdims=True)
        probs = jnp.exp(scores - row_max)
        probs = probs / jnp.sum(probs, axis=1, keepdims=True)
        probs_low = probs.astype(jnp.bfloat16)
        out_rows = jnp.dot(probs_low, value_rows, preferred_element_type=jnp.float32).astype(
            jnp.bfloat16
        )
        prob_grad = jnp.dot(grad_block, value_rows.T, preferred_element_type=jnp.float32)
        row_dot = jnp.sum(
            grad_block.astype(jnp.float32) * out_rows.astype(jnp.float32), axis=1, keepdims=True
        )
        score_grad = (probs * (prob_grad - row_dot)).astype(jnp.bfloat16)
        query_grad = (
            jnp.dot(score_grad, key_rows, preferred_element_type=jnp.float32) * score_scale
        ).astype(jnp.bfloat16)
        key_grad = (
            accumulated[0]
            + jnp.dot(score_grad.T, query_block, preferred_element_type=jnp.float32) * score_scale
        )
        value_grad = accumulated[1] + jnp.dot(
            probs_low.T, grad_block, preferred_element_type=jnp.float32
        )
        return ((key_grad, value_grad), (query_grad, out_rows))

    empty = jnp.zeros((key_rows.shape[0], HD), jnp.float32)
    (key_grad, value_grad), (query_grad, out_rows) = lax.scan(
        one_block, (empty, empty), (query_blocks, grad_blocks)
    )
    return (
        query_grad.reshape(query_count, HD),
        out_rows.reshape(query_count, HD),
        key_grad,
        value_grad,
    )


def local_general(q_img, k_img, v_img, k_txt, v_txt, out_weight, d_out):
    rows_here = q_img.shape[0]
    heads_here = q_img.shape[1] // HD
    seq_count = lax.axis_size("seq")
    share_count = seq_count // heads_here
    part_rows = rows_here // share_count
    seq_index = lax.axis_index("seq")
    head_index = seq_index // share_count
    column_cut = d_out
    attn_grad = jnp.dot(
        column_cut,
        lax.all_gather(out_weight, "seq", axis=0, tiled=True),
        preferred_element_type=jnp.float32,
    ).astype(jnp.bfloat16)

    def to_heads(array_in):
        shaped = array_in.reshape(share_count, part_rows, heads_here, HD).transpose(2, 0, 1, 3)
        return shaped.reshape(seq_count, part_rows, HD)

    def whole_heads(array_in):
        shaped = array_in.reshape(rows_here, heads_here, HD).transpose(1, 0, 2)
        shaped = jnp.broadcast_to(shaped[:, None], (heads_here, share_count, rows_here, HD))
        return shaped.reshape(seq_count, rows_here, HD)

    def from_heads(array_in):
        shaped = array_in.reshape(heads_here, share_count, part_rows, HD).transpose(1, 2, 0, 3)
        return shaped.reshape(rows_here, heads_here * HD)

    text_keys = lax.dynamic_slice_in_dim(k_txt, head_index * HD, HD, 1)
    text_values = lax.dynamic_slice_in_dim(v_txt, head_index * HD, HD, 1)
    query_side = jnp.concatenate([to_heads(q_img), to_heads(attn_grad)], axis=2)
    key_side = jnp.concatenate([whole_heads(k_img), whole_heads(v_img)], axis=2)
    packed = jnp.concatenate([query_side, key_side], axis=1)
    received = lax.all_to_all(packed, "seq", split_axis=0, concat_axis=0, tiled=True)
    queries = received[:, :part_rows, :HD].reshape(seq_count * part_rows, HD)
    cotangents = received[:, :part_rows, HD:].reshape(seq_count * part_rows, HD)
    image_keys = received[:, part_rows:, :HD].reshape(seq_count * rows_here, HD)
    image_values = received[:, part_rows:, HD:].reshape(seq_count * rows_here, HD)
    key_rows = jnp.concatenate([image_keys, text_keys], axis=0)
    value_rows = jnp.concatenate([image_values, text_values], axis=0)
    query_grad, out_rows, key_grad, value_grad = attend(
        queries, cotangents, key_rows, value_rows, min(512, queries.shape[0])
    )
    image_count = image_keys.shape[0]
    query_part = (
        jnp.concatenate([query_grad, out_rows], axis=1)
        .astype(jnp.float32)
        .reshape(seq_count, part_rows, 2 * HD)
    )
    key_part = jnp.concatenate([key_grad[:image_count], value_grad[:image_count]], axis=1).reshape(
        seq_count, rows_here, 2 * HD
    )
    returned = lax.all_to_all(
        jnp.concatenate([query_part, key_part], axis=1).astype(jnp.bfloat16),
        "seq",
        split_axis=0,
        concat_axis=0,
        tiled=True,
    ).astype(jnp.float32)
    q_grad = from_heads(returned[:, :part_rows, :HD]).astype(jnp.bfloat16)
    out_tok = from_heads(returned[:, :part_rows, HD:]).astype(jnp.bfloat16)
    summed = jnp.sum(
        returned[:, part_rows:, :].reshape(heads_here, share_count, rows_here, 2 * HD), axis=1
    )
    summed = summed.transpose(1, 0, 2)
    k_grad = summed[:, :, :HD].reshape(rows_here, heads_here * HD).astype(jnp.bfloat16)
    v_grad = summed[:, :, HD:].reshape(rows_here, heads_here * HD).astype(jnp.bfloat16)
    column_cut = d_out
    d_weight = lax.psum_scatter(
        jnp.dot(column_cut.T, out_tok, preferred_element_type=jnp.float32).astype(jnp.bfloat16),
        "seq",
        scatter_dimension=0,
        tiled=True,
    ).astype(jnp.float32)
    return (q_grad, k_grad, v_grad, d_weight)


def call(kernel, outs, args, specs=None, scratch=(), scalars=0, out_specs=None, flops=0, moved=0, limit=LIMIT):
    vmem = pl.BlockSpec(memory_space=pltpu.VMEM)
    if specs is None:
        specs = [vmem] * (len(args) - scalars)
    if out_specs is None:
        out_specs = [vmem] * len(outs)
    return pl.pallas_call(
        kernel,
        out_shape=outs,
        grid_spec=pltpu.PrefetchScalarGridSpec(
            num_scalar_prefetch=scalars,
            grid=(1,),
            in_specs=specs,
            out_specs=out_specs,
            scratch_shapes=list(scratch),
        ),
        compiler_params=pltpu.CompilerParams(vmem_limit_bytes=limit),
        cost_estimate=pl.CostEstimate(flops=flops, bytes_accessed=moved, transcendentals=0),
    )(*args)


STEPS = (0, 2, 4, 6)


def head_columns(step, other_row):
    return pl.ds(pl.multiple_of(jnp.bitwise_xor(lax.axis_index("seq"), step + other_row) * HD, HD), HD)


def pack_kernel(me_ref, q_ref, k_ref, v_ref, kt_ref, vt_ref, tok_ref, text_ref):
    rows = q_ref.shape[0]
    for h in range(tok_ref.shape[0]):
        for i, ref in enumerate((q_ref, k_ref, v_ref)):
            tok_ref[h, i * rows : (i + 1) * rows, :] = ref[:, h * HD : (h + 1) * HD]
    text_ref[0] = kt_ref[...]
    text_ref[1] = vt_ref[...]


def query_order(n):
    y = lax.rem(lax.axis_index("seq"), 2)
    return [2 * z + y for z in range(n // 2)] + [2 * z + 1 - y for z in range(n // 2)]


def forward_kernel(tok_ref, text_ref, probs_ref, out_ref, queries_ref, keys_t_ref, vals_ref, keys, vals_t, *, chunk):
    n, three, _ = tok_ref.shape
    rows = three // 3
    image = n * rows
    text = text_ref.shape[1]
    for i, source in enumerate(query_order(n)):
        queries_ref[i * rows : (i + 1) * rows, :] = tok_ref[source, 0:rows, :]
    keys[0:image, :] = tok_ref[:, rows : 2 * rows, :].reshape(image, HD)
    keys[image : image + text, :] = text_ref[0]
    vals_ref[0:image, :] = tok_ref[:, 2 * rows : 3 * rows, :].reshape(image, HD)
    vals_ref[image : image + text, :] = text_ref[1]
    keys_t_ref[...] = keys[...].T
    vals_t[...] = vals_ref[...].T
    factor = HD ** (-0.5) * math.log2(math.e)
    for c in range(image // chunk):
        span = slice(c * chunk, (c + 1) * chunk)
        scores = lax.dot_general(keys[...], queries_ref[span, :], NT, preferred_element_type=F32)
        top = jnp.max(scores, axis=0, keepdims=True)
        weights = jnp.exp2((scores - top) * factor)
        total = jnp.sum(weights, axis=0, keepdims=True)
        low = (weights * (1.0 / total)).astype(BF16)
        probs_ref[:, span] = low
        out_ref[:, span] = jnp.dot(vals_t[...], low, preferred_element_type=F32).astype(BF16)


def place_rows(piece_ref, swapped_ref, cot, start):
    me = lax.axis_index("seq")
    core = lax.axis_index("fsdp")
    part = piece_ref.shape[0] // len(STEPS)
    for piece, shift in ((piece_ref, core), (swapped_ref, 1 - core)):
        for i, step in enumerate(STEPS):
            z = jnp.bitwise_xor(me, step) // 2
            at = pl.multiple_of(start + z * (2 * part) + shift * part, 16)
            cot[pl.ds(at, part), :] = piece[i * part : (i + 1) * part, :]


def partial_kernel(piece_ref, swapped_ref, own_ref, other_ref, mine_ref, near_ref, far_ref, send_ref, cot, weight):
    place_rows(piece_ref, swapped_ref, cot, 0)
    me = lax.axis_index("seq")
    depth = own_ref.shape[0]
    y = lax.rem(me, 2)
    weight[pl.ds(pl.multiple_of(y * depth, 16), depth), :] = own_ref[...]
    weight[pl.ds(pl.multiple_of((1 - y) * depth, 16), depth), :] = other_ref[...]
    for step, ref in zip(STEPS, (mine_ref, near_ref, far_ref, send_ref)):
        z = jnp.bitwise_xor(me, step) // 2
        cols = pl.ds(pl.multiple_of(z * 2 * HD, 2 * HD), 2 * HD)
        ref[...] = jnp.dot(cot[...], weight[:, cols], preferred_element_type=F32).astype(ref.dtype)


def add_kernel(kept_ref, received_ref, out_ref):
    out_ref[...] = (kept_ref[...] + received_ref[...].astype(F32)).astype(BF16)


def finish_kernel(mine_ref, near_ref, far_ref, kept_ref, give_ref):
    heads = mine_ref[...] + near_ref[...].astype(F32) + far_ref[...].astype(F32)
    first, second = heads[:, :HD].astype(BF16), heads[:, HD:].astype(BF16)
    first_row = lax.rem(lax.axis_index("seq"), 2) == 0
    kept_ref[...] = jnp.where(first_row, first, second)
    give_ref[...] = jnp.where(first_row, second, first)


def weight_grad_kernel(*refs):
    *pieces, out0, out1, out2, out3, own_ref, other_ref, cot, outs = refs
    tokens = cot.shape[0]
    place_rows(pieces[0], pieces[1], cot, 0)
    place_rows(pieces[2], pieces[3], cot, tokens // 2)
    for i, ref in enumerate((out0, out1, out2, out3)):
        outs[i * HD : (i + 1) * HD, :] = ref[...]
    depth = own_ref.shape[1]
    y = lax.rem(lax.axis_index("seq"), 2)
    for ref, row in ((own_ref, y), (other_ref, 1 - y)):
        cols = pl.ds(pl.multiple_of(row * depth, HD), depth)
        ref[...] = jnp.dot(outs[...], cot[:, cols], preferred_element_type=F32).astype(BF16)


def backward_kernel(queries_ref, keys_t_ref, vals_ref, probs_ref, out_ref, *refs, chunk):
    *grad_refs, send_ref, dk, dv = refs
    n, three, _ = send_ref.shape
    rows = three // 3
    image = n * rows
    scale = HD ** (-0.5)
    per = chunk // rows
    order = query_order(n)
    half = image // chunk // 2
    for c in range(image // chunk):
        span = slice(c * chunk, (c + 1) * chunk)
        within = slice(c % half * chunk, (c % half + 1) * chunk)
        grads = grad_refs[c // half][within, :]
        row_dot = jnp.sum(
            grads.astype(F32).T * out_ref[:, span].astype(F32), axis=0, keepdims=True
        )
        prob_grad = lax.dot_general(vals_ref[...], grads, NT, preferred_element_type=F32)
        low = probs_ref[:, span]
        score_grad = (low.astype(F32) * (prob_grad - row_dot)).astype(BF16)
        dq = (jnp.dot(keys_t_ref[...], score_grad, preferred_element_type=F32) * scale).T.astype(BF16)
        for i in range(per):
            send_ref[order[c * per + i], 0:rows, :] = dq[i * rows : (i + 1) * rows, :]
        dk_part = jnp.dot(score_grad[0:image, :], queries_ref[span, :], preferred_element_type=F32)
        dv_part = jnp.dot(low[0:image, :], grads, preferred_element_type=F32)
        if c == 0:
            dk[...] = dk_part
            dv[...] = dv_part
        else:
            dk[...] += dk_part
            dv[...] += dv_part
    send_ref[:, rows : 2 * rows, :] = (dk[...] * scale).astype(BF16).reshape(n, rows, HD)
    send_ref[:, 2 * rows : 3 * rows, :] = dv[...].astype(BF16).reshape(n, rows, HD)


def unpack_kernel(tok_ref, q_ref, k_ref, v_ref):
    rows = q_ref.shape[0]
    for h in range(tok_ref.shape[0]):
        for i, ref in enumerate((q_ref, k_ref, v_ref)):
            ref[:, h * HD : (h + 1) * HD] = tok_ref[h, i * rows : (i + 1) * rows, :]


def unpack_weight_kernel(own_ref, other_ref, w_ref):
    for other_row, ref in enumerate((own_ref, other_ref)):
        for i, step in enumerate(STEPS):
            w_ref[:, head_columns(step, other_row)] = ref[i * HD : (i + 1) * HD, :].astype(F32).T


def exchange(array, distance=0, cores=False):
    if not distance and not cores:
        return array
    size = 2 * lax.axis_size("seq")
    pairs = [(i, i ^ (2 * distance + int(cores))) for i in range(size)]
    return lax.ppermute(array, ("seq", "fsdp"), pairs)


def send_cotangents(d_out):
    rows, width = d_out.shape
    part, columns = rows // 2, width // len(STEPS)
    z = lax.axis_index("seq") // 2
    first = lax.axis_index("fsdp") * part
    return [
        exchange(lax.dynamic_slice(d_out, (first, (z ^ (step // 2)) * columns), (part, columns)), step)
        for step in STEPS
    ]


def local(q_img, k_img, v_img, k_txt, v_txt, out_weight, d_out):
    n = lax.axis_size("seq")
    rows, width = q_img.shape
    args = (q_img, k_img, v_img, k_txt, v_txt, out_weight, d_out)
    if n != 2 * len(STEPS) or width // HD != n or lax.axis_size("fsdp") != 2 or rows % 32:
        return local_general(*args)
    depth = out_weight.shape[0]
    image = n * rows
    text = k_txt.shape[0]
    total = image + text
    chunk = 2 * rows
    shape = jax.ShapeDtypeStruct
    vmem = pl.BlockSpec(memory_space=pltpu.VMEM)

    head = pl.BlockSpec((text, HD), lambda i, me_ref: (0, me_ref[0]))
    given = exchange(out_weight, 1)
    along = send_cotangents(d_out)
    tok_out, text_head = call(
        pack_kernel,
        [shape((n, 3 * rows, HD), BF16), shape((2, text, HD), BF16)],
        [lax.axis_index("seq").astype(jnp.int32)[None], q_img, k_img, v_img, k_txt, v_txt],
        specs=[vmem] * 3 + [head] * 2,
        scalars=1,
        moved=4 * 3 * rows * width,
        limit=60 * 1024 * 1024,
    )
    tok_out, along = lax.optimization_barrier((tok_out, along))
    along, given = lax.optimization_barrier((along, given))
    row = jnp.concatenate(along, axis=0)
    row_swapped = exchange(row, cores=True)
    tok_in = lax.all_to_all(tok_out, "seq", split_axis=0, concat_axis=0, tiled=True)

    probs, out_t, queries, keys_t, vals = call(
        functools.partial(forward_kernel, chunk=chunk),
        [shape(dims, BF16) for dims in ((total, image), (HD, image), (image, HD), (HD, total), (total, HD))],
        [tok_in, text_head],
        scratch=[pltpu.VMEM((total, HD), BF16), pltpu.VMEM((HD, total), BF16)],
        flops=4 * total * image * HD,
        moved=4 * total * image,
    )
    columns = row.shape[1]
    mine, near, far, send = call(
        partial_kernel,
        [shape((image // 2, 2 * HD), kind) for kind in (F32, BF16, F32, BF16)],
        [row, row_swapped, out_weight, given],
        scratch=[pltpu.VMEM((image // 2, columns), BF16), pltpu.VMEM((columns, width), BF16)],
        flops=8 * image * columns * HD,
        moved=2 * image * columns,
    )
    send, near = lax.optimization_barrier((exchange(send, 2), near))
    (far,) = call(add_kernel, [shape(far.shape, BF16)], [far, send])
    far, near = exchange(far, 4), exchange(near, 2)
    out_late, far, near = lax.optimization_barrier((out_t, far, near))
    kept, give = call(finish_kernel, [shape((image // 2, HD), BF16)] * 2, [mine, near, far])
    got = exchange(give, 1)
    out_near, out_far = exchange(out_late, 2), exchange(out_late, 4)
    row, _ = lax.optimization_barrier((row, out_t))
    other_row = exchange(row, 1)
    other_swapped = exchange(other_row, cores=True)
    (grad_out,) = call(
        functools.partial(backward_kernel, chunk=chunk),
        [shape((n, 3 * rows, HD), BF16)],
        [queries, keys_t, vals, probs, out_t, kept, got],
        scratch=[pltpu.VMEM((image, HD), F32), pltpu.VMEM((image, HD), F32)],
        flops=8 * total * image * HD,
        moved=4 * total * image,
    )
    grad_in = lax.all_to_all(grad_out, "seq", split_axis=0, concat_axis=0, tiled=True)
    out_far, out_near, other_row, _ = lax.optimization_barrier((out_far, out_near, other_row, grad_out))
    outs = [out_t, out_near, out_far, exchange(out_far, 2)]
    dw_own, dw_other = call(
        weight_grad_kernel,
        [shape((4 * HD, depth), BF16)] * 2,
        [row, row_swapped, other_row, other_swapped, *outs],
        scratch=[pltpu.VMEM((image, columns), BF16), pltpu.VMEM((4 * HD, image), BF16)],
        flops=96 * image * columns * HD,
        moved=2 * image * columns,
    )
    grads = call(
        unpack_kernel,
        [shape((rows, width), BF16)] * 3,
        [grad_in],
        moved=4 * 3 * rows * width,
    )
    (d_weight,) = call(
        unpack_weight_kernel,
        [shape((depth, width), F32)],
        [dw_own, exchange(dw_other, 1)],
        moved=6 * depth * width,
    )
    return (*grads, d_weight)


def solution(mesh):
    in_specs = (
        P(("group", "seq"), "fsdp"),
        P(("group", "seq"), "fsdp"),
        P(("group", "seq"), "fsdp"),
        P("group", "fsdp"),
        P("group", "fsdp"),
        P("seq", "fsdp"),
        P(("group", "seq"), None),
    )
    out_specs = (
        P(("group", "seq"), "fsdp"),
        P(("group", "seq"), "fsdp"),
        P(("group", "seq"), "fsdp"),
        P(("group", "seq"), "fsdp"),
    )
    return jax.shard_map(local, mesh=mesh, in_specs=in_specs, out_specs=out_specs, check_vma=False)
```

```python
import functools
import math

import jax
import jax.numpy as jnp
from jax import lax
from jax.experimental import pallas as pl
from jax.experimental.pallas import tpu as pltpu
from jax.sharding import PartitionSpec as P

HD = 128
F32 = jnp.float32
BF16 = jnp.bfloat16
LIMIT = 16 * 1024 * 1024
NT = (((1,), (1,)), ((), ()))


def attend(queries, cotangents, key_rows, value_rows, block_rows):
    score_scale = HD ** (-0.5)
    query_count = queries.shape[0]
    block_count = query_count // block_rows
    query_blocks = queries.reshape(block_count, block_rows, HD)
    grad_blocks = cotangents.reshape(block_count, block_rows, HD)

    def one_block(accumulated, pair_item):
        query_block, grad_block = pair_item
        scores = jnp.dot(query_block, key_rows.T, preferred_element_type=jnp.float32) * score_scale
        row_max = jnp.max(scores, axis=1, keepdims=True)
        probs = jnp.exp(scores - row_max)
        probs = probs / jnp.sum(probs, axis=1, keepdims=True)
        probs_low = probs.astype(jnp.bfloat16)
        out_rows = jnp.dot(probs_low, value_rows, preferred_element_type=jnp.float32).astype(
            jnp.bfloat16
        )
        prob_grad = jnp.dot(grad_block, value_rows.T, preferred_element_type=jnp.float32)
        row_dot = jnp.sum(
            grad_block.astype(jnp.float32) * out_rows.astype(jnp.float32), axis=1, keepdims=True
        )
        score_grad = (probs * (prob_grad - row_dot)).astype(jnp.bfloat16)
        query_grad = (
            jnp.dot(score_grad, key_rows, preferred_element_type=jnp.float32) * score_scale
        ).astype(jnp.bfloat16)
        key_grad = (
            accumulated[0]
            + jnp.dot(score_grad.T, query_block, preferred_element_type=jnp.float32) * score_scale
        )
        value_grad = accumulated[1] + jnp.dot(
            probs_low.T, grad_block, preferred_element_type=jnp.float32
        )
        return ((key_grad, value_grad), (query_grad, out_rows))

    empty = jnp.zeros((key_rows.shape[0], HD), jnp.float32)
    (key_grad, value_grad), (query_grad, out_rows) = lax.scan(
        one_block, (empty, empty), (query_blocks, grad_blocks)
    )
    return (
        query_grad.reshape(query_count, HD),
        out_rows.reshape(query_count, HD),
        key_grad,
        value_grad,
    )


def local_general(q_img, k_img, v_img, k_txt, v_txt, out_weight, d_out):
    rows_here = q_img.shape[0]
    heads_here = q_img.shape[1] // HD
    seq_count = lax.axis_size("seq")
    share_count = seq_count // heads_here
    part_rows = rows_here // share_count
    seq_index = lax.axis_index("seq")
    head_index = seq_index // share_count
    column_cut = d_out
    attn_grad = jnp.dot(
        column_cut,
        lax.all_gather(out_weight, "seq", axis=0, tiled=True),
        preferred_element_type=jnp.float32,
    ).astype(jnp.bfloat16)

    def to_heads(array_in):
        shaped = array_in.reshape(share_count, part_rows, heads_here, HD).transpose(2, 0, 1, 3)
        return shaped.reshape(seq_count, part_rows, HD)

    def whole_heads(array_in):
        shaped = array_in.reshape(rows_here, heads_here, HD).transpose(1, 0, 2)
        shaped = jnp.broadcast_to(shaped[:, None], (heads_here, share_count, rows_here, HD))
        return shaped.reshape(seq_count, rows_here, HD)

    def from_heads(array_in):
        shaped = array_in.reshape(heads_here, share_count, part_rows, HD).transpose(1, 2, 0, 3)
        return shaped.reshape(rows_here, heads_here * HD)

    text_keys = lax.dynamic_slice_in_dim(k_txt, head_index * HD, HD, 1)
    text_values = lax.dynamic_slice_in_dim(v_txt, head_index * HD, HD, 1)
    query_side = jnp.concatenate([to_heads(q_img), to_heads(attn_grad)], axis=2)
    key_side = jnp.concatenate([whole_heads(k_img), whole_heads(v_img)], axis=2)
    packed = jnp.concatenate([query_side, key_side], axis=1)
    received = lax.all_to_all(packed, "seq", split_axis=0, concat_axis=0, tiled=True)
    queries = received[:, :part_rows, :HD].reshape(seq_count * part_rows, HD)
    cotangents = received[:, :part_rows, HD:].reshape(seq_count * part_rows, HD)
    image_keys = received[:, part_rows:, :HD].reshape(seq_count * rows_here, HD)
    image_values = received[:, part_rows:, HD:].reshape(seq_count * rows_here, HD)
    key_rows = jnp.concatenate([image_keys, text_keys], axis=0)
    value_rows = jnp.concatenate([image_values, text_values], axis=0)
    query_grad, out_rows, key_grad, value_grad = attend(
        queries, cotangents, key_rows, value_rows, min(512, queries.shape[0])
    )
    image_count = image_keys.shape[0]
    query_part = (
        jnp.concatenate([query_grad, out_rows], axis=1)
        .astype(jnp.float32)
        .reshape(seq_count, part_rows, 2 * HD)
    )
    key_part = jnp.concatenate([key_grad[:image_count], value_grad[:image_count]], axis=1).reshape(
        seq_count, rows_here, 2 * HD
    )
    returned = lax.all_to_all(
        jnp.concatenate([query_part, key_part], axis=1).astype(jnp.bfloat16),
        "seq",
        split_axis=0,
        concat_axis=0,
        tiled=True,
    ).astype(jnp.float32)
    q_grad = from_heads(returned[:, :part_rows, :HD]).astype(jnp.bfloat16)
    out_tok = from_heads(returned[:, :part_rows, HD:]).astype(jnp.bfloat16)
    summed = jnp.sum(
        returned[:, part_rows:, :].reshape(heads_here, share_count, rows_here, 2 * HD), axis=1
    )
    summed = summed.transpose(1, 0, 2)
    k_grad = summed[:, :, :HD].reshape(rows_here, heads_here * HD).astype(jnp.bfloat16)
    v_grad = summed[:, :, HD:].reshape(rows_here, heads_here * HD).astype(jnp.bfloat16)
    column_cut = d_out
    d_weight = lax.psum_scatter(
        jnp.dot(column_cut.T, out_tok, preferred_element_type=jnp.float32).astype(jnp.bfloat16),
        "seq",
        scatter_dimension=0,
        tiled=True,
    ).astype(jnp.float32)
    return (q_grad, k_grad, v_grad, d_weight)


def call(kernel, outs, args, specs=None, scratch=(), scalars=0, out_specs=None, flops=0, moved=0, limit=LIMIT):
    vmem = pl.BlockSpec(memory_space=pltpu.VMEM)
    if specs is None:
        specs = [vmem] * (len(args) - scalars)
    if out_specs is None:
        out_specs = [vmem] * len(outs)
    return pl.pallas_call(
        kernel,
        out_shape=outs,
        grid_spec=pltpu.PrefetchScalarGridSpec(
            num_scalar_prefetch=scalars,
            grid=(1,),
            in_specs=specs,
            out_specs=out_specs,
            scratch_shapes=list(scratch),
        ),
        compiler_params=pltpu.CompilerParams(vmem_limit_bytes=limit),
        cost_estimate=pl.CostEstimate(flops=flops, bytes_accessed=moved, transcendentals=0),
    )(*args)


STEPS = (0, 2, 4, 6)


def head_columns(step, other_row):
    return pl.ds(pl.multiple_of(jnp.bitwise_xor(lax.axis_index("seq"), step + other_row) * HD, HD), HD)


def pack_kernel(me_ref, q_ref, k_ref, v_ref, kt_ref, vt_ref, tok_ref, text_ref):
    rows = q_ref.shape[0]
    for h in range(tok_ref.shape[0]):
        for i, ref in enumerate((q_ref, k_ref, v_ref)):
            tok_ref[h, i * rows : (i + 1) * rows, :] = ref[:, h * HD : (h + 1) * HD]
    text_ref[0] = kt_ref[...]
    text_ref[1] = vt_ref[...]


def query_order(n):
    y = lax.rem(lax.axis_index("seq"), 2)
    return [2 * z + y for z in range(n // 2)] + [2 * z + 1 - y for z in range(n // 2)]


def forward_kernel(tok_ref, text_ref, probs_ref, out_ref, queries_ref, keys_t_ref, vals_ref, keys, vals_t, *, chunk):
    n, three, _ = tok_ref.shape
    rows = three // 3
    image = n * rows
    text = text_ref.shape[1]
    for i, source in enumerate(query_order(n)):
        queries_ref[i * rows : (i + 1) * rows, :] = tok_ref[source, 0:rows, :]
    keys[0:image, :] = tok_ref[:, rows : 2 * rows, :].reshape(image, HD)
    keys[image : image + text, :] = text_ref[0]
    vals_ref[0:image, :] = tok_ref[:, 2 * rows : 3 * rows, :].reshape(image, HD)
    vals_ref[image : image + text, :] = text_ref[1]
    keys_t_ref[...] = keys[...].T
    vals_t[...] = vals_ref[...].T
    factor = HD ** (-0.5) * math.log2(math.e)
    for c in range(image // chunk):
        span = slice(c * chunk, (c + 1) * chunk)
        scores = lax.dot_general(keys[...], queries_ref[span, :], NT, preferred_element_type=F32)
        top = jnp.max(scores, axis=0, keepdims=True)
        weights = jnp.exp2((scores - top) * factor)
        total = jnp.sum(weights, axis=0, keepdims=True)
        low = (weights * (1.0 / total)).astype(BF16)
        probs_ref[:, span] = low
        out_ref[:, span] = jnp.dot(vals_t[...], low, preferred_element_type=F32).astype(BF16)


def place_rows(piece_ref, swapped_ref, cot, start):
    me = lax.axis_index("seq")
    core = lax.axis_index("fsdp")
    part = piece_ref.shape[0] // len(STEPS)
    for piece, shift in ((piece_ref, core), (swapped_ref, 1 - core)):
        for i, step in enumerate(STEPS):
            z = jnp.bitwise_xor(me, step) // 2
            at = pl.multiple_of(start + z * (2 * part) + shift * part, 16)
            cot[pl.ds(at, part), :] = piece[i * part : (i + 1) * part, :]


def partial_kernel(piece_ref, swapped_ref, own_ref, other_ref, mine_ref, near_ref, far_ref, send_ref, cot, weight):
    place_rows(piece_ref, swapped_ref, cot, 0)
    me = lax.axis_index("seq")
    depth = own_ref.shape[0]
    y = lax.rem(me, 2)
    weight[pl.ds(pl.multiple_of(y * depth, 16), depth), :] = own_ref[...]
    weight[pl.ds(pl.multiple_of((1 - y) * depth, 16), depth), :] = other_ref[...]
    for step, ref in zip(STEPS, (mine_ref, near_ref, far_ref, send_ref)):
        z = jnp.bitwise_xor(me, step) // 2
        cols = pl.ds(pl.multiple_of(z * 2 * HD, 2 * HD), 2 * HD)
        ref[...] = jnp.dot(cot[...], weight[:, cols], preferred_element_type=F32).astype(ref.dtype)


def add_kernel(kept_ref, received_ref, out_ref):
    out_ref[...] = (kept_ref[...] + received_ref[...].astype(F32)).astype(BF16)


def finish_kernel(mine_ref, near_ref, far_ref, kept_ref, give_ref):
    heads = mine_ref[...] + near_ref[...].astype(F32) + far_ref[...].astype(F32)
    first, second = heads[:, :HD].astype(BF16), heads[:, HD:].astype(BF16)
    first_row = lax.rem(lax.axis_index("seq"), 2) == 0
    kept_ref[...] = jnp.where(first_row, first, second)
    give_ref[...] = jnp.where(first_row, second, first)


def weight_grad_kernel(*refs):
    *pieces, out0, out1, out2, out3, own_ref, other_ref, cot, outs = refs
    tokens = cot.shape[0]
    place_rows(pieces[0], pieces[1], cot, 0)
    place_rows(pieces[2], pieces[3], cot, tokens // 2)
    for i, ref in enumerate((out0, out1, out2, out3)):
        outs[i * HD : (i + 1) * HD, :] = ref[...]
    depth = own_ref.shape[1]
    y = lax.rem(lax.axis_index("seq"), 2)
    for ref, row in ((own_ref, y), (other_ref, 1 - y)):
        cols = pl.ds(pl.multiple_of(row * depth, HD), depth)
        ref[...] = jnp.dot(outs[...], cot[:, cols], preferred_element_type=F32).astype(BF16)


def backward_half(first, queries_ref, keys_t_ref, vals_ref, probs_ref, out_ref, grads_ref, dq_ref, dk, dv, chunk):
    image = dk.shape[0]
    scale = HD ** (-0.5)
    tokens = grads_ref.shape[0]
    start = 0 if first else tokens
    for c in range(tokens // chunk):
        span = slice(start + c * chunk, start + (c + 1) * chunk)
        within = slice(c * chunk, (c + 1) * chunk)
        grads = grads_ref[within, :]
        row_dot = jnp.sum(
            grads.astype(F32).T * out_ref[:, span].astype(F32), axis=0, keepdims=True
        )
        prob_grad = lax.dot_general(vals_ref[...], grads, NT, preferred_element_type=F32)
        low = probs_ref[:, span]
        score_grad = (low.astype(F32) * (prob_grad - row_dot)).astype(BF16)
        dq = jnp.dot(keys_t_ref[...], score_grad, preferred_element_type=F32) * scale
        dq_ref[within, :] = dq.T.astype(BF16)
        dk_part = jnp.dot(score_grad[0:image, :], queries_ref[span, :], preferred_element_type=F32)
        dv_part = jnp.dot(low[0:image, :], grads, preferred_element_type=F32)
        if first and c == 0:
            dk[...] = dk_part
            dv[...] = dv_part
        else:
            dk[...] += dk_part
            dv[...] += dv_part


def backward_first_kernel(queries_ref, keys_t_ref, vals_ref, probs_ref, out_ref, grads_ref, dq_ref, dk_ref, dv_ref, *, chunk):
    backward_half(
        True, queries_ref, keys_t_ref, vals_ref, probs_ref, out_ref, grads_ref, dq_ref, dk_ref, dv_ref, chunk
    )


def backward_second_kernel(
    queries_ref, keys_t_ref, vals_ref, probs_ref, out_ref, grads_ref, dq0_ref, dk_ref, dv_ref, send_ref, dq1_ref, dk, dv, *, chunk
):
    n, three, _ = send_ref.shape
    rows = three // 3
    dk[...] = dk_ref[...]
    dv[...] = dv_ref[...]
    backward_half(
        False, queries_ref, keys_t_ref, vals_ref, probs_ref, out_ref, grads_ref, dq1_ref, dk, dv, chunk
    )
    for i, source in enumerate(query_order(n)):
        ref, at = (dq0_ref, i) if 2 * i < n else (dq1_ref, i - n // 2)
        send_ref[source, 0:rows, :] = ref[at * rows : (at + 1) * rows, :]
    send_ref[:, rows : 2 * rows, :] = (dk[...] * HD ** (-0.5)).astype(BF16).reshape(n, rows, HD)
    send_ref[:, 2 * rows : 3 * rows, :] = dv[...].astype(BF16).reshape(n, rows, HD)


def unpack_kernel(tok_ref, q_ref, k_ref, v_ref):
    rows = q_ref.shape[0]
    for h in range(tok_ref.shape[0]):
        for i, ref in enumerate((q_ref, k_ref, v_ref)):
            ref[:, h * HD : (h + 1) * HD] = tok_ref[h, i * rows : (i + 1) * rows, :]


def unpack_weight_kernel(own_ref, other_ref, w_ref):
    for other_row, ref in enumerate((own_ref, other_ref)):
        for i, step in enumerate(STEPS):
            w_ref[:, head_columns(step, other_row)] = ref[i * HD : (i + 1) * HD, :].astype(F32).T


def exchange(array, distance=0, cores=False):
    if not distance and not cores:
        return array
    size = 2 * lax.axis_size("seq")
    pairs = [(i, i ^ (2 * distance + int(cores))) for i in range(size)]
    return lax.ppermute(array, ("seq", "fsdp"), pairs)


def send_cotangents(d_out):
    rows, width = d_out.shape
    part, columns = rows // 2, width // len(STEPS)
    z = lax.axis_index("seq") // 2
    first = lax.axis_index("fsdp") * part
    return [
        exchange(lax.dynamic_slice(d_out, (first, (z ^ (step // 2)) * columns), (part, columns)), step)
        for step in STEPS
    ]


def local(q_img, k_img, v_img, k_txt, v_txt, out_weight, d_out):
    n = lax.axis_size("seq")
    rows, width = q_img.shape
    args = (q_img, k_img, v_img, k_txt, v_txt, out_weight, d_out)
    if n != 2 * len(STEPS) or width // HD != n or lax.axis_size("fsdp") != 2 or rows % 32:
        return local_general(*args)
    depth = out_weight.shape[0]
    image = n * rows
    text = k_txt.shape[0]
    total = image + text
    chunk = 2 * rows
    shape = jax.ShapeDtypeStruct
    vmem = pl.BlockSpec(memory_space=pltpu.VMEM)

    head = pl.BlockSpec((text, HD), lambda i, me_ref: (0, me_ref[0]))
    given = exchange(out_weight, 1)
    along = send_cotangents(d_out)
    tok_out, text_head = call(
        pack_kernel,
        [shape((n, 3 * rows, HD), BF16), shape((2, text, HD), BF16)],
        [lax.axis_index("seq").astype(jnp.int32)[None], q_img, k_img, v_img, k_txt, v_txt],
        specs=[vmem] * 3 + [head] * 2,
        scalars=1,
        moved=4 * 3 * rows * width,
        limit=60 * 1024 * 1024,
    )
    tok_out, along = lax.optimization_barrier((tok_out, along))
    along, given = lax.optimization_barrier((along, given))
    row = jnp.concatenate(along, axis=0)
    row_swapped = exchange(row, cores=True)
    tok_in = lax.all_to_all(tok_out, "seq", split_axis=0, concat_axis=0, tiled=True)

    probs, out_t, queries, keys_t, vals = call(
        functools.partial(forward_kernel, chunk=chunk),
        [shape(dims, BF16) for dims in ((total, image), (HD, image), (image, HD), (HD, total), (total, HD))],
        [tok_in, text_head],
        scratch=[pltpu.VMEM((total, HD), BF16), pltpu.VMEM((HD, total), BF16)],
        flops=4 * total * image * HD,
        moved=4 * total * image,
    )
    columns = row.shape[1]
    mine, near, far, send = call(
        partial_kernel,
        [shape((image // 2, 2 * HD), kind) for kind in (F32, BF16, F32, BF16)],
        [row, row_swapped, out_weight, given],
        scratch=[pltpu.VMEM((image // 2, columns), BF16), pltpu.VMEM((columns, width), BF16)],
        flops=8 * image * columns * HD,
        moved=2 * image * columns,
    )
    send, near = lax.optimization_barrier((exchange(send, 2), near))
    (far,) = call(add_kernel, [shape(far.shape, BF16)], [far, send])
    far, near = exchange(far, 4), exchange(near, 2)
    out_late, far, near = lax.optimization_barrier((out_t, far, near))
    kept, give = call(finish_kernel, [shape((image // 2, HD), BF16)] * 2, [mine, near, far])
    got = exchange(give, 1)
    out_near, out_far = exchange(out_late, 2), exchange(out_late, 4)
    row, got = lax.optimization_barrier((row, got))
    other_row = exchange(row, 1)
    other_swapped = exchange(other_row, cores=True)
    dq, dk, dv = call(
        functools.partial(backward_first_kernel, chunk=chunk),
        [shape((image // 2, HD), BF16)] + [shape((image, HD), F32)] * 2,
        [queries, keys_t, vals, probs, out_t, kept],
        flops=4 * total * image * HD,
        moved=2 * total * image,
    )
    (grad_out,) = call(
        functools.partial(backward_second_kernel, chunk=chunk),
        [shape((n, 3 * rows, HD), BF16)],
        [queries, keys_t, vals, probs, out_t, got, dq, dk, dv],
        scratch=[pltpu.VMEM((image // 2, HD), BF16)] + [pltpu.VMEM((image, HD), F32)] * 2,
        flops=4 * total * image * HD,
        moved=2 * total * image,
    )
    grad_in = lax.all_to_all(grad_out, "seq", split_axis=0, concat_axis=0, tiled=True)
    out_far, out_near, other_row, _ = lax.optimization_barrier((out_far, out_near, other_row, grad_out))
    outs = [out_t, out_near, out_far, exchange(out_far, 2)]
    dw_own, dw_other = call(
        weight_grad_kernel,
        [shape((4 * HD, depth), BF16)] * 2,
        [row, row_swapped, other_row, other_swapped, *outs],
        scratch=[pltpu.VMEM((image, columns), BF16), pltpu.VMEM((4 * HD, image), BF16)],
        flops=96 * image * columns * HD,
        moved=2 * image * columns,
    )
    grads = call(
        unpack_kernel,
        [shape((rows, width), BF16)] * 3,
        [grad_in],
        moved=4 * 3 * rows * width,
    )
    (d_weight,) = call(
        unpack_weight_kernel,
        [shape((depth, width), F32)],
        [dw_own, exchange(dw_other, 1)],
        moved=6 * depth * width,
    )
    return (*grads, d_weight)


def solution(mesh):
    in_specs = (
        P(("group", "seq"), "fsdp"),
        P(("group", "seq"), "fsdp"),
        P(("group", "seq"), "fsdp"),
        P("group", "fsdp"),
        P("group", "fsdp"),
        P("seq", "fsdp"),
        P(("group", "seq"), None),
    )
    out_specs = (
        P(("group", "seq"), "fsdp"),
        P(("group", "seq"), "fsdp"),
        P(("group", "seq"), "fsdp"),
        P(("group", "seq"), "fsdp"),
    )
    return jax.shard_map(local, mesh=mesh, in_specs=in_specs, out_specs=out_specs, check_vma=False)
```

```python
import functools
import math

import jax
import jax.numpy as jnp
from jax import lax
from jax.experimental import pallas as pl
from jax.experimental.pallas import tpu as pltpu
from jax.sharding import PartitionSpec as P

HD = 128
F32 = jnp.float32
BF16 = jnp.bfloat16
LIMIT = 16 * 1024 * 1024
NT = (((1,), (1,)), ((), ()))


def attend(queries, cotangents, key_rows, value_rows, block_rows):
    score_scale = HD ** (-0.5)
    query_count = queries.shape[0]
    block_count = query_count // block_rows
    query_blocks = queries.reshape(block_count, block_rows, HD)
    grad_blocks = cotangents.reshape(block_count, block_rows, HD)

    def one_block(accumulated, pair_item):
        query_block, grad_block = pair_item
        scores = jnp.dot(query_block, key_rows.T, preferred_element_type=jnp.float32) * score_scale
        row_max = jnp.max(scores, axis=1, keepdims=True)
        probs = jnp.exp(scores - row_max)
        probs = probs / jnp.sum(probs, axis=1, keepdims=True)
        probs_low = probs.astype(jnp.bfloat16)
        out_rows = jnp.dot(probs_low, value_rows, preferred_element_type=jnp.float32).astype(
            jnp.bfloat16
        )
        prob_grad = jnp.dot(grad_block, value_rows.T, preferred_element_type=jnp.float32)
        row_dot = jnp.sum(
            grad_block.astype(jnp.float32) * out_rows.astype(jnp.float32), axis=1, keepdims=True
        )
        score_grad = (probs * (prob_grad - row_dot)).astype(jnp.bfloat16)
        query_grad = (
            jnp.dot(score_grad, key_rows, preferred_element_type=jnp.float32) * score_scale
        ).astype(jnp.bfloat16)
        key_grad = (
            accumulated[0]
            + jnp.dot(score_grad.T, query_block, preferred_element_type=jnp.float32) * score_scale
        )
        value_grad = accumulated[1] + jnp.dot(
            probs_low.T, grad_block, preferred_element_type=jnp.float32
        )
        return ((key_grad, value_grad), (query_grad, out_rows))

    empty = jnp.zeros((key_rows.shape[0], HD), jnp.float32)
    (key_grad, value_grad), (query_grad, out_rows) = lax.scan(
        one_block, (empty, empty), (query_blocks, grad_blocks)
    )
    return (
        query_grad.reshape(query_count, HD),
        out_rows.reshape(query_count, HD),
        key_grad,
        value_grad,
    )


def local_general(q_img, k_img, v_img, k_txt, v_txt, out_weight, d_out):
    rows_here = q_img.shape[0]
    heads_here = q_img.shape[1] // HD
    seq_count = lax.axis_size("seq")
    share_count = seq_count // heads_here
    part_rows = rows_here // share_count
    seq_index = lax.axis_index("seq")
    head_index = seq_index // share_count
    column_cut = d_out
    attn_grad = jnp.dot(
        column_cut,
        lax.all_gather(out_weight, "seq", axis=0, tiled=True),
        preferred_element_type=jnp.float32,
    ).astype(jnp.bfloat16)

    def to_heads(array_in):
        shaped = array_in.reshape(share_count, part_rows, heads_here, HD).transpose(2, 0, 1, 3)
        return shaped.reshape(seq_count, part_rows, HD)

    def whole_heads(array_in):
        shaped = array_in.reshape(rows_here, heads_here, HD).transpose(1, 0, 2)
        shaped = jnp.broadcast_to(shaped[:, None], (heads_here, share_count, rows_here, HD))
        return shaped.reshape(seq_count, rows_here, HD)

    def from_heads(array_in):
        shaped = array_in.reshape(heads_here, share_count, part_rows, HD).transpose(1, 2, 0, 3)
        return shaped.reshape(rows_here, heads_here * HD)

    text_keys = lax.dynamic_slice_in_dim(k_txt, head_index * HD, HD, 1)
    text_values = lax.dynamic_slice_in_dim(v_txt, head_index * HD, HD, 1)
    query_side = jnp.concatenate([to_heads(q_img), to_heads(attn_grad)], axis=2)
    key_side = jnp.concatenate([whole_heads(k_img), whole_heads(v_img)], axis=2)
    packed = jnp.concatenate([query_side, key_side], axis=1)
    received = lax.all_to_all(packed, "seq", split_axis=0, concat_axis=0, tiled=True)
    queries = received[:, :part_rows, :HD].reshape(seq_count * part_rows, HD)
    cotangents = received[:, :part_rows, HD:].reshape(seq_count * part_rows, HD)
    image_keys = received[:, part_rows:, :HD].reshape(seq_count * rows_here, HD)
    image_values = received[:, part_rows:, HD:].reshape(seq_count * rows_here, HD)
    key_rows = jnp.concatenate([image_keys, text_keys], axis=0)
    value_rows = jnp.concatenate([image_values, text_values], axis=0)
    query_grad, out_rows, key_grad, value_grad = attend(
        queries, cotangents, key_rows, value_rows, min(512, queries.shape[0])
    )
    image_count = image_keys.shape[0]
    query_part = (
        jnp.concatenate([query_grad, out_rows], axis=1)
        .astype(jnp.float32)
        .reshape(seq_count, part_rows, 2 * HD)
    )
    key_part = jnp.concatenate([key_grad[:image_count], value_grad[:image_count]], axis=1).reshape(
        seq_count, rows_here, 2 * HD
    )
    returned = lax.all_to_all(
        jnp.concatenate([query_part, key_part], axis=1).astype(jnp.bfloat16),
        "seq",
        split_axis=0,
        concat_axis=0,
        tiled=True,
    ).astype(jnp.float32)
    q_grad = from_heads(returned[:, :part_rows, :HD]).astype(jnp.bfloat16)
    out_tok = from_heads(returned[:, :part_rows, HD:]).astype(jnp.bfloat16)
    summed = jnp.sum(
        returned[:, part_rows:, :].reshape(heads_here, share_count, rows_here, 2 * HD), axis=1
    )
    summed = summed.transpose(1, 0, 2)
    k_grad = summed[:, :, :HD].reshape(rows_here, heads_here * HD).astype(jnp.bfloat16)
    v_grad = summed[:, :, HD:].reshape(rows_here, heads_here * HD).astype(jnp.bfloat16)
    column_cut = d_out
    d_weight = lax.psum_scatter(
        jnp.dot(column_cut.T, out_tok, preferred_element_type=jnp.float32).astype(jnp.bfloat16),
        "seq",
        scatter_dimension=0,
        tiled=True,
    ).astype(jnp.float32)
    return (q_grad, k_grad, v_grad, d_weight)


def call(kernel, outs, args, specs=None, scratch=(), scalars=0, out_specs=None, flops=0, moved=0, limit=LIMIT):
    vmem = pl.BlockSpec(memory_space=pltpu.VMEM)
    if specs is None:
        specs = [vmem] * (len(args) - scalars)
    if out_specs is None:
        out_specs = [vmem] * len(outs)
    return pl.pallas_call(
        kernel,
        out_shape=outs,
        grid_spec=pltpu.PrefetchScalarGridSpec(
            num_scalar_prefetch=scalars,
            grid=(1,),
            in_specs=specs,
            out_specs=out_specs,
            scratch_shapes=list(scratch),
        ),
        compiler_params=pltpu.CompilerParams(vmem_limit_bytes=limit),
        cost_estimate=pl.CostEstimate(flops=flops, bytes_accessed=moved, transcendentals=0),
    )(*args)


STEPS = (0, 2, 4, 6)


def head_columns(step, other_row):
    return pl.ds(pl.multiple_of(jnp.bitwise_xor(lax.axis_index("seq"), step + other_row) * HD, HD), HD)


def pack_kernel(me_ref, q_ref, k_ref, v_ref, kt_ref, vt_ref, tok_ref, text_ref):
    rows = q_ref.shape[0]
    for h in range(tok_ref.shape[0]):
        for i, ref in enumerate((q_ref, k_ref, v_ref)):
            tok_ref[h, i * rows : (i + 1) * rows, :] = ref[:, h * HD : (h + 1) * HD]
    text_ref[0] = kt_ref[...]
    text_ref[1] = vt_ref[...]


def query_order(n):
    y = lax.rem(lax.axis_index("seq"), 2)
    return [2 * z + y for z in range(n // 2)] + [2 * z + 1 - y for z in range(n // 2)]


def forward_kernel(tok_ref, text_ref, probs_ref, out_ref, queries_ref, keys_t_ref, vals_ref, keys, vals_t, *, chunk):
    n, three, _ = tok_ref.shape
    rows = three // 3
    image = n * rows
    text = text_ref.shape[1]
    for i, source in enumerate(query_order(n)):
        queries_ref[i * rows : (i + 1) * rows, :] = tok_ref[source, 0:rows, :]
    keys[0:image, :] = tok_ref[:, rows : 2 * rows, :].reshape(image, HD)
    keys[image : image + text, :] = text_ref[0]
    vals_ref[0:image, :] = tok_ref[:, 2 * rows : 3 * rows, :].reshape(image, HD)
    vals_ref[image : image + text, :] = text_ref[1]
    keys_t_ref[...] = keys[...].T
    vals_t[...] = vals_ref[...].T
    factor = HD ** (-0.5) * math.log2(math.e)
    for c in range(image // chunk):
        span = slice(c * chunk, (c + 1) * chunk)
        scores = lax.dot_general(keys[...], queries_ref[span, :], NT, preferred_element_type=F32)
        top = jnp.max(scores, axis=0, keepdims=True)
        weights = jnp.exp2((scores - top) * factor)
        total = jnp.sum(weights, axis=0, keepdims=True)
        low = (weights * (1.0 / total)).astype(BF16)
        probs_ref[:, span] = low
        out_ref[:, span] = jnp.dot(vals_t[...], low, preferred_element_type=F32).astype(BF16)


def place_rows(piece_ref, swapped_ref, cot, start):
    me = lax.axis_index("seq")
    core = lax.axis_index("fsdp")
    part = piece_ref.shape[0] // len(STEPS)
    for piece, shift in ((piece_ref, core), (swapped_ref, 1 - core)):
        for i, step in enumerate(STEPS):
            z = jnp.bitwise_xor(me, step) // 2
            at = pl.multiple_of(start + z * (2 * part) + shift * part, 16)
            cot[pl.ds(at, part), :] = piece[i * part : (i + 1) * part, :]


def partial_kernel(piece_ref, swapped_ref, own_ref, other_ref, mine_ref, near_ref, far_ref, send_ref, cot, weight):
    place_rows(piece_ref, swapped_ref, cot, 0)
    me = lax.axis_index("seq")
    depth = own_ref.shape[0]
    y = lax.rem(me, 2)
    weight[pl.ds(pl.multiple_of(y * depth, 16), depth), :] = own_ref[...]
    weight[pl.ds(pl.multiple_of((1 - y) * depth, 16), depth), :] = other_ref[...]
    for step, ref in zip(STEPS, (mine_ref, near_ref, far_ref, send_ref)):
        z = jnp.bitwise_xor(me, step) // 2
        cols = pl.ds(pl.multiple_of(z * 2 * HD, 2 * HD), 2 * HD)
        ref[...] = jnp.dot(cot[...], weight[:, cols], preferred_element_type=F32).astype(ref.dtype)


def add_kernel(kept_ref, received_ref, out_ref):
    out_ref[...] = (kept_ref[...] + received_ref[...].astype(F32)).astype(BF16)


def finish_kernel(mine_ref, near_ref, far_ref, kept_ref, give_ref):
    heads = mine_ref[...] + near_ref[...].astype(F32) + far_ref[...].astype(F32)
    first, second = heads[:, :HD].astype(BF16), heads[:, HD:].astype(BF16)
    first_row = lax.rem(lax.axis_index("seq"), 2) == 0
    kept_ref[...] = jnp.where(first_row, first, second)
    give_ref[...] = jnp.where(first_row, second, first)


def weight_grad_kernel(*refs):
    *pieces, out0, out1, out2, out3, own_ref, other_ref, cot, outs = refs
    tokens = cot.shape[0]
    place_rows(pieces[0], pieces[1], cot, 0)
    place_rows(pieces[2], pieces[3], cot, tokens // 2)
    for i, ref in enumerate((out0, out1, out2, out3)):
        outs[i * HD : (i + 1) * HD, :] = ref[...]
    depth = own_ref.shape[1]
    y = lax.rem(lax.axis_index("seq"), 2)
    for ref, row in ((own_ref, y), (other_ref, 1 - y)):
        cols = pl.ds(pl.multiple_of(row * depth, HD), depth)
        ref[...] = jnp.dot(outs[...], cot[:, cols], preferred_element_type=F32).astype(BF16)


def backward_kernel(queries_ref, keys_t_ref, vals_ref, probs_ref, out_ref, *refs, chunk):
    *grad_refs, send_ref, dk, dv = refs
    n, three, _ = send_ref.shape
    rows = three // 3
    image = n * rows
    scale = HD ** (-0.5)
    per = chunk // rows
    order = query_order(n)
    half = image // chunk // 2
    for c in range(image // chunk):
        span = slice(c * chunk, (c + 1) * chunk)
        within = slice(c % half * chunk, (c % half + 1) * chunk)
        grads = grad_refs[c // half][within, :]
        row_dot = jnp.sum(
            grads.astype(F32).T * out_ref[:, span].astype(F32), axis=0, keepdims=True
        )
        prob_grad = lax.dot_general(vals_ref[...], grads, NT, preferred_element_type=F32)
        low = probs_ref[:, span]
        score_grad = (low.astype(F32) * (prob_grad - row_dot)).astype(BF16)
        dq = (jnp.dot(keys_t_ref[...], score_grad, preferred_element_type=F32) * scale).T.astype(BF16)
        for i in range(per):
            send_ref[order[c * per + i], 0:rows, :] = dq[i * rows : (i + 1) * rows, :]
        dk_part = jnp.dot(score_grad[0:image, :], queries_ref[span, :], preferred_element_type=F32)
        dv_part = jnp.dot(low[0:image, :], grads, preferred_element_type=F32)
        if c == 0:
            dk[...] = dk_part
            dv[...] = dv_part
        else:
            dk[...] += dk_part
            dv[...] += dv_part
    send_ref[:, rows : 2 * rows, :] = (dk[...] * scale).astype(BF16).reshape(n, rows, HD)
    send_ref[:, 2 * rows : 3 * rows, :] = dv[...].astype(BF16).reshape(n, rows, HD)


def unpack_kernel(tok_ref, q_ref, k_ref, v_ref):
    rows = q_ref.shape[0]
    for h in range(tok_ref.shape[0]):
        for i, ref in enumerate((q_ref, k_ref, v_ref)):
            ref[:, h * HD : (h + 1) * HD] = tok_ref[h, i * rows : (i + 1) * rows, :]


def unpack_weight_kernel(own_ref, other_ref, w_ref):
    for other_row, ref in enumerate((own_ref, other_ref)):
        for i, step in enumerate(STEPS):
            w_ref[:, head_columns(step, other_row)] = ref[i * HD : (i + 1) * HD, :].astype(F32).T


def exchange(array, distance=0, cores=False):
    if not distance and not cores:
        return array
    size = 2 * lax.axis_size("seq")
    pairs = [(i, i ^ (2 * distance + int(cores))) for i in range(size)]
    return lax.ppermute(array, ("seq", "fsdp"), pairs)


def send_cotangents(d_out):
    rows, width = d_out.shape
    part, columns = rows // 2, width // len(STEPS)
    z = lax.axis_index("seq") // 2
    first = lax.axis_index("fsdp") * part
    return [
        exchange(lax.dynamic_slice(d_out, (first, (z ^ (step // 2)) * columns), (part, columns)), step)
        for step in STEPS
    ]


def local(q_img, k_img, v_img, k_txt, v_txt, out_weight, d_out):
    n = lax.axis_size("seq")
    rows, width = q_img.shape
    args = (q_img, k_img, v_img, k_txt, v_txt, out_weight, d_out)
    if n != 2 * len(STEPS) or width // HD != n or lax.axis_size("fsdp") != 2 or rows % 32:
        return local_general(*args)
    depth = out_weight.shape[0]
    image = n * rows
    text = k_txt.shape[0]
    total = image + text
    chunk = 2 * rows
    shape = jax.ShapeDtypeStruct
    vmem = pl.BlockSpec(memory_space=pltpu.VMEM)

    head = pl.BlockSpec((text, HD), lambda i, me_ref: (0, me_ref[0]))
    given = exchange(out_weight, 1)
    along = send_cotangents(d_out)
    tok_out, text_head = call(
        pack_kernel,
        [shape((n, 3 * rows, HD), BF16), shape((2, text, HD), BF16)],
        [lax.axis_index("seq").astype(jnp.int32)[None], q_img, k_img, v_img, k_txt, v_txt],
        specs=[vmem] * 3 + [head] * 2,
        scalars=1,
        moved=4 * 3 * rows * width,
        limit=60 * 1024 * 1024,
    )
    tok_out, along = lax.optimization_barrier((tok_out, along))
    along, given = lax.optimization_barrier((along, given))
    row = jnp.concatenate(along, axis=0)
    row_swapped = exchange(row, cores=True)
    tok_in = lax.all_to_all(tok_out, "seq", split_axis=0, concat_axis=0, tiled=True)

    probs, out_t, queries, keys_t, vals = call(
        functools.partial(forward_kernel, chunk=chunk),
        [shape(dims, BF16) for dims in ((total, image), (HD, image), (image, HD), (HD, total), (total, HD))],
        [tok_in, text_head],
        scratch=[pltpu.VMEM((total, HD), BF16), pltpu.VMEM((HD, total), BF16)],
        flops=4 * total * image * HD,
        moved=4 * total * image,
    )
    columns = row.shape[1]
    mine, near, far, send = call(
        partial_kernel,
        [shape((image // 2, 2 * HD), kind) for kind in (F32, BF16, F32, BF16)],
        [row, row_swapped, out_weight, given],
        scratch=[pltpu.VMEM((image // 2, columns), BF16), pltpu.VMEM((columns, width), BF16)],
        flops=8 * image * columns * HD,
        moved=2 * image * columns,
    )
    row, send = lax.optimization_barrier((row, send))
    other_row = exchange(row, 1)
    send, near, other_row = lax.optimization_barrier((exchange(send, 2), near, other_row))
    (far,) = call(add_kernel, [shape(far.shape, BF16)], [far, send])
    far, near = exchange(far, 4), exchange(near, 2)
    out_near, out_far = exchange(out_t, 2), exchange(out_t, 4)
    kept, give = call(finish_kernel, [shape((image // 2, HD), BF16)] * 2, [mine, near, far])
    got = exchange(give, 1)
    other_swapped = exchange(other_row, cores=True)
    (grad_out,) = call(
        functools.partial(backward_kernel, chunk=chunk),
        [shape((n, 3 * rows, HD), BF16)],
        [queries, keys_t, vals, probs, out_t, kept, got],
        scratch=[pltpu.VMEM((image, HD), F32), pltpu.VMEM((image, HD), F32)],
    )
    grad_in = lax.all_to_all(grad_out, "seq", split_axis=0, concat_axis=0, tiled=True)
    out_far, out_near, _ = lax.optimization_barrier((out_far, out_near, grad_out))
    outs = [out_t, out_near, out_far, exchange(out_far, 2)]
    dw_own, dw_other = call(
        weight_grad_kernel,
        [shape((4 * HD, depth), BF16)] * 2,
        [row, row_swapped, other_row, other_swapped, *outs],
        scratch=[pltpu.VMEM((image, columns), BF16), pltpu.VMEM((4 * HD, image), BF16)],
        flops=96 * image * columns * HD,
        moved=2 * image * columns,
    )
    grads = call(
        unpack_kernel,
        [shape((rows, width), BF16)] * 3,
        [grad_in],
        moved=4 * 3 * rows * width,
    )
    (d_weight,) = call(
        unpack_weight_kernel,
        [shape((depth, width), F32)],
        [dw_own, exchange(dw_other, 1)],
        moved=6 * depth * width,
    )
    return (*grads, d_weight)


def solution(mesh):
    in_specs = (
        P(("group", "seq"), "fsdp"),
        P(("group", "seq"), "fsdp"),
        P(("group", "seq"), "fsdp"),
        P("group", "fsdp"),
        P("group", "fsdp"),
        P("seq", "fsdp"),
        P(("group", "seq"), None),
    )
    out_specs = (
        P(("group", "seq"), "fsdp"),
        P(("group", "seq"), "fsdp"),
        P(("group", "seq"), "fsdp"),
        P(("group", "seq"), "fsdp"),
    )
    return jax.shard_map(local, mesh=mesh, in_specs=in_specs, out_specs=out_specs, check_vma=False)
```

```python
import functools
import math

import jax
import jax.numpy as jnp
from jax import lax
from jax.experimental import pallas as pl
from jax.experimental.pallas import tpu as pltpu
from jax.sharding import PartitionSpec as P

HD = 128
F32 = jnp.float32
BF16 = jnp.bfloat16
LIMIT = 16 * 1024 * 1024
NT = (((1,), (1,)), ((), ()))


def attend(queries, cotangents, key_rows, value_rows, block_rows):
    score_scale = HD ** (-0.5)
    query_count = queries.shape[0]
    block_count = query_count // block_rows
    query_blocks = queries.reshape(block_count, block_rows, HD)
    grad_blocks = cotangents.reshape(block_count, block_rows, HD)

    def one_block(accumulated, pair_item):
        query_block, grad_block = pair_item
        scores = jnp.dot(query_block, key_rows.T, preferred_element_type=jnp.float32) * score_scale
        row_max = jnp.max(scores, axis=1, keepdims=True)
        probs = jnp.exp(scores - row_max)
        probs = probs / jnp.sum(probs, axis=1, keepdims=True)
        probs_low = probs.astype(jnp.bfloat16)
        out_rows = jnp.dot(probs_low, value_rows, preferred_element_type=jnp.float32).astype(
            jnp.bfloat16
        )
        prob_grad = jnp.dot(grad_block, value_rows.T, preferred_element_type=jnp.float32)
        row_dot = jnp.sum(
            grad_block.astype(jnp.float32) * out_rows.astype(jnp.float32), axis=1, keepdims=True
        )
        score_grad = (probs * (prob_grad - row_dot)).astype(jnp.bfloat16)
        query_grad = (
            jnp.dot(score_grad, key_rows, preferred_element_type=jnp.float32) * score_scale
        ).astype(jnp.bfloat16)
        key_grad = (
            accumulated[0]
            + jnp.dot(score_grad.T, query_block, preferred_element_type=jnp.float32) * score_scale
        )
        value_grad = accumulated[1] + jnp.dot(
            probs_low.T, grad_block, preferred_element_type=jnp.float32
        )
        return ((key_grad, value_grad), (query_grad, out_rows))

    empty = jnp.zeros((key_rows.shape[0], HD), jnp.float32)
    (key_grad, value_grad), (query_grad, out_rows) = lax.scan(
        one_block, (empty, empty), (query_blocks, grad_blocks)
    )
    return (
        query_grad.reshape(query_count, HD),
        out_rows.reshape(query_count, HD),
        key_grad,
        value_grad,
    )


def local_general(q_img, k_img, v_img, k_txt, v_txt, out_weight, d_out):
    rows_here = q_img.shape[0]
    heads_here = q_img.shape[1] // HD
    seq_count = lax.axis_size("seq")
    share_count = seq_count // heads_here
    part_rows = rows_here // share_count
    seq_index = lax.axis_index("seq")
    head_index = seq_index // share_count
    column_cut = d_out
    attn_grad = jnp.dot(
        column_cut,
        lax.all_gather(out_weight, "seq", axis=0, tiled=True),
        preferred_element_type=jnp.float32,
    ).astype(jnp.bfloat16)

    def to_heads(array_in):
        shaped = array_in.reshape(share_count, part_rows, heads_here, HD).transpose(2, 0, 1, 3)
        return shaped.reshape(seq_count, part_rows, HD)

    def whole_heads(array_in):
        shaped = array_in.reshape(rows_here, heads_here, HD).transpose(1, 0, 2)
        shaped = jnp.broadcast_to(shaped[:, None], (heads_here, share_count, rows_here, HD))
        return shaped.reshape(seq_count, rows_here, HD)

    def from_heads(array_in):
        shaped = array_in.reshape(heads_here, share_count, part_rows, HD).transpose(1, 2, 0, 3)
        return shaped.reshape(rows_here, heads_here * HD)

    text_keys = lax.dynamic_slice_in_dim(k_txt, head_index * HD, HD, 1)
    text_values = lax.dynamic_slice_in_dim(v_txt, head_index * HD, HD, 1)
    query_side = jnp.concatenate([to_heads(q_img), to_heads(attn_grad)], axis=2)
    key_side = jnp.concatenate([whole_heads(k_img), whole_heads(v_img)], axis=2)
    packed = jnp.concatenate([query_side, key_side], axis=1)
    received = lax.all_to_all(packed, "seq", split_axis=0, concat_axis=0, tiled=True)
    queries = received[:, :part_rows, :HD].reshape(seq_count * part_rows, HD)
    cotangents = received[:, :part_rows, HD:].reshape(seq_count * part_rows, HD)
    image_keys = received[:, part_rows:, :HD].reshape(seq_count * rows_here, HD)
    image_values = received[:, part_rows:, HD:].reshape(seq_count * rows_here, HD)
    key_rows = jnp.concatenate([image_keys, text_keys], axis=0)
    value_rows = jnp.concatenate([image_values, text_values], axis=0)
    query_grad, out_rows, key_grad, value_grad = attend(
        queries, cotangents, key_rows, value_rows, min(512, queries.shape[0])
    )
    image_count = image_keys.shape[0]
    query_part = (
        jnp.concatenate([query_grad, out_rows], axis=1)
        .astype(jnp.float32)
        .reshape(seq_count, part_rows, 2 * HD)
    )
    key_part = jnp.concatenate([key_grad[:image_count], value_grad[:image_count]], axis=1).reshape(
        seq_count, rows_here, 2 * HD
    )
    returned = lax.all_to_all(
        jnp.concatenate([query_part, key_part], axis=1).astype(jnp.bfloat16),
        "seq",
        split_axis=0,
        concat_axis=0,
        tiled=True,
    ).astype(jnp.float32)
    q_grad = from_heads(returned[:, :part_rows, :HD]).astype(jnp.bfloat16)
    out_tok = from_heads(returned[:, :part_rows, HD:]).astype(jnp.bfloat16)
    summed = jnp.sum(
        returned[:, part_rows:, :].reshape(heads_here, share_count, rows_here, 2 * HD), axis=1
    )
    summed = summed.transpose(1, 0, 2)
    k_grad = summed[:, :, :HD].reshape(rows_here, heads_here * HD).astype(jnp.bfloat16)
    v_grad = summed[:, :, HD:].reshape(rows_here, heads_here * HD).astype(jnp.bfloat16)
    column_cut = d_out
    d_weight = lax.psum_scatter(
        jnp.dot(column_cut.T, out_tok, preferred_element_type=jnp.float32).astype(jnp.bfloat16),
        "seq",
        scatter_dimension=0,
        tiled=True,
    ).astype(jnp.float32)
    return (q_grad, k_grad, v_grad, d_weight)


def call(kernel, outs, args, specs=None, scratch=(), scalars=0, out_specs=None, flops=0, moved=0, limit=LIMIT):
    vmem = pl.BlockSpec(memory_space=pltpu.VMEM)
    if specs is None:
        specs = [vmem] * (len(args) - scalars)
    if out_specs is None:
        out_specs = [vmem] * len(outs)
    return pl.pallas_call(
        kernel,
        out_shape=outs,
        grid_spec=pltpu.PrefetchScalarGridSpec(
            num_scalar_prefetch=scalars,
            grid=(1,),
            in_specs=specs,
            out_specs=out_specs,
            scratch_shapes=list(scratch),
        ),
        compiler_params=pltpu.CompilerParams(vmem_limit_bytes=limit),
        cost_estimate=pl.CostEstimate(flops=flops, bytes_accessed=moved, transcendentals=0),
    )(*args)


STEPS = (0, 2, 4, 6)


def head_columns(step, other_row):
    return pl.ds(pl.multiple_of(jnp.bitwise_xor(lax.axis_index("seq"), step + other_row) * HD, HD), HD)


def pack_kernel(me_ref, q_ref, k_ref, v_ref, kt_ref, vt_ref, tok_ref, text_ref):
    rows = q_ref.shape[0]
    for h in range(tok_ref.shape[0]):
        for i, ref in enumerate((q_ref, k_ref, v_ref)):
            tok_ref[h, i * rows : (i + 1) * rows, :] = ref[:, h * HD : (h + 1) * HD]
    text_ref[0] = kt_ref[...]
    text_ref[1] = vt_ref[...]


def query_order(n):
    y = lax.rem(lax.axis_index("seq"), 2)
    return [2 * z + y for z in range(n // 2)] + [2 * z + 1 - y for z in range(n // 2)]


def forward_kernel(tok_ref, text_ref, probs_ref, out_ref, queries_ref, keys_t_ref, vals_ref, keys, vals_t, *, chunk):
    n, three, _ = tok_ref.shape
    rows = three // 3
    image = n * rows
    text = text_ref.shape[1]
    for i, source in enumerate(query_order(n)):
        queries_ref[i * rows : (i + 1) * rows, :] = tok_ref[source, 0:rows, :]
    keys[0:image, :] = tok_ref[:, rows : 2 * rows, :].reshape(image, HD)
    keys[image : image + text, :] = text_ref[0]
    vals_ref[0:image, :] = tok_ref[:, 2 * rows : 3 * rows, :].reshape(image, HD)
    vals_ref[image : image + text, :] = text_ref[1]
    keys_t_ref[...] = keys[...].T
    vals_t[...] = vals_ref[...].T
    factor = HD ** (-0.5) * math.log2(math.e)
    for c in range(image // chunk):
        span = slice(c * chunk, (c + 1) * chunk)
        scores = lax.dot_general(keys[...], queries_ref[span, :], NT, preferred_element_type=F32)
        top = jnp.max(scores, axis=0, keepdims=True)
        weights = jnp.exp2((scores - top) * factor)
        total = jnp.sum(weights, axis=0, keepdims=True)
        low = (weights * (1.0 / total)).astype(BF16)
        probs_ref[:, span] = low
        out_ref[:, span] = jnp.dot(vals_t[...], low, preferred_element_type=F32).astype(BF16)


def place_rows(piece_ref, swapped_ref, cot, start):
    me = lax.axis_index("seq")
    core = lax.axis_index("fsdp")
    part = piece_ref.shape[0] // len(STEPS)
    for piece, shift in ((piece_ref, core), (swapped_ref, 1 - core)):
        for i, step in enumerate(STEPS):
            z = jnp.bitwise_xor(me, step) // 2
            at = pl.multiple_of(start + z * (2 * part) + shift * part, 16)
            cot[pl.ds(at, part), :] = piece[i * part : (i + 1) * part, :]


def partial_kernel(piece_ref, swapped_ref, own_ref, other_ref, mine_ref, near_ref, far_ref, send_ref, cot, weight):
    place_rows(piece_ref, swapped_ref, cot, 0)
    me = lax.axis_index("seq")
    depth = own_ref.shape[0]
    y = lax.rem(me, 2)
    weight[pl.ds(pl.multiple_of(y * depth, 16), depth), :] = own_ref[...]
    weight[pl.ds(pl.multiple_of((1 - y) * depth, 16), depth), :] = other_ref[...]
    for step, ref in zip(STEPS, (mine_ref, near_ref, far_ref, send_ref)):
        z = jnp.bitwise_xor(me, step) // 2
        cols = pl.ds(pl.multiple_of(z * 2 * HD, 2 * HD), 2 * HD)
        ref[...] = jnp.dot(cot[...], weight[:, cols], preferred_element_type=F32).astype(ref.dtype)


def add_kernel(kept_ref, received_ref, out_ref):
    out_ref[...] = (kept_ref[...] + received_ref[...].astype(F32)).astype(BF16)


def finish_kernel(mine_ref, near_ref, far_ref, kept_ref, give_ref):
    heads = mine_ref[...] + near_ref[...].astype(F32) + far_ref[...].astype(F32)
    first, second = heads[:, :HD].astype(BF16), heads[:, HD:].astype(BF16)
    first_row = lax.rem(lax.axis_index("seq"), 2) == 0
    kept_ref[...] = jnp.where(first_row, first, second)
    give_ref[...] = jnp.where(first_row, second, first)


def weight_grad_kernel(*refs):
    *pieces, out0, out1, out2, out3, own_ref, other_ref, cot, outs = refs
    tokens = cot.shape[0]
    place_rows(pieces[0], pieces[1], cot, 0)
    place_rows(pieces[2], pieces[3], cot, tokens // 2)
    for i, ref in enumerate((out0, out1, out2, out3)):
        outs[i * HD : (i + 1) * HD, :] = ref[...]
    depth = own_ref.shape[1]
    y = lax.rem(lax.axis_index("seq"), 2)
    for ref, row in ((own_ref, y), (other_ref, 1 - y)):
        cols = pl.ds(pl.multiple_of(row * depth, HD), depth)
        ref[...] = jnp.dot(outs[...], cot[:, cols], preferred_element_type=F32).astype(BF16)


def backward_kernel(queries_ref, keys_t_ref, vals_ref, probs_ref, out_ref, *refs, chunk):
    *grad_refs, send_ref, dk, dv = refs
    n, three, _ = send_ref.shape
    rows = three // 3
    image = n * rows
    scale = HD ** (-0.5)
    per = chunk // rows
    order = query_order(n)
    half = image // chunk // 2
    for c in range(image // chunk):
        span = slice(c * chunk, (c + 1) * chunk)
        within = slice(c % half * chunk, (c % half + 1) * chunk)
        grads = grad_refs[c // half][within, :]
        row_dot = jnp.sum(
            grads.astype(F32).T * out_ref[:, span].astype(F32), axis=0, keepdims=True
        )
        prob_grad = lax.dot_general(vals_ref[...], grads, NT, preferred_element_type=F32)
        low = probs_ref[:, span]
        score_grad = (low.astype(F32) * (prob_grad - row_dot)).astype(BF16)
        dq = (jnp.dot(keys_t_ref[...], score_grad, preferred_element_type=F32) * scale).T.astype(BF16)
        for i in range(per):
            send_ref[order[c * per + i], 0:rows, :] = dq[i * rows : (i + 1) * rows, :]
        dk_part = jnp.dot(score_grad[0:image, :], queries_ref[span, :], preferred_element_type=F32)
        dv_part = jnp.dot(low[0:image, :], grads, preferred_element_type=F32)
        if c == 0:
            dk[...] = dk_part
            dv[...] = dv_part
        else:
            dk[...] += dk_part
            dv[...] += dv_part
    send_ref[:, rows : 2 * rows, :] = (dk[...] * scale).astype(BF16).reshape(n, rows, HD)
    send_ref[:, 2 * rows : 3 * rows, :] = dv[...].astype(BF16).reshape(n, rows, HD)


def unpack_kernel(tok_ref, q_ref, k_ref, v_ref):
    rows = q_ref.shape[0]
    for h in range(tok_ref.shape[0]):
        for i, ref in enumerate((q_ref, k_ref, v_ref)):
            ref[:, h * HD : (h + 1) * HD] = tok_ref[h, i * rows : (i + 1) * rows, :]


def unpack_weight_kernel(own_ref, other_ref, w_ref):
    for other_row, ref in enumerate((own_ref, other_ref)):
        for i, step in enumerate(STEPS):
            w_ref[:, head_columns(step, other_row)] = ref[i * HD : (i + 1) * HD, :].astype(F32).T


def exchange(array, distance=0, cores=False):
    if not distance and not cores:
        return array
    size = 2 * lax.axis_size("seq")
    pairs = [(i, i ^ (2 * distance + int(cores))) for i in range(size)]
    return lax.ppermute(array, ("seq", "fsdp"), pairs)


def send_cotangents(d_out):
    rows, width = d_out.shape
    part, columns = rows // 2, width // len(STEPS)
    z = lax.axis_index("seq") // 2
    first = lax.axis_index("fsdp") * part
    return [
        exchange(lax.dynamic_slice(d_out, (first, (z ^ (step // 2)) * columns), (part, columns)), step)
        for step in STEPS
    ]


def local(q_img, k_img, v_img, k_txt, v_txt, out_weight, d_out):
    n = lax.axis_size("seq")
    rows, width = q_img.shape
    args = (q_img, k_img, v_img, k_txt, v_txt, out_weight, d_out)
    if n != 2 * len(STEPS) or width // HD != n or lax.axis_size("fsdp") != 2 or rows % 32:
        return local_general(*args)
    depth = out_weight.shape[0]
    image = n * rows
    text = k_txt.shape[0]
    total = image + text
    chunk = 2 * rows
    shape = jax.ShapeDtypeStruct
    vmem = pl.BlockSpec(memory_space=pltpu.VMEM)

    head = pl.BlockSpec((text, HD), lambda i, me_ref: (0, me_ref[0]))
    given = exchange(out_weight, 1)
    along = send_cotangents(d_out)
    tok_out, text_head = call(
        pack_kernel,
        [shape((n, 3 * rows, HD), BF16), shape((2, text, HD), BF16)],
        [lax.axis_index("seq").astype(jnp.int32)[None], q_img, k_img, v_img, k_txt, v_txt],
        specs=[vmem] * 3 + [head] * 2,
        scalars=1,
        moved=4 * 3 * rows * width,
        limit=60 * 1024 * 1024,
    )
    tok_out, along = lax.optimization_barrier((tok_out, along))
    along, given = lax.optimization_barrier((along, given))
    row = jnp.concatenate(along, axis=0)
    row_swapped = exchange(row, cores=True)
    tok_in = lax.all_to_all(tok_out, "seq", split_axis=0, concat_axis=0, tiled=True)

    probs, out_t, queries, keys_t, vals = call(
        functools.partial(forward_kernel, chunk=chunk),
        [shape(dims, BF16) for dims in ((total, image), (HD, image), (image, HD), (HD, total), (total, HD))],
        [tok_in, text_head],
        scratch=[pltpu.VMEM((total, HD), BF16), pltpu.VMEM((HD, total), BF16)],
        flops=4 * total * image * HD,
        moved=4 * total * image,
    )
    columns = row.shape[1]
    mine, near, far, send = call(
        partial_kernel,
        [shape((image // 2, 2 * HD), kind) for kind in (F32, BF16, F32, BF16)],
        [row, row_swapped, out_weight, given],
        scratch=[pltpu.VMEM((image // 2, columns), BF16), pltpu.VMEM((columns, width), BF16)],
        flops=8 * image * columns * HD,
        moved=2 * image * columns,
    )
    send, near = lax.optimization_barrier((exchange(send, 2), near))
    (far,) = call(add_kernel, [shape(far.shape, BF16)], [far, send])
    far, near = exchange(far, 4), exchange(near, 2)
    out_near, out_far = exchange(out_t, 2), exchange(out_t, 4)
    kept, give = call(finish_kernel, [shape((image // 2, HD), BF16)] * 2, [mine, near, far])
    got = exchange(give, 1)
    row, _ = lax.optimization_barrier((row, out_t))
    other_row = exchange(row, 1)
    other_swapped = exchange(other_row, cores=True)
    (grad_out,) = call(
        functools.partial(backward_kernel, chunk=chunk),
        [shape((n, 3 * rows, HD), BF16)],
        [queries, keys_t, vals, probs, out_t, kept, got],
        scratch=[pltpu.VMEM((image, HD), F32), pltpu.VMEM((image, HD), F32)],
    )
    grad_in = lax.all_to_all(grad_out, "seq", split_axis=0, concat_axis=0, tiled=True)
    out_far, out_near, _ = lax.optimization_barrier((out_far, out_near, grad_out))
    outs = [out_t, out_near, out_far, exchange(out_far, 2)]
    dw_own, dw_other = call(
        weight_grad_kernel,
        [shape((4 * HD, depth), BF16)] * 2,
        [row, row_swapped, other_row, other_swapped, *outs],
        scratch=[pltpu.VMEM((image, columns), BF16), pltpu.VMEM((4 * HD, image), BF16)],
        flops=96 * image * columns * HD,
        moved=2 * image * columns,
    )
    grads = call(
        unpack_kernel,
        [shape((rows, width), BF16)] * 3,
        [grad_in],
        moved=4 * 3 * rows * width,
    )
    (d_weight,) = call(
        unpack_weight_kernel,
        [shape((depth, width), F32)],
        [dw_own, exchange(dw_other, 1)],
        moved=6 * depth * width,
    )
    return (*grads, d_weight)


def solution(mesh):
    in_specs = (
        P(("group", "seq"), "fsdp"),
        P(("group", "seq"), "fsdp"),
        P(("group", "seq"), "fsdp"),
        P("group", "fsdp"),
        P("group", "fsdp"),
        P("seq", "fsdp"),
        P(("group", "seq"), None),
    )
    out_specs = (
        P(("group", "seq"), "fsdp"),
        P(("group", "seq"), "fsdp"),
        P(("group", "seq"), "fsdp"),
        P(("group", "seq"), "fsdp"),
    )
    return jax.shard_map(local, mesh=mesh, in_specs=in_specs, out_specs=out_specs, check_vma=False)
```

```python
import functools
import math

import jax
import jax.numpy as jnp
from jax import lax
from jax.experimental import pallas as pl
from jax.experimental.pallas import tpu as pltpu
from jax.sharding import PartitionSpec as P

HD = 128
F32 = jnp.float32
BF16 = jnp.bfloat16
LIMIT = 16 * 1024 * 1024
NT = (((1,), (1,)), ((), ()))


def attend(queries, cotangents, key_rows, value_rows, block_rows):
    score_scale = HD ** (-0.5)
    query_count = queries.shape[0]
    block_count = query_count // block_rows
    query_blocks = queries.reshape(block_count, block_rows, HD)
    grad_blocks = cotangents.reshape(block_count, block_rows, HD)

    def one_block(accumulated, pair_item):
        query_block, grad_block = pair_item
        scores = jnp.dot(query_block, key_rows.T, preferred_element_type=jnp.float32) * score_scale
        row_max = jnp.max(scores, axis=1, keepdims=True)
        probs = jnp.exp(scores - row_max)
        probs = probs / jnp.sum(probs, axis=1, keepdims=True)
        probs_low = probs.astype(jnp.bfloat16)
        out_rows = jnp.dot(probs_low, value_rows, preferred_element_type=jnp.float32).astype(
            jnp.bfloat16
        )
        prob_grad = jnp.dot(grad_block, value_rows.T, preferred_element_type=jnp.float32)
        row_dot = jnp.sum(
            grad_block.astype(jnp.float32) * out_rows.astype(jnp.float32), axis=1, keepdims=True
        )
        score_grad = (probs * (prob_grad - row_dot)).astype(jnp.bfloat16)
        query_grad = (
            jnp.dot(score_grad, key_rows, preferred_element_type=jnp.float32) * score_scale
        ).astype(jnp.bfloat16)
        key_grad = (
            accumulated[0]
            + jnp.dot(score_grad.T, query_block, preferred_element_type=jnp.float32) * score_scale
        )
        value_grad = accumulated[1] + jnp.dot(
            probs_low.T, grad_block, preferred_element_type=jnp.float32
        )
        return ((key_grad, value_grad), (query_grad, out_rows))

    empty = jnp.zeros((key_rows.shape[0], HD), jnp.float32)
    (key_grad, value_grad), (query_grad, out_rows) = lax.scan(
        one_block, (empty, empty), (query_blocks, grad_blocks)
    )
    return (
        query_grad.reshape(query_count, HD),
        out_rows.reshape(query_count, HD),
        key_grad,
        value_grad,
    )


def local_general(q_img, k_img, v_img, k_txt, v_txt, out_weight, d_out):
    rows_here = q_img.shape[0]
    heads_here = q_img.shape[1] // HD
    seq_count = lax.axis_size("seq")
    share_count = seq_count // heads_here
    part_rows = rows_here // share_count
    seq_index = lax.axis_index("seq")
    head_index = seq_index // share_count
    column_cut = d_out
    attn_grad = jnp.dot(
        column_cut,
        lax.all_gather(out_weight, "seq", axis=0, tiled=True),
        preferred_element_type=jnp.float32,
    ).astype(jnp.bfloat16)

    def to_heads(array_in):
        shaped = array_in.reshape(share_count, part_rows, heads_here, HD).transpose(2, 0, 1, 3)
        return shaped.reshape(seq_count, part_rows, HD)

    def whole_heads(array_in):
        shaped = array_in.reshape(rows_here, heads_here, HD).transpose(1, 0, 2)
        shaped = jnp.broadcast_to(shaped[:, None], (heads_here, share_count, rows_here, HD))
        return shaped.reshape(seq_count, rows_here, HD)

    def from_heads(array_in):
        shaped = array_in.reshape(heads_here, share_count, part_rows, HD).transpose(1, 2, 0, 3)
        return shaped.reshape(rows_here, heads_here * HD)

    text_keys = lax.dynamic_slice_in_dim(k_txt, head_index * HD, HD, 1)
    text_values = lax.dynamic_slice_in_dim(v_txt, head_index * HD, HD, 1)
    query_side = jnp.concatenate([to_heads(q_img), to_heads(attn_grad)], axis=2)
    key_side = jnp.concatenate([whole_heads(k_img), whole_heads(v_img)], axis=2)
    packed = jnp.concatenate([query_side, key_side], axis=1)
    received = lax.all_to_all(packed, "seq", split_axis=0, concat_axis=0, tiled=True)
    queries = received[:, :part_rows, :HD].reshape(seq_count * part_rows, HD)
    cotangents = received[:, :part_rows, HD:].reshape(seq_count * part_rows, HD)
    image_keys = received[:, part_rows:, :HD].reshape(seq_count * rows_here, HD)
    image_values = received[:, part_rows:, HD:].reshape(seq_count * rows_here, HD)
    key_rows = jnp.concatenate([image_keys, text_keys], axis=0)
    value_rows = jnp.concatenate([image_values, text_values], axis=0)
    query_grad, out_rows, key_grad, value_grad = attend(
        queries, cotangents, key_rows, value_rows, min(512, queries.shape[0])
    )
    image_count = image_keys.shape[0]
    query_part = (
        jnp.concatenate([query_grad, out_rows], axis=1)
        .astype(jnp.float32)
        .reshape(seq_count, part_rows, 2 * HD)
    )
    key_part = jnp.concatenate([key_grad[:image_count], value_grad[:image_count]], axis=1).reshape(
        seq_count, rows_here, 2 * HD
    )
    returned = lax.all_to_all(
        jnp.concatenate([query_part, key_part], axis=1).astype(jnp.bfloat16),
        "seq",
        split_axis=0,
        concat_axis=0,
        tiled=True,
    ).astype(jnp.float32)
    q_grad = from_heads(returned[:, :part_rows, :HD]).astype(jnp.bfloat16)
    out_tok = from_heads(returned[:, :part_rows, HD:]).astype(jnp.bfloat16)
    summed = jnp.sum(
        returned[:, part_rows:, :].reshape(heads_here, share_count, rows_here, 2 * HD), axis=1
    )
    summed = summed.transpose(1, 0, 2)
    k_grad = summed[:, :, :HD].reshape(rows_here, heads_here * HD).astype(jnp.bfloat16)
    v_grad = summed[:, :, HD:].reshape(rows_here, heads_here * HD).astype(jnp.bfloat16)
    column_cut = d_out
    d_weight = lax.psum_scatter(
        jnp.dot(column_cut.T, out_tok, preferred_element_type=jnp.float32).astype(jnp.bfloat16),
        "seq",
        scatter_dimension=0,
        tiled=True,
    ).astype(jnp.float32)
    return (q_grad, k_grad, v_grad, d_weight)


def call(kernel, outs, args, specs=None, scratch=(), scalars=0, out_specs=None, flops=0, moved=0, limit=LIMIT):
    vmem = pl.BlockSpec(memory_space=pltpu.VMEM)
    if specs is None:
        specs = [vmem] * (len(args) - scalars)
    if out_specs is None:
        out_specs = [vmem] * len(outs)
    return pl.pallas_call(
        kernel,
        out_shape=outs,
        grid_spec=pltpu.PrefetchScalarGridSpec(
            num_scalar_prefetch=scalars,
            grid=(1,),
            in_specs=specs,
            out_specs=out_specs,
            scratch_shapes=list(scratch),
        ),
        compiler_params=pltpu.CompilerParams(vmem_limit_bytes=limit),
        cost_estimate=pl.CostEstimate(flops=flops, bytes_accessed=moved, transcendentals=0),
    )(*args)


STEPS = (0, 2, 4, 6)


def head_columns(step, other_row):
    return pl.ds(pl.multiple_of(jnp.bitwise_xor(lax.axis_index("seq"), step + other_row) * HD, HD), HD)


def pack_kernel(me_ref, q_ref, k_ref, v_ref, kt_ref, vt_ref, tok_ref, text_ref):
    rows = q_ref.shape[0]
    for h in range(tok_ref.shape[0]):
        for i, ref in enumerate((q_ref, k_ref, v_ref)):
            tok_ref[h, i * rows : (i + 1) * rows, :] = ref[:, h * HD : (h + 1) * HD]
    text_ref[0] = kt_ref[...]
    text_ref[1] = vt_ref[...]


def query_order(n):
    y = lax.rem(lax.axis_index("seq"), 2)
    return [2 * z + y for z in range(n // 2)] + [2 * z + 1 - y for z in range(n // 2)]


def forward_kernel(tok_ref, text_ref, probs_ref, out_ref, queries_ref, keys_t_ref, vals_ref, keys, vals_t, *, chunk):
    n, three, _ = tok_ref.shape
    rows = three // 3
    image = n * rows
    text = text_ref.shape[1]
    for i, source in enumerate(query_order(n)):
        queries_ref[i * rows : (i + 1) * rows, :] = tok_ref[source, 0:rows, :]
    keys[0:image, :] = tok_ref[:, rows : 2 * rows, :].reshape(image, HD)
    keys[image : image + text, :] = text_ref[0]
    vals_ref[0:image, :] = tok_ref[:, 2 * rows : 3 * rows, :].reshape(image, HD)
    vals_ref[image : image + text, :] = text_ref[1]
    keys_t_ref[...] = keys[...].T
    vals_t[...] = vals_ref[...].T
    factor = HD ** (-0.5) * math.log2(math.e)
    for c in range(image // chunk):
        span = slice(c * chunk, (c + 1) * chunk)
        scores = lax.dot_general(keys[...], queries_ref[span, :], NT, preferred_element_type=F32)
        top = jnp.max(scores, axis=0, keepdims=True)
        weights = jnp.exp2((scores - top) * factor)
        total = jnp.sum(weights, axis=0, keepdims=True)
        low = (weights * (1.0 / total)).astype(BF16)
        probs_ref[:, span] = low
        out_ref[:, span] = jnp.dot(vals_t[...], low, preferred_element_type=F32).astype(BF16)


def place_rows(piece_ref, swapped_ref, cot, start):
    me = lax.axis_index("seq")
    core = lax.axis_index("fsdp")
    part = piece_ref.shape[0] // len(STEPS)
    for piece, shift in ((piece_ref, core), (swapped_ref, 1 - core)):
        for i, step in enumerate(STEPS):
            z = jnp.bitwise_xor(me, step) // 2
            at = pl.multiple_of(start + z * (2 * part) + shift * part, 16)
            cot[pl.ds(at, part), :] = piece[i * part : (i + 1) * part, :]


def partial_kernel(piece_ref, swapped_ref, own_ref, other_ref, mine_ref, near_ref, far_ref, send_ref, cot, weight):
    place_rows(piece_ref, swapped_ref, cot, 0)
    me = lax.axis_index("seq")
    depth = own_ref.shape[0]
    y = lax.rem(me, 2)
    weight[pl.ds(pl.multiple_of(y * depth, 16), depth), :] = own_ref[...]
    weight[pl.ds(pl.multiple_of((1 - y) * depth, 16), depth), :] = other_ref[...]
    for step, ref in zip(STEPS, (mine_ref, near_ref, far_ref, send_ref)):
        z = jnp.bitwise_xor(me, step) // 2
        cols = pl.ds(pl.multiple_of(z * 2 * HD, 2 * HD), 2 * HD)
        ref[...] = jnp.dot(cot[...], weight[:, cols], preferred_element_type=F32).astype(ref.dtype)


def add_kernel(kept_ref, received_ref, out_ref):
    out_ref[...] = (kept_ref[...] + received_ref[...].astype(F32)).astype(BF16)


def finish_kernel(mine_ref, near_ref, far_ref, kept_ref, give_ref):
    heads = mine_ref[...] + near_ref[...].astype(F32) + far_ref[...].astype(F32)
    first, second = heads[:, :HD].astype(BF16), heads[:, HD:].astype(BF16)
    first_row = lax.rem(lax.axis_index("seq"), 2) == 0
    kept_ref[...] = jnp.where(first_row, first, second)
    give_ref[...] = jnp.where(first_row, second, first)


def weight_grad_kernel(*refs):
    *pieces, out0, out1, own_ref, other_ref, cot, outs = refs
    tokens = cot.shape[0]
    place_rows(pieces[0], pieces[1], cot, 0)
    place_rows(pieces[2], pieces[3], cot, tokens // 2)
    outs[0:HD, :] = out0[...]
    outs[HD : 2 * HD, :] = out1[...]
    depth = own_ref.shape[1]
    y = lax.rem(lax.axis_index("seq"), 2)
    for ref, row in ((own_ref, y), (other_ref, 1 - y)):
        cols = pl.ds(pl.multiple_of(row * depth, HD), depth)
        ref[...] = jnp.dot(outs[...], cot[:, cols], preferred_element_type=F32).astype(BF16)


def backward_kernel(queries_ref, keys_t_ref, vals_ref, probs_ref, out_ref, *refs, chunk):
    *grad_refs, send_ref, dk, dv = refs
    n, three, _ = send_ref.shape
    rows = three // 3
    image = n * rows
    scale = HD ** (-0.5)
    per = chunk // rows
    order = query_order(n)
    half = image // chunk // 2
    for c in range(image // chunk):
        span = slice(c * chunk, (c + 1) * chunk)
        within = slice(c % half * chunk, (c % half + 1) * chunk)
        grads = grad_refs[c // half][within, :]
        row_dot = jnp.sum(
            grads.astype(F32).T * out_ref[:, span].astype(F32), axis=0, keepdims=True
        )
        prob_grad = lax.dot_general(vals_ref[...], grads, NT, preferred_element_type=F32)
        low = probs_ref[:, span]
        score_grad = (low.astype(F32) * (prob_grad - row_dot)).astype(BF16)
        dq = (jnp.dot(keys_t_ref[...], score_grad, preferred_element_type=F32) * scale).T.astype(BF16)
        for i in range(per):
            send_ref[order[c * per + i], 0:rows, :] = dq[i * rows : (i + 1) * rows, :]
        dk_part = jnp.dot(score_grad[0:image, :], queries_ref[span, :], preferred_element_type=F32)
        dv_part = jnp.dot(low[0:image, :], grads, preferred_element_type=F32)
        if c == 0:
            dk[...] = dk_part
            dv[...] = dv_part
        else:
            dk[...] += dk_part
            dv[...] += dv_part
    send_ref[:, rows : 2 * rows, :] = (dk[...] * scale).astype(BF16).reshape(n, rows, HD)
    send_ref[:, 2 * rows : 3 * rows, :] = dv[...].astype(BF16).reshape(n, rows, HD)


def unpack_kernel(tok_ref, q_ref, k_ref, v_ref):
    rows = q_ref.shape[0]
    for h in range(tok_ref.shape[0]):
        for i, ref in enumerate((q_ref, k_ref, v_ref)):
            ref[:, h * HD : (h + 1) * HD] = tok_ref[h, i * rows : (i + 1) * rows, :]


def unpack_weight_kernel(own0_ref, other0_ref, own1_ref, other1_ref, w_ref):
    for i, step in enumerate(STEPS):
        rows = slice(i % 2 * HD, (i % 2 + 1) * HD)
        for other_row, ref in enumerate((own0_ref, other0_ref) if i < 2 else (own1_ref, other1_ref)):
            w_ref[:, head_columns(step, other_row)] = ref[rows, :].astype(F32).T


def exchange(array, distance=0, cores=False):
    if not distance and not cores:
        return array
    size = 2 * lax.axis_size("seq")
    pairs = [(i, i ^ (2 * distance + int(cores))) for i in range(size)]
    return lax.ppermute(array, ("seq", "fsdp"), pairs)


def send_cotangents(d_out):
    rows, width = d_out.shape
    part, columns = rows // 2, width // len(STEPS)
    z = lax.axis_index("seq") // 2
    first = lax.axis_index("fsdp") * part
    return [
        exchange(lax.dynamic_slice(d_out, (first, (z ^ (step // 2)) * columns), (part, columns)), step)
        for step in STEPS
    ]


def local(q_img, k_img, v_img, k_txt, v_txt, out_weight, d_out):
    n = lax.axis_size("seq")
    rows, width = q_img.shape
    args = (q_img, k_img, v_img, k_txt, v_txt, out_weight, d_out)
    if n != 2 * len(STEPS) or width // HD != n or lax.axis_size("fsdp") != 2 or rows % 32:
        return local_general(*args)
    depth = out_weight.shape[0]
    image = n * rows
    text = k_txt.shape[0]
    total = image + text
    chunk = 2 * rows
    shape = jax.ShapeDtypeStruct
    vmem = pl.BlockSpec(memory_space=pltpu.VMEM)

    head = pl.BlockSpec((text, HD), lambda i, me_ref: (0, me_ref[0]))
    given = exchange(out_weight, 1)
    along = send_cotangents(d_out)
    tok_out, text_head = call(
        pack_kernel,
        [shape((n, 3 * rows, HD), BF16), shape((2, text, HD), BF16)],
        [lax.axis_index("seq").astype(jnp.int32)[None], q_img, k_img, v_img, k_txt, v_txt],
        specs=[vmem] * 3 + [head] * 2,
        scalars=1,
        moved=4 * 3 * rows * width,
        limit=60 * 1024 * 1024,
    )
    tok_out, along = lax.optimization_barrier((tok_out, along))
    along, given = lax.optimization_barrier((along, given))
    row = jnp.concatenate(along, axis=0)
    row_swapped = exchange(row, cores=True)
    tok_in = lax.all_to_all(tok_out, "seq", split_axis=0, concat_axis=0, tiled=True)

    probs, out_t, queries, keys_t, vals = call(
        functools.partial(forward_kernel, chunk=chunk),
        [shape(dims, BF16) for dims in ((total, image), (HD, image), (image, HD), (HD, total), (total, HD))],
        [tok_in, text_head],
        scratch=[pltpu.VMEM((total, HD), BF16), pltpu.VMEM((HD, total), BF16)],
        flops=4 * total * image * HD,
        moved=4 * total * image,
    )
    columns = row.shape[1]
    mine, near, far, send = call(
        partial_kernel,
        [shape((image // 2, 2 * HD), kind) for kind in (F32, BF16, F32, BF16)],
        [row, row_swapped, out_weight, given],
        scratch=[pltpu.VMEM((image // 2, columns), BF16), pltpu.VMEM((columns, width), BF16)],
        flops=8 * image * columns * HD,
        moved=2 * image * columns,
    )
    send, near = lax.optimization_barrier((exchange(send, 2), near))
    (far,) = call(add_kernel, [shape(far.shape, BF16)], [far, send])
    far, near = exchange(far, 4), exchange(near, 2)
    out_late, far, near = lax.optimization_barrier((out_t, far, near))
    kept, give = call(finish_kernel, [shape((image // 2, HD), BF16)] * 2, [mine, near, far])
    got = exchange(give, 1)
    out_near, out_far = exchange(out_late, 2), exchange(out_late, 4)
    row, _ = lax.optimization_barrier((row, out_t))
    other_row = exchange(row, 1)
    other_swapped = exchange(other_row, cores=True)
    (grad_out,) = call(
        functools.partial(backward_kernel, chunk=chunk),
        [shape((n, 3 * rows, HD), BF16)],
        [queries, keys_t, vals, probs, out_t, kept, got],
        scratch=[pltpu.VMEM((image, HD), F32), pltpu.VMEM((image, HD), F32)],
        flops=8 * total * image * HD,
        moved=4 * total * image,
    )
    grad_in = lax.all_to_all(grad_out, "seq", split_axis=0, concat_axis=0, tiled=True)

    def weight_grad(flops, *outs):
        return call(
            weight_grad_kernel,
            [shape((2 * HD, depth), BF16)] * 2,
            [row, row_swapped, other_row, other_swapped, *outs],
            scratch=[pltpu.VMEM((image, columns), BF16), pltpu.VMEM((2 * HD, image), BF16)],
            flops=flops,
            moved=image * columns,
        )

    own0, other0 = weight_grad(0, out_t, out_near)
    out_far, other0, _ = lax.optimization_barrier((out_far, other0, grad_out))
    other0 = exchange(other0, 1)
    last = exchange(out_far, 2)
    last, other0 = lax.optimization_barrier((last, other0))
    own1, other1 = weight_grad(96 * image * columns * HD, out_far, last)
    grads = call(
        unpack_kernel,
        [shape((rows, width), BF16)] * 3,
        [grad_in],
        moved=4 * 3 * rows * width,
    )
    (d_weight,) = call(
        unpack_weight_kernel,
        [shape((depth, width), F32)],
        [own0, other0, own1, exchange(other1, 1)],
        moved=6 * depth * width,
    )
    return (*grads, d_weight)


def solution(mesh):
    in_specs = (
        P(("group", "seq"), "fsdp"),
        P(("group", "seq"), "fsdp"),
        P(("group", "seq"), "fsdp"),
        P("group", "fsdp"),
        P("group", "fsdp"),
        P("seq", "fsdp"),
        P(("group", "seq"), None),
    )
    out_specs = (
        P(("group", "seq"), "fsdp"),
        P(("group", "seq"), "fsdp"),
        P(("group", "seq"), "fsdp"),
        P(("group", "seq"), "fsdp"),
    )
    return jax.shard_map(local, mesh=mesh, in_specs=in_specs, out_specs=out_specs, check_vma=False)
```

```python
import functools
import math

import jax
import jax.numpy as jnp
from jax import lax
from jax.experimental import pallas as pl
from jax.experimental.pallas import tpu as pltpu
from jax.sharding import PartitionSpec as P

HD = 128
F32 = jnp.float32
BF16 = jnp.bfloat16
LIMIT = 16 * 1024 * 1024
NT = (((1,), (1,)), ((), ()))


def attend(queries, cotangents, key_rows, value_rows, block_rows):
    score_scale = HD ** (-0.5)
    query_count = queries.shape[0]
    block_count = query_count // block_rows
    query_blocks = queries.reshape(block_count, block_rows, HD)
    grad_blocks = cotangents.reshape(block_count, block_rows, HD)

    def one_block(accumulated, pair_item):
        query_block, grad_block = pair_item
        scores = jnp.dot(query_block, key_rows.T, preferred_element_type=jnp.float32) * score_scale
        row_max = jnp.max(scores, axis=1, keepdims=True)
        probs = jnp.exp(scores - row_max)
        probs = probs / jnp.sum(probs, axis=1, keepdims=True)
        probs_low = probs.astype(jnp.bfloat16)
        out_rows = jnp.dot(probs_low, value_rows, preferred_element_type=jnp.float32).astype(
            jnp.bfloat16
        )
        prob_grad = jnp.dot(grad_block, value_rows.T, preferred_element_type=jnp.float32)
        row_dot = jnp.sum(
            grad_block.astype(jnp.float32) * out_rows.astype(jnp.float32), axis=1, keepdims=True
        )
        score_grad = (probs * (prob_grad - row_dot)).astype(jnp.bfloat16)
        query_grad = (
            jnp.dot(score_grad, key_rows, preferred_element_type=jnp.float32) * score_scale
        ).astype(jnp.bfloat16)
        key_grad = (
            accumulated[0]
            + jnp.dot(score_grad.T, query_block, preferred_element_type=jnp.float32) * score_scale
        )
        value_grad = accumulated[1] + jnp.dot(
            probs_low.T, grad_block, preferred_element_type=jnp.float32
        )
        return ((key_grad, value_grad), (query_grad, out_rows))

    empty = jnp.zeros((key_rows.shape[0], HD), jnp.float32)
    (key_grad, value_grad), (query_grad, out_rows) = lax.scan(
        one_block, (empty, empty), (query_blocks, grad_blocks)
    )
    return (
        query_grad.reshape(query_count, HD),
        out_rows.reshape(query_count, HD),
        key_grad,
        value_grad,
    )


def local_general(q_img, k_img, v_img, k_txt, v_txt, out_weight, d_out):
    rows_here = q_img.shape[0]
    heads_here = q_img.shape[1] // HD
    seq_count = lax.axis_size("seq")
    share_count = seq_count // heads_here
    part_rows = rows_here // share_count
    seq_index = lax.axis_index("seq")
    head_index = seq_index // share_count
    column_cut = d_out
    attn_grad = jnp.dot(
        column_cut,
        lax.all_gather(out_weight, "seq", axis=0, tiled=True),
        preferred_element_type=jnp.float32,
    ).astype(jnp.bfloat16)

    def to_heads(array_in):
        shaped = array_in.reshape(share_count, part_rows, heads_here, HD).transpose(2, 0, 1, 3)
        return shaped.reshape(seq_count, part_rows, HD)

    def whole_heads(array_in):
        shaped = array_in.reshape(rows_here, heads_here, HD).transpose(1, 0, 2)
        shaped = jnp.broadcast_to(shaped[:, None], (heads_here, share_count, rows_here, HD))
        return shaped.reshape(seq_count, rows_here, HD)

    def from_heads(array_in):
        shaped = array_in.reshape(heads_here, share_count, part_rows, HD).transpose(1, 2, 0, 3)
        return shaped.reshape(rows_here, heads_here * HD)

    text_keys = lax.dynamic_slice_in_dim(k_txt, head_index * HD, HD, 1)
    text_values = lax.dynamic_slice_in_dim(v_txt, head_index * HD, HD, 1)
    query_side = jnp.concatenate([to_heads(q_img), to_heads(attn_grad)], axis=2)
    key_side = jnp.concatenate([whole_heads(k_img), whole_heads(v_img)], axis=2)
    packed = jnp.concatenate([query_side, key_side], axis=1)
    received = lax.all_to_all(packed, "seq", split_axis=0, concat_axis=0, tiled=True)
    queries = received[:, :part_rows, :HD].reshape(seq_count * part_rows, HD)
    cotangents = received[:, :part_rows, HD:].reshape(seq_count * part_rows, HD)
    image_keys = received[:, part_rows:, :HD].reshape(seq_count * rows_here, HD)
    image_values = received[:, part_rows:, HD:].reshape(seq_count * rows_here, HD)
    key_rows = jnp.concatenate([image_keys, text_keys], axis=0)
    value_rows = jnp.concatenate([image_values, text_values], axis=0)
    query_grad, out_rows, key_grad, value_grad = attend(
        queries, cotangents, key_rows, value_rows, min(512, queries.shape[0])
    )
    image_count = image_keys.shape[0]
    query_part = (
        jnp.concatenate([query_grad, out_rows], axis=1)
        .astype(jnp.float32)
        .reshape(seq_count, part_rows, 2 * HD)
    )
    key_part = jnp.concatenate([key_grad[:image_count], value_grad[:image_count]], axis=1).reshape(
        seq_count, rows_here, 2 * HD
    )
    returned = lax.all_to_all(
        jnp.concatenate([query_part, key_part], axis=1).astype(jnp.bfloat16),
        "seq",
        split_axis=0,
        concat_axis=0,
        tiled=True,
    ).astype(jnp.float32)
    q_grad = from_heads(returned[:, :part_rows, :HD]).astype(jnp.bfloat16)
    out_tok = from_heads(returned[:, :part_rows, HD:]).astype(jnp.bfloat16)
    summed = jnp.sum(
        returned[:, part_rows:, :].reshape(heads_here, share_count, rows_here, 2 * HD), axis=1
    )
    summed = summed.transpose(1, 0, 2)
    k_grad = summed[:, :, :HD].reshape(rows_here, heads_here * HD).astype(jnp.bfloat16)
    v_grad = summed[:, :, HD:].reshape(rows_here, heads_here * HD).astype(jnp.bfloat16)
    column_cut = d_out
    d_weight = lax.psum_scatter(
        jnp.dot(column_cut.T, out_tok, preferred_element_type=jnp.float32).astype(jnp.bfloat16),
        "seq",
        scatter_dimension=0,
        tiled=True,
    ).astype(jnp.float32)
    return (q_grad, k_grad, v_grad, d_weight)


def call(kernel, outs, args, specs=None, scratch=(), scalars=0, out_specs=None, flops=0, moved=0, limit=LIMIT):
    vmem = pl.BlockSpec(memory_space=pltpu.VMEM)
    if specs is None:
        specs = [vmem] * (len(args) - scalars)
    if out_specs is None:
        out_specs = [vmem] * len(outs)
    return pl.pallas_call(
        kernel,
        out_shape=outs,
        grid_spec=pltpu.PrefetchScalarGridSpec(
            num_scalar_prefetch=scalars,
            grid=(1,),
            in_specs=specs,
            out_specs=out_specs,
            scratch_shapes=list(scratch),
        ),
        compiler_params=pltpu.CompilerParams(vmem_limit_bytes=limit),
        cost_estimate=pl.CostEstimate(flops=flops, bytes_accessed=moved, transcendentals=0),
    )(*args)


STEPS = (0, 2, 4, 6)


def head_columns(step, other_row):
    return pl.ds(pl.multiple_of(jnp.bitwise_xor(lax.axis_index("seq"), step + other_row) * HD, HD), HD)


def pack_kernel(me_ref, q_ref, k_ref, v_ref, kt_ref, vt_ref, tok_ref, text_ref):
    rows = q_ref.shape[0]
    for h in range(tok_ref.shape[0]):
        for i, ref in enumerate((q_ref, k_ref, v_ref)):
            tok_ref[h, i * rows : (i + 1) * rows, :] = ref[:, h * HD : (h + 1) * HD]
    text_ref[0] = kt_ref[...]
    text_ref[1] = vt_ref[...]


def query_order(n):
    y = lax.rem(lax.axis_index("seq"), 2)
    return [2 * z + y for z in range(n // 2)] + [2 * z + 1 - y for z in range(n // 2)]


def forward_kernel(tok_ref, text_ref, probs_ref, out_ref, queries_ref, keys_t_ref, vals_ref, keys, vals_t, *, chunk):
    n, three, _ = tok_ref.shape
    rows = three // 3
    image = n * rows
    text = text_ref.shape[1]
    for i, source in enumerate(query_order(n)):
        queries_ref[i * rows : (i + 1) * rows, :] = tok_ref[source, 0:rows, :]
    keys[0:image, :] = tok_ref[:, rows : 2 * rows, :].reshape(image, HD)
    keys[image : image + text, :] = text_ref[0]
    vals_ref[0:image, :] = tok_ref[:, 2 * rows : 3 * rows, :].reshape(image, HD)
    vals_ref[image : image + text, :] = text_ref[1]
    keys_t_ref[...] = keys[...].T
    vals_t[...] = vals_ref[...].T
    factor = HD ** (-0.5) * math.log2(math.e)
    for c in range(image // chunk):
        span = slice(c * chunk, (c + 1) * chunk)
        scores = lax.dot_general(keys[...], queries_ref[span, :], NT, preferred_element_type=F32)
        top = jnp.max(scores, axis=0, keepdims=True)
        weights = jnp.exp2((scores - top) * factor)
        total = jnp.sum(weights, axis=0, keepdims=True)
        low = (weights * (1.0 / total)).astype(BF16)
        probs_ref[:, span] = low
        out_ref[:, span] = jnp.dot(vals_t[...], low, preferred_element_type=F32).astype(BF16)


def place_rows(piece_ref, swapped_ref, cot, start):
    me = lax.axis_index("seq")
    core = lax.axis_index("fsdp")
    part = piece_ref.shape[0] // len(STEPS)
    for piece, shift in ((piece_ref, core), (swapped_ref, 1 - core)):
        for i, step in enumerate(STEPS):
            z = jnp.bitwise_xor(me, step) // 2
            at = pl.multiple_of(start + z * (2 * part) + shift * part, 16)
            cot[pl.ds(at, part), :] = piece[i * part : (i + 1) * part, :]


def partial_kernel(piece_ref, swapped_ref, own_ref, other_ref, mine_ref, near_ref, far_ref, send_ref, cot, weight):
    place_rows(piece_ref, swapped_ref, cot, 0)
    me = lax.axis_index("seq")
    depth = own_ref.shape[0]
    y = lax.rem(me, 2)
    weight[pl.ds(pl.multiple_of(y * depth, 16), depth), :] = own_ref[...]
    weight[pl.ds(pl.multiple_of((1 - y) * depth, 16), depth), :] = other_ref[...]
    for step, ref in zip(STEPS, (mine_ref, near_ref, far_ref, send_ref)):
        z = jnp.bitwise_xor(me, step) // 2
        cols = pl.ds(pl.multiple_of(z * 2 * HD, 2 * HD), 2 * HD)
        ref[...] = jnp.dot(cot[...], weight[:, cols], preferred_element_type=F32).astype(ref.dtype)


def add_kernel(kept_ref, received_ref, out_ref):
    out_ref[...] = (kept_ref[...] + received_ref[...].astype(F32)).astype(BF16)


def finish_kernel(mine_ref, near_ref, far_ref, kept_ref, give_ref):
    heads = mine_ref[...] + near_ref[...].astype(F32) + far_ref[...].astype(F32)
    first, second = heads[:, :HD].astype(BF16), heads[:, HD:].astype(BF16)
    first_row = lax.rem(lax.axis_index("seq"), 2) == 0
    kept_ref[...] = jnp.where(first_row, first, second)
    give_ref[...] = jnp.where(first_row, second, first)


def weight_grad_kernel(*refs):
    *pieces, out0, out1, out2, out3, own_ref, other_ref, cot, outs = refs
    tokens = cot.shape[0]
    place_rows(pieces[0], pieces[1], cot, 0)
    place_rows(pieces[2], pieces[3], cot, tokens // 2)
    for i, ref in enumerate((out0, out1, out2, out3)):
        outs[i * HD : (i + 1) * HD, :] = ref[...]
    depth = own_ref.shape[1]
    y = lax.rem(lax.axis_index("seq"), 2)
    for ref, row in ((own_ref, y), (other_ref, 1 - y)):
        cols = pl.ds(pl.multiple_of(row * depth, HD), depth)
        ref[...] = jnp.dot(outs[...], cot[:, cols], preferred_element_type=F32).astype(BF16)


def backward_kernel(queries_ref, keys_t_ref, vals_ref, probs_ref, out_ref, *refs, chunk):
    *grad_refs, send_ref, dk, dv = refs
    n, three, _ = send_ref.shape
    rows = three // 3
    image = n * rows
    scale = HD ** (-0.5)
    per = chunk // rows
    order = query_order(n)
    half = image // chunk // 2
    for c in range(image // chunk):
        span = slice(c * chunk, (c + 1) * chunk)
        within = slice(c % half * chunk, (c % half + 1) * chunk)
        grads = grad_refs[c // half][within, :]
        row_dot = jnp.sum(
            grads.astype(F32).T * out_ref[:, span].astype(F32), axis=0, keepdims=True
        )
        prob_grad = lax.dot_general(vals_ref[...], grads, NT, preferred_element_type=F32)
        low = probs_ref[:, span]
        score_grad = (low.astype(F32) * (prob_grad - row_dot)).astype(BF16)
        dq = (jnp.dot(keys_t_ref[...], score_grad, preferred_element_type=F32) * scale).T.astype(BF16)
        for i in range(per):
            send_ref[order[c * per + i], 0:rows, :] = dq[i * rows : (i + 1) * rows, :]
        dk_part = jnp.dot(score_grad[0:image, :], queries_ref[span, :], preferred_element_type=F32)
        dv_part = jnp.dot(low[0:image, :], grads, preferred_element_type=F32)
        if c == 0:
            dk[...] = dk_part
            dv[...] = dv_part
        else:
            dk[...] += dk_part
            dv[...] += dv_part
    send_ref[:, rows : 2 * rows, :] = (dk[...] * scale).astype(BF16).reshape(n, rows, HD)
    send_ref[:, 2 * rows : 3 * rows, :] = dv[...].astype(BF16).reshape(n, rows, HD)


def unpack_kernel(tok_ref, q_ref, k_ref, v_ref):
    rows = q_ref.shape[0]
    for h in range(tok_ref.shape[0]):
        for i, ref in enumerate((q_ref, k_ref, v_ref)):
            ref[:, h * HD : (h + 1) * HD] = tok_ref[h, i * rows : (i + 1) * rows, :]


def unpack_weight_kernel(own_ref, other_ref, w_ref):
    for other_row, ref in enumerate((own_ref, other_ref)):
        for i, step in enumerate(STEPS):
            w_ref[:, head_columns(step, other_row)] = ref[i * HD : (i + 1) * HD, :].astype(F32).T


def exchange(array, distance=0, cores=False):
    if not distance and not cores:
        return array
    size = 2 * lax.axis_size("seq")
    pairs = [(i, i ^ (2 * distance + int(cores))) for i in range(size)]
    return lax.ppermute(array, ("seq", "fsdp"), pairs)


def send_cotangents(d_out):
    rows, width = d_out.shape
    part, columns = rows // 2, width // len(STEPS)
    z = lax.axis_index("seq") // 2
    first = lax.axis_index("fsdp") * part
    return [
        exchange(lax.dynamic_slice(d_out, (first, (z ^ (step // 2)) * columns), (part, columns)), step)
        for step in STEPS
    ]


def local(q_img, k_img, v_img, k_txt, v_txt, out_weight, d_out):
    n = lax.axis_size("seq")
    rows, width = q_img.shape
    args = (q_img, k_img, v_img, k_txt, v_txt, out_weight, d_out)
    if n != 2 * len(STEPS) or width // HD != n or lax.axis_size("fsdp") != 2 or rows % 32:
        return local_general(*args)
    depth = out_weight.shape[0]
    image = n * rows
    text = k_txt.shape[0]
    total = image + text
    chunk = 2 * rows
    shape = jax.ShapeDtypeStruct
    vmem = pl.BlockSpec(memory_space=pltpu.VMEM)

    head = pl.BlockSpec((text, HD), lambda i, me_ref: (0, me_ref[0]))
    given = exchange(out_weight, 1)
    along = send_cotangents(d_out)
    tok_out, text_head = call(
        pack_kernel,
        [shape((n, 3 * rows, HD), BF16), shape((2, text, HD), BF16)],
        [lax.axis_index("seq").astype(jnp.int32)[None], q_img, k_img, v_img, k_txt, v_txt],
        specs=[vmem] * 3 + [head] * 2,
        scalars=1,
        moved=4 * 3 * rows * width,
        limit=60 * 1024 * 1024,
    )
    tok_out, along = lax.optimization_barrier((tok_out, along))
    along, given = lax.optimization_barrier((along, given))
    row = jnp.concatenate(along, axis=0)
    row_swapped = exchange(row, cores=True)
    tok_in = lax.all_to_all(tok_out, "seq", split_axis=0, concat_axis=0, tiled=True)

    columns = row.shape[1]
    mine, near, far, send = call(
        partial_kernel,
        [shape((image // 2, 2 * HD), kind) for kind in (F32, BF16, F32, BF16)],
        [row, row_swapped, out_weight, given],
        scratch=[pltpu.VMEM((image // 2, columns), BF16), pltpu.VMEM((columns, width), BF16)],
        flops=8 * image * columns * HD,
        moved=2 * image * columns,
    )
    send, near, tok_in = lax.optimization_barrier((exchange(send, 2), near, tok_in))
    probs, out_t, queries, keys_t, vals = call(
        functools.partial(forward_kernel, chunk=chunk),
        [shape(dims, BF16) for dims in ((total, image), (HD, image), (image, HD), (HD, total), (total, HD))],
        [tok_in, text_head],
        scratch=[pltpu.VMEM((total, HD), BF16), pltpu.VMEM((HD, total), BF16)],
        flops=4 * total * image * HD,
        moved=4 * total * image,
    )
    (far,) = call(add_kernel, [shape(far.shape, BF16)], [far, send])
    far, near = exchange(far, 4), exchange(near, 2)
    out_near, out_far = exchange(out_t, 2), exchange(out_t, 4)
    kept, give = call(finish_kernel, [shape((image // 2, HD), BF16)] * 2, [mine, near, far])
    got = exchange(give, 1)
    row, _ = lax.optimization_barrier((row, out_t))
    other_row = exchange(row, 1)
    other_swapped = exchange(other_row, cores=True)
    (grad_out,) = call(
        functools.partial(backward_kernel, chunk=chunk),
        [shape((n, 3 * rows, HD), BF16)],
        [queries, keys_t, vals, probs, out_t, kept, got],
        scratch=[pltpu.VMEM((image, HD), F32), pltpu.VMEM((image, HD), F32)],
    )
    grad_in = lax.all_to_all(grad_out, "seq", split_axis=0, concat_axis=0, tiled=True)
    out_far, out_near, _ = lax.optimization_barrier((out_far, out_near, grad_out))
    outs = [out_t, out_near, out_far, exchange(out_far, 2)]
    dw_own, dw_other = call(
        weight_grad_kernel,
        [shape((4 * HD, depth), BF16)] * 2,
        [row, row_swapped, other_row, other_swapped, *outs],
        scratch=[pltpu.VMEM((image, columns), BF16), pltpu.VMEM((4 * HD, image), BF16)],
        flops=96 * image * columns * HD,
        moved=2 * image * columns,
    )
    grads = call(
        unpack_kernel,
        [shape((rows, width), BF16)] * 3,
        [grad_in],
        moved=4 * 3 * rows * width,
    )
    (d_weight,) = call(
        unpack_weight_kernel,
        [shape((depth, width), F32)],
        [dw_own, exchange(dw_other, 1)],
        moved=6 * depth * width,
    )
    return (*grads, d_weight)


def solution(mesh):
    in_specs = (
        P(("group", "seq"), "fsdp"),
        P(("group", "seq"), "fsdp"),
        P(("group", "seq"), "fsdp"),
        P("group", "fsdp"),
        P("group", "fsdp"),
        P("seq", "fsdp"),
        P(("group", "seq"), None),
    )
    out_specs = (
        P(("group", "seq"), "fsdp"),
        P(("group", "seq"), "fsdp"),
        P(("group", "seq"), "fsdp"),
        P(("group", "seq"), "fsdp"),
    )
    return jax.shard_map(local, mesh=mesh, in_specs=in_specs, out_specs=out_specs, check_vma=False)
```

```python
import functools
import math

import jax
import jax.numpy as jnp
from jax import lax
from jax.experimental import pallas as pl
from jax.experimental.pallas import tpu as pltpu
from jax.sharding import PartitionSpec as P

HD = 128
F32 = jnp.float32
BF16 = jnp.bfloat16
LIMIT = 16 * 1024 * 1024
NT = (((1,), (1,)), ((), ()))


def attend(queries, cotangents, key_rows, value_rows, block_rows):
    score_scale = HD ** (-0.5)
    query_count = queries.shape[0]
    block_count = query_count // block_rows
    query_blocks = queries.reshape(block_count, block_rows, HD)
    grad_blocks = cotangents.reshape(block_count, block_rows, HD)

    def one_block(accumulated, pair_item):
        query_block, grad_block = pair_item
        scores = jnp.dot(query_block, key_rows.T, preferred_element_type=jnp.float32) * score_scale
        row_max = jnp.max(scores, axis=1, keepdims=True)
        probs = jnp.exp(scores - row_max)
        probs = probs / jnp.sum(probs, axis=1, keepdims=True)
        probs_low = probs.astype(jnp.bfloat16)
        out_rows = jnp.dot(probs_low, value_rows, preferred_element_type=jnp.float32).astype(
            jnp.bfloat16
        )
        prob_grad = jnp.dot(grad_block, value_rows.T, preferred_element_type=jnp.float32)
        row_dot = jnp.sum(
            grad_block.astype(jnp.float32) * out_rows.astype(jnp.float32), axis=1, keepdims=True
        )
        score_grad = (probs * (prob_grad - row_dot)).astype(jnp.bfloat16)
        query_grad = (
            jnp.dot(score_grad, key_rows, preferred_element_type=jnp.float32) * score_scale
        ).astype(jnp.bfloat16)
        key_grad = (
            accumulated[0]
            + jnp.dot(score_grad.T, query_block, preferred_element_type=jnp.float32) * score_scale
        )
        value_grad = accumulated[1] + jnp.dot(
            probs_low.T, grad_block, preferred_element_type=jnp.float32
        )
        return ((key_grad, value_grad), (query_grad, out_rows))

    empty = jnp.zeros((key_rows.shape[0], HD), jnp.float32)
    (key_grad, value_grad), (query_grad, out_rows) = lax.scan(
        one_block, (empty, empty), (query_blocks, grad_blocks)
    )
    return (
        query_grad.reshape(query_count, HD),
        out_rows.reshape(query_count, HD),
        key_grad,
        value_grad,
    )


def local_general(q_img, k_img, v_img, k_txt, v_txt, out_weight, d_out):
    rows_here = q_img.shape[0]
    heads_here = q_img.shape[1] // HD
    seq_count = lax.axis_size("seq")
    share_count = seq_count // heads_here
    part_rows = rows_here // share_count
    seq_index = lax.axis_index("seq")
    head_index = seq_index // share_count
    column_cut = d_out
    attn_grad = jnp.dot(
        column_cut,
        lax.all_gather(out_weight, "seq", axis=0, tiled=True),
        preferred_element_type=jnp.float32,
    ).astype(jnp.bfloat16)

    def to_heads(array_in):
        shaped = array_in.reshape(share_count, part_rows, heads_here, HD).transpose(2, 0, 1, 3)
        return shaped.reshape(seq_count, part_rows, HD)

    def whole_heads(array_in):
        shaped = array_in.reshape(rows_here, heads_here, HD).transpose(1, 0, 2)
        shaped = jnp.broadcast_to(shaped[:, None], (heads_here, share_count, rows_here, HD))
        return shaped.reshape(seq_count, rows_here, HD)

    def from_heads(array_in):
        shaped = array_in.reshape(heads_here, share_count, part_rows, HD).transpose(1, 2, 0, 3)
        return shaped.reshape(rows_here, heads_here * HD)

    text_keys = lax.dynamic_slice_in_dim(k_txt, head_index * HD, HD, 1)
    text_values = lax.dynamic_slice_in_dim(v_txt, head_index * HD, HD, 1)
    query_side = jnp.concatenate([to_heads(q_img), to_heads(attn_grad)], axis=2)
    key_side = jnp.concatenate([whole_heads(k_img), whole_heads(v_img)], axis=2)
    packed = jnp.concatenate([query_side, key_side], axis=1)
    received = lax.all_to_all(packed, "seq", split_axis=0, concat_axis=0, tiled=True)
    queries = received[:, :part_rows, :HD].reshape(seq_count * part_rows, HD)
    cotangents = received[:, :part_rows, HD:].reshape(seq_count * part_rows, HD)
    image_keys = received[:, part_rows:, :HD].reshape(seq_count * rows_here, HD)
    image_values = received[:, part_rows:, HD:].reshape(seq_count * rows_here, HD)
    key_rows = jnp.concatenate([image_keys, text_keys], axis=0)
    value_rows = jnp.concatenate([image_values, text_values], axis=0)
    query_grad, out_rows, key_grad, value_grad = attend(
        queries, cotangents, key_rows, value_rows, min(512, queries.shape[0])
    )
    image_count = image_keys.shape[0]
    query_part = (
        jnp.concatenate([query_grad, out_rows], axis=1)
        .astype(jnp.float32)
        .reshape(seq_count, part_rows, 2 * HD)
    )
    key_part = jnp.concatenate([key_grad[:image_count], value_grad[:image_count]], axis=1).reshape(
        seq_count, rows_here, 2 * HD
    )
    returned = lax.all_to_all(
        jnp.concatenate([query_part, key_part], axis=1).astype(jnp.bfloat16),
        "seq",
        split_axis=0,
        concat_axis=0,
        tiled=True,
    ).astype(jnp.float32)
    q_grad = from_heads(returned[:, :part_rows, :HD]).astype(jnp.bfloat16)
    out_tok = from_heads(returned[:, :part_rows, HD:]).astype(jnp.bfloat16)
    summed = jnp.sum(
        returned[:, part_rows:, :].reshape(heads_here, share_count, rows_here, 2 * HD), axis=1
    )
    summed = summed.transpose(1, 0, 2)
    k_grad = summed[:, :, :HD].reshape(rows_here, heads_here * HD).astype(jnp.bfloat16)
    v_grad = summed[:, :, HD:].reshape(rows_here, heads_here * HD).astype(jnp.bfloat16)
    column_cut = d_out
    d_weight = lax.psum_scatter(
        jnp.dot(column_cut.T, out_tok, preferred_element_type=jnp.float32).astype(jnp.bfloat16),
        "seq",
        scatter_dimension=0,
        tiled=True,
    ).astype(jnp.float32)
    return (q_grad, k_grad, v_grad, d_weight)


def call(kernel, outs, args, specs=None, scratch=(), scalars=0, out_specs=None, flops=0, moved=0, limit=LIMIT):
    vmem = pl.BlockSpec(memory_space=pltpu.VMEM)
    if specs is None:
        specs = [vmem] * (len(args) - scalars)
    if out_specs is None:
        out_specs = [vmem] * len(outs)
    return pl.pallas_call(
        kernel,
        out_shape=outs,
        grid_spec=pltpu.PrefetchScalarGridSpec(
            num_scalar_prefetch=scalars,
            grid=(1,),
            in_specs=specs,
            out_specs=out_specs,
            scratch_shapes=list(scratch),
        ),
        compiler_params=pltpu.CompilerParams(vmem_limit_bytes=limit),
        cost_estimate=pl.CostEstimate(flops=flops, bytes_accessed=moved, transcendentals=0),
    )(*args)


STEPS = (0, 2, 4, 6)


def head_columns(step, other_row):
    return pl.ds(pl.multiple_of(jnp.bitwise_xor(lax.axis_index("seq"), step + other_row) * HD, HD), HD)


def pack_kernel(me_ref, q_ref, k_ref, v_ref, kt_ref, vt_ref, tok_ref, text_ref):
    rows = q_ref.shape[0]
    for h in range(tok_ref.shape[0]):
        for i, ref in enumerate((q_ref, k_ref, v_ref)):
            tok_ref[h, i * rows : (i + 1) * rows, :] = ref[:, h * HD : (h + 1) * HD]
    text_ref[0] = kt_ref[...]
    text_ref[1] = vt_ref[...]


def query_order(n):
    y = lax.rem(lax.axis_index("seq"), 2)
    return [2 * z + y for z in range(n // 2)] + [2 * z + 1 - y for z in range(n // 2)]


def forward_kernel(tok_ref, text_ref, probs_ref, out_ref, queries_ref, keys_t_ref, vals_ref, keys, vals_t, *, chunk):
    n, three, _ = tok_ref.shape
    rows = three // 3
    image = n * rows
    text = text_ref.shape[1]
    for i, source in enumerate(query_order(n)):
        queries_ref[i * rows : (i + 1) * rows, :] = tok_ref[source, 0:rows, :]
    keys[0:image, :] = tok_ref[:, rows : 2 * rows, :].reshape(image, HD)
    keys[image : image + text, :] = text_ref[0]
    vals_ref[0:image, :] = tok_ref[:, 2 * rows : 3 * rows, :].reshape(image, HD)
    vals_ref[image : image + text, :] = text_ref[1]
    keys_t_ref[...] = keys[...].T
    vals_t[...] = vals_ref[...].T
    factor = HD ** (-0.5) * math.log2(math.e)
    for c in range(image // chunk):
        span = slice(c * chunk, (c + 1) * chunk)
        scores = lax.dot_general(keys[...], queries_ref[span, :], NT, preferred_element_type=F32)
        top = jnp.max(scores, axis=0, keepdims=True)
        weights = jnp.exp2((scores - top) * factor)
        total = jnp.sum(weights, axis=0, keepdims=True)
        low = (weights * (1.0 / total)).astype(BF16)
        probs_ref[:, span] = low
        out_ref[:, span] = jnp.dot(vals_t[...], low, preferred_element_type=F32).astype(BF16)


def place_rows(piece_ref, swapped_ref, cot, start):
    me = lax.axis_index("seq")
    core = lax.axis_index("fsdp")
    part = piece_ref.shape[0] // len(STEPS)
    for piece, shift in ((piece_ref, core), (swapped_ref, 1 - core)):
        for i, step in enumerate(STEPS):
            z = jnp.bitwise_xor(me, step) // 2
            at = pl.multiple_of(start + z * (2 * part) + shift * part, 16)
            cot[pl.ds(at, part), :] = piece[i * part : (i + 1) * part, :]


def partial_kernel(piece_ref, swapped_ref, own_ref, other_ref, mine_ref, near_ref, far_ref, send_ref, cot, weight):
    place_rows(piece_ref, swapped_ref, cot, 0)
    me = lax.axis_index("seq")
    depth = own_ref.shape[0]
    y = lax.rem(me, 2)
    weight[pl.ds(pl.multiple_of(y * depth, 16), depth), :] = own_ref[...]
    weight[pl.ds(pl.multiple_of((1 - y) * depth, 16), depth), :] = other_ref[...]
    for step, ref in zip(STEPS, (mine_ref, near_ref, far_ref, send_ref)):
        z = jnp.bitwise_xor(me, step) // 2
        cols = pl.ds(pl.multiple_of(z * 2 * HD, 2 * HD), 2 * HD)
        ref[...] = jnp.dot(cot[...], weight[:, cols], preferred_element_type=F32).astype(ref.dtype)


def add_kernel(kept_ref, received_ref, out_ref):
    out_ref[...] = (kept_ref[...] + received_ref[...].astype(F32)).astype(BF16)


def finish_kernel(mine_ref, near_ref, far_ref, kept_ref, give_ref):
    heads = mine_ref[...] + near_ref[...].astype(F32) + far_ref[...].astype(F32)
    first, second = heads[:, :HD].astype(BF16), heads[:, HD:].astype(BF16)
    first_row = lax.rem(lax.axis_index("seq"), 2) == 0
    kept_ref[...] = jnp.where(first_row, first, second)
    give_ref[...] = jnp.where(first_row, second, first)


def weight_grad_kernel(*refs):
    *pieces, out0, out1, out2, out3, own_ref, other_ref, cot, outs = refs
    tokens = cot.shape[0]
    place_rows(pieces[0], pieces[1], cot, 0)
    place_rows(pieces[2], pieces[3], cot, tokens // 2)
    for i, ref in enumerate((out0, out1, out2, out3)):
        outs[i * HD : (i + 1) * HD, :] = ref[...]
    depth = own_ref.shape[1]
    y = lax.rem(lax.axis_index("seq"), 2)
    for ref, row in ((own_ref, y), (other_ref, 1 - y)):
        cols = pl.ds(pl.multiple_of(row * depth, HD), depth)
        ref[...] = jnp.dot(outs[...], cot[:, cols], preferred_element_type=F32).astype(BF16)


def backward_kernel(queries_ref, keys_t_ref, vals_ref, probs_ref, out_ref, *refs, chunk):
    *grad_refs, send_ref, dk, dv = refs
    n, three, _ = send_ref.shape
    rows = three // 3
    image = n * rows
    scale = HD ** (-0.5)
    per = chunk // rows
    order = query_order(n)
    half = image // chunk // 2
    for c in range(image // chunk):
        span = slice(c * chunk, (c + 1) * chunk)
        within = slice(c % half * chunk, (c % half + 1) * chunk)
        grads = grad_refs[c // half][within, :]
        row_dot = jnp.sum(
            grads.astype(F32).T * out_ref[:, span].astype(F32), axis=0, keepdims=True
        )
        prob_grad = lax.dot_general(vals_ref[...], grads, NT, preferred_element_type=F32)
        low = probs_ref[:, span]
        score_grad = (low.astype(F32) * (prob_grad - row_dot)).astype(BF16)
        dq = (jnp.dot(keys_t_ref[...], score_grad, preferred_element_type=F32) * scale).T.astype(BF16)
        for i in range(per):
            send_ref[order[c * per + i], 0:rows, :] = dq[i * rows : (i + 1) * rows, :]
        dk_part = jnp.dot(score_grad[0:image, :], queries_ref[span, :], preferred_element_type=F32)
        dv_part = jnp.dot(low[0:image, :], grads, preferred_element_type=F32)
        if c == 0:
            dk[...] = dk_part
            dv[...] = dv_part
        else:
            dk[...] += dk_part
            dv[...] += dv_part
    send_ref[:, rows : 2 * rows, :] = (dk[...] * scale).astype(BF16).reshape(n, rows, HD)
    send_ref[:, 2 * rows : 3 * rows, :] = dv[...].astype(BF16).reshape(n, rows, HD)


def unpack_kernel(tok_ref, q_ref, k_ref, v_ref):
    rows = q_ref.shape[0]
    for h in range(tok_ref.shape[0]):
        for i, ref in enumerate((q_ref, k_ref, v_ref)):
            ref[:, h * HD : (h + 1) * HD] = tok_ref[h, i * rows : (i + 1) * rows, :]


def unpack_weight_kernel(own_ref, other_ref, w_ref):
    for other_row, ref in enumerate((own_ref, other_ref)):
        for i, step in enumerate(STEPS):
            w_ref[:, head_columns(step, other_row)] = ref[i * HD : (i + 1) * HD, :].astype(F32).T


def exchange(array, distance=0, cores=False):
    if not distance and not cores:
        return array
    size = 2 * lax.axis_size("seq")
    pairs = [(i, i ^ (2 * distance + int(cores))) for i in range(size)]
    return lax.ppermute(array, ("seq", "fsdp"), pairs)


def send_cotangents(d_out):
    rows, width = d_out.shape
    part, columns = rows // 2, width // len(STEPS)
    z = lax.axis_index("seq") // 2
    first = lax.axis_index("fsdp") * part
    return [
        exchange(lax.dynamic_slice(d_out, (first, (z ^ (step // 2)) * columns), (part, columns)), step)
        for step in STEPS
    ]


def local(q_img, k_img, v_img, k_txt, v_txt, out_weight, d_out):
    n = lax.axis_size("seq")
    rows, width = q_img.shape
    args = (q_img, k_img, v_img, k_txt, v_txt, out_weight, d_out)
    if n != 2 * len(STEPS) or width // HD != n or lax.axis_size("fsdp") != 2 or rows % 32:
        return local_general(*args)
    depth = out_weight.shape[0]
    image = n * rows
    text = k_txt.shape[0]
    total = image + text
    chunk = 2 * rows
    shape = jax.ShapeDtypeStruct
    vmem = pl.BlockSpec(memory_space=pltpu.VMEM)

    head = pl.BlockSpec((text, HD), lambda i, me_ref: (0, me_ref[0]))
    given = exchange(out_weight, 1)
    along = send_cotangents(d_out)
    tok_out, text_head = call(
        pack_kernel,
        [shape((n, 3 * rows, HD), BF16), shape((2, text, HD), BF16)],
        [lax.axis_index("seq").astype(jnp.int32)[None], q_img, k_img, v_img, k_txt, v_txt],
        specs=[vmem] * 3 + [head] * 2,
        scalars=1,
        moved=4 * 3 * rows * width,
        limit=60 * 1024 * 1024,
    )
    tok_out, along = lax.optimization_barrier((tok_out, along))
    along, given = lax.optimization_barrier((along, given))
    row = jnp.concatenate(along, axis=0)
    row_swapped = exchange(row, cores=True)
    tok_in = lax.all_to_all(tok_out, "seq", split_axis=0, concat_axis=0, tiled=True)

    probs, out_t, queries, keys_t, vals = call(
        functools.partial(forward_kernel, chunk=chunk),
        [shape(dims, BF16) for dims in ((total, image), (HD, image), (image, HD), (HD, total), (total, HD))],
        [tok_in, text_head],
        scratch=[pltpu.VMEM((total, HD), BF16), pltpu.VMEM((HD, total), BF16)],
        flops=4 * total * image * HD,
        moved=4 * total * image,
    )
    columns = row.shape[1]
    mine, near, far, send = call(
        partial_kernel,
        [shape((image // 2, 2 * HD), kind) for kind in (F32, BF16, F32, BF16)],
        [row, row_swapped, out_weight, given],
        scratch=[pltpu.VMEM((image // 2, columns), BF16), pltpu.VMEM((columns, width), BF16)],
        flops=8 * image * columns * HD,
        moved=2 * image * columns,
    )
    send, near = lax.optimization_barrier((exchange(send, 2), near))
    (far,) = call(add_kernel, [shape(far.shape, BF16)], [far, send])
    row, far = lax.optimization_barrier((row, far))
    far, near, other_row = exchange(far, 4), exchange(near, 2), exchange(row, 1)
    out_near, out_far = exchange(out_t, 2), exchange(out_t, 4)
    far, near, other_row = lax.optimization_barrier((far, near, other_row))
    kept, give = call(finish_kernel, [shape((image // 2, HD), BF16)] * 2, [mine, near, far])
    got = exchange(give, 1)
    other_swapped = exchange(other_row, cores=True)
    (grad_out,) = call(
        functools.partial(backward_kernel, chunk=chunk),
        [shape((n, 3 * rows, HD), BF16)],
        [queries, keys_t, vals, probs, out_t, kept, got],
        scratch=[pltpu.VMEM((image, HD), F32), pltpu.VMEM((image, HD), F32)],
    )
    grad_in = lax.all_to_all(grad_out, "seq", split_axis=0, concat_axis=0, tiled=True)
    out_far, out_near, _ = lax.optimization_barrier((out_far, out_near, grad_out))
    outs = [out_t, out_near, out_far, exchange(out_far, 2)]
    dw_own, dw_other = call(
        weight_grad_kernel,
        [shape((4 * HD, depth), BF16)] * 2,
        [row, row_swapped, other_row, other_swapped, *outs],
        scratch=[pltpu.VMEM((image, columns), BF16), pltpu.VMEM((4 * HD, image), BF16)],
        flops=96 * image * columns * HD,
        moved=2 * image * columns,
    )
    grads = call(
        unpack_kernel,
        [shape((rows, width), BF16)] * 3,
        [grad_in],
        moved=4 * 3 * rows * width,
    )
    (d_weight,) = call(
        unpack_weight_kernel,
        [shape((depth, width), F32)],
        [dw_own, exchange(dw_other, 1)],
        moved=6 * depth * width,
    )
    return (*grads, d_weight)


def solution(mesh):
    in_specs = (
        P(("group", "seq"), "fsdp"),
        P(("group", "seq"), "fsdp"),
        P(("group", "seq"), "fsdp"),
        P("group", "fsdp"),
        P("group", "fsdp"),
        P("seq", "fsdp"),
        P(("group", "seq"), None),
    )
    out_specs = (
        P(("group", "seq"), "fsdp"),
        P(("group", "seq"), "fsdp"),
        P(("group", "seq"), "fsdp"),
        P(("group", "seq"), "fsdp"),
    )
    return jax.shard_map(local, mesh=mesh, in_specs=in_specs, out_specs=out_specs, check_vma=False)
```

```python
import functools
import math

import jax
import jax.numpy as jnp
from jax import lax
from jax.experimental import pallas as pl
from jax.experimental.pallas import tpu as pltpu
from jax.sharding import PartitionSpec as P

HD = 128
F32 = jnp.float32
BF16 = jnp.bfloat16
LIMIT = 16 * 1024 * 1024
NT = (((1,), (1,)), ((), ()))


def attend(queries, cotangents, key_rows, value_rows, block_rows):
    score_scale = HD ** (-0.5)
    query_count = queries.shape[0]
    block_count = query_count // block_rows
    query_blocks = queries.reshape(block_count, block_rows, HD)
    grad_blocks = cotangents.reshape(block_count, block_rows, HD)

    def one_block(accumulated, pair_item):
        query_block, grad_block = pair_item
        scores = jnp.dot(query_block, key_rows.T, preferred_element_type=jnp.float32) * score_scale
        row_max = jnp.max(scores, axis=1, keepdims=True)
        probs = jnp.exp(scores - row_max)
        probs = probs / jnp.sum(probs, axis=1, keepdims=True)
        probs_low = probs.astype(jnp.bfloat16)
        out_rows = jnp.dot(probs_low, value_rows, preferred_element_type=jnp.float32).astype(
            jnp.bfloat16
        )
        prob_grad = jnp.dot(grad_block, value_rows.T, preferred_element_type=jnp.float32)
        row_dot = jnp.sum(
            grad_block.astype(jnp.float32) * out_rows.astype(jnp.float32), axis=1, keepdims=True
        )
        score_grad = (probs * (prob_grad - row_dot)).astype(jnp.bfloat16)
        query_grad = (
            jnp.dot(score_grad, key_rows, preferred_element_type=jnp.float32) * score_scale
        ).astype(jnp.bfloat16)
        key_grad = (
            accumulated[0]
            + jnp.dot(score_grad.T, query_block, preferred_element_type=jnp.float32) * score_scale
        )
        value_grad = accumulated[1] + jnp.dot(
            probs_low.T, grad_block, preferred_element_type=jnp.float32
        )
        return ((key_grad, value_grad), (query_grad, out_rows))

    empty = jnp.zeros((key_rows.shape[0], HD), jnp.float32)
    (key_grad, value_grad), (query_grad, out_rows) = lax.scan(
        one_block, (empty, empty), (query_blocks, grad_blocks)
    )
    return (
        query_grad.reshape(query_count, HD),
        out_rows.reshape(query_count, HD),
        key_grad,
        value_grad,
    )


def local_general(q_img, k_img, v_img, k_txt, v_txt, out_weight, d_out):
    rows_here = q_img.shape[0]
    heads_here = q_img.shape[1] // HD
    seq_count = lax.axis_size("seq")
    share_count = seq_count // heads_here
    part_rows = rows_here // share_count
    seq_index = lax.axis_index("seq")
    head_index = seq_index // share_count
    column_cut = d_out
    attn_grad = jnp.dot(
        column_cut,
        lax.all_gather(out_weight, "seq", axis=0, tiled=True),
        preferred_element_type=jnp.float32,
    ).astype(jnp.bfloat16)

    def to_heads(array_in):
        shaped = array_in.reshape(share_count, part_rows, heads_here, HD).transpose(2, 0, 1, 3)
        return shaped.reshape(seq_count, part_rows, HD)

    def whole_heads(array_in):
        shaped = array_in.reshape(rows_here, heads_here, HD).transpose(1, 0, 2)
        shaped = jnp.broadcast_to(shaped[:, None], (heads_here, share_count, rows_here, HD))
        return shaped.reshape(seq_count, rows_here, HD)

    def from_heads(array_in):
        shaped = array_in.reshape(heads_here, share_count, part_rows, HD).transpose(1, 2, 0, 3)
        return shaped.reshape(rows_here, heads_here * HD)

    text_keys = lax.dynamic_slice_in_dim(k_txt, head_index * HD, HD, 1)
    text_values = lax.dynamic_slice_in_dim(v_txt, head_index * HD, HD, 1)
    query_side = jnp.concatenate([to_heads(q_img), to_heads(attn_grad)], axis=2)
    key_side = jnp.concatenate([whole_heads(k_img), whole_heads(v_img)], axis=2)
    packed = jnp.concatenate([query_side, key_side], axis=1)
    received = lax.all_to_all(packed, "seq", split_axis=0, concat_axis=0, tiled=True)
    queries = received[:, :part_rows, :HD].reshape(seq_count * part_rows, HD)
    cotangents = received[:, :part_rows, HD:].reshape(seq_count * part_rows, HD)
    image_keys = received[:, part_rows:, :HD].reshape(seq_count * rows_here, HD)
    image_values = received[:, part_rows:, HD:].reshape(seq_count * rows_here, HD)
    key_rows = jnp.concatenate([image_keys, text_keys], axis=0)
    value_rows = jnp.concatenate([image_values, text_values], axis=0)
    query_grad, out_rows, key_grad, value_grad = attend(
        queries, cotangents, key_rows, value_rows, min(512, queries.shape[0])
    )
    image_count = image_keys.shape[0]
    query_part = (
        jnp.concatenate([query_grad, out_rows], axis=1)
        .astype(jnp.float32)
        .reshape(seq_count, part_rows, 2 * HD)
    )
    key_part = jnp.concatenate([key_grad[:image_count], value_grad[:image_count]], axis=1).reshape(
        seq_count, rows_here, 2 * HD
    )
    returned = lax.all_to_all(
        jnp.concatenate([query_part, key_part], axis=1).astype(jnp.bfloat16),
        "seq",
        split_axis=0,
        concat_axis=0,
        tiled=True,
    ).astype(jnp.float32)
    q_grad = from_heads(returned[:, :part_rows, :HD]).astype(jnp.bfloat16)
    out_tok = from_heads(returned[:, :part_rows, HD:]).astype(jnp.bfloat16)
    summed = jnp.sum(
        returned[:, part_rows:, :].reshape(heads_here, share_count, rows_here, 2 * HD), axis=1
    )
    summed = summed.transpose(1, 0, 2)
    k_grad = summed[:, :, :HD].reshape(rows_here, heads_here * HD).astype(jnp.bfloat16)
    v_grad = summed[:, :, HD:].reshape(rows_here, heads_here * HD).astype(jnp.bfloat16)
    column_cut = d_out
    d_weight = lax.psum_scatter(
        jnp.dot(column_cut.T, out_tok, preferred_element_type=jnp.float32).astype(jnp.bfloat16),
        "seq",
        scatter_dimension=0,
        tiled=True,
    ).astype(jnp.float32)
    return (q_grad, k_grad, v_grad, d_weight)


def call(kernel, outs, args, specs=None, scratch=(), scalars=0, out_specs=None, flops=0, moved=0, limit=LIMIT):
    vmem = pl.BlockSpec(memory_space=pltpu.VMEM)
    if specs is None:
        specs = [vmem] * (len(args) - scalars)
    if out_specs is None:
        out_specs = [vmem] * len(outs)
    return pl.pallas_call(
        kernel,
        out_shape=outs,
        grid_spec=pltpu.PrefetchScalarGridSpec(
            num_scalar_prefetch=scalars,
            grid=(1,),
            in_specs=specs,
            out_specs=out_specs,
            scratch_shapes=list(scratch),
        ),
        compiler_params=pltpu.CompilerParams(vmem_limit_bytes=limit),
        cost_estimate=pl.CostEstimate(flops=flops, bytes_accessed=moved, transcendentals=0),
    )(*args)


STEPS = (0, 2, 4, 6)


def head_columns(step, other_row):
    return pl.ds(pl.multiple_of(jnp.bitwise_xor(lax.axis_index("seq"), step + other_row) * HD, HD), HD)


def pack_kernel(me_ref, q_ref, k_ref, v_ref, kt_ref, vt_ref, tok_ref, text_ref):
    rows = q_ref.shape[0]
    for h in range(tok_ref.shape[0]):
        for i, ref in enumerate((q_ref, k_ref, v_ref)):
            tok_ref[h, i * rows : (i + 1) * rows, :] = ref[:, h * HD : (h + 1) * HD]
    text_ref[0] = kt_ref[...]
    text_ref[1] = vt_ref[...]


def query_order(n):
    y = lax.rem(lax.axis_index("seq"), 2)
    return [2 * z + y for z in range(n // 2)] + [2 * z + 1 - y for z in range(n // 2)]


def forward_kernel(tok_ref, text_ref, probs_ref, out_ref, queries_ref, keys_t_ref, vals_ref, keys, vals_t, *, chunk):
    n, three, _ = tok_ref.shape
    rows = three // 3
    image = n * rows
    text = text_ref.shape[1]
    for i, source in enumerate(query_order(n)):
        queries_ref[i * rows : (i + 1) * rows, :] = tok_ref[source, 0:rows, :]
    keys[0:image, :] = tok_ref[:, rows : 2 * rows, :].reshape(image, HD)
    keys[image : image + text, :] = text_ref[0]
    vals_ref[0:image, :] = tok_ref[:, 2 * rows : 3 * rows, :].reshape(image, HD)
    vals_ref[image : image + text, :] = text_ref[1]
    keys_t_ref[...] = keys[...].T
    vals_t[...] = vals_ref[...].T
    factor = HD ** (-0.5) * math.log2(math.e)
    for c in range(image // chunk):
        span = slice(c * chunk, (c + 1) * chunk)
        scores = lax.dot_general(keys[...], queries_ref[span, :], NT, preferred_element_type=F32)
        top = jnp.max(scores, axis=0, keepdims=True)
        weights = jnp.exp2((scores - top) * factor)
        total = jnp.sum(weights, axis=0, keepdims=True)
        low = (weights * (1.0 / total)).astype(BF16)
        probs_ref[:, span] = low
        out_ref[:, span] = jnp.dot(vals_t[...], low, preferred_element_type=F32).astype(BF16)


def place_rows(piece_ref, swapped_ref, cot, start):
    me = lax.axis_index("seq")
    core = lax.axis_index("fsdp")
    part = piece_ref.shape[0] // len(STEPS)
    for piece, shift in ((piece_ref, core), (swapped_ref, 1 - core)):
        for i, step in enumerate(STEPS):
            z = jnp.bitwise_xor(me, step) // 2
            at = pl.multiple_of(start + z * (2 * part) + shift * part, 16)
            cot[pl.ds(at, part), :] = piece[i * part : (i + 1) * part, :]


def partial_kernel(piece_ref, swapped_ref, own_ref, other_ref, mine_ref, near_ref, far_ref, send_ref, cot, weight):
    place_rows(piece_ref, swapped_ref, cot, 0)
    me = lax.axis_index("seq")
    depth = own_ref.shape[0]
    y = lax.rem(me, 2)
    weight[pl.ds(pl.multiple_of(y * depth, 16), depth), :] = own_ref[...]
    weight[pl.ds(pl.multiple_of((1 - y) * depth, 16), depth), :] = other_ref[...]
    for step, ref in zip(STEPS, (mine_ref, near_ref, far_ref, send_ref)):
        z = jnp.bitwise_xor(me, step) // 2
        cols = pl.ds(pl.multiple_of(z * 2 * HD, 2 * HD), 2 * HD)
        ref[...] = jnp.dot(cot[...], weight[:, cols], preferred_element_type=F32).astype(ref.dtype)


def add_kernel(kept_ref, received_ref, out_ref):
    out_ref[...] = (kept_ref[...] + received_ref[...].astype(F32)).astype(BF16)


def finish_kernel(mine_ref, near_ref, far_ref, kept_ref, give_ref):
    heads = mine_ref[...] + near_ref[...].astype(F32) + far_ref[...].astype(F32)
    first, second = heads[:, :HD].astype(BF16), heads[:, HD:].astype(BF16)
    first_row = lax.rem(lax.axis_index("seq"), 2) == 0
    kept_ref[...] = jnp.where(first_row, first, second)
    give_ref[...] = jnp.where(first_row, second, first)


def weight_grad_kernel(*refs):
    *pieces, out0, out1, out2, out3, own_ref, other_ref, cot, outs = refs
    tokens = cot.shape[0]
    place_rows(pieces[0], pieces[1], cot, 0)
    place_rows(pieces[2], pieces[3], cot, tokens // 2)
    for i, ref in enumerate((out0, out1, out2, out3)):
        outs[i * HD : (i + 1) * HD, :] = ref[...]
    depth = own_ref.shape[1]
    y = lax.rem(lax.axis_index("seq"), 2)
    for ref, row in ((own_ref, y), (other_ref, 1 - y)):
        cols = pl.ds(pl.multiple_of(row * depth, HD), depth)
        ref[...] = jnp.dot(outs[...], cot[:, cols], preferred_element_type=F32).astype(BF16)


def backward_kernel(queries_ref, keys_t_ref, vals_ref, probs_ref, out_ref, *refs, chunk):
    *grad_refs, send_ref, dk, dv = refs
    n, three, _ = send_ref.shape
    rows = three // 3
    image = n * rows
    scale = HD ** (-0.5)
    per = chunk // rows
    order = query_order(n)
    half = image // chunk // 2
    for c in range(image // chunk):
        span = slice(c * chunk, (c + 1) * chunk)
        within = slice(c % half * chunk, (c % half + 1) * chunk)
        grads = grad_refs[c // half][within, :]
        row_dot = jnp.sum(
            grads.astype(F32).T * out_ref[:, span].astype(F32), axis=0, keepdims=True
        )
        prob_grad = lax.dot_general(vals_ref[...], grads, NT, preferred_element_type=F32)
        low = probs_ref[:, span]
        score_grad = (low.astype(F32) * (prob_grad - row_dot)).astype(BF16)
        dq = (jnp.dot(keys_t_ref[...], score_grad, preferred_element_type=F32) * scale).T.astype(BF16)
        for i in range(per):
            send_ref[order[c * per + i], 0:rows, :] = dq[i * rows : (i + 1) * rows, :]
        dk_part = jnp.dot(score_grad[0:image, :], queries_ref[span, :], preferred_element_type=F32)
        dv_part = jnp.dot(low[0:image, :], grads, preferred_element_type=F32)
        if c == 0:
            dk[...] = dk_part
            dv[...] = dv_part
        else:
            dk[...] += dk_part
            dv[...] += dv_part
    send_ref[:, rows : 2 * rows, :] = (dk[...] * scale).astype(BF16).reshape(n, rows, HD)
    send_ref[:, 2 * rows : 3 * rows, :] = dv[...].astype(BF16).reshape(n, rows, HD)


def unpack_kernel(tok_ref, q_ref, k_ref, v_ref):
    rows = q_ref.shape[0]
    for h in range(tok_ref.shape[0]):
        for i, ref in enumerate((q_ref, k_ref, v_ref)):
            ref[:, h * HD : (h + 1) * HD] = tok_ref[h, i * rows : (i + 1) * rows, :]


def unpack_weight_kernel(own_ref, other_ref, w_ref):
    for other_row, ref in enumerate((own_ref, other_ref)):
        for i, step in enumerate(STEPS):
            w_ref[:, head_columns(step, other_row)] = ref[i * HD : (i + 1) * HD, :].astype(F32).T


def exchange(array, distance=0, cores=False):
    if not distance and not cores:
        return array
    size = 2 * lax.axis_size("seq")
    pairs = [(i, i ^ (2 * distance + int(cores))) for i in range(size)]
    return lax.ppermute(array, ("seq", "fsdp"), pairs)


def send_cotangents(d_out):
    rows, width = d_out.shape
    part, columns = rows // 2, width // len(STEPS)
    z = lax.axis_index("seq") // 2
    first = lax.axis_index("fsdp") * part
    return [
        exchange(lax.dynamic_slice(d_out, (first, (z ^ (step // 2)) * columns), (part, columns)), step)
        for step in STEPS
    ]


def local(q_img, k_img, v_img, k_txt, v_txt, out_weight, d_out):
    n = lax.axis_size("seq")
    rows, width = q_img.shape
    args = (q_img, k_img, v_img, k_txt, v_txt, out_weight, d_out)
    if n != 2 * len(STEPS) or width // HD != n or lax.axis_size("fsdp") != 2 or rows % 32:
        return local_general(*args)
    depth = out_weight.shape[0]
    image = n * rows
    text = k_txt.shape[0]
    total = image + text
    chunk = 2 * rows
    shape = jax.ShapeDtypeStruct
    vmem = pl.BlockSpec(memory_space=pltpu.VMEM)

    head = pl.BlockSpec((text, HD), lambda i, me_ref: (0, me_ref[0]))
    given = exchange(out_weight, 1)
    along = send_cotangents(d_out)
    tok_out, text_head = call(
        pack_kernel,
        [shape((n, 3 * rows, HD), BF16), shape((2, text, HD), BF16)],
        [lax.axis_index("seq").astype(jnp.int32)[None], q_img, k_img, v_img, k_txt, v_txt],
        specs=[vmem] * 3 + [head] * 2,
        scalars=1,
        moved=4 * 3 * rows * width,
    )
    tok_out, along = lax.optimization_barrier((tok_out, along))
    along, given = lax.optimization_barrier((along, given))
    row = jnp.concatenate(along, axis=0)
    row_swapped = exchange(row, cores=True)
    tok_in = lax.all_to_all(tok_out, "seq", split_axis=0, concat_axis=0, tiled=True)

    probs, out_t, queries, keys_t, vals = call(
        functools.partial(forward_kernel, chunk=chunk),
        [shape(dims, BF16) for dims in ((total, image), (HD, image), (image, HD), (HD, total), (total, HD))],
        [tok_in, text_head],
        scratch=[pltpu.VMEM((total, HD), BF16), pltpu.VMEM((HD, total), BF16)],
        flops=4 * total * image * HD,
        moved=4 * total * image,
    )
    columns = row.shape[1]
    mine, near, far, send = call(
        partial_kernel,
        [shape((image // 2, 2 * HD), kind) for kind in (F32, BF16, F32, BF16)],
        [row, row_swapped, out_weight, given],
        scratch=[pltpu.VMEM((image // 2, columns), BF16), pltpu.VMEM((columns, width), BF16)],
        flops=8 * image * columns * HD,
        moved=2 * image * columns,
    )
    send, near = lax.optimization_barrier((exchange(send, 2), near))
    (far,) = call(add_kernel, [shape(far.shape, BF16)], [far, send])
    row, far = lax.optimization_barrier((row, far))
    far, near, other_row = exchange(far, 4), exchange(near, 2), exchange(row, 1)
    out_near, out_far = exchange(out_t, 2), exchange(out_t, 4)
    far, near, other_row = lax.optimization_barrier((far, near, other_row))
    kept, give = call(finish_kernel, [shape((image // 2, HD), BF16)] * 2, [mine, near, far])
    got = exchange(give, 1)
    other_swapped = exchange(other_row, cores=True)
    (grad_out,) = call(
        functools.partial(backward_kernel, chunk=chunk),
        [shape((n, 3 * rows, HD), BF16)],
        [queries, keys_t, vals, probs, out_t, kept, got],
        scratch=[pltpu.VMEM((image, HD), F32), pltpu.VMEM((image, HD), F32)],
    )
    grad_in = lax.all_to_all(grad_out, "seq", split_axis=0, concat_axis=0, tiled=True)
    out_far, out_near, _ = lax.optimization_barrier((out_far, out_near, grad_out))
    outs = [out_t, out_near, out_far, exchange(out_far, 2)]
    dw_own, dw_other = call(
        weight_grad_kernel,
        [shape((4 * HD, depth), BF16)] * 2,
        [row, row_swapped, other_row, other_swapped, *outs],
        scratch=[pltpu.VMEM((image, columns), BF16), pltpu.VMEM((4 * HD, image), BF16)],
        flops=96 * image * columns * HD,
        moved=2 * image * columns,
    )
    grads = call(
        unpack_kernel,
        [shape((rows, width), BF16)] * 3,
        [grad_in],
        moved=4 * 3 * rows * width,
    )
    (d_weight,) = call(
        unpack_weight_kernel,
        [shape((depth, width), F32)],
        [dw_own, exchange(dw_other, 1)],
        moved=6 * depth * width,
    )
    return (*grads, d_weight)


def solution(mesh):
    in_specs = (
        P(("group", "seq"), "fsdp"),
        P(("group", "seq"), "fsdp"),
        P(("group", "seq"), "fsdp"),
        P("group", "fsdp"),
        P("group", "fsdp"),
        P("seq", "fsdp"),
        P(("group", "seq"), None),
    )
    out_specs = (
        P(("group", "seq"), "fsdp"),
        P(("group", "seq"), "fsdp"),
        P(("group", "seq"), "fsdp"),
        P(("group", "seq"), "fsdp"),
    )
    return jax.shard_map(local, mesh=mesh, in_specs=in_specs, out_specs=out_specs, check_vma=False)
```

```python
import functools
import math

import jax
import jax.numpy as jnp
from jax import lax
from jax.experimental import pallas as pl
from jax.experimental.pallas import tpu as pltpu
from jax.sharding import PartitionSpec as P

HD = 128
F32 = jnp.float32
BF16 = jnp.bfloat16
LIMIT = 16 * 1024 * 1024
NT = (((1,), (1,)), ((), ()))


def attend(queries, cotangents, key_rows, value_rows, block_rows):
    score_scale = HD ** (-0.5)
    query_count = queries.shape[0]
    block_count = query_count // block_rows
    query_blocks = queries.reshape(block_count, block_rows, HD)
    grad_blocks = cotangents.reshape(block_count, block_rows, HD)

    def one_block(accumulated, pair_item):
        query_block, grad_block = pair_item
        scores = jnp.dot(query_block, key_rows.T, preferred_element_type=jnp.float32) * score_scale
        row_max = jnp.max(scores, axis=1, keepdims=True)
        probs = jnp.exp(scores - row_max)
        probs = probs / jnp.sum(probs, axis=1, keepdims=True)
        probs_low = probs.astype(jnp.bfloat16)
        out_rows = jnp.dot(probs_low, value_rows, preferred_element_type=jnp.float32).astype(
            jnp.bfloat16
        )
        prob_grad = jnp.dot(grad_block, value_rows.T, preferred_element_type=jnp.float32)
        row_dot = jnp.sum(
            grad_block.astype(jnp.float32) * out_rows.astype(jnp.float32), axis=1, keepdims=True
        )
        score_grad = (probs * (prob_grad - row_dot)).astype(jnp.bfloat16)
        query_grad = (
            jnp.dot(score_grad, key_rows, preferred_element_type=jnp.float32) * score_scale
        ).astype(jnp.bfloat16)
        key_grad = (
            accumulated[0]
            + jnp.dot(score_grad.T, query_block, preferred_element_type=jnp.float32) * score_scale
        )
        value_grad = accumulated[1] + jnp.dot(
            probs_low.T, grad_block, preferred_element_type=jnp.float32
        )
        return ((key_grad, value_grad), (query_grad, out_rows))

    empty = jnp.zeros((key_rows.shape[0], HD), jnp.float32)
    (key_grad, value_grad), (query_grad, out_rows) = lax.scan(
        one_block, (empty, empty), (query_blocks, grad_blocks)
    )
    return (
        query_grad.reshape(query_count, HD),
        out_rows.reshape(query_count, HD),
        key_grad,
        value_grad,
    )


def local_general(q_img, k_img, v_img, k_txt, v_txt, out_weight, d_out):
    rows_here = q_img.shape[0]
    heads_here = q_img.shape[1] // HD
    seq_count = lax.axis_size("seq")
    share_count = seq_count // heads_here
    part_rows = rows_here // share_count
    seq_index = lax.axis_index("seq")
    head_index = seq_index // share_count
    column_cut = d_out
    attn_grad = jnp.dot(
        column_cut,
        lax.all_gather(out_weight, "seq", axis=0, tiled=True),
        preferred_element_type=jnp.float32,
    ).astype(jnp.bfloat16)

    def to_heads(array_in):
        shaped = array_in.reshape(share_count, part_rows, heads_here, HD).transpose(2, 0, 1, 3)
        return shaped.reshape(seq_count, part_rows, HD)

    def whole_heads(array_in):
        shaped = array_in.reshape(rows_here, heads_here, HD).transpose(1, 0, 2)
        shaped = jnp.broadcast_to(shaped[:, None], (heads_here, share_count, rows_here, HD))
        return shaped.reshape(seq_count, rows_here, HD)

    def from_heads(array_in):
        shaped = array_in.reshape(heads_here, share_count, part_rows, HD).transpose(1, 2, 0, 3)
        return shaped.reshape(rows_here, heads_here * HD)

    text_keys = lax.dynamic_slice_in_dim(k_txt, head_index * HD, HD, 1)
    text_values = lax.dynamic_slice_in_dim(v_txt, head_index * HD, HD, 1)
    query_side = jnp.concatenate([to_heads(q_img), to_heads(attn_grad)], axis=2)
    key_side = jnp.concatenate([whole_heads(k_img), whole_heads(v_img)], axis=2)
    packed = jnp.concatenate([query_side, key_side], axis=1)
    received = lax.all_to_all(packed, "seq", split_axis=0, concat_axis=0, tiled=True)
    queries = received[:, :part_rows, :HD].reshape(seq_count * part_rows, HD)
    cotangents = received[:, :part_rows, HD:].reshape(seq_count * part_rows, HD)
    image_keys = received[:, part_rows:, :HD].reshape(seq_count * rows_here, HD)
    image_values = received[:, part_rows:, HD:].reshape(seq_count * rows_here, HD)
    key_rows = jnp.concatenate([image_keys, text_keys], axis=0)
    value_rows = jnp.concatenate([image_values, text_values], axis=0)
    query_grad, out_rows, key_grad, value_grad = attend(
        queries, cotangents, key_rows, value_rows, min(512, queries.shape[0])
    )
    image_count = image_keys.shape[0]
    query_part = (
        jnp.concatenate([query_grad, out_rows], axis=1)
        .astype(jnp.float32)
        .reshape(seq_count, part_rows, 2 * HD)
    )
    key_part = jnp.concatenate([key_grad[:image_count], value_grad[:image_count]], axis=1).reshape(
        seq_count, rows_here, 2 * HD
    )
    returned = lax.all_to_all(
        jnp.concatenate([query_part, key_part], axis=1).astype(jnp.bfloat16),
        "seq",
        split_axis=0,
        concat_axis=0,
        tiled=True,
    ).astype(jnp.float32)
    q_grad = from_heads(returned[:, :part_rows, :HD]).astype(jnp.bfloat16)
    out_tok = from_heads(returned[:, :part_rows, HD:]).astype(jnp.bfloat16)
    summed = jnp.sum(
        returned[:, part_rows:, :].reshape(heads_here, share_count, rows_here, 2 * HD), axis=1
    )
    summed = summed.transpose(1, 0, 2)
    k_grad = summed[:, :, :HD].reshape(rows_here, heads_here * HD).astype(jnp.bfloat16)
    v_grad = summed[:, :, HD:].reshape(rows_here, heads_here * HD).astype(jnp.bfloat16)
    column_cut = d_out
    d_weight = lax.psum_scatter(
        jnp.dot(column_cut.T, out_tok, preferred_element_type=jnp.float32).astype(jnp.bfloat16),
        "seq",
        scatter_dimension=0,
        tiled=True,
    ).astype(jnp.float32)
    return (q_grad, k_grad, v_grad, d_weight)


def call(kernel, outs, args, specs=None, scratch=(), scalars=0, out_specs=None, flops=0, moved=0, limit=LIMIT):
    vmem = pl.BlockSpec(memory_space=pltpu.VMEM)
    if specs is None:
        specs = [vmem] * (len(args) - scalars)
    if out_specs is None:
        out_specs = [vmem] * len(outs)
    return pl.pallas_call(
        kernel,
        out_shape=outs,
        grid_spec=pltpu.PrefetchScalarGridSpec(
            num_scalar_prefetch=scalars,
            grid=(1,),
            in_specs=specs,
            out_specs=out_specs,
            scratch_shapes=list(scratch),
        ),
        compiler_params=pltpu.CompilerParams(vmem_limit_bytes=limit),
        cost_estimate=pl.CostEstimate(flops=flops, bytes_accessed=moved, transcendentals=0),
    )(*args)


STEPS = (0, 2, 4, 6)


def head_columns(step, other_row):
    return pl.ds(pl.multiple_of(jnp.bitwise_xor(lax.axis_index("seq"), step + other_row) * HD, HD), HD)


def pack_kernel(me_ref, q_ref, k_ref, v_ref, kt_ref, vt_ref, tok_ref, text_ref):
    rows = q_ref.shape[0]
    for h in range(tok_ref.shape[0]):
        for i, ref in enumerate((q_ref, k_ref, v_ref)):
            tok_ref[h, i * rows : (i + 1) * rows, :] = ref[:, h * HD : (h + 1) * HD]
    text_ref[0] = kt_ref[...]
    text_ref[1] = vt_ref[...]


def query_order(n):
    y = lax.rem(lax.axis_index("seq"), 2)
    return [2 * z + y for z in range(n // 2)] + [2 * z + 1 - y for z in range(n // 2)]


def forward_kernel(tok_ref, text_ref, probs_ref, out_ref, queries_ref, keys_t_ref, vals_ref, keys, vals_t, *, chunk):
    n, three, _ = tok_ref.shape
    rows = three // 3
    image = n * rows
    text = text_ref.shape[1]
    for i, source in enumerate(query_order(n)):
        queries_ref[i * rows : (i + 1) * rows, :] = tok_ref[source, 0:rows, :]
    keys[0:image, :] = tok_ref[:, rows : 2 * rows, :].reshape(image, HD)
    keys[image : image + text, :] = text_ref[0]
    vals_ref[0:image, :] = tok_ref[:, 2 * rows : 3 * rows, :].reshape(image, HD)
    vals_ref[image : image + text, :] = text_ref[1]
    keys_t_ref[...] = keys[...].T
    vals_t[...] = vals_ref[...].T
    factor = HD ** (-0.5) * math.log2(math.e)
    for c in range(image // chunk):
        span = slice(c * chunk, (c + 1) * chunk)
        scores = lax.dot_general(keys[...], queries_ref[span, :], NT, preferred_element_type=F32)
        top = jnp.max(scores, axis=0, keepdims=True)
        weights = jnp.exp2((scores - top) * factor)
        total = jnp.sum(weights, axis=0, keepdims=True)
        low = (weights * (1.0 / total)).astype(BF16)
        probs_ref[:, span] = low
        out_ref[:, span] = jnp.dot(vals_t[...], low, preferred_element_type=F32).astype(BF16)


def place_rows(piece_ref, swapped_ref, cot, start):
    me = lax.axis_index("seq")
    core = lax.axis_index("fsdp")
    part = piece_ref.shape[0] // len(STEPS)
    for piece, shift in ((piece_ref, core), (swapped_ref, 1 - core)):
        for i, step in enumerate(STEPS):
            z = jnp.bitwise_xor(me, step) // 2
            at = pl.multiple_of(start + z * (2 * part) + shift * part, 16)
            cot[pl.ds(at, part), :] = piece[i * part : (i + 1) * part, :]


def partial_kernel(piece_ref, swapped_ref, own_ref, other_ref, mine_ref, near_ref, far_ref, send_ref, cot, weight):
    place_rows(piece_ref, swapped_ref, cot, 0)
    me = lax.axis_index("seq")
    depth = own_ref.shape[0]
    y = lax.rem(me, 2)
    weight[pl.ds(pl.multiple_of(y * depth, 16), depth), :] = own_ref[...]
    weight[pl.ds(pl.multiple_of((1 - y) * depth, 16), depth), :] = other_ref[...]
    for step, ref in zip(STEPS, (mine_ref, near_ref, far_ref, send_ref)):
        z = jnp.bitwise_xor(me, step) // 2
        cols = pl.ds(pl.multiple_of(z * 2 * HD, 2 * HD), 2 * HD)
        ref[...] = jnp.dot(cot[...], weight[:, cols], preferred_element_type=F32).astype(ref.dtype)


def add_kernel(kept_ref, received_ref, out_ref):
    out_ref[...] = (kept_ref[...] + received_ref[...].astype(F32)).astype(BF16)


def finish_kernel(mine_ref, near_ref, far_ref, kept_ref, give_ref):
    heads = mine_ref[...] + near_ref[...].astype(F32) + far_ref[...].astype(F32)
    first, second = heads[:, :HD].astype(BF16), heads[:, HD:].astype(BF16)
    first_row = lax.rem(lax.axis_index("seq"), 2) == 0
    kept_ref[...] = jnp.where(first_row, first, second)
    give_ref[...] = jnp.where(first_row, second, first)


def weight_grad_kernel(*refs):
    *pieces, out0, out1, out2, out3, own_ref, other_ref, cot, outs = refs
    tokens = cot.shape[0]
    place_rows(pieces[0], pieces[1], cot, 0)
    place_rows(pieces[2], pieces[3], cot, tokens // 2)
    for i, ref in enumerate((out0, out1, out2, out3)):
        outs[i * HD : (i + 1) * HD, :] = ref[...]
    depth = own_ref.shape[1]
    y = lax.rem(lax.axis_index("seq"), 2)
    for ref, row in ((own_ref, y), (other_ref, 1 - y)):
        cols = pl.ds(pl.multiple_of(row * depth, HD), depth)
        ref[...] = jnp.dot(outs[...], cot[:, cols], preferred_element_type=F32).astype(BF16)


def backward_half(first, queries_ref, keys_t_ref, vals_ref, probs_ref, out_ref, grads_ref, dq_ref, dk, dv, chunk):
    image = dk.shape[0]
    scale = HD ** (-0.5)
    tokens = grads_ref.shape[0]
    start = 0 if first else tokens
    for c in range(tokens // chunk):
        span = slice(start + c * chunk, start + (c + 1) * chunk)
        within = slice(c * chunk, (c + 1) * chunk)
        grads = grads_ref[within, :]
        row_dot = jnp.sum(
            grads.astype(F32).T * out_ref[:, span].astype(F32), axis=0, keepdims=True
        )
        prob_grad = lax.dot_general(vals_ref[...], grads, NT, preferred_element_type=F32)
        low = probs_ref[:, span]
        score_grad = (low.astype(F32) * (prob_grad - row_dot)).astype(BF16)
        dq = jnp.dot(keys_t_ref[...], score_grad, preferred_element_type=F32) * scale
        dq_ref[within, :] = dq.T.astype(BF16)
        dk_part = jnp.dot(score_grad[0:image, :], queries_ref[span, :], preferred_element_type=F32)
        dv_part = jnp.dot(low[0:image, :], grads, preferred_element_type=F32)
        if first and c == 0:
            dk[...] = dk_part
            dv[...] = dv_part
        else:
            dk[...] += dk_part
            dv[...] += dv_part


def backward_first_kernel(queries_ref, keys_t_ref, vals_ref, probs_ref, out_ref, grads_ref, dq_ref, dk_ref, dv_ref, *, chunk):
    backward_half(
        True, queries_ref, keys_t_ref, vals_ref, probs_ref, out_ref, grads_ref, dq_ref, dk_ref, dv_ref, chunk
    )


def backward_second_kernel(
    queries_ref, keys_t_ref, vals_ref, probs_ref, out_ref, grads_ref, dq0_ref, dk_ref, dv_ref, send_ref, dq1_ref, dk, dv, *, chunk
):
    n, three, _ = send_ref.shape
    rows = three // 3
    dk[...] = dk_ref[...]
    dv[...] = dv_ref[...]
    backward_half(
        False, queries_ref, keys_t_ref, vals_ref, probs_ref, out_ref, grads_ref, dq1_ref, dk, dv, chunk
    )
    for i, source in enumerate(query_order(n)):
        ref, at = (dq0_ref, i) if 2 * i < n else (dq1_ref, i - n // 2)
        send_ref[source, 0:rows, :] = ref[at * rows : (at + 1) * rows, :]
    send_ref[:, rows : 2 * rows, :] = (dk[...] * HD ** (-0.5)).astype(BF16).reshape(n, rows, HD)
    send_ref[:, 2 * rows : 3 * rows, :] = dv[...].astype(BF16).reshape(n, rows, HD)


def unpack_kernel(tok_ref, q_ref, k_ref, v_ref):
    rows = q_ref.shape[0]
    for h in range(tok_ref.shape[0]):
        for i, ref in enumerate((q_ref, k_ref, v_ref)):
            ref[:, h * HD : (h + 1) * HD] = tok_ref[h, i * rows : (i + 1) * rows, :]


def unpack_weight_kernel(own_ref, other_ref, w_ref):
    for other_row, ref in enumerate((own_ref, other_ref)):
        for i, step in enumerate(STEPS):
            w_ref[:, head_columns(step, other_row)] = ref[i * HD : (i + 1) * HD, :].astype(F32).T


def exchange(array, distance=0, cores=False):
    if not distance and not cores:
        return array
    size = 2 * lax.axis_size("seq")
    pairs = [(i, i ^ (2 * distance + int(cores))) for i in range(size)]
    return lax.ppermute(array, ("seq", "fsdp"), pairs)


def send_cotangents(d_out):
    rows, width = d_out.shape
    part, columns = rows // 2, width // len(STEPS)
    z = lax.axis_index("seq") // 2
    first = lax.axis_index("fsdp") * part
    return [
        exchange(lax.dynamic_slice(d_out, (first, (z ^ (step // 2)) * columns), (part, columns)), step)
        for step in STEPS
    ]


def local(q_img, k_img, v_img, k_txt, v_txt, out_weight, d_out):
    n = lax.axis_size("seq")
    rows, width = q_img.shape
    args = (q_img, k_img, v_img, k_txt, v_txt, out_weight, d_out)
    if n != 2 * len(STEPS) or width // HD != n or lax.axis_size("fsdp") != 2 or rows % 32:
        return local_general(*args)
    depth = out_weight.shape[0]
    image = n * rows
    text = k_txt.shape[0]
    total = image + text
    chunk = 2 * rows
    shape = jax.ShapeDtypeStruct
    vmem = pl.BlockSpec(memory_space=pltpu.VMEM)

    head = pl.BlockSpec((text, HD), lambda i, me_ref: (0, me_ref[0]))
    given = exchange(out_weight, 1)
    along = send_cotangents(d_out)
    tok_out, text_head = call(
        pack_kernel,
        [shape((n, 3 * rows, HD), BF16), shape((2, text, HD), BF16)],
        [lax.axis_index("seq").astype(jnp.int32)[None], q_img, k_img, v_img, k_txt, v_txt],
        specs=[vmem] * 3 + [head] * 2,
        scalars=1,
        moved=4 * 3 * rows * width,
        limit=60 * 1024 * 1024,
    )
    tok_out, along = lax.optimization_barrier((tok_out, along))
    along, given = lax.optimization_barrier((along, given))
    row = jnp.concatenate(along, axis=0)
    row_swapped = exchange(row, cores=True)
    tok_in = lax.all_to_all(tok_out, "seq", split_axis=0, concat_axis=0, tiled=True)

    probs, out_t, queries, keys_t, vals = call(
        functools.partial(forward_kernel, chunk=chunk),
        [shape(dims, BF16) for dims in ((total, image), (HD, image), (image, HD), (HD, total), (total, HD))],
        [tok_in, text_head],
        scratch=[pltpu.VMEM((total, HD), BF16), pltpu.VMEM((HD, total), BF16)],
        flops=4 * total * image * HD,
        moved=4 * total * image,
    )
    columns = row.shape[1]
    mine, near, far, send = call(
        partial_kernel,
        [shape((image // 2, 2 * HD), kind) for kind in (F32, BF16, F32, BF16)],
        [row, row_swapped, out_weight, given],
        scratch=[pltpu.VMEM((image // 2, columns), BF16), pltpu.VMEM((columns, width), BF16)],
        flops=8 * image * columns * HD,
        moved=2 * image * columns,
    )
    send, near = lax.optimization_barrier((exchange(send, 2), near))
    (far,) = call(add_kernel, [shape(far.shape, BF16)], [far, send])
    row, far = lax.optimization_barrier((row, far))
    far, near, other_row = exchange(far, 4), exchange(near, 2), exchange(row, 1)
    out_near, out_far = exchange(out_t, 2), exchange(out_t, 4)
    far, near, other_row = lax.optimization_barrier((far, near, other_row))
    kept, give = call(finish_kernel, [shape((image // 2, HD), BF16)] * 2, [mine, near, far])
    got = exchange(give, 1)
    other_swapped = exchange(other_row, cores=True)
    dq, dk, dv = call(
        functools.partial(backward_first_kernel, chunk=chunk),
        [shape((image // 2, HD), BF16)] + [shape((image, HD), F32)] * 2,
        [queries, keys_t, vals, probs, out_t, kept],
    )
    (grad_out,) = call(
        functools.partial(backward_second_kernel, chunk=chunk),
        [shape((n, 3 * rows, HD), BF16)],
        [queries, keys_t, vals, probs, out_t, got, dq, dk, dv],
        scratch=[pltpu.VMEM((image // 2, HD), BF16)] + [pltpu.VMEM((image, HD), F32)] * 2,
    )
    grad_in = lax.all_to_all(grad_out, "seq", split_axis=0, concat_axis=0, tiled=True)
    out_far, out_near, _ = lax.optimization_barrier((out_far, out_near, grad_out))
    outs = [out_t, out_near, out_far, exchange(out_far, 2)]
    dw_own, dw_other = call(
        weight_grad_kernel,
        [shape((4 * HD, depth), BF16)] * 2,
        [row, row_swapped, other_row, other_swapped, *outs],
        scratch=[pltpu.VMEM((image, columns), BF16), pltpu.VMEM((4 * HD, image), BF16)],
        flops=96 * image * columns * HD,
        moved=2 * image * columns,
    )
    grads = call(
        unpack_kernel,
        [shape((rows, width), BF16)] * 3,
        [grad_in],
        moved=4 * 3 * rows * width,
    )
    (d_weight,) = call(
        unpack_weight_kernel,
        [shape((depth, width), F32)],
        [dw_own, exchange(dw_other, 1)],
        moved=6 * depth * width,
    )
    return (*grads, d_weight)


def solution(mesh):
    in_specs = (
        P(("group", "seq"), "fsdp"),
        P(("group", "seq"), "fsdp"),
        P(("group", "seq"), "fsdp"),
        P("group", "fsdp"),
        P("group", "fsdp"),
        P("seq", "fsdp"),
        P(("group", "seq"), None),
    )
    out_specs = (
        P(("group", "seq"), "fsdp"),
        P(("group", "seq"), "fsdp"),
        P(("group", "seq"), "fsdp"),
        P(("group", "seq"), "fsdp"),
    )
    return jax.shard_map(local, mesh=mesh, in_specs=in_specs, out_specs=out_specs, check_vma=False)
```

```python
import functools
import math

import jax
import jax.numpy as jnp
from jax import lax
from jax.experimental import pallas as pl
from jax.experimental.pallas import tpu as pltpu
from jax.sharding import PartitionSpec as P

HD = 128
F32 = jnp.float32
BF16 = jnp.bfloat16
LIMIT = 16 * 1024 * 1024
NT = (((1,), (1,)), ((), ()))


def attend(queries, cotangents, key_rows, value_rows, block_rows):
    score_scale = HD ** (-0.5)
    query_count = queries.shape[0]
    block_count = query_count // block_rows
    query_blocks = queries.reshape(block_count, block_rows, HD)
    grad_blocks = cotangents.reshape(block_count, block_rows, HD)

    def one_block(accumulated, pair_item):
        query_block, grad_block = pair_item
        scores = jnp.dot(query_block, key_rows.T, preferred_element_type=jnp.float32) * score_scale
        row_max = jnp.max(scores, axis=1, keepdims=True)
        probs = jnp.exp(scores - row_max)
        probs = probs / jnp.sum(probs, axis=1, keepdims=True)
        probs_low = probs.astype(jnp.bfloat16)
        out_rows = jnp.dot(probs_low, value_rows, preferred_element_type=jnp.float32).astype(
            jnp.bfloat16
        )
        prob_grad = jnp.dot(grad_block, value_rows.T, preferred_element_type=jnp.float32)
        row_dot = jnp.sum(
            grad_block.astype(jnp.float32) * out_rows.astype(jnp.float32), axis=1, keepdims=True
        )
        score_grad = (probs * (prob_grad - row_dot)).astype(jnp.bfloat16)
        query_grad = (
            jnp.dot(score_grad, key_rows, preferred_element_type=jnp.float32) * score_scale
        ).astype(jnp.bfloat16)
        key_grad = (
            accumulated[0]
            + jnp.dot(score_grad.T, query_block, preferred_element_type=jnp.float32) * score_scale
        )
        value_grad = accumulated[1] + jnp.dot(
            probs_low.T, grad_block, preferred_element_type=jnp.float32
        )
        return ((key_grad, value_grad), (query_grad, out_rows))

    empty = jnp.zeros((key_rows.shape[0], HD), jnp.float32)
    (key_grad, value_grad), (query_grad, out_rows) = lax.scan(
        one_block, (empty, empty), (query_blocks, grad_blocks)
    )
    return (
        query_grad.reshape(query_count, HD),
        out_rows.reshape(query_count, HD),
        key_grad,
        value_grad,
    )


def local_general(q_img, k_img, v_img, k_txt, v_txt, out_weight, d_out):
    rows_here = q_img.shape[0]
    heads_here = q_img.shape[1] // HD
    seq_count = lax.axis_size("seq")
    share_count = seq_count // heads_here
    part_rows = rows_here // share_count
    seq_index = lax.axis_index("seq")
    head_index = seq_index // share_count
    column_cut = d_out
    attn_grad = jnp.dot(
        column_cut,
        lax.all_gather(out_weight, "seq", axis=0, tiled=True),
        preferred_element_type=jnp.float32,
    ).astype(jnp.bfloat16)

    def to_heads(array_in):
        shaped = array_in.reshape(share_count, part_rows, heads_here, HD).transpose(2, 0, 1, 3)
        return shaped.reshape(seq_count, part_rows, HD)

    def whole_heads(array_in):
        shaped = array_in.reshape(rows_here, heads_here, HD).transpose(1, 0, 2)
        shaped = jnp.broadcast_to(shaped[:, None], (heads_here, share_count, rows_here, HD))
        return shaped.reshape(seq_count, rows_here, HD)

    def from_heads(array_in):
        shaped = array_in.reshape(heads_here, share_count, part_rows, HD).transpose(1, 2, 0, 3)
        return shaped.reshape(rows_here, heads_here * HD)

    text_keys = lax.dynamic_slice_in_dim(k_txt, head_index * HD, HD, 1)
    text_values = lax.dynamic_slice_in_dim(v_txt, head_index * HD, HD, 1)
    query_side = jnp.concatenate([to_heads(q_img), to_heads(attn_grad)], axis=2)
    key_side = jnp.concatenate([whole_heads(k_img), whole_heads(v_img)], axis=2)
    packed = jnp.concatenate([query_side, key_side], axis=1)
    received = lax.all_to_all(packed, "seq", split_axis=0, concat_axis=0, tiled=True)
    queries = received[:, :part_rows, :HD].reshape(seq_count * part_rows, HD)
    cotangents = received[:, :part_rows, HD:].reshape(seq_count * part_rows, HD)
    image_keys = received[:, part_rows:, :HD].reshape(seq_count * rows_here, HD)
    image_values = received[:, part_rows:, HD:].reshape(seq_count * rows_here, HD)
    key_rows = jnp.concatenate([image_keys, text_keys], axis=0)
    value_rows = jnp.concatenate([image_values, text_values], axis=0)
    query_grad, out_rows, key_grad, value_grad = attend(
        queries, cotangents, key_rows, value_rows, min(512, queries.shape[0])
    )
    image_count = image_keys.shape[0]
    query_part = (
        jnp.concatenate([query_grad, out_rows], axis=1)
        .astype(jnp.float32)
        .reshape(seq_count, part_rows, 2 * HD)
    )
    key_part = jnp.concatenate([key_grad[:image_count], value_grad[:image_count]], axis=1).reshape(
        seq_count, rows_here, 2 * HD
    )
    returned = lax.all_to_all(
        jnp.concatenate([query_part, key_part], axis=1).astype(jnp.bfloat16),
        "seq",
        split_axis=0,
        concat_axis=0,
        tiled=True,
    ).astype(jnp.float32)
    q_grad = from_heads(returned[:, :part_rows, :HD]).astype(jnp.bfloat16)
    out_tok = from_heads(returned[:, :part_rows, HD:]).astype(jnp.bfloat16)
    summed = jnp.sum(
        returned[:, part_rows:, :].reshape(heads_here, share_count, rows_here, 2 * HD), axis=1
    )
    summed = summed.transpose(1, 0, 2)
    k_grad = summed[:, :, :HD].reshape(rows_here, heads_here * HD).astype(jnp.bfloat16)
    v_grad = summed[:, :, HD:].reshape(rows_here, heads_here * HD).astype(jnp.bfloat16)
    column_cut = d_out
    d_weight = lax.psum_scatter(
        jnp.dot(column_cut.T, out_tok, preferred_element_type=jnp.float32).astype(jnp.bfloat16),
        "seq",
        scatter_dimension=0,
        tiled=True,
    ).astype(jnp.float32)
    return (q_grad, k_grad, v_grad, d_weight)


def call(kernel, outs, args, specs=None, scratch=(), scalars=0, out_specs=None, flops=0, moved=0, limit=LIMIT):
    vmem = pl.BlockSpec(memory_space=pltpu.VMEM)
    if specs is None:
        specs = [vmem] * (len(args) - scalars)
    if out_specs is None:
        out_specs = [vmem] * len(outs)
    return pl.pallas_call(
        kernel,
        out_shape=outs,
        grid_spec=pltpu.PrefetchScalarGridSpec(
            num_scalar_prefetch=scalars,
            grid=(1,),
            in_specs=specs,
            out_specs=out_specs,
            scratch_shapes=list(scratch),
        ),
        compiler_params=pltpu.CompilerParams(vmem_limit_bytes=limit),
        cost_estimate=pl.CostEstimate(flops=flops, bytes_accessed=moved, transcendentals=0),
    )(*args)


STEPS = (0, 2, 4, 6)


def head_columns(step, other_row):
    return pl.ds(pl.multiple_of(jnp.bitwise_xor(lax.axis_index("seq"), step + other_row) * HD, HD), HD)


def pack_kernel(me_ref, q_ref, k_ref, v_ref, kt_ref, vt_ref, tok_ref, text_ref):
    rows = q_ref.shape[0]
    for h in range(tok_ref.shape[0]):
        for i, ref in enumerate((q_ref, k_ref, v_ref)):
            tok_ref[h, i * rows : (i + 1) * rows, :] = ref[:, h * HD : (h + 1) * HD]
    text_ref[0] = kt_ref[...]
    text_ref[1] = vt_ref[...]


def query_order(n):
    y = lax.rem(lax.axis_index("seq"), 2)
    return [2 * z + y for z in range(n // 2)] + [2 * z + 1 - y for z in range(n // 2)]


def forward_kernel(tok_ref, text_ref, probs_ref, out_ref, queries_ref, keys_t_ref, vals_ref, keys, vals_t, *, chunk):
    n, three, _ = tok_ref.shape
    rows = three // 3
    image = n * rows
    text = text_ref.shape[1]
    for i, source in enumerate(query_order(n)):
        queries_ref[i * rows : (i + 1) * rows, :] = tok_ref[source, 0:rows, :]
    keys[0:image, :] = tok_ref[:, rows : 2 * rows, :].reshape(image, HD)
    keys[image : image + text, :] = text_ref[0]
    vals_ref[0:image, :] = tok_ref[:, 2 * rows : 3 * rows, :].reshape(image, HD)
    vals_ref[image : image + text, :] = text_ref[1]
    keys_t_ref[...] = keys[...].T
    vals_t[...] = vals_ref[...].T
    factor = HD ** (-0.5) * math.log2(math.e)
    for c in range(image // chunk):
        span = slice(c * chunk, (c + 1) * chunk)
        scores = lax.dot_general(keys[...], queries_ref[span, :], NT, preferred_element_type=F32)
        top = jnp.max(scores, axis=0, keepdims=True)
        weights = jnp.exp2((scores - top) * factor)
        total = jnp.sum(weights, axis=0, keepdims=True)
        low = (weights * (1.0 / total)).astype(BF16)
        probs_ref[:, span] = low
        out_ref[:, span] = jnp.dot(vals_t[...], low, preferred_element_type=F32).astype(BF16)


def place_rows(piece_ref, swapped_ref, cot, start):
    me = lax.axis_index("seq")
    core = lax.axis_index("fsdp")
    part = piece_ref.shape[0] // len(STEPS)
    for piece, shift in ((piece_ref, core), (swapped_ref, 1 - core)):
        for i, step in enumerate(STEPS):
            z = jnp.bitwise_xor(me, step) // 2
            at = pl.multiple_of(start + z * (2 * part) + shift * part, 16)
            cot[pl.ds(at, part), :] = piece[i * part : (i + 1) * part, :]


def partial_kernel(piece_ref, swapped_ref, own_ref, other_ref, mine_ref, near_ref, far_ref, send_ref, cot, weight):
    place_rows(piece_ref, swapped_ref, cot, 0)
    me = lax.axis_index("seq")
    depth = own_ref.shape[0]
    y = lax.rem(me, 2)
    weight[pl.ds(pl.multiple_of(y * depth, 16), depth), :] = own_ref[...]
    weight[pl.ds(pl.multiple_of((1 - y) * depth, 16), depth), :] = other_ref[...]
    for step, ref in zip(STEPS, (mine_ref, near_ref, far_ref, send_ref)):
        z = jnp.bitwise_xor(me, step) // 2
        cols = pl.ds(pl.multiple_of(z * 2 * HD, 2 * HD), 2 * HD)
        ref[...] = jnp.dot(cot[...], weight[:, cols], preferred_element_type=F32).astype(ref.dtype)


def add_kernel(kept_ref, received_ref, out_ref):
    out_ref[...] = (kept_ref[...] + received_ref[...].astype(F32)).astype(BF16)


def finish_kernel(mine_ref, near_ref, far_ref, kept_ref, give_ref):
    heads = mine_ref[...] + near_ref[...].astype(F32) + far_ref[...].astype(F32)
    first, second = heads[:, :HD].astype(BF16), heads[:, HD:].astype(BF16)
    first_row = lax.rem(lax.axis_index("seq"), 2) == 0
    kept_ref[...] = jnp.where(first_row, first, second)
    give_ref[...] = jnp.where(first_row, second, first)


def weight_grad_kernel(*refs):
    *pieces, out0, out1, out2, out3, own_ref, other_ref, cot, outs = refs
    tokens = cot.shape[0]
    place_rows(pieces[0], pieces[1], cot, 0)
    place_rows(pieces[2], pieces[3], cot, tokens // 2)
    for i, ref in enumerate((out0, out1, out2, out3)):
        outs[i * HD : (i + 1) * HD, :] = ref[...]
    depth = own_ref.shape[1]
    y = lax.rem(lax.axis_index("seq"), 2)
    for ref, row in ((own_ref, y), (other_ref, 1 - y)):
        cols = pl.ds(pl.multiple_of(row * depth, HD), depth)
        ref[...] = jnp.dot(outs[...], cot[:, cols], preferred_element_type=F32).astype(BF16)


def backward_kernel(queries_ref, keys_t_ref, vals_ref, probs_ref, out_ref, *refs, chunk):
    *grad_refs, send_ref, dk, dv = refs
    n, three, _ = send_ref.shape
    rows = three // 3
    image = n * rows
    scale = HD ** (-0.5)
    per = chunk // rows
    order = query_order(n)
    half = image // chunk // 2
    for c in range(image // chunk):
        span = slice(c * chunk, (c + 1) * chunk)
        within = slice(c % half * chunk, (c % half + 1) * chunk)
        grads = grad_refs[c // half][within, :]
        row_dot = jnp.sum(
            grads.astype(F32).T * out_ref[:, span].astype(F32), axis=0, keepdims=True
        )
        prob_grad = lax.dot_general(vals_ref[...], grads, NT, preferred_element_type=F32)
        low = probs_ref[:, span]
        score_grad = (low.astype(F32) * (prob_grad - row_dot)).astype(BF16)
        dq = (jnp.dot(keys_t_ref[...], score_grad, preferred_element_type=F32) * scale).T.astype(BF16)
        for i in range(per):
            send_ref[order[c * per + i], 0:rows, :] = dq[i * rows : (i + 1) * rows, :]
        dk_part = jnp.dot(score_grad[0:image, :], queries_ref[span, :], preferred_element_type=F32)
        dv_part = jnp.dot(low[0:image, :], grads, preferred_element_type=F32)
        if c == 0:
            dk[...] = dk_part
            dv[...] = dv_part
        else:
            dk[...] += dk_part
            dv[...] += dv_part
    send_ref[:, rows : 2 * rows, :] = (dk[...] * scale).astype(BF16).reshape(n, rows, HD)
    send_ref[:, 2 * rows : 3 * rows, :] = dv[...].astype(BF16).reshape(n, rows, HD)


def unpack_kernel(tok_ref, q_ref, k_ref, v_ref):
    rows = q_ref.shape[0]
    for h in range(tok_ref.shape[0]):
        for i, ref in enumerate((q_ref, k_ref, v_ref)):
            ref[:, h * HD : (h + 1) * HD] = tok_ref[h, i * rows : (i + 1) * rows, :]


def unpack_weight_kernel(own_ref, other_ref, w_ref):
    for other_row, ref in enumerate((own_ref, other_ref)):
        for i, step in enumerate(STEPS):
            w_ref[:, head_columns(step, other_row)] = ref[i * HD : (i + 1) * HD, :].astype(F32).T


def exchange(array, distance=0, cores=False):
    if not distance and not cores:
        return array
    size = 2 * lax.axis_size("seq")
    pairs = [(i, i ^ (2 * distance + int(cores))) for i in range(size)]
    return lax.ppermute(array, ("seq", "fsdp"), pairs)


def send_cotangents(d_out):
    rows, width = d_out.shape
    part, columns = rows // 2, width // len(STEPS)
    z = lax.axis_index("seq") // 2
    first = lax.axis_index("fsdp") * part
    return [
        exchange(lax.dynamic_slice(d_out, (first, (z ^ (step // 2)) * columns), (part, columns)), step)
        for step in STEPS
    ]


def local(q_img, k_img, v_img, k_txt, v_txt, out_weight, d_out):
    n = lax.axis_size("seq")
    rows, width = q_img.shape
    args = (q_img, k_img, v_img, k_txt, v_txt, out_weight, d_out)
    if n != 2 * len(STEPS) or width // HD != n or lax.axis_size("fsdp") != 2 or rows % 32:
        return local_general(*args)
    depth = out_weight.shape[0]
    image = n * rows
    text = k_txt.shape[0]
    total = image + text
    chunk = 2 * rows
    shape = jax.ShapeDtypeStruct
    vmem = pl.BlockSpec(memory_space=pltpu.VMEM)

    head = pl.BlockSpec((text, HD), lambda i, me_ref: (0, me_ref[0]))
    given = exchange(out_weight, 1)
    along = send_cotangents(d_out)
    tok_out, text_head = call(
        pack_kernel,
        [shape((n, 3 * rows, HD), BF16), shape((2, text, HD), BF16)],
        [lax.axis_index("seq").astype(jnp.int32)[None], q_img, k_img, v_img, k_txt, v_txt],
        specs=[vmem] * 3 + [head] * 2,
        scalars=1,
        moved=4 * 3 * rows * width,
        limit=60 * 1024 * 1024,
    )
    tok_out, along = lax.optimization_barrier((tok_out, along))
    along, given = lax.optimization_barrier((along, given))
    row = jnp.concatenate(along, axis=0)
    row_swapped = exchange(row, cores=True)
    tok_in = lax.all_to_all(tok_out, "seq", split_axis=0, concat_axis=0, tiled=True)

    probs, out_t, queries, keys_t, vals = call(
        functools.partial(forward_kernel, chunk=chunk),
        [shape(dims, BF16) for dims in ((total, image), (HD, image), (image, HD), (HD, total), (total, HD))],
        [tok_in, text_head],
        scratch=[pltpu.VMEM((total, HD), BF16), pltpu.VMEM((HD, total), BF16)],
        flops=4 * total * image * HD,
        moved=4 * total * image,
    )
    columns = row.shape[1]
    mine, near, far, send = call(
        partial_kernel,
        [shape((image // 2, 2 * HD), kind) for kind in (F32, BF16, F32, BF16)],
        [row, row_swapped, out_weight, given],
        scratch=[pltpu.VMEM((image // 2, columns), BF16), pltpu.VMEM((columns, width), BF16)],
        flops=8 * image * columns * HD,
        moved=2 * image * columns,
    )
    send, near = lax.optimization_barrier((exchange(send, 2), near))
    (far,) = call(add_kernel, [shape(far.shape, BF16)], [far, send])
    row, far = lax.optimization_barrier((row, far))
    far, near, other_row = exchange(far, 4), exchange(near, 2), exchange(row, 1)
    out_near, out_far = exchange(out_t, 2), exchange(out_t, 4)
    far, near, other_row = lax.optimization_barrier((far, near, other_row))
    kept, give = call(finish_kernel, [shape((image // 2, HD), BF16)] * 2, [mine, near, far])
    got = exchange(give, 1)
    other_swapped = exchange(other_row, cores=True)
    (grad_out,) = call(
        functools.partial(backward_kernel, chunk=chunk),
        [shape((n, 3 * rows, HD), BF16)],
        [queries, keys_t, vals, probs, out_t, kept, got],
        scratch=[pltpu.VMEM((image, HD), F32), pltpu.VMEM((image, HD), F32)],
    )
    grad_in = lax.all_to_all(grad_out, "seq", split_axis=0, concat_axis=0, tiled=True)
    out_far, out_near, _ = lax.optimization_barrier((out_far, out_near, grad_out))
    outs = [out_t, out_near, out_far, exchange(out_far, 2)]
    dw_own, dw_other = call(
        weight_grad_kernel,
        [shape((4 * HD, depth), BF16)] * 2,
        [row, row_swapped, other_row, other_swapped, *outs],
        scratch=[pltpu.VMEM((image, columns), BF16), pltpu.VMEM((4 * HD, image), BF16)],
        flops=96 * image * columns * HD,
        moved=2 * image * columns,
    )
    grads = call(
        unpack_kernel,
        [shape((rows, width), BF16)] * 3,
        [grad_in],
        moved=4 * 3 * rows * width,
    )
    dw_other, *grads = lax.optimization_barrier((exchange(dw_other, 1), *grads))
    (d_weight,) = call(
        unpack_weight_kernel,
        [shape((depth, width), F32)],
        [dw_own, dw_other],
        moved=6 * depth * width,
    )
    return (*grads, d_weight)


def solution(mesh):
    in_specs = (
        P(("group", "seq"), "fsdp"),
        P(("group", "seq"), "fsdp"),
        P(("group", "seq"), "fsdp"),
        P("group", "fsdp"),
        P("group", "fsdp"),
        P("seq", "fsdp"),
        P(("group", "seq"), None),
    )
    out_specs = (
        P(("group", "seq"), "fsdp"),
        P(("group", "seq"), "fsdp"),
        P(("group", "seq"), "fsdp"),
        P(("group", "seq"), "fsdp"),
    )
    return jax.shard_map(local, mesh=mesh, in_specs=in_specs, out_specs=out_specs, check_vma=False)
```

```python
import functools
import math

import jax
import jax.numpy as jnp
from jax import lax
from jax.experimental import pallas as pl
from jax.experimental.pallas import tpu as pltpu
from jax.sharding import PartitionSpec as P

HD = 128
F32 = jnp.float32
BF16 = jnp.bfloat16
LIMIT = 16 * 1024 * 1024
NT = (((1,), (1,)), ((), ()))


def attend(queries, cotangents, key_rows, value_rows, block_rows):
    score_scale = HD ** (-0.5)
    query_count = queries.shape[0]
    block_count = query_count // block_rows
    query_blocks = queries.reshape(block_count, block_rows, HD)
    grad_blocks = cotangents.reshape(block_count, block_rows, HD)

    def one_block(accumulated, pair_item):
        query_block, grad_block = pair_item
        scores = jnp.dot(query_block, key_rows.T, preferred_element_type=jnp.float32) * score_scale
        row_max = jnp.max(scores, axis=1, keepdims=True)
        probs = jnp.exp(scores - row_max)
        probs = probs / jnp.sum(probs, axis=1, keepdims=True)
        probs_low = probs.astype(jnp.bfloat16)
        out_rows = jnp.dot(probs_low, value_rows, preferred_element_type=jnp.float32).astype(
            jnp.bfloat16
        )
        prob_grad = jnp.dot(grad_block, value_rows.T, preferred_element_type=jnp.float32)
        row_dot = jnp.sum(
            grad_block.astype(jnp.float32) * out_rows.astype(jnp.float32), axis=1, keepdims=True
        )
        score_grad = (probs * (prob_grad - row_dot)).astype(jnp.bfloat16)
        query_grad = (
            jnp.dot(score_grad, key_rows, preferred_element_type=jnp.float32) * score_scale
        ).astype(jnp.bfloat16)
        key_grad = (
            accumulated[0]
            + jnp.dot(score_grad.T, query_block, preferred_element_type=jnp.float32) * score_scale
        )
        value_grad = accumulated[1] + jnp.dot(
            probs_low.T, grad_block, preferred_element_type=jnp.float32
        )
        return ((key_grad, value_grad), (query_grad, out_rows))

    empty = jnp.zeros((key_rows.shape[0], HD), jnp.float32)
    (key_grad, value_grad), (query_grad, out_rows) = lax.scan(
        one_block, (empty, empty), (query_blocks, grad_blocks)
    )
    return (
        query_grad.reshape(query_count, HD),
        out_rows.reshape(query_count, HD),
        key_grad,
        value_grad,
    )


def local_general(q_img, k_img, v_img, k_txt, v_txt, out_weight, d_out):
    rows_here = q_img.shape[0]
    heads_here = q_img.shape[1] // HD
    seq_count = lax.axis_size("seq")
    share_count = seq_count // heads_here
    part_rows = rows_here // share_count
    seq_index = lax.axis_index("seq")
    head_index = seq_index // share_count
    column_cut = d_out
    attn_grad = jnp.dot(
        column_cut,
        lax.all_gather(out_weight, "seq", axis=0, tiled=True),
        preferred_element_type=jnp.float32,
    ).astype(jnp.bfloat16)

    def to_heads(array_in):
        shaped = array_in.reshape(share_count, part_rows, heads_here, HD).transpose(2, 0, 1, 3)
        return shaped.reshape(seq_count, part_rows, HD)

    def whole_heads(array_in):
        shaped = array_in.reshape(rows_here, heads_here, HD).transpose(1, 0, 2)
        shaped = jnp.broadcast_to(shaped[:, None], (heads_here, share_count, rows_here, HD))
        return shaped.reshape(seq_count, rows_here, HD)

    def from_heads(array_in):
        shaped = array_in.reshape(heads_here, share_count, part_rows, HD).transpose(1, 2, 0, 3)
        return shaped.reshape(rows_here, heads_here * HD)

    text_keys = lax.dynamic_slice_in_dim(k_txt, head_index * HD, HD, 1)
    text_values = lax.dynamic_slice_in_dim(v_txt, head_index * HD, HD, 1)
    query_side = jnp.concatenate([to_heads(q_img), to_heads(attn_grad)], axis=2)
    key_side = jnp.concatenate([whole_heads(k_img), whole_heads(v_img)], axis=2)
    packed = jnp.concatenate([query_side, key_side], axis=1)
    received = lax.all_to_all(packed, "seq", split_axis=0, concat_axis=0, tiled=True)
    queries = received[:, :part_rows, :HD].reshape(seq_count * part_rows, HD)
    cotangents = received[:, :part_rows, HD:].reshape(seq_count * part_rows, HD)
    image_keys = received[:, part_rows:, :HD].reshape(seq_count * rows_here, HD)
    image_values = received[:, part_rows:, HD:].reshape(seq_count * rows_here, HD)
    key_rows = jnp.concatenate([image_keys, text_keys], axis=0)
    value_rows = jnp.concatenate([image_values, text_values], axis=0)
    query_grad, out_rows, key_grad, value_grad = attend(
        queries, cotangents, key_rows, value_rows, min(512, queries.shape[0])
    )
    image_count = image_keys.shape[0]
    query_part = (
        jnp.concatenate([query_grad, out_rows], axis=1)
        .astype(jnp.float32)
        .reshape(seq_count, part_rows, 2 * HD)
    )
    key_part = jnp.concatenate([key_grad[:image_count], value_grad[:image_count]], axis=1).reshape(
        seq_count, rows_here, 2 * HD
    )
    returned = lax.all_to_all(
        jnp.concatenate([query_part, key_part], axis=1).astype(jnp.bfloat16),
        "seq",
        split_axis=0,
        concat_axis=0,
        tiled=True,
    ).astype(jnp.float32)
    q_grad = from_heads(returned[:, :part_rows, :HD]).astype(jnp.bfloat16)
    out_tok = from_heads(returned[:, :part_rows, HD:]).astype(jnp.bfloat16)
    summed = jnp.sum(
        returned[:, part_rows:, :].reshape(heads_here, share_count, rows_here, 2 * HD), axis=1
    )
    summed = summed.transpose(1, 0, 2)
    k_grad = summed[:, :, :HD].reshape(rows_here, heads_here * HD).astype(jnp.bfloat16)
    v_grad = summed[:, :, HD:].reshape(rows_here, heads_here * HD).astype(jnp.bfloat16)
    column_cut = d_out
    d_weight = lax.psum_scatter(
        jnp.dot(column_cut.T, out_tok, preferred_element_type=jnp.float32).astype(jnp.bfloat16),
        "seq",
        scatter_dimension=0,
        tiled=True,
    ).astype(jnp.float32)
    return (q_grad, k_grad, v_grad, d_weight)


def call(kernel, outs, args, specs=None, scratch=(), scalars=0, out_specs=None, flops=0, moved=0, limit=LIMIT):
    vmem = pl.BlockSpec(memory_space=pltpu.VMEM)
    if specs is None:
        specs = [vmem] * (len(args) - scalars)
    if out_specs is None:
        out_specs = [vmem] * len(outs)
    return pl.pallas_call(
        kernel,
        out_shape=outs,
        grid_spec=pltpu.PrefetchScalarGridSpec(
            num_scalar_prefetch=scalars,
            grid=(1,),
            in_specs=specs,
            out_specs=out_specs,
            scratch_shapes=list(scratch),
        ),
        compiler_params=pltpu.CompilerParams(vmem_limit_bytes=limit),
        cost_estimate=pl.CostEstimate(flops=flops, bytes_accessed=moved, transcendentals=0),
    )(*args)


STEPS = (0, 2, 4, 6)


def head_columns(step, other_row):
    return pl.ds(pl.multiple_of(jnp.bitwise_xor(lax.axis_index("seq"), step + other_row) * HD, HD), HD)


def pack_kernel(me_ref, q_ref, k_ref, v_ref, kt_ref, vt_ref, tok_ref, text_ref):
    rows = q_ref.shape[0]
    for h in range(tok_ref.shape[0]):
        for i, ref in enumerate((q_ref, k_ref, v_ref)):
            tok_ref[h, i * rows : (i + 1) * rows, :] = ref[:, h * HD : (h + 1) * HD]
    text_ref[0] = kt_ref[...]
    text_ref[1] = vt_ref[...]


def query_order(n):
    y = lax.rem(lax.axis_index("seq"), 2)
    return [2 * z + y for z in range(n // 2)] + [2 * z + 1 - y for z in range(n // 2)]


def forward_kernel(tok_ref, text_ref, probs_ref, out_ref, queries_ref, keys_t_ref, vals_ref, keys, vals_t, *, chunk):
    n, three, _ = tok_ref.shape
    rows = three // 3
    image = n * rows
    text = text_ref.shape[1]
    for i, source in enumerate(query_order(n)):
        queries_ref[i * rows : (i + 1) * rows, :] = tok_ref[source, 0:rows, :]
    keys[0:image, :] = tok_ref[:, rows : 2 * rows, :].reshape(image, HD)
    keys[image : image + text, :] = text_ref[0]
    vals_ref[0:image, :] = tok_ref[:, 2 * rows : 3 * rows, :].reshape(image, HD)
    vals_ref[image : image + text, :] = text_ref[1]
    keys_t_ref[...] = keys[...].T
    vals_t[...] = vals_ref[...].T
    factor = HD ** (-0.5) * math.log2(math.e)
    for c in range(image // chunk):
        span = slice(c * chunk, (c + 1) * chunk)
        scores = lax.dot_general(keys[...], queries_ref[span, :], NT, preferred_element_type=F32)
        top = jnp.max(scores, axis=0, keepdims=True)
        weights = jnp.exp2((scores - top) * factor)
        total = jnp.sum(weights, axis=0, keepdims=True)
        low = (weights * (1.0 / total)).astype(BF16)
        probs_ref[:, span] = low
        out_ref[:, span] = jnp.dot(vals_t[...], low, preferred_element_type=F32).astype(BF16)


def place_rows(piece_ref, swapped_ref, cot, start):
    me = lax.axis_index("seq")
    core = lax.axis_index("fsdp")
    part = piece_ref.shape[0] // len(STEPS)
    for piece, shift in ((piece_ref, core), (swapped_ref, 1 - core)):
        for i, step in enumerate(STEPS):
            z = jnp.bitwise_xor(me, step) // 2
            at = pl.multiple_of(start + z * (2 * part) + shift * part, 16)
            cot[pl.ds(at, part), :] = piece[i * part : (i + 1) * part, :]


def partial_kernel(piece_ref, swapped_ref, own_ref, other_ref, mine_ref, near_ref, far_ref, send_ref, cot, weight):
    place_rows(piece_ref, swapped_ref, cot, 0)
    me = lax.axis_index("seq")
    depth = own_ref.shape[0]
    y = lax.rem(me, 2)
    weight[pl.ds(pl.multiple_of(y * depth, 16), depth), :] = own_ref[...]
    weight[pl.ds(pl.multiple_of((1 - y) * depth, 16), depth), :] = other_ref[...]
    for step, ref in zip(STEPS, (mine_ref, near_ref, far_ref, send_ref)):
        z = jnp.bitwise_xor(me, step) // 2
        cols = pl.ds(pl.multiple_of(z * 2 * HD, 2 * HD), 2 * HD)
        ref[...] = jnp.dot(cot[...], weight[:, cols], preferred_element_type=F32).astype(ref.dtype)


def add_kernel(kept_ref, received_ref, out_ref):
    out_ref[...] = (kept_ref[...] + received_ref[...].astype(F32)).astype(BF16)


def finish_kernel(mine_ref, near_ref, far_ref, kept_ref, give_ref):
    heads = mine_ref[...] + near_ref[...].astype(F32) + far_ref[...].astype(F32)
    first, second = heads[:, :HD].astype(BF16), heads[:, HD:].astype(BF16)
    first_row = lax.rem(lax.axis_index("seq"), 2) == 0
    kept_ref[...] = jnp.where(first_row, first, second)
    give_ref[...] = jnp.where(first_row, second, first)


def weight_grad_kernel(*refs):
    *pieces, out0, out1, out2, out3, own_ref, other_ref, cot, outs = refs
    tokens = cot.shape[0]
    place_rows(pieces[0], pieces[1], cot, 0)
    place_rows(pieces[2], pieces[3], cot, tokens // 2)
    for i, ref in enumerate((out0, out1, out2, out3)):
        outs[i * HD : (i + 1) * HD, :] = ref[...]
    depth = own_ref.shape[1]
    y = lax.rem(lax.axis_index("seq"), 2)
    for ref, row in ((own_ref, y), (other_ref, 1 - y)):
        cols = pl.ds(pl.multiple_of(row * depth, HD), depth)
        ref[...] = jnp.dot(outs[...], cot[:, cols], preferred_element_type=F32).astype(BF16)


def backward_kernel(queries_ref, keys_t_ref, vals_ref, probs_ref, out_ref, *refs, chunk):
    *grad_refs, send_ref, dk, dv = refs
    n, three, _ = send_ref.shape
    rows = three // 3
    image = n * rows
    scale = HD ** (-0.5)
    per = chunk // rows
    order = query_order(n)
    half = image // chunk // 2
    for c in range(image // chunk):
        span = slice(c * chunk, (c + 1) * chunk)
        within = slice(c % half * chunk, (c % half + 1) * chunk)
        grads = grad_refs[c // half][within, :]
        row_dot = jnp.sum(
            grads.astype(F32).T * out_ref[:, span].astype(F32), axis=0, keepdims=True
        )
        prob_grad = lax.dot_general(vals_ref[...], grads, NT, preferred_element_type=F32)
        low = probs_ref[:, span]
        score_grad = (low.astype(F32) * (prob_grad - row_dot)).astype(BF16)
        dq = (jnp.dot(keys_t_ref[...], score_grad, preferred_element_type=F32) * scale).T.astype(BF16)
        for i in range(per):
            send_ref[order[c * per + i], 0:rows, :] = dq[i * rows : (i + 1) * rows, :]
        dk_part = jnp.dot(score_grad[0:image, :], queries_ref[span, :], preferred_element_type=F32)
        dv_part = jnp.dot(low[0:image, :], grads, preferred_element_type=F32)
        if c == 0:
            dk[...] = dk_part
            dv[...] = dv_part
        else:
            dk[...] += dk_part
            dv[...] += dv_part
    send_ref[:, rows : 2 * rows, :] = (dk[...] * scale).astype(BF16).reshape(n, rows, HD)
    send_ref[:, 2 * rows : 3 * rows, :] = dv[...].astype(BF16).reshape(n, rows, HD)


def unpack_kernel(tok_ref, q_ref, k_ref, v_ref):
    rows = q_ref.shape[0]
    for h in range(tok_ref.shape[0]):
        for i, ref in enumerate((q_ref, k_ref, v_ref)):
            ref[:, h * HD : (h + 1) * HD] = tok_ref[h, i * rows : (i + 1) * rows, :]


def unpack_weight_kernel(own_ref, other_ref, w_ref):
    for other_row, ref in enumerate((own_ref, other_ref)):
        for i, step in enumerate(STEPS):
            w_ref[:, head_columns(step, other_row)] = ref[i * HD : (i + 1) * HD, :].T.astype(F32)


def exchange(array, distance=0, cores=False):
    if not distance and not cores:
        return array
    size = 2 * lax.axis_size("seq")
    pairs = [(i, i ^ (2 * distance + int(cores))) for i in range(size)]
    return lax.ppermute(array, ("seq", "fsdp"), pairs)


def send_cotangents(d_out):
    rows, width = d_out.shape
    part, columns = rows // 2, width // len(STEPS)
    z = lax.axis_index("seq") // 2
    first = lax.axis_index("fsdp") * part
    return [
        exchange(lax.dynamic_slice(d_out, (first, (z ^ (step // 2)) * columns), (part, columns)), step)
        for step in STEPS
    ]


def local(q_img, k_img, v_img, k_txt, v_txt, out_weight, d_out):
    n = lax.axis_size("seq")
    rows, width = q_img.shape
    args = (q_img, k_img, v_img, k_txt, v_txt, out_weight, d_out)
    if n != 2 * len(STEPS) or width // HD != n or lax.axis_size("fsdp") != 2 or rows % 32:
        return local_general(*args)
    depth = out_weight.shape[0]
    image = n * rows
    text = k_txt.shape[0]
    total = image + text
    chunk = 2 * rows
    shape = jax.ShapeDtypeStruct
    vmem = pl.BlockSpec(memory_space=pltpu.VMEM)

    head = pl.BlockSpec((text, HD), lambda i, me_ref: (0, me_ref[0]))
    given = exchange(out_weight, 1)
    along = send_cotangents(d_out)
    tok_out, text_head = call(
        pack_kernel,
        [shape((n, 3 * rows, HD), BF16), shape((2, text, HD), BF16)],
        [lax.axis_index("seq").astype(jnp.int32)[None], q_img, k_img, v_img, k_txt, v_txt],
        specs=[vmem] * 3 + [head] * 2,
        scalars=1,
        moved=4 * 3 * rows * width,
        limit=60 * 1024 * 1024,
    )
    tok_out, along = lax.optimization_barrier((tok_out, along))
    along, given = lax.optimization_barrier((along, given))
    row = jnp.concatenate(along, axis=0)
    row_swapped = exchange(row, cores=True)
    tok_in = lax.all_to_all(tok_out, "seq", split_axis=0, concat_axis=0, tiled=True)

    probs, out_t, queries, keys_t, vals = call(
        functools.partial(forward_kernel, chunk=chunk),
        [shape(dims, BF16) for dims in ((total, image), (HD, image), (image, HD), (HD, total), (total, HD))],
        [tok_in, text_head],
        scratch=[pltpu.VMEM((total, HD), BF16), pltpu.VMEM((HD, total), BF16)],
        flops=4 * total * image * HD,
        moved=4 * total * image,
    )
    columns = row.shape[1]
    mine, near, far, send = call(
        partial_kernel,
        [shape((image // 2, 2 * HD), kind) for kind in (F32, BF16, F32, BF16)],
        [row, row_swapped, out_weight, given],
        scratch=[pltpu.VMEM((image // 2, columns), BF16), pltpu.VMEM((columns, width), BF16)],
        flops=8 * image * columns * HD,
        moved=2 * image * columns,
    )
    send, near = lax.optimization_barrier((exchange(send, 2), near))
    (far,) = call(add_kernel, [shape(far.shape, BF16)], [far, send])
    row, far = lax.optimization_barrier((row, far))
    far, near, other_row = exchange(far, 4), exchange(near, 2), exchange(row, 1)
    out_near, out_far = exchange(out_t, 2), exchange(out_t, 4)
    far, near, other_row = lax.optimization_barrier((far, near, other_row))
    kept, give = call(finish_kernel, [shape((image // 2, HD), BF16)] * 2, [mine, near, far])
    got = exchange(give, 1)
    other_swapped = exchange(other_row, cores=True)
    (grad_out,) = call(
        functools.partial(backward_kernel, chunk=chunk),
        [shape((n, 3 * rows, HD), BF16)],
        [queries, keys_t, vals, probs, out_t, kept, got],
        scratch=[pltpu.VMEM((image, HD), F32), pltpu.VMEM((image, HD), F32)],
    )
    grad_in = lax.all_to_all(grad_out, "seq", split_axis=0, concat_axis=0, tiled=True)
    out_far, out_near, _ = lax.optimization_barrier((out_far, out_near, grad_out))
    outs = [out_t, out_near, out_far, exchange(out_far, 2)]
    dw_own, dw_other = call(
        weight_grad_kernel,
        [shape((4 * HD, depth), BF16)] * 2,
        [row, row_swapped, other_row, other_swapped, *outs],
        scratch=[pltpu.VMEM((image, columns), BF16), pltpu.VMEM((4 * HD, image), BF16)],
        flops=96 * image * columns * HD,
        moved=2 * image * columns,
    )
    grads = call(
        unpack_kernel,
        [shape((rows, width), BF16)] * 3,
        [grad_in],
        moved=4 * 3 * rows * width,
    )
    dw_other, *grads = lax.optimization_barrier((exchange(dw_other, 1), *grads))
    (d_weight,) = call(
        unpack_weight_kernel,
        [shape((depth, width), F32)],
        [dw_own, dw_other],
        moved=6 * depth * width,
    )
    return (*grads, d_weight)


def solution(mesh):
    in_specs = (
        P(("group", "seq"), "fsdp"),
        P(("group", "seq"), "fsdp"),
        P(("group", "seq"), "fsdp"),
        P("group", "fsdp"),
        P("group", "fsdp"),
        P("seq", "fsdp"),
        P(("group", "seq"), None),
    )
    out_specs = (
        P(("group", "seq"), "fsdp"),
        P(("group", "seq"), "fsdp"),
        P(("group", "seq"), "fsdp"),
        P(("group", "seq"), "fsdp"),
    )
    return jax.shard_map(local, mesh=mesh, in_specs=in_specs, out_specs=out_specs, check_vma=False)
```
